32 devices in a mesh: fsdp: 16 (over z, y, x), dp: 2 (over core).
Axes of the slice: x: 2, y: 2, z: 4, core: 2. Of those that a mesh axis runs over, the one named last changes fastest.
Arguments:
- inputs: bfloat16 [768, 256, 1024], P(('fsdp', 'dp')), may hold values from -6 to 6
- sides: int32 [768], P(('fsdp', 'dp')), may hold values from 0 to 2
- weight_one: bfloat16 [1024, 256], P('fsdp'), may hold values from -0.1875 to 0.1875
- weight_two: bfloat16 [1152, 512], P('fsdp'), may hold values from -0.1875 to 0.1875
- weight_three: bfloat16 [256, 1024], P('fsdp'), may hold values from -0.375 to 0.375
- fc_first: float32 [256, 128], replicated, may hold values from -0.375 to 0.375
- fc_second: float32 [128, 512], replicated, may hold values from -0.5 to 0.5
- fc_bias: float32 [512], replicated, may hold values from -3 to 3
- bn_gain: float32 [1920], replicated, may hold values from 0.25 to 1.75
- bn_shift: float32 [1920], replicated, may hold values from -3 to 3
- cotangent: bfloat16 [768, 256, 1024], P(('fsdp', 'dp')), may hold values from -6 to 6
Outputs:
- outputs: bfloat16 [768, 256, 1024], P(('fsdp', 'dp'))
- input_grad: bfloat16 [768, 256, 1024], P(('fsdp', 'dp'))
- weight_one_grad: float32 [1024, 256], P('fsdp')
- weight_two_grad: float32 [1152, 512], P('fsdp')
- weight_three_grad: float32 [256, 1024], P('fsdp')
- fc_first_grad: float32 [256, 128], replicated
- fc_second_grad: float32 [128, 512], replicated
- fc_bias_grad: float32 [512], replicated
- gain_grad: float32 [1920], replicated
- shift_grad: float32 [1920], replicated
The draws below stay inside these ranges and needn't reach their ends.
All inputs are finite; a program needn't handle non-finite values.
Results may differ from the reference program's by a relative error of at most 0.017.
Values may be sent and summed in bfloat16 or wider, within the bound.
No kernel may reach another device: no remote copies, remote signals or barrier semaphores. Data moves between devices by JAX's collectives and lax.ppermute only.
A program may use at most 384 MiB of HBM per device.

```python
import jax
import jax.numpy as jnp
from jax import lax

C_IN = 1024
WIDTH = 256
INTER = 128
SIDE_MAX = 16
PIXELS = 256
IMAGES = 768
TAP_ROWS = 1152
NORM_CHANNELS = 1920


def set_ends(array, own_key, least, top_value):
    place = [jax.random.randint(jax.random.fold_in(own_key, axis), (), 0, length) for axis, length in enumerate(array.shape)]
    longest = array.shape.index(max(array.shape))
    neighbour = place[:longest] + [(place[longest] + 1) % array.shape[longest]] + place[longest + 1:]
    return array.at[tuple(place)].set(least).at[tuple(neighbour)].set(top_value)


def steps_of(stream_key, extent, split, least, largest):
    def one(axis_at, blocks):
        draws = jax.random.uniform(jax.random.fold_in(jax.random.fold_in(stream_key, 6), axis_at), (blocks,), jnp.float32, least / len(split), largest / len(split))
        return jnp.repeat(jnp.exp(draws), extent[axis_at] // blocks).reshape((-1,) + (1,) * (len(extent) - axis_at - 1))

    loudness = one(*split[0])
    for cut in split[1:]:
        loudness = loudness * one(*cut)
    return loudness


def normal_values(rng, dims, spread, bound, cuts=(), held_as=jnp.bfloat16):
    values = jax.random.normal(rng, dims, jnp.float32) * spread
    if len(cuts) > 0:
        values = steps_of(rng, dims, cuts, -0.22, 0.18) * values
    return jnp.clip(values, min=-bound, max=bound).astype(held_as)


def setup_inputs(seed: int = 0) -> dict:
    streams_of = jax.random.split(jax.random.key(seed), 12)
    inputs = normal_values(streams_of[0], (IMAGES, PIXELS, C_IN), 1.0, 6.0, ((0, 32),))
    sides = set_ends(jax.random.randint(streams_of[1], (IMAGES,), 0, 3), jax.random.fold_in(streams_of[1], 1), 0, 2).astype(jnp.int32)
    weight_one = normal_values(streams_of[2], (C_IN, WIDTH), C_IN ** -0.5, 0.1875, ((0, 16),))
    weight_two = normal_values(streams_of[3], (TAP_ROWS, 2 * WIDTH), TAP_ROWS ** -0.5, 0.1875, ((0, 16),))
    weight_three = normal_values(streams_of[4], (WIDTH, C_IN), WIDTH ** -0.5, 0.375, ((0, 16),))
    fc_first = normal_values(streams_of[5], (WIDTH, INTER), WIDTH ** -0.5, 0.375, (), jnp.float32)
    fc_second = normal_values(streams_of[6], (INTER, 2 * WIDTH), INTER ** -0.5, 0.5, (), jnp.float32)
    fc_bias = normal_values(streams_of[7], (2 * WIDTH,), 0.5, 3.0, (), jnp.float32)
    bn_gain = jnp.clip(1.0 + 0.15 * jax.random.normal(streams_of[8], (NORM_CHANNELS,), jnp.float32), 0.25, 1.75)
    bn_shift = normal_values(streams_of[9], (NORM_CHANNELS,), 0.5, 3.0, (), jnp.float32)
    cotangent = normal_values(streams_of[10], (IMAGES, PIXELS, C_IN), 1.0, 6.0, ((0, 32),))
    return dict(inputs=inputs, sides=sides, weight_one=weight_one, weight_two=weight_two, weight_three=weight_three, fc_first=fc_first, fc_second=fc_second, fc_bias=fc_bias, bn_gain=bn_gain, bn_shift=bn_shift, cotangent=cotangent)


highest = lax.Precision.HIGHEST

@jax.custom_vjp
def low(v):
    return lax.optimization_barrier(v.astype(jnp.bfloat16)).astype(jnp.float32)

@jax.custom_vjp
def low_back(v):
    return v

def low_keep(v):
    return (low(v), None)

def low_pass(kept, grad):
    return (grad,)

def back_keep(v):
    return (v, None)

def back_low(kept, grad):
    return (low(grad),)
low.defvjp(low_keep, low_pass)
low_back.defvjp(back_keep, back_low)

def image_mask(sides):
    image_side = SIDE_MAX - 2 * sides
    position = jnp.arange(SIDE_MAX * SIDE_MAX)
    inside = (position[None, :] // SIDE_MAX < image_side[:, None]) & (position[None, :] % SIDE_MAX < image_side[:, None])
    return inside.astype(jnp.float32)

def batch_norm(values, weights_mask, norm_count, norm_gain, norm_shift):
    mean_value = lax.optimization_barrier(jnp.sum(values * weights_mask, axis=0)) / norm_count
    mean_square = lax.optimization_barrier(jnp.sum(values * values * weights_mask, axis=0)) / norm_count
    variance = mean_square - mean_value * mean_value
    return (values - mean_value) * lax.rsqrt(variance + 1e-05) * norm_gain + norm_shift

def gather_taps(act_grid, radix_part):
    half_width = WIDTH // 2
    padded = jnp.pad(act_grid[..., radix_part * half_width:(radix_part + 1) * half_width], ((0, 0), (1, 1), (1, 1), (0, 0)))
    pieces = [padded[:, row_off:row_off + SIDE_MAX, col_off:col_off + SIDE_MAX, :] for row_off in range(3) for col_off in range(3)]
    return jnp.concatenate(pieces, axis=-1).reshape(-1, 9 * half_width)

def forward(inputs, weight_one, weight_two, weight_three, fc_first, fc_second, fc_bias, bn_gain, bn_shift, pixel_mask):
    images = inputs.shape[0]
    rows_mask = pixel_mask.reshape(-1, 1)
    pixel_count = jnp.sum(pixel_mask)
    image_pixels = lax.optimization_barrier(jnp.sum(pixel_mask, axis=1, keepdims=True))
    flat_rows = inputs.reshape(-1, C_IN)
    first_conv = low_back(jnp.dot(flat_rows, weight_one, precision=highest))
    first_pre = batch_norm(first_conv, rows_mask, pixel_count, bn_gain[:WIDTH], bn_shift[:WIDTH])
    act_one = low(rows_mask * jax.nn.silu(first_pre))
    act_grid = act_one.reshape(images, SIDE_MAX, SIDE_MAX, WIDTH)
    second = low_back(jnp.concatenate([jnp.dot(gather_taps(act_grid, radix_part), weight_two[:, radix_part * WIDTH:(radix_part + 1) * WIDTH], precision=highest) for radix_part in range(2)], axis=1))
    second_pre = batch_norm(second, rows_mask, pixel_count, bn_gain[WIDTH:3 * WIDTH], bn_shift[WIDTH:3 * WIDTH])
    act_two = rows_mask * jax.nn.silu(second_pre)
    halves = act_two[:, :WIDTH] + act_two[:, WIDTH:]
    pooled = lax.optimization_barrier(jnp.sum(halves.reshape(images, SIDE_MAX * SIDE_MAX, WIDTH), axis=1)) / image_pixels
    pre_hidden = jnp.dot(pooled, fc_first, precision=highest)
    hidden_pre = batch_norm(pre_hidden, jnp.ones((images, 1), jnp.float32), float(images), bn_gain[3 * WIDTH:3 * WIDTH + INTER], bn_shift[3 * WIDTH:3 * WIDTH + INTER])
    logits = jnp.dot(jax.nn.silu(hidden_pre), fc_second, precision=highest) + fc_bias
    attention = jax.nn.softmax(logits.reshape(images, 2, WIDTH), axis=1)
    split_act = act_two.reshape(images, SIDE_MAX * SIDE_MAX, 2, WIDTH)
    combined = low(lax.optimization_barrier(jnp.sum(attention[:, None, :, :] * split_act, axis=2)).reshape(-1, WIDTH))
    third_conv = low_back(jnp.dot(combined, weight_three, precision=highest))
    offset = 3 * WIDTH + INTER
    third_pre = batch_norm(third_conv, rows_mask, pixel_count, bn_gain[offset:], bn_shift[offset:]) + flat_rows
    result = rows_mask * jax.nn.silu(third_pre)
    return result.reshape(inputs.shape)

def reference(inputs, sides, weight_one, weight_two, weight_three, fc_first, fc_second, fc_bias, bn_gain, bn_shift, cotangent):
    pixel_mask = image_mask(sides)
    floats = (inputs.astype(jnp.float32), weight_one.astype(jnp.float32), weight_two.astype(jnp.float32), weight_three.astype(jnp.float32), fc_first, fc_second, fc_bias, bn_gain, bn_shift)

    def apply_block(*operands):
        return forward(*operands, pixel_mask)
    result, pullback = jax.vjp(apply_block, *floats)
    grads = pullback(cotangent.astype(jnp.float32))
    return (result.astype(jnp.bfloat16), grads[0].astype(jnp.bfloat16), grads[1], grads[2], grads[3], grads[4], grads[5], grads[6], grads[7], grads[8])
```

```python
import functools

import jax
import jax.numpy as jnp
from jax import lax
from jax.experimental import pallas as pl
from jax.experimental.pallas import tpu as pltpu
from jax.sharding import PartitionSpec as P

C_IN = 1024
WIDTH = 256
INTER = 128
SIDE = 16
PIX = SIDE * SIDE
HALF = WIDTH // 2
EPS = 1e-05
AXES = ("fsdp", "dp")
HIGH = lax.Precision.HIGHEST
F32 = jnp.float32
BF16 = jnp.bfloat16
MIB = 1024 * 1024


def dot_f(left, right):
    return jnp.dot(left, right, preferred_element_type=F32)


def dot_rows(left, right):
    return lax.dot_general(left, right, (((0,), (0,)), ((), ())), preferred_element_type=F32)


def dot_last(left, right):
    return lax.dot_general(left, right, (((1,), (1,)), ((), ())), preferred_element_type=F32)


def high_f(left, right):
    return jnp.dot(left, right, preferred_element_type=F32, precision=HIGH)


def high_rows(left, right):
    return lax.dot_general(
        left, right, (((0,), (0,)), ((), ())), preferred_element_type=F32, precision=HIGH
    )


def high_last(left, right):
    return lax.dot_general(
        left, right, (((1,), (1,)), ((), ())), preferred_element_type=F32, precision=HIGH
    )


def pixel_mask(image_side, width):
    row = lax.broadcasted_iota(jnp.int32, (PIX, 128), 0)
    inside = ((row >> 4) < image_side) & ((row & 15) < image_side)
    return wide(jnp.where(inside, 1.0, 0.0).astype(F32), width)


def wide(mask, width):
    if width == 128:
        return mask
    return jnp.concatenate([mask] * (width // 128), axis=1)


def fold(values):
    rows, n = values.shape
    return jnp.sum(values.reshape(rows // 8, 8, n), axis=0)


def row_sum(values):
    return jnp.sum(values, axis=0, keepdims=True)


def total(payload_ref):
    return jnp.sum(payload_ref[...], axis=0)


def norm_terms(sums, count):
    mean = sums[0:1] / count
    variance = sums[1:2] / count - mean * mean
    return mean, lax.rsqrt(variance + EPS)


def send_rows(payload_ref, rows):
    block = jnp.concatenate(rows, axis=0)
    payload_ref[...] = jnp.broadcast_to(block[None], payload_ref.shape)


def silu_parts(half_pre):
    t = jnp.tanh(half_pre)
    a = 1.0 + t
    value = half_pre * a
    slope = 0.5 * a * (1.0 + half_pre * (1.0 - t))
    return value, slope


def whole(shape):
    zeros = (0,) * len(shape)
    return pl.BlockSpec(shape, lambda *_: zeros)


def rows_of(n_rows, width):
    return pl.BlockSpec((n_rows, width), lambda i: (i, 0))


SMEM_SPEC = pl.BlockSpec(memory_space=pltpu.SMEM)


def call(kernel, grid, ins, outs, scratch=(), vmem=48, flops=0, moved=0, name=None):
    return pl.pallas_call(
        kernel,
        grid=(grid,),
        in_specs=[spec for _, spec in ins],
        out_specs=[spec for _, _, spec in outs],
        out_shape=[jax.ShapeDtypeStruct(shape, dtype) for shape, dtype, _ in outs],
        scratch_shapes=list(scratch),
        compiler_params=pltpu.CompilerParams(
            dimension_semantics=("arbitrary",), vmem_limit_bytes=vmem * MIB
        ),
        cost_estimate=pl.CostEstimate(flops=flops, bytes_accessed=moved, transcendentals=0),
        name=name,
    )(*[array for array, _ in ins])


def conv_one_kernel(per, sides_ref, x_ref, w_ref, h_ref, send_ref, acc_ref, count_ref):
    step = pl.program_id(0)

    @pl.when(step == 0)
    def _():
        acc_ref[...] = jnp.zeros_like(acc_ref)
        count_ref[0] = 0.0

    h = dot_f(x_ref[...], w_ref[...])
    h_ref[...] = h
    for j in range(per):
        side = SIDE - 2 * sides_ref[step * per + j]
        mask = pixel_mask(side, WIDTH)
        one = h[j * PIX : (j + 1) * PIX]
        kept = one * mask
        acc_ref[0:8] += fold(kept)
        acc_ref[8:16] += fold(kept * one)
        count_ref[0] += (side * side).astype(F32)

    @pl.when(step == pl.num_programs(0) - 1)
    def _():
        count = jnp.full((1, WIDTH), count_ref[0], F32)
        send_rows(
            send_ref,
            [row_sum(acc_ref[0:8]), row_sum(acc_ref[8:16]), count, jnp.zeros((1, WIDTH), F32)],
        )


def conv_two_kernel(
    per, sides_ref, got_ref, h_ref, w_ref, gain_ref, shift_ref, hat_ref, h2_ref, send_ref,
    vec_ref, taps_ref, acc_ref,
):
    step = pl.program_id(0)

    @pl.when(step == 0)
    def _():
        sums = total(got_ref)
        mean, inv = norm_terms(sums, sums[2:3])
        vec_ref[0:1] = mean
        vec_ref[1:2] = inv
        acc_ref[...] = jnp.zeros_like(acc_ref)
        taps_ref[...] = jnp.zeros_like(taps_ref)

    gain = gain_ref[:, :WIDTH] * 0.5
    shift = shift_ref[:, :WIDTH] * 0.5
    column = lax.broadcasted_iota(jnp.int32, (PIX, 128), 0) & 15
    first = wide(jnp.where(column == 0, 0.0, 1.0).astype(F32), WIDTH)
    last = wide(jnp.where(column == 15, 0.0, 1.0).astype(F32), WIDTH)
    for j in range(per):
        side = SIDE - 2 * sides_ref[step * per + j]
        mask = pixel_mask(side, WIDTH)
        rows = pl.ds(j * PIX, PIX)
        hat = (h_ref[rows] - vec_ref[0:1]) * vec_ref[1:2]
        hat_ref[rows] = hat.astype(BF16)
        half_pre = hat * gain + shift
        act = half_pre * (1.0 + jnp.tanh(half_pre)) * mask
        shifted = (
            pltpu.roll(act, 1, 0) * first,
            act,
            pltpu.roll(act, PIX - 1, 0) * last,
        )
        for d in range(3):
            piece = shifted[d].astype(BF16)
            for q in range(2):
                taps_ref[j, pl.ds(SIDE, PIX), pl.ds(q * 384 + d * 128, 128)] = piece[
                    :, q * HALF : (q + 1) * HALF
                ]
    for q in range(2):
        cols = pl.ds(q * WIDTH, WIDTH)
        for j in range(per):
            patches = jnp.concatenate(
                [taps_ref[j, pl.ds(SIDE * d, PIX), pl.ds(q * 384, 384)] for d in range(3)], axis=1
            )
            h2 = dot_f(patches, w_ref[:, cols])
            h2_ref[pl.ds(j * PIX, PIX), cols] = h2
            side = SIDE - 2 * sides_ref[step * per + j]
            kept = h2 * pixel_mask(side, WIDTH)
            acc_ref[0:8, cols] += fold(kept)
            acc_ref[8:16, cols] += fold(kept * h2)

    @pl.when(step == pl.num_programs(0) - 1)
    def _():
        send_rows(send_ref, [row_sum(acc_ref[0:8]), row_sum(acc_ref[8:16])])


def act_two_kernel(
    per, sides_ref, one_ref, got_ref, h2_ref, gain_ref, shift_ref, fc_ref,
    a2_ref, hat_ref, slope_ref, pooled_ref, zin_ref, t2_ref, t4_ref, send_ref, vec_ref,
):
    step = pl.program_id(0)

    @pl.when(step == 0)
    def _():
        sums = total(got_ref)
        mean, inv = norm_terms(sums, jnp.concatenate([total(one_ref)[2:3]] * 2, axis=1))
        vec_ref[0:1] = mean
        vec_ref[1:2] = inv

    gain = gain_ref[:, WIDTH : 3 * WIDTH] * 0.5
    shift = shift_ref[:, WIDTH : 3 * WIDTH] * 0.5
    for j in range(per):
        side = SIDE - 2 * sides_ref[step * per + j]
        mask = pixel_mask(side, 2 * WIDTH)
        rows = pl.ds(j * PIX, PIX)
        hat = (h2_ref[rows] - vec_ref[0:1]) * vec_ref[1:2]
        half_pre = hat * gain + shift
        value, slope = silu_parts(half_pre)
        value = value * mask
        slope = slope * mask
        a2_ref[rows] = value.astype(BF16)
        hat_ref[rows] = hat.astype(BF16)
        slope_ref[rows] = slope.astype(BF16)
        sums = row_sum(fold(value))
        image = pl.ds(step * per + j, 1)
        pixels = (side * side).astype(F32)
        pooled_ref[image] = (sums[:, :WIDTH] + sums[:, WIDTH:]) / pixels
        t2_ref[image] = row_sum(fold(slope))
        t4_ref[image] = row_sum(fold(slope * hat))

    @pl.when(step == pl.num_programs(0) - 1)
    def _():
        z = high_f(pooled_ref[...], fc_ref[...])
        zin_ref[...] = z
        send_rows(send_ref, [row_sum(z), row_sum(z * z)])


def hidden_terms(zin, sums, n_images, gain_ref, shift_ref):
    mean, inv = norm_terms(sums, n_images)
    zhat = (zin - mean) * inv
    cols = slice(3 * WIDTH, 3 * WIDTH + INTER)
    half_z = (zhat * gain_ref[:, cols] + shift_ref[:, cols]) * 0.5
    value, slope = silu_parts(half_z)
    return zhat, inv, value, slope


def combine_kernel(
    per, n_images, got_ref, zin_ref, a2_ref, w3_ref, fc_ref, bias_ref, gain_ref, shift_ref,
    att_ref, comb_ref, gw_ref, csum_ref, send_ref, gram_ref, acc_ref,
):
    step = pl.program_id(0)

    @pl.when(step == 0)
    def _():
        _, _, hidden, _ = hidden_terms(zin_ref[...], total(got_ref), n_images, gain_ref, shift_ref)
        logits = high_f(hidden, fc_ref[...]) + bias_ref[...]
        left, right = logits[:, :WIDTH], logits[:, WIDTH:]
        top = jnp.maximum(left, right)
        left, right = jnp.exp(left - top), jnp.exp(right - top)
        both = left + right
        att_ref[:, :WIDTH] = left / both
        att_ref[:, WIDTH:] = right / both
        gram_ref[...] = jnp.zeros_like(gram_ref)
        acc_ref[...] = jnp.zeros_like(acc_ref)

    for j in range(per):
        rows = pl.ds(j * PIX, PIX)
        att = att_ref[pl.ds(step * per + j, 1)]
        a2 = a2_ref[rows].astype(F32)
        comb = (att[:, :WIDTH] * a2[:, :WIDTH] + att[:, WIDTH:] * a2[:, WIDTH:]).astype(BF16)
        comb_ref[rows] = comb
        acc_ref[...] += fold(comb.astype(F32))
    comb = comb_ref[...]
    gram_ref[...] += dot_rows(comb, comb)

    @pl.when(step == pl.num_programs(0) - 1)
    def _():
        w3 = w3_ref[...].astype(F32)
        csum = row_sum(acc_ref[...])
        csum_ref[...] = csum
        gw = high_f(gram_ref[...], w3)
        gw_ref[...] = gw
        send_rows(send_ref, [high_f(csum, w3), row_sum(w3 * gw)])


def norm_three(one_ref, got_ref, gain_ref):
    count = total(one_ref)[2:3]
    count = jnp.concatenate([count] * 4, axis=1)
    mean, inv = norm_terms(total(got_ref), count)
    offset = 3 * WIDTH + INTER
    return mean, inv, inv * gain_ref[:, offset:], count


def output_kernel(
    per, sides_ref, one_ref, got_ref, comb_ref, x_ref, cot_ref, w3_ref, gain_ref, shift_ref,
    out_ref, u3_ref, p_ref, cu_ref, send_ref, vec_ref, ones_ref,
):
    step = pl.program_id(0)

    @pl.when(step == 0)
    def _():
        mean, _, scale, _ = norm_three(one_ref, got_ref, gain_ref)
        vec_ref[0:1] = 0.5 * scale
        vec_ref[1:2] = 0.5 * (shift_ref[:, 3 * WIDTH + INTER :] - mean * scale)
        vec_ref[2:3] = scale
        cu_ref[...] = jnp.zeros_like(cu_ref)
        ones_ref[...] = jnp.zeros_like(ones_ref)

    w3 = w3_ref[...]
    chunk = 16
    for j in range(per):
        side = SIDE - 2 * sides_ref[step * per + j]
        mask = pixel_mask(side, 128)
        h3 = dot_f(comb_ref[pl.ds(j * PIX, PIX)], w3)
        for c in range(PIX // chunk):
            rows = pl.ds(j * PIX + c * chunk, chunk)
            m = wide(mask[c * chunk : (c + 1) * chunk], C_IN)
            half_pre = (
                h3[c * chunk : (c + 1) * chunk] * vec_ref[0:1]
                + vec_ref[1:2]
                + x_ref[rows].astype(F32) * 0.5
            )
            t = jnp.tanh(half_pre)
            a = (1.0 + t) * m
            out_ref[rows] = (half_pre * a).astype(BF16)
            slope = a * (1.0 + half_pre * (1.0 - t))
            u3_ref[rows] = (cot_ref[rows].astype(F32) * slope * vec_ref[0:1]).astype(BF16)
    u3 = u3_ref[...]
    p_ref[...] = dot_last(u3, w3)
    cu_ref[...] += dot_rows(comb_ref[...], u3)
    ones_ref[...] += dot_f(jnp.ones((8, per * PIX), BF16), u3)

    @pl.when(step == pl.num_programs(0) - 1)
    def _():
        scale = vec_ref[2:3]
        products = row_sum(w3_ref[...].astype(F32) * cu_ref[...]) / scale
        send_rows(send_ref, [ones_ref[0:1] / scale, products])


def back_three_kernel(
    per, n_images, one_ref, three_ref, got_ref, att_got_ref, comb_ref, p_ref, a2_ref, slope_ref,
    hat_ref, w3_ref, cu_ref, gw_ref, csum_ref, att_ref, zin_ref, fc_ref, gain_ref, shift_ref,
    dcomb_ref, t1_ref, t3_ref, duz_ref, w3g_ref, fcg_ref, biasg_ref, norm_ref, send_ref,
    s_ref, c_ref, datt_ref,
):
    step = pl.program_id(0)

    @pl.when(step == 0)
    def _():
        mean, inv, scale, count = norm_three(one_ref, three_ref, gain_ref)
        sums = total(got_ref)
        dshift = sums[0:1]
        dgain = (sums[1:2] - mean * dshift) * inv
        norm_ref[0:1] = dgain
        norm_ref[1:2] = dshift
        k2 = scale * inv * dgain / count
        k1 = scale * dshift / count - mean * k2
        w3 = w3_ref[...].astype(F32)
        s_ref[...] = dot_last((w3 * k2).astype(BF16), w3_ref[...]).astype(BF16)
        c_ref[...] = high_last(jnp.broadcast_to(k1, (8, C_IN)), w3)
        csum = jnp.broadcast_to(csum_ref[...], (8, WIDTH))
        outer = high_rows(csum, jnp.broadcast_to(k1, (8, C_IN))) * 0.125
        w3g_ref[...] = cu_ref[...] - outer - gw_ref[...] * k2

    corr = dot_f(comb_ref[...], s_ref[...])
    for j in range(per):
        rows = pl.ds(j * PIX, PIX)
        dcomb = p_ref[rows] - corr[j * PIX : (j + 1) * PIX] - c_ref[0:1]
        dcomb_ref[rows] = dcomb.astype(BF16)
        image = pl.ds(step * per + j, 1)
        for q in range(2):
            cols = pl.ds(q * WIDTH, WIDTH)
            datt_ref[image, cols] = row_sum(fold(dcomb * a2_ref[rows, cols].astype(F32)))
            u = dcomb * slope_ref[rows, cols].astype(F32)
            t1_ref[image, cols] = row_sum(fold(u))
            t3_ref[image, cols] = row_sum(fold(u * hat_ref[rows, cols].astype(F32)))

    @pl.when(step == pl.num_programs(0) - 1)
    def _():
        att = att_ref[...]
        datt = datt_ref[...]
        both = att * datt
        inner = both[:, :WIDTH] + both[:, WIDTH:]
        dlog = both - att * jnp.concatenate([inner, inner], axis=1)
        zhat, _, hidden, slope = hidden_terms(
            zin_ref[...], total(att_got_ref), n_images, gain_ref, shift_ref
        )
        biasg_ref[...] = row_sum(dlog)
        fcg_ref[...] = high_rows(hidden, dlog)
        duz = high_last(dlog, fc_ref[...]) * slope
        duz_ref[...] = duz
        send_rows(send_ref, [row_sum(duz), row_sum(duz * zhat)])


def back_att_kernel(
    n_images, got_ref, att_got_ref, zin_ref, duz_ref, pooled_ref, pixels_ref, fc_ref, att_ref,
    t1_ref, t2_ref, t3_ref, t4_ref, gain_ref, shift_ref, dpool_ref, fcg_ref, norm_ref, send_ref,
):
    zhat, inv, _, _ = hidden_terms(
        zin_ref[...], total(att_got_ref), n_images, gain_ref, shift_ref
    )
    sums = total(got_ref)
    norm_ref[0:1] = sums[1:2]
    norm_ref[1:2] = sums[0:1]
    scale = inv * gain_ref[:, 3 * WIDTH : 3 * WIDTH + INTER]
    dzin = scale * (duz_ref[...] - (sums[0:1] + zhat * sums[1:2]) / n_images)
    fcg_ref[...] = high_rows(pooled_ref[...], dzin)
    dpool = high_last(dzin, fc_ref[...]) / pixels_ref[...]
    dpool_ref[...] = dpool
    both = jnp.concatenate([dpool, dpool], axis=1)
    att = att_ref[...]
    send_rows(
        send_ref,
        [
            row_sum(att * t1_ref[...] + both * t2_ref[...]),
            row_sum(att * t3_ref[...] + both * t4_ref[...]),
        ],
    )


def back_two_kernel(
    per, sides_ref, one_ref, two_ref, got_ref, dcomb_ref, slope_ref, hat2_ref, hat1_ref, att_ref,
    dpool_ref, w_ref, gain_ref, shift_ref, dh2_ref, u1_ref, norm_ref, send_ref,
    vec_ref, pad_ref, acc_ref,
):
    step = pl.program_id(0)

    @pl.when(step == 0)
    def _():
        count = jnp.concatenate([total(one_ref)[2:3]] * 2, axis=1)
        _, inv = norm_terms(total(two_ref), count)
        scale = inv * gain_ref[:, WIDTH : 3 * WIDTH]
        sums = total(got_ref)
        norm_ref[0:1] = sums[1:2]
        norm_ref[1:2] = sums[0:1]
        vec_ref[0:1] = scale
        vec_ref[1:2] = scale * sums[0:1] / count
        vec_ref[2:3] = scale * sums[1:2] / count
        acc_ref[...] = jnp.zeros_like(acc_ref)
        pad_ref[...] = jnp.zeros_like(pad_ref)

    column = lax.broadcasted_iota(jnp.int32, (PIX, 128), 0) & 15
    first = jnp.where(column == 0, 0.0, 1.0).astype(F32)
    last = jnp.where(column == 15, 0.0, 1.0).astype(F32)
    for j in range(per):
        rows = pl.ds(j * PIX, PIX)
        side = SIDE - 2 * sides_ref[step * per + j]
        mask = pixel_mask(side, WIDTH)
        image = pl.ds(step * per + j, 1)
        dcomb = dcomb_ref[rows].astype(F32)
        dpool = dpool_ref[image]
        for q in range(2):
            cols = pl.ds(q * WIDTH, WIDTH)
            scale = vec_ref[0:1, cols]
            up = dcomb * (att_ref[image, cols] * scale) + dpool * scale
            dh2 = slope_ref[rows, cols].astype(F32) * up - mask * (
                vec_ref[1:2, cols] + hat2_ref[rows, cols].astype(F32) * vec_ref[2:3, cols]
            )
            dh2 = dh2.astype(BF16)
            dh2_ref[rows, cols] = dh2
            pad_ref[j, pl.ds(SIDE, PIX), cols] = dh2
    for j in range(per):
        rows = pl.ds(j * PIX, PIX)
        side = SIDE - 2 * sides_ref[step * per + j]
        mask = pixel_mask(side, 128)
        for q in range(2):
            lines = jnp.concatenate(
                [
                    pad_ref[j, pl.ds(SIDE * (2 - d), PIX), pl.ds(q * WIDTH, WIDTH)]
                    for d in range(3)
                ],
                axis=1,
            )
            y = dot_f(lines, w_ref[q])
            da1 = (
                y[:, HALF : 2 * HALF]
                + pltpu.roll(y[:, :HALF], PIX - 1, 0) * last
                + pltpu.roll(y[:, 2 * HALF :], 1, 0) * first
            )
            cols = pl.ds(q * HALF, HALF)
            hat = hat1_ref[rows, cols].astype(F32)
            half_pre = 0.5 * (hat * gain_ref[:, cols] + shift_ref[:, cols])
            _, slope = silu_parts(half_pre)
            u1 = da1 * slope * mask
            u1_ref[rows, cols] = u1.astype(BF16)
            acc_ref[0:8, cols] += fold(u1)
            acc_ref[8:16, cols] += fold(u1 * hat)

    @pl.when(step == pl.num_programs(0) - 1)
    def _():
        send_rows(send_ref, [row_sum(acc_ref[0:8]), row_sum(acc_ref[8:16])])


def weight_two_kernel(
    per, sides_ref, hat_ref, dh2_ref, gain_ref, shift_ref, out_ref, taps_ref, acc_ref
):
    step = pl.program_id(0)

    @pl.when(step == 0)
    def _():
        acc_ref[...] = jnp.zeros_like(acc_ref)
        taps_ref[...] = jnp.zeros_like(taps_ref)

    gain = gain_ref[:, :WIDTH] * 0.5
    shift = shift_ref[:, :WIDTH] * 0.5
    column = lax.broadcasted_iota(jnp.int32, (PIX, 128), 0) & 15
    first = wide(jnp.where(column == 0, 0.0, 1.0).astype(F32), WIDTH)
    last = wide(jnp.where(column == 15, 0.0, 1.0).astype(F32), WIDTH)
    for j in range(per):
        side = SIDE - 2 * sides_ref[step * per + j]
        mask = pixel_mask(side, WIDTH)
        rows = pl.ds(j * PIX, PIX)
        half_pre = hat_ref[rows].astype(F32) * gain + shift
        act = half_pre * (1.0 + jnp.tanh(half_pre)) * mask
        shifted = (
            pltpu.roll(act, 1, 0) * first,
            act,
            pltpu.roll(act, PIX - 1, 0) * last,
        )
        for d in range(3):
            piece = shifted[d].astype(BF16)
            for q in range(2):
                taps_ref[j, pl.ds(SIDE, PIX), pl.ds(q * 384 + d * 128, 128)] = piece[
                    :, q * HALF : (q + 1) * HALF
                ]
    for q in range(2):
        for j in range(per):
            patches = jnp.concatenate(
                [taps_ref[j, pl.ds(SIDE * d, PIX), pl.ds(q * 384, 384)] for d in range(3)], axis=1
            )
            acc_ref[q] += dot_rows(
                dh2_ref[pl.ds(j * PIX, PIX), pl.ds(q * WIDTH, WIDTH)], patches
            )

    @pl.when(step == pl.num_programs(0) - 1)
    def _():
        for q in range(2):
            out_ref[:, q * WIDTH : (q + 1) * WIDTH] = acc_ref[q].T


def back_one_kernel(
    per, sides_ref, one_ref, three_ref, got_ref, u1_ref, hat_ref, u3_ref, x_ref, w_ref, gain_ref,
    ig_ref, wg_ref, norm_ref, vec_ref, wide_ref, dh_ref, acc_ref,
):
    step = pl.program_id(0)

    @pl.when(step == 0)
    def _():
        one = total(one_ref)
        count = one[2:3]
        _, inv = norm_terms(one, count)
        scale = inv * gain_ref[:, :WIDTH]
        sums = total(got_ref)
        norm_ref[0:1] = sums[1:2]
        norm_ref[1:2] = sums[0:1]
        vec_ref[0:1] = scale
        vec_ref[1:2] = scale * sums[0:1] / count
        vec_ref[2:3] = scale * sums[1:2] / count
        _, _, scale_three, _ = norm_three(one_ref, three_ref, gain_ref)
        wide_ref[...] = 1.0 / scale_three
        acc_ref[...] = jnp.zeros_like(acc_ref)

    for j in range(per):
        rows = pl.ds(j * PIX, PIX)
        side = SIDE - 2 * sides_ref[step * per + j]
        mask = pixel_mask(side, WIDTH)
        dh_ref[rows] = (
            u1_ref[rows].astype(F32) * vec_ref[0:1]
            - mask * (vec_ref[1:2] + hat_ref[rows].astype(F32) * vec_ref[2:3])
        ).astype(BF16)
    dh = dh_ref[...]
    acc_ref[...] += dot_rows(dh, x_ref[...])
    dx = dot_last(dh, w_ref[...])
    ig_ref[...] = (u3_ref[...].astype(F32) * wide_ref[...] + dx).astype(BF16)

    @pl.when(step == pl.num_programs(0) - 1)
    def _():
        wg_ref[...] = acc_ref[...].T


def everyone(payload):
    return lax.all_to_all(payload, AXES, 0, 0, tiled=True)


def other_core(array):
    return lax.ppermute(array, "dp", [(0, 1), (1, 0)])


def gather_rows(weight):
    rows, cols = weight.shape
    core = lax.axis_index("dp")
    shards = lax.axis_size("fsdp")
    half = lax.dynamic_slice_in_dim(weight, core * (cols // 2), cols // 2, 1)
    half = jnp.broadcast_to(half[None], (shards, rows, cols // 2))
    mine = lax.all_to_all(half, "fsdp", 0, 0, tiled=True).reshape(shards * rows, cols // 2)
    other = other_core(mine)
    return jnp.where(
        core == 0,
        jnp.concatenate([mine, other], axis=1),
        jnp.concatenate([other, mine], axis=1),
    )


def scatter_rows(grad):
    rows, cols = grad.shape
    core = lax.axis_index("dp")
    shards = lax.axis_size("fsdp")
    keep = lax.dynamic_slice_in_dim(grad, core * (cols // 2), cols // 2, 1)
    give = lax.dynamic_slice_in_dim(grad, (1 - core) * (cols // 2), cols // 2, 1).astype(BF16)
    both = (keep + other_core(give).astype(F32)).astype(BF16)
    both = both.reshape(shards, rows // shards, cols // 2)
    mine = jnp.sum(lax.all_to_all(both, "fsdp", 0, 0, tiled=True).astype(F32), axis=0)
    other = other_core(mine)
    return jnp.where(
        core == 0,
        jnp.concatenate([mine, other], axis=1),
        jnp.concatenate([other, mine], axis=1),
    )


def sum_everywhere(array, devices):
    rows = array.shape[0]
    each = -(-rows // devices)
    padded = jnp.pad(array, ((0, each * devices - rows), (0, 0))).reshape(devices, each, 128)
    mine = jnp.sum(lax.all_to_all(padded, AXES, 0, 0, tiled=True), axis=0)
    spread = jnp.broadcast_to(mine[None], (devices, each, 128))
    return lax.all_to_all(spread, AXES, 0, 0, tiled=True).reshape(-1, 128)[:rows]


def body(
    inputs,
    sides,
    weight_one,
    weight_two,
    weight_three,
    fc_first,
    fc_second,
    fc_bias,
    bn_gain,
    bn_shift,
    cotangent,
):
    images = inputs.shape[0]
    rows = images * PIX
    devices = lax.axis_size("fsdp") * lax.axis_size("dp")
    n_images = float(images * devices)
    x = inputs.reshape(rows, C_IN)
    cot = cotangent.reshape(rows, C_IN)
    gain = bn_gain.reshape(1, -1)
    shift = bn_shift.reshape(1, -1)
    bias = fc_bias.reshape(1, -1)
    per = 2 if images % 2 == 0 else 1
    steps = images // per
    block = per * PIX
    n_ch = gain.shape[1]

    full_one = gather_rows(weight_one)
    full_one, weight_two, weight_three = lax.optimization_barrier(
        (full_one, weight_two, weight_three)
    )
    full_two = gather_rows(weight_two)
    back_weight = full_two.reshape(3, 3, HALF, 2, WIDTH).transpose(3, 0, 4, 1, 2)
    back_weight = back_weight.reshape(2, 3 * WIDTH, 3 * HALF)
    pixels = SIDE - 2 * sides
    pixels = (pixels * pixels).astype(F32).reshape(images, 1)

    sides_in = (sides, SMEM_SPEC)
    gain_in = (gain, whole((1, n_ch)))
    shift_in = (shift, whole((1, n_ch)))

    def payload(k, n):
        return ((devices, k, n), F32, whole((devices, k, n)))

    def full(array):
        return (array, whole(array.shape))

    def by_rows(array):
        return (array, rows_of(block, array.shape[1]))

    h1, send = call(
        functools.partial(conv_one_kernel, per),
        steps,
        [sides_in, by_rows(x), full(full_one)],
        [((rows, WIDTH), F32, rows_of(block, WIDTH)), payload(4, WIDTH)],
        [pltpu.VMEM((16, WIDTH), F32), pltpu.SMEM((1,), F32)],
        flops=2 * rows * C_IN * WIDTH,
        moved=rows * C_IN * 2 + rows * WIDTH * 4,
        name="conv_one",
    )
    got_one = everyone(send)
    full_two, weight_three = lax.optimization_barrier((full_two, weight_three))
    full_three = gather_rows(weight_three)

    hat1, h2, send = call(
        functools.partial(conv_two_kernel, per),
        steps,
        [sides_in, full(got_one), by_rows(h1), full(full_two), gain_in, shift_in],
        [
            ((rows, WIDTH), BF16, rows_of(block, WIDTH)),
            ((rows, 2 * WIDTH), F32, rows_of(block, 2 * WIDTH)),
            payload(2, 2 * WIDTH),
        ],
        [
            pltpu.VMEM((8, WIDTH), F32),
            pltpu.VMEM((per, PIX + 2 * SIDE, 6 * HALF), BF16),
            pltpu.VMEM((16, 2 * WIDTH), F32),
        ],
        flops=2 * rows * 9 * HALF * 2 * WIDTH,
        moved=rows * WIDTH * 14,
        name="conv_two",
    )
    got_two = everyone(send)

    a2, hat2, slope2, pooled, zin, t2, t4, send = call(
        functools.partial(act_two_kernel, per),
        steps,
        [
            sides_in,
            full(got_one),
            full(got_two),
            by_rows(h2),
            gain_in,
            shift_in,
            full(fc_first),
        ],
        [
            ((rows, 2 * WIDTH), BF16, rows_of(block, 2 * WIDTH)),
            ((rows, 2 * WIDTH), BF16, rows_of(block, 2 * WIDTH)),
            ((rows, 2 * WIDTH), BF16, rows_of(block, 2 * WIDTH)),
            ((images, WIDTH), F32, whole((images, WIDTH))),
            ((images, INTER), F32, whole((images, INTER))),
            ((images, 2 * WIDTH), F32, whole((images, 2 * WIDTH))),
            ((images, 2 * WIDTH), F32, whole((images, 2 * WIDTH))),
            payload(2, INTER),
        ],
        [pltpu.VMEM((8, 2 * WIDTH), F32)],
        flops=rows * 2 * WIDTH * 20,
        moved=rows * 2 * WIDTH * 10,
        name="act_two",
    )
    got_att = everyone(send)

    att, comb, gw, csum, send = call(
        functools.partial(combine_kernel, per, n_images),
        steps,
        [
            full(got_att),
            full(zin),
            by_rows(a2),
            full(full_three),
            full(fc_second),
            full(bias),
            gain_in,
            shift_in,
        ],
        [
            ((images, 2 * WIDTH), F32, whole((images, 2 * WIDTH))),
            ((rows, WIDTH), BF16, rows_of(block, WIDTH)),
            ((WIDTH, C_IN), F32, whole((WIDTH, C_IN))),
            ((1, WIDTH), F32, whole((1, WIDTH))),
            payload(2, C_IN),
        ],
        [pltpu.VMEM((WIDTH, WIDTH), F32), pltpu.VMEM((8, WIDTH), F32)],
        flops=2 * rows * WIDTH * WIDTH,
        moved=rows * WIDTH * 6,
        name="combine",
    )
    got_three = everyone(send)

    outputs, u3, p, cu, send = call(
        functools.partial(output_kernel, per),
        steps,
        [
            sides_in,
            full(got_one),
            full(got_three),
            by_rows(comb),
            by_rows(x),
            by_rows(cot),
            full(full_three),
            gain_in,
            shift_in,
        ],
        [
            ((rows, C_IN), BF16, rows_of(block, C_IN)),
            ((rows, C_IN), BF16, rows_of(block, C_IN)),
            ((rows, WIDTH), F32, rows_of(block, WIDTH)),
            ((WIDTH, C_IN), F32, whole((WIDTH, C_IN))),
            payload(2, C_IN),
        ],
        [pltpu.VMEM((8, C_IN), F32), pltpu.VMEM((8, C_IN), F32)],
        flops=6 * rows * WIDTH * C_IN,
        moved=rows * C_IN * 8,
        name="output",
    )
    got_back_three = everyone(send)

    dcomb, t1, t3, duz, w3_local, fc2_local, bias_local, norm3, send = call(
        functools.partial(back_three_kernel, per, n_images),
        steps,
        [
            full(got_one),
            full(got_three),
            full(got_back_three),
            full(got_att),
            by_rows(comb),
            by_rows(p),
            by_rows(a2),
            by_rows(slope2),
            by_rows(hat2),
            full(full_three),
            full(cu),
            full(gw),
            full(csum),
            full(att),
            full(zin),
            full(fc_second),
            gain_in,
            shift_in,
        ],
        [
            ((rows, WIDTH), BF16, rows_of(block, WIDTH)),
            ((images, 2 * WIDTH), F32, whole((images, 2 * WIDTH))),
            ((images, 2 * WIDTH), F32, whole((images, 2 * WIDTH))),
            ((images, INTER), F32, whole((images, INTER))),
            ((WIDTH, C_IN), F32, whole((WIDTH, C_IN))),
            ((INTER, 2 * WIDTH), F32, whole((INTER, 2 * WIDTH))),
            ((1, 2 * WIDTH), F32, whole((1, 2 * WIDTH))),
            ((2, C_IN), F32, whole((2, C_IN))),
            payload(2, INTER),
        ],
        [
            pltpu.VMEM((WIDTH, WIDTH), BF16),
            pltpu.VMEM((8, WIDTH), F32),
            pltpu.VMEM((images, 2 * WIDTH), F32),
        ],
        flops=2 * rows * WIDTH * WIDTH,
        moved=rows * WIDTH * 18,
        name="back_three",
    )
    got_back_att = everyone(send)

    dpool, fc1_local, norm_att, send = call(
        functools.partial(back_att_kernel, n_images),
        1,
        [
            full(got_back_att),
            full(got_att),
            full(zin),
            full(duz),
            full(pooled),
            full(pixels),
            full(fc_first),
            full(att),
            full(t1),
            full(t2),
            full(t3),
            full(t4),
            gain_in,
            shift_in,
        ],
        [
            ((images, WIDTH), F32, whole((images, WIDTH))),
            ((WIDTH, INTER), F32, whole((WIDTH, INTER))),
            ((2, INTER), F32, whole((2, INTER))),
            payload(2, 2 * WIDTH),
        ],
        flops=10000000,
        moved=1000000,
        name="back_att",
    )
    got_back_two = everyone(send)

    dh2, u1, norm2, send = call(
        functools.partial(back_two_kernel, per),
        steps,
        [
            sides_in,
            full(got_one),
            full(got_two),
            full(got_back_two),
            by_rows(dcomb),
            by_rows(slope2),
            by_rows(hat2),
            by_rows(hat1),
            full(att),
            full(dpool),
            full(back_weight),
            gain_in,
            shift_in,
        ],
        [
            ((rows, 2 * WIDTH), BF16, rows_of(block, 2 * WIDTH)),
            ((rows, WIDTH), BF16, rows_of(block, WIDTH)),
            ((2, 2 * WIDTH), F32, whole((2, 2 * WIDTH))),
            payload(2, WIDTH),
        ],
        [
            pltpu.VMEM((8, 2 * WIDTH), F32),
            pltpu.VMEM((per, PIX + 2 * SIDE, 2 * WIDTH), BF16),
            pltpu.VMEM((16, WIDTH), F32),
        ],
        flops=2 * rows * 9 * HALF * 2 * WIDTH,
        moved=rows * WIDTH * 18,
        name="back_two",
    )
    got_back_one = everyone(send)

    (w2_local,) = call(
        functools.partial(weight_two_kernel, per),
        steps,
        [sides_in, by_rows(hat1), by_rows(dh2), gain_in, shift_in],
        [((9 * HALF, 2 * WIDTH), F32, whole((9 * HALF, 2 * WIDTH)))],
        [
            pltpu.VMEM((per, PIX + 2 * SIDE, 6 * HALF), BF16),
            pltpu.VMEM((2, WIDTH, 9 * HALF), F32),
        ],
        flops=2 * rows * 9 * HALF * 2 * WIDTH,
        moved=rows * WIDTH * 6,
        name="weight_two",
    )
    w2_local, u1 = lax.optimization_barrier((w2_local, u1))

    input_grad, w1_local, norm1 = call(
        functools.partial(back_one_kernel, per),
        steps,
        [
            sides_in,
            full(got_one),
            full(got_three),
            full(got_back_one),
            by_rows(u1),
            by_rows(hat1),
            by_rows(u3),
            by_rows(x),
            full(full_one),
            gain_in,
        ],
        [
            ((rows, C_IN), BF16, rows_of(block, C_IN)),
            ((C_IN, WIDTH), F32, whole((C_IN, WIDTH))),
            ((2, WIDTH), F32, whole((2, WIDTH))),
        ],
        [
            pltpu.VMEM((8, WIDTH), F32),
            pltpu.VMEM((1, C_IN), F32),
            pltpu.VMEM((block, WIDTH), BF16),
            pltpu.VMEM((WIDTH, C_IN), F32),
        ],
        flops=4 * rows * WIDTH * C_IN,
        moved=rows * C_IN * 6,
        name="back_one",
    )

    packed = jnp.concatenate(
        [fc1_local, fc2_local.reshape(-1, 128), bias_local.reshape(-1, 128)], axis=0
    )
    summed = sum_everywhere(packed, devices)
    fc_first_grad = summed[:WIDTH]
    fc_second_grad = summed[WIDTH : WIDTH + INTER * 4].reshape(INTER, 2 * WIDTH)
    fc_bias_grad = summed[WIDTH + INTER * 4 :].reshape(2 * WIDTH)
    weight_three_grad = scatter_rows(w3_local)
    weight_two_grad = scatter_rows(w2_local)
    weight_one_grad = scatter_rows(w1_local)
    norms = jnp.concatenate([norm1, norm2, norm_att, norm3], axis=1)
    return (
        outputs.reshape(inputs.shape),
        input_grad.reshape(inputs.shape),
        weight_one_grad,
        weight_two_grad,
        weight_three_grad,
        fc_first_grad,
        fc_second_grad,
        fc_bias_grad,
        norms[0],
        norms[1],
    )


def solution(mesh):
    return jax.shard_map(
        body,
        mesh=mesh,
        in_specs=(
            P(("fsdp", "dp"), None, None),
            P(("fsdp", "dp")),
            P("fsdp", None),
            P("fsdp", None),
            P("fsdp", None),
            P(),
            P(),
            P(),
            P(),
            P(),
            P(("fsdp", "dp"), None, None),
        ),
        out_specs=(
            P(("fsdp", "dp"), None, None),
            P(("fsdp", "dp"), None, None),
            P("fsdp", None),
            P("fsdp", None),
            P("fsdp", None),
            P(),
            P(),
            P(),
            P(),
            P(),
        ),
        check_vma=False,
    )
```

```python
import functools

import jax
import jax.numpy as jnp
from jax import lax
from jax.experimental import pallas as pl
from jax.experimental.pallas import tpu as pltpu
from jax.sharding import PartitionSpec as P

C_IN = 1024
WIDTH = 256
INTER = 128
SIDE = 16
PIX = SIDE * SIDE
HALF = WIDTH // 2
EPS = 1e-05
AXES = ("fsdp", "dp")
HIGH = lax.Precision.HIGHEST
F32 = jnp.float32
BF16 = jnp.bfloat16
MIB = 1024 * 1024

PER_CONV_ONE = 4
PER_CONV_TWO = 4
PER_ACT_TWO = 4
PER_SLOPE_TWO = 4
PER_COMBINE = 4
PER_OUTPUT = 2
PER_PROJECT = 4
PER_BACK_THREE = 4
PER_BACK_TWO = 4
PER_WEIGHT_TWO = 2
PER_BACK_ONE = 2


def dot_f(left, right):
    return jnp.dot(left, right, preferred_element_type=F32)


def dot_rows(left, right):
    return lax.dot_general(left, right, (((0,), (0,)), ((), ())), preferred_element_type=F32)


def dot_last(left, right):
    return lax.dot_general(left, right, (((1,), (1,)), ((), ())), preferred_element_type=F32)


def high_f(left, right):
    return jnp.dot(left, right, preferred_element_type=F32, precision=HIGH)


def high_rows(left, right):
    return lax.dot_general(
        left, right, (((0,), (0,)), ((), ())), preferred_element_type=F32, precision=HIGH
    )


def high_last(left, right):
    return lax.dot_general(
        left, right, (((1,), (1,)), ((), ())), preferred_element_type=F32, precision=HIGH
    )


def pixel_mask(image_side, width):
    row = lax.broadcasted_iota(jnp.int32, (PIX, 128), 0)
    inside = ((row >> 4) < image_side) & ((row & 15) < image_side)
    return wide(jnp.where(inside, 1.0, 0.0).astype(F32), width)


def wide(mask, width):
    if width == 128:
        return mask
    return jnp.concatenate([mask] * (width // 128), axis=1)


def fold(values):
    rows, n = values.shape
    return jnp.sum(values.reshape(rows // 8, 8, n), axis=0)


def row_sum(values):
    return jnp.sum(values, axis=0, keepdims=True)


def total(payload_ref):
    return jnp.sum(payload_ref[...], axis=0)


def norm_terms(sums, count):
    mean = sums[0:1] / count
    variance = sums[1:2] / count - mean * mean
    return mean, lax.rsqrt(variance + EPS)


def send_rows(payload_ref, rows):
    block = jnp.concatenate(rows, axis=0)
    payload_ref[...] = jnp.broadcast_to(block[None], payload_ref.shape)


def silu_parts(half_pre):
    t = jnp.tanh(half_pre)
    a = 1.0 + t
    value = half_pre * a
    slope = 0.5 * a * (1.0 + half_pre * (1.0 - t))
    return value, slope


def whole(shape):
    zeros = (0,) * len(shape)
    return pl.BlockSpec(shape, lambda *_: zeros)


def rows_of(n_rows, width):
    return pl.BlockSpec((n_rows, width), lambda i: (i, 0))


SMEM_SPEC = pl.BlockSpec(memory_space=pltpu.SMEM)


def call(kernel, grid, ins, outs, scratch=(), vmem=32, flops=0, moved=0, name=None):
    arrays = [
        array
        if spec is SMEM_SPEC or near
        else pltpu.with_memory_space_constraint(array, pltpu.HBM)
        for array, spec, *near in ins
    ]
    shapes = [pltpu.HBM(shape, dtype) for shape, dtype, _ in outs]
    return pl.pallas_call(
        kernel,
        grid=(grid,),
        in_specs=[spec for _, spec, *_ in ins],
        out_specs=[spec for _, _, spec in outs],
        out_shape=shapes,
        scratch_shapes=list(scratch),
        compiler_params=pltpu.CompilerParams(
            dimension_semantics=("arbitrary",), vmem_limit_bytes=vmem * MIB
        ),
        cost_estimate=pl.CostEstimate(flops=flops, bytes_accessed=moved, transcendentals=0),
        name=name,
    )(*arrays)


def pack_kernel(core_ref, one_ref, two_ref, three_ref, first_ref, second_ref):
    def put(half):
        first_ref[...] = jnp.broadcast_to(
            one_ref[:, half * HALF : (half + 1) * HALF][None], first_ref.shape
        )
        at = 0
        for ref, blocks in ((two_ref, 2), (three_ref, 4)):
            rows = ref.shape[0]
            for b in range(blocks):
                low = (half * blocks + b) * 128
                piece = ref[:, low : low + 128]
                for f in range(second_ref.shape[0]):
                    second_ref[f, pl.ds(at, rows)] = piece
                at += rows

    for core in range(2):
        pl.when(core_ref[0] == core)(functools.partial(put, core))


def unpack_kernel(core_ref, mine_ref, other_ref, two_ref, three_ref, wide_ref):
    shards = mine_ref.shape[0]
    two_rows = two_ref.shape[0] // shards
    three_rows = three_ref.shape[0] // shards

    def put(half, source_ref):
        for f in range(shards):
            at = 0
            for b in range(2):
                piece = source_ref[f, pl.ds(at, two_rows)].astype(F32)
                wide_ref[pl.ds(f * two_rows, two_rows), pl.ds(half * WIDTH + b * 128, 128)] = piece
                at += two_rows
            for b in range(4):
                piece = source_ref[f, pl.ds(at, three_rows)]
                three_ref[pl.ds(f * three_rows, three_rows), pl.ds(half * 512 + b * 128, 128)] = piece
                at += three_rows

    for core in range(2):

        @pl.when(core_ref[0] == core)
        def _():
            put(core, mine_ref)
            put(1 - core, other_ref)

    two_ref[...] = wide_ref[...].astype(BF16)


def conv_one_kernel(
    per, core_ref, sides_ref, x_ref, mine_ref, other_ref, h_ref, w_out_ref, send_ref,
    acc_ref, count_ref,
):
    step = pl.program_id(0)

    @pl.when(step == 0)
    def _():
        acc_ref[...] = jnp.zeros_like(acc_ref)
        count_ref[0] = 0.0

        def put(core):
            for half, ref in ((core, mine_ref), (1 - core, other_ref)):
                w_out_ref[:, half * HALF : (half + 1) * HALF] = ref[...].reshape(C_IN, HALF)

        for core in range(2):
            pl.when(core_ref[0] == core)(functools.partial(put, core))

    h = dot_f(x_ref[...], w_out_ref[...])
    h_ref[...] = h
    for j in range(per):
        side = SIDE - 2 * sides_ref[step * per + j]
        mask = pixel_mask(side, WIDTH)
        one = h[j * PIX : (j + 1) * PIX]
        kept = one * mask
        acc_ref[0:8] += fold(kept)
        acc_ref[8:16] += fold(kept * one)
        count_ref[0] += (side * side).astype(F32)

    @pl.when(step == pl.num_programs(0) - 1)
    def _():
        count = jnp.full((1, WIDTH), count_ref[0], F32)
        send_rows(
            send_ref,
            [row_sum(acc_ref[0:8]), row_sum(acc_ref[8:16]), count, jnp.zeros((1, WIDTH), F32)],
        )


def edge_masks(width):
    column = lax.broadcasted_iota(jnp.int32, (PIX, 128), 0) & 15
    first = jnp.where(column == 0, 0.0, 1.0).astype(F32)
    last = jnp.where(column == 15, 0.0, 1.0).astype(F32)
    return wide(first, width), wide(last, width)


def put_taps(taps_ref, j, act, first, last):
    shifted = (pltpu.roll(act, 1, 0) * first, act, pltpu.roll(act, PIX - 1, 0) * last)
    for d in range(3):
        piece = shifted[d].astype(BF16)
        for q in range(2):
            taps_ref[pl.ds(SIDE + j * (PIX + SIDE), PIX), pl.ds(q * 384 + d * 128, 128)] = piece[
                :, q * HALF : (q + 1) * HALF
            ]


def conv_two_kernel(
    per, sides_ref, got_ref, h_ref, w_ref, gain_ref, shift_ref, hat_ref, h2_ref, vec_ref, send_ref,
    taps_ref, acc_ref,
):
    step = pl.program_id(0)

    @pl.when(step == 0)
    def _():
        sums = total(got_ref)
        mean, inv = norm_terms(sums, sums[2:3])
        vec_ref[0:1] = mean
        vec_ref[1:2] = inv
        vec_ref[2:3] = sums[2:3]
        acc_ref[...] = jnp.zeros_like(acc_ref)
        taps_ref[...] = jnp.zeros_like(taps_ref)

    gain = gain_ref[:, :WIDTH] * 0.5
    shift = shift_ref[:, :WIDTH] * 0.5
    first, last = edge_masks(WIDTH)
    for j in range(per):
        side = SIDE - 2 * sides_ref[step * per + j]
        mask = pixel_mask(side, WIDTH)
        rows = pl.ds(j * PIX, PIX)
        hat = (h_ref[rows] - vec_ref[0:1]) * vec_ref[1:2]
        hat_ref[pl.ds(j * PIX, PIX)] = hat.astype(BF16)
        half_pre = hat * gain + shift
        act = half_pre * (1.0 + jnp.tanh(half_pre)) * mask
        put_taps(taps_ref, j, act, first, last)
    height = per * (PIX + SIDE)
    for q in range(2):
        cols = pl.ds(q * WIDTH, WIDTH)
        patches = jnp.concatenate(
            [taps_ref[pl.ds(SIDE * d, height), pl.ds(q * 384, 384)] for d in range(3)], axis=1
        )
        both = dot_f(patches, w_ref[:, cols])
        for j in range(per):
            h2 = both[j * (PIX + SIDE) : j * (PIX + SIDE) + PIX]
            h2_ref[pl.ds(j * PIX, PIX), cols] = h2
            side = SIDE - 2 * sides_ref[step * per + j]
            kept = h2 * pixel_mask(side, WIDTH)
            acc_ref[0:8, cols] += fold(kept)
            acc_ref[8:16, cols] += fold(kept * h2)

    @pl.when(step == pl.num_programs(0) - 1)
    def _():
        send_rows(send_ref, [row_sum(acc_ref[0:8]), row_sum(acc_ref[8:16])])


def act_two_kernel(
    per, sides_ref, one_ref, got_ref, h2_ref, gain_ref, shift_ref, fc_ref,
    hat_ref, pooled_ref, zin_ref, vec_ref, send_ref,
):
    step = pl.program_id(0)

    @pl.when(step == 0)
    def _():
        sums = total(got_ref)
        mean, inv = norm_terms(sums, jnp.concatenate([one_ref[2:3]] * 2, axis=1))
        vec_ref[0:1] = mean
        vec_ref[1:2] = inv

    gain = gain_ref[:, WIDTH : 3 * WIDTH] * 0.5
    shift = shift_ref[:, WIDTH : 3 * WIDTH] * 0.5
    for j in range(per):
        side = SIDE - 2 * sides_ref[step * per + j]
        mask = pixel_mask(side, 2 * WIDTH)
        rows = pl.ds(j * PIX, PIX)
        hat = (h2_ref[rows] - vec_ref[0:1]) * vec_ref[1:2]
        hat_ref[rows] = hat.astype(BF16)
        half_pre = hat * gain + shift
        value = half_pre * ((1.0 + jnp.tanh(half_pre)) * mask)
        sums = row_sum(fold(value))
        image = pl.ds(step * per + j, 1)
        pixels = (side * side).astype(F32)
        pooled_ref[image] = (sums[:, :WIDTH] + sums[:, WIDTH:]) / pixels

    @pl.when(step == pl.num_programs(0) - 1)
    def _():
        z = high_f(pooled_ref[...], fc_ref[...])
        zin_ref[...] = z
        send_rows(send_ref, [row_sum(z), row_sum(z * z)])


def slope_two_kernel(
    per, sides_ref, hat_ref, gain_ref, shift_ref, a2_ref, slope_ref, t2_ref, t4_ref
):
    step = pl.program_id(0)
    gain = gain_ref[:, WIDTH : 3 * WIDTH] * 0.5
    shift = shift_ref[:, WIDTH : 3 * WIDTH] * 0.5
    for j in range(per):
        side = SIDE - 2 * sides_ref[step * per + j]
        mask = pixel_mask(side, 2 * WIDTH)
        rows = pl.ds(j * PIX, PIX)
        hat = hat_ref[rows].astype(F32)
        half_pre = hat * gain + shift
        a = (1.0 + jnp.tanh(half_pre)) * mask
        value = half_pre * a
        slope = (0.5 * a) * (1.0 + 2.0 * half_pre - value)
        a2_ref[rows] = value.astype(BF16)
        slope_ref[rows] = slope.astype(BF16)
        image = pl.ds(step * per + j, 1)
        t2_ref[image] = row_sum(fold(slope))
        t4_ref[image] = row_sum(fold(slope * hat))


def hidden_terms(zin, sums, n_images, gain_ref, shift_ref):
    mean, inv = norm_terms(sums, n_images)
    zhat = (zin - mean) * inv
    cols = slice(3 * WIDTH, 3 * WIDTH + INTER)
    half_z = (zhat * gain_ref[:, cols] + shift_ref[:, cols]) * 0.5
    value, slope = silu_parts(half_z)
    return zhat, inv, value, slope


def combine_kernel(
    per, n_images, got_ref, zin_ref, a2_ref, w3_ref, fc_ref, bias_ref, gain_ref, shift_ref,
    att_ref, comb_ref, gw_ref, csum_ref, hid_ref, send_ref, gram_ref, acc_ref,
):
    step = pl.program_id(0)

    @pl.when(step == 0)
    def _():
        zhat, inv, hidden, slope = hidden_terms(
            zin_ref[...], total(got_ref), n_images, gain_ref, shift_ref
        )
        hid_ref[0] = zhat
        hid_ref[1] = hidden
        hid_ref[2] = slope
        hid_ref[3] = jnp.broadcast_to(inv, slope.shape)
        logits = high_f(hidden, fc_ref[...]) + bias_ref[...]
        left, right = logits[:, :WIDTH], logits[:, WIDTH:]
        top = jnp.maximum(left, right)
        left, right = jnp.exp(left - top), jnp.exp(right - top)
        both = left + right
        att_ref[:, :WIDTH] = left / both
        att_ref[:, WIDTH:] = right / both
        gram_ref[...] = jnp.zeros_like(gram_ref)
        acc_ref[...] = jnp.zeros_like(acc_ref)

    for j in range(per):
        rows = pl.ds(j * PIX, PIX)
        att = att_ref[pl.ds(step * per + j, 1)]
        a2 = a2_ref[rows].astype(F32)
        comb = (att[:, :WIDTH] * a2[:, :WIDTH] + att[:, WIDTH:] * a2[:, WIDTH:]).astype(BF16)
        comb_ref[rows] = comb
        acc_ref[...] += fold(comb.astype(F32))
    comb = comb_ref[...]
    gram_ref[...] += dot_rows(comb, comb)

    @pl.when(step == pl.num_programs(0) - 1)
    def _():
        w3 = w3_ref[...].astype(F32)
        csum = row_sum(acc_ref[...])
        csum_ref[...] = csum
        gw = high_f(gram_ref[...], w3)
        gw_ref[...] = gw
        send_rows(send_ref, [high_f(csum, w3), row_sum(w3 * gw)])


def output_kernel(
    per, sides_ref, one_ref, got_ref, comb_ref, x_ref, cot_ref, w3_ref, gain_ref, shift_ref,
    out_ref, u3_ref, stat_ref, send_ref, vec_ref, acc_ref,
):
    step = pl.program_id(0)

    @pl.when(step == 0)
    def _():
        count = jnp.concatenate([one_ref[2:3]] * 4, axis=1)
        mean, inv = norm_terms(total(got_ref), count)
        scale = inv * gain_ref[:, 3 * WIDTH + INTER :]
        stat_ref[0:1] = mean
        stat_ref[1:2] = inv
        stat_ref[2:3] = scale
        stat_ref[3:4] = count
        vec_ref[0:1] = scale
        vec_ref[1:2] = shift_ref[:, 3 * WIDTH + INTER :] - mean * scale
        vec_ref[2:3] = 0.5 * scale
        acc_ref[...] = jnp.zeros_like(acc_ref)

    chunk = 16
    lanes = 512
    for j in range(per):
        side = SIDE - 2 * sides_ref[step * per + j]
        mask = pixel_mask(side, 128)
        h3 = dot_f(comb_ref[pl.ds(j * PIX, PIX)], w3_ref[...])
        for n in range(C_IN // lanes):
            cols = pl.ds(n * lanes, lanes)
            ups = jnp.zeros((8, lanes), F32)
            products = jnp.zeros((8, lanes), F32)
            for c in range(PIX // chunk):
                rows = pl.ds(j * PIX + c * chunk, chunk)
                scaled = (
                    h3[c * chunk : (c + 1) * chunk, n * lanes : (n + 1) * lanes] * vec_ref[0:1, cols]
                )
                pre = scaled + vec_ref[1:2, cols] + x_ref[rows, cols].astype(F32)
                half_pre = pre * 0.5
                a = (1.0 + jnp.tanh(half_pre)) * wide(mask[c * chunk : (c + 1) * chunk], lanes)
                value = half_pre * a
                out_ref[rows, cols] = value.astype(BF16)
                up = cot_ref[rows, cols].astype(F32) * (a * (1.0 + pre - value))
                u3_ref[rows, cols] = (up * vec_ref[2:3, cols]).astype(BF16)
                ups = ups + fold(up)
                products = products + fold(up * scaled)
            acc_ref[0:8, cols] += ups
            acc_ref[8:16, cols] += products

    @pl.when(step == pl.num_programs(0) - 1)
    def _():
        send_rows(
            send_ref,
            [0.5 * row_sum(acc_ref[0:8]), 0.5 * row_sum(acc_ref[8:16]) / vec_ref[0:1]],
        )


def project_kernel(comb_ref, u3_ref, w3_ref, p_ref, cu_ref):
    @pl.when(pl.program_id(0) == 0)
    def _():
        cu_ref[...] = jnp.zeros_like(cu_ref)

    u3 = u3_ref[...]
    p_ref[...] = dot_last(u3, w3_ref[...]).astype(BF16)
    cu_ref[...] += dot_rows(comb_ref[...], u3)


def back_three_kernel(
    per, three_ref, got_ref, hid_ref, comb_ref, p_ref, a2_ref, slope_ref,
    hat_ref, w3_ref, cu_ref, gw_ref, csum_ref, att_ref, fc_ref,
    t1_ref, t3_ref, duz_ref, w3g_ref, fcg_ref, norm_ref, s_ref, c_ref, send_ref, datt_ref,
):
    step = pl.program_id(0)

    @pl.when(step == 0)
    def _():
        mean, inv = three_ref[0:1], three_ref[1:2]
        scale, count = three_ref[2:3], three_ref[3:4]
        sums = total(got_ref)
        dshift = sums[0:1]
        dgain = (sums[1:2] - mean * dshift) * inv
        norm_ref[0:1] = dgain
        norm_ref[1:2] = dshift
        k2 = scale * inv * dgain / count
        k1 = scale * dshift / count - mean * k2
        w3 = w3_ref[...].astype(F32)
        s_ref[...] = dot_last((w3 * k2).astype(BF16), w3_ref[...]).astype(BF16)
        c_ref[...] = high_last(jnp.broadcast_to(k1, (8, C_IN)), w3)
        csum = jnp.broadcast_to(csum_ref[...], (8, WIDTH))
        outer = high_rows(csum, jnp.broadcast_to(k1, (8, C_IN))) * 0.125
        w3g_ref[...] = cu_ref[...] - outer - gw_ref[...] * k2

    corr = dot_f(comb_ref[...], s_ref[...])
    for j in range(per):
        rows = pl.ds(j * PIX, PIX)
        dcomb = p_ref[rows].astype(F32) - corr[j * PIX : (j + 1) * PIX] - c_ref[0:1]
        image = pl.ds(step * per + j, 1)
        for q in range(2):
            cols = pl.ds(q * WIDTH, WIDTH)
            datt_ref[image, cols] = row_sum(fold(dcomb * a2_ref[rows, cols].astype(F32)))
            u = dcomb * slope_ref[rows, cols].astype(F32)
            t1_ref[image, cols] = row_sum(fold(u))
            t3_ref[image, cols] = row_sum(fold(u * hat_ref[rows, cols].astype(F32)))

    @pl.when(step == pl.num_programs(0) - 1)
    def _():
        att = att_ref[...]
        datt = datt_ref[...]
        both = att * datt
        inner = both[:, :WIDTH] + both[:, WIDTH:]
        dlog = both - att * jnp.concatenate([inner, inner], axis=1)
        zhat, hidden, slope = hid_ref[0], hid_ref[1], hid_ref[2]
        fcg = high_rows(hidden, dlog)
        duz = high_last(dlog, fc_ref[...]) * slope
        duz_ref[...] = duz
        bias = row_sum(dlog)
        rows = [row_sum(duz), row_sum(duz * zhat)]
        for b in range(4):
            cols = slice(b * 128, (b + 1) * 128)
            fcg_ref[pl.ds(b * INTER, INTER)] = fcg[:, cols]
            rows.append(bias[:, cols])
        send_rows(send_ref, rows + [jnp.zeros((2, 128), F32)])


def back_att_kernel(
    n_images, got_ref, hid_ref, duz_ref, pooled_ref, sides_ref, fc_ref, att_ref,
    t1_ref, t2_ref, t3_ref, t4_ref, fcg_ref, gain_ref,
    dpool_ref, pack_ref, bias_ref, norm_ref, send_ref,
):
    zhat, inv = hid_ref[0], hid_ref[3, 0:1]
    sums = total(got_ref)
    norm_ref[0:1] = sums[1:2]
    norm_ref[1:2] = sums[0:1]
    for b in range(4):
        bias_ref[:, b * 128 : (b + 1) * 128] = sums[2 + b : 3 + b]
    scale = inv * gain_ref[:, 3 * WIDTH : 3 * WIDTH + INTER]
    dzin = scale * (duz_ref[...] - (sums[0:1] + zhat * sums[1:2]) / n_images)
    pack_ref[0:WIDTH] = high_rows(pooled_ref[...], dzin)
    pack_ref[WIDTH:] = fcg_ref[...]
    dpool_ref[...] = high_last(dzin, fc_ref[...])
    for i in range(dpool_ref.shape[0]):
        side = SIDE - 2 * sides_ref[i]
        dpool_ref[i : i + 1] = dpool_ref[i : i + 1] / (side * side).astype(F32)
    dpool = dpool_ref[...]
    both = jnp.concatenate([dpool, dpool], axis=1)
    att = att_ref[...]
    send_rows(
        send_ref,
        [
            row_sum(att * t1_ref[...] + both * t2_ref[...]),
            row_sum(att * t3_ref[...] + both * t4_ref[...]),
        ],
    )


def back_two_kernel(
    per, sides_ref, one_ref, two_ref, got_ref, comb_ref, p_ref, s_ref, c_ref, slope_ref, hat2_ref, hat1_ref, att_ref,
    dpool_ref, w_ref, gain_ref, shift_ref, dh2_ref, u1_ref, norm_ref, send_ref,
    vec_ref, pad_ref, acc_ref,
):
    step = pl.program_id(0)

    @pl.when(step == 0)
    def _():
        count = jnp.concatenate([one_ref[2:3]] * 2, axis=1)
        scale = two_ref[1:2] * gain_ref[:, WIDTH : 3 * WIDTH]
        sums = total(got_ref)
        norm_ref[0:1] = sums[1:2]
        norm_ref[1:2] = sums[0:1]
        vec_ref[0:1] = scale
        vec_ref[1:2] = scale * sums[0:1] / count
        vec_ref[2:3] = scale * sums[1:2] / count
        acc_ref[...] = jnp.zeros_like(acc_ref)
        pad_ref[...] = jnp.zeros_like(pad_ref)

    first, last = edge_masks(HALF)
    corr = dot_f(comb_ref[...], s_ref[...])
    for j in range(per):
        rows = pl.ds(j * PIX, PIX)
        side = SIDE - 2 * sides_ref[step * per + j]
        mask = pixel_mask(side, WIDTH)
        image = pl.ds(step * per + j, 1)
        dcomb = p_ref[rows].astype(F32) - corr[j * PIX : (j + 1) * PIX] - c_ref[0:1]
        dpool = dpool_ref[image]
        for q in range(2):
            cols = pl.ds(q * WIDTH, WIDTH)
            scale = vec_ref[0:1, cols]
            up = dcomb * (att_ref[image, cols] * scale) + dpool * scale
            dh2 = slope_ref[rows, cols].astype(F32) * up - mask * (
                vec_ref[1:2, cols] + hat2_ref[rows, cols].astype(F32) * vec_ref[2:3, cols]
            )
            dh2 = dh2.astype(BF16)
            dh2_ref[rows, cols] = dh2
            pad_ref[pl.ds(SIDE + j * (PIX + SIDE), PIX), cols] = dh2
    height = per * (PIX + SIDE)
    for q in range(2):
        lines = jnp.concatenate(
            [pad_ref[pl.ds(SIDE * (2 - d), height), pl.ds(q * WIDTH, WIDTH)] for d in range(3)],
            axis=1,
        )
        weight = jnp.concatenate(
            [
                jnp.concatenate(
                    [
                        w_ref[pl.ds((3 * r + d) * HALF, HALF), pl.ds(q * WIDTH, WIDTH)]
                        for r in range(3)
                    ],
                    axis=1,
                )
                for d in range(3)
            ],
            axis=0,
        )
        both = dot_last(lines, weight)
        for j in range(per):
            rows = pl.ds(j * PIX, PIX)
            side = SIDE - 2 * sides_ref[step * per + j]
            mask = pixel_mask(side, 128)
            y = both[j * (PIX + SIDE) : j * (PIX + SIDE) + PIX]
            da1 = (
                y[:, HALF : 2 * HALF]
                + pltpu.roll(y[:, :HALF], PIX - 1, 0) * last
                + pltpu.roll(y[:, 2 * HALF :], 1, 0) * first
            )
            cols = pl.ds(q * HALF, HALF)
            hat = hat1_ref[rows, cols].astype(F32)
            half_pre = 0.5 * (hat * gain_ref[:, cols] + shift_ref[:, cols])
            _, slope = silu_parts(half_pre)
            u1 = da1 * slope * mask
            u1_ref[rows, cols] = u1.astype(BF16)
            acc_ref[0:8, cols] += fold(u1)
            acc_ref[8:16, cols] += fold(u1 * hat)

    @pl.when(step == pl.num_programs(0) - 1)
    def _():
        send_rows(send_ref, [row_sum(acc_ref[0:8]), row_sum(acc_ref[8:16])])


def weight_two_kernel(
    per, core_ref, sides_ref, hat_ref, dh2_ref, gain_ref, shift_ref, keep_ref, give_ref,
    taps_ref, acc_ref,
):
    step = pl.program_id(0)

    @pl.when(step == 0)
    def _():
        acc_ref[...] = jnp.zeros_like(acc_ref)
        taps_ref[...] = jnp.zeros_like(taps_ref)

    gain = gain_ref[:, :WIDTH] * 0.5
    shift = shift_ref[:, :WIDTH] * 0.5
    first, last = edge_masks(WIDTH)
    height = PIX + SIDE
    for j in range(per):
        side = SIDE - 2 * sides_ref[step * per + j]
        mask = pixel_mask(side, WIDTH)
        rows = pl.ds(j * PIX, PIX)
        half_pre = hat_ref[rows].astype(F32) * gain + shift
        act = half_pre * (1.0 + jnp.tanh(half_pre)) * mask
        put_taps(taps_ref, j, act, first, last)
    for q in range(2):
        patches = jnp.concatenate(
            [
                jnp.concatenate(
                    [
                        taps_ref[pl.ds(SIDE * d + j * height, PIX), pl.ds(q * 384, 384)]
                        for d in range(3)
                    ],
                    axis=1,
                )
                for j in range(per)
            ],
            axis=0,
        )
        acc_ref[q] += dot_rows(dh2_ref[:, q * WIDTH : (q + 1) * WIDTH], patches)

    @pl.when(step == pl.num_programs(0) - 1)
    def _():
        def put(core):
            keep_ref[...] = acc_ref[core].T
            give_ref[...] = acc_ref[1 - core].T

        for core in range(2):
            pl.when(core_ref[0] == core)(functools.partial(put, core))


def back_one_kernel(
    per, core_ref, sides_ref, one_ref, three_ref, got_ref, u1_ref, hat_ref, u3_ref, x_ref, w_ref, gain_ref,
    norm2_ref, norm_att_ref, norm3_ref,
    ig_ref, keep_ref, give_ref, gain_out_ref, shift_out_ref, vec_ref, wide_ref, dh_ref, acc_ref,
):
    step = pl.program_id(0)

    @pl.when(step == 0)
    def _():
        count = one_ref[2:3]
        scale = one_ref[1:2] * gain_ref[:, :WIDTH]
        sums = total(got_ref)
        for row, out_ref in ((0, gain_out_ref), (1, shift_out_ref)):
            out_ref[:, :WIDTH] = sums[1 - row : 2 - row]
            out_ref[:, WIDTH : 3 * WIDTH] = norm2_ref[row : row + 1]
            out_ref[:, 3 * WIDTH : 3 * WIDTH + INTER] = norm_att_ref[row : row + 1]
            out_ref[:, 3 * WIDTH + INTER :] = norm3_ref[row : row + 1]
        vec_ref[0:1] = scale
        vec_ref[1:2] = scale * sums[0:1] / count
        vec_ref[2:3] = scale * sums[1:2] / count
        wide_ref[...] = 1.0 / three_ref[2:3]
        acc_ref[...] = jnp.zeros_like(acc_ref)

    for j in range(per):
        rows = pl.ds(j * PIX, PIX)
        side = SIDE - 2 * sides_ref[step * per + j]
        mask = pixel_mask(side, WIDTH)
        dh_ref[rows] = (
            u1_ref[rows].astype(F32) * vec_ref[0:1]
            - mask * (vec_ref[1:2] + hat_ref[rows].astype(F32) * vec_ref[2:3])
        ).astype(BF16)
    dh = dh_ref[...]
    acc_ref[...] += dot_rows(dh, x_ref[...])
    dx = dot_last(dh, w_ref[...])
    ig_ref[...] = (u3_ref[...].astype(F32) * wide_ref[...] + dx).astype(BF16)

    @pl.when(step == pl.num_programs(0) - 1)
    def _():
        def put(core):
            keep_ref[...] = acc_ref[core * HALF : (core + 1) * HALF].T
            give_ref[...] = acc_ref[(1 - core) * HALF : (2 - core) * HALF].T

        for core in range(2):
            pl.when(core_ref[0] == core)(functools.partial(put, core))


def round_up(value, multiple):
    return -(-value // multiple) * multiple


def pack_three_kernel(core_ref, w_ref, fc_ref, keep_ref, give_ref):
    shards = keep_ref.shape[0]
    w_rows = w_ref.shape[0] // shards
    fc_rows = fc_ref.shape[0] // (2 * shards)

    def put(half, out_ref):
        for f in range(shards):
            for b in range(4):
                low = (half * 4 + b) * 128
                out_ref[f, pl.ds(b * w_rows, w_rows)] = w_ref[
                    pl.ds(f * w_rows, w_rows), pl.ds(low, 128)
                ]
            out_ref[f, pl.ds(4 * w_rows, fc_rows)] = fc_ref[
                pl.ds((half * shards + f) * fc_rows, fc_rows)
            ]

    for core in range(2):

        @pl.when(core_ref[0] == core)
        def _():
            put(core, keep_ref)
            put(1 - core, give_ref)


def pack_two_kernel(keep_ref, other_ref, fc_ref, out_ref):
    shards, slot, _ = out_ref.shape
    rows = keep_ref.shape[0] // shards
    padded = round_up(rows, 16)
    fc = fc_ref[...]
    fc_half = (slot - padded) * 2 - fc.shape[0]
    if fc_half:
        fc = jnp.concatenate([fc, jnp.zeros((fc_half, 128), F32)], axis=0)
    fc = jnp.concatenate([fc[: slot - padded], fc[slot - padded :]], axis=1).astype(BF16)
    for f in range(shards):
        part = keep_ref[pl.ds(f * rows, rows)] + other_ref[pl.ds(f * rows, rows)]
        if padded > rows:
            part = jnp.concatenate([part, jnp.zeros((padded - rows, WIDTH), F32)], axis=0)
        out_ref[f, pl.ds(0, padded)] = part.astype(BF16)
        out_ref[f, pl.ds(padded, slot - padded)] = fc


def everyone(payload):
    return lax.all_to_all(payload, AXES, 0, 0, tiled=True)


def other_core(array):
    return lax.ppermute(array, "dp", [(0, 1), (1, 0)])


def both_halves(mine, axis=1):
    core = lax.axis_index("dp")
    other = other_core(mine)
    return jnp.where(
        core == 0,
        jnp.concatenate([mine, other], axis=axis),
        jnp.concatenate([other, mine], axis=axis),
    )


def gather_weights(core, weights):
    shards = lax.axis_size("fsdp")
    one, two, three = weights
    first = (shards, one.shape[0], HALF)
    second = (shards, 2 * two.shape[0] + 4 * three.shape[0], 128)
    spread_one, spread_two = call(
        pack_kernel,
        1,
        [(core, SMEM_SPEC)] + [(weight, whole(weight.shape)) for weight in weights],
        [(first, BF16, whole(first)), (second, BF16, whole(second))],
        flops=1000000,
        moved=4000000,
        name="pack",
    )
    mine = lax.all_to_all(spread_one, "fsdp", 0, 0, tiled=True)
    other = other_core(mine)
    spread_two, mine, other = lax.optimization_barrier((spread_two, mine, other))
    mine_two = lax.all_to_all(spread_two, "fsdp", 0, 0, tiled=True)

    def others(mine_two, after):
        mine_two, _ = lax.optimization_barrier((mine_two, after))
        other_two = other_core(mine_two)
        shapes = [(shards * weight.shape[0], weight.shape[1]) for weight in (two, three)]
        return call(
            unpack_kernel,
            1,
            [(core, SMEM_SPEC), (mine_two, whole(second), True), (other_two, whole(second), True)],
            [(shape, BF16, whole(shape)) for shape in shapes],
            [pltpu.VMEM(shapes[0], F32)],
            flops=1000000,
            moved=4000000,
            name="unpack",
        )

    return mine, other, functools.partial(others, mine_two)


def slots(parts):
    return lax.all_to_all(parts, "fsdp", 0, 0, tiled=True)


def body(
    inputs,
    sides,
    weight_one,
    weight_two,
    weight_three,
    fc_first,
    fc_second,
    fc_bias,
    bn_gain,
    bn_shift,
    cotangent,
):
    images = inputs.shape[0]
    rows = images * PIX
    devices = lax.axis_size("fsdp") * lax.axis_size("dp")
    n_images = float(images * devices)
    x = inputs.reshape(rows, C_IN)
    cot = cotangent.reshape(rows, C_IN)
    gain = bn_gain.reshape(1, -1)
    shift = bn_shift.reshape(1, -1)
    bias = fc_bias.reshape(1, -1)
    n_ch = gain.shape[1]
    core = lax.axis_index("dp").astype(jnp.int32).reshape(1)

    def split(most):
        per = max(n for n in range(1, most + 1) if images % n == 0)
        return per, images // per

    core_in = (core, SMEM_SPEC)
    sides_in = (sides, SMEM_SPEC)
    gain_in = (gain, whole((1, n_ch)))
    shift_in = (shift, whole((1, n_ch)))

    def payload(k, n):
        return ((devices, k, n), F32, whole((devices, k, n)))

    def small(*shape):
        return (shape, F32, whole(shape))

    def full(array):
        return (array, whole(array.shape))

    def near(array):
        return (array, whole(array.shape), True)

    def blocks(array):
        return (array, rows_of(per * PIX, array.shape[1]))

    def blocks_out(width, dtype=BF16):
        return ((rows, width), dtype, rows_of(per * PIX, width))

    mine, other, others = gather_weights(core, (weight_one, weight_two, weight_three))

    per, steps = split(PER_CONV_ONE)
    h1, full_one, send = call(
        functools.partial(conv_one_kernel, per),
        steps,
        [core_in, sides_in, blocks(x), near(mine), near(other)],
        [blocks_out(WIDTH, F32), ((C_IN, WIDTH), BF16, whole((C_IN, WIDTH))), payload(4, WIDTH)],
        [pltpu.VMEM((16, WIDTH), F32), pltpu.SMEM((1,), F32)],
        flops=2 * rows * C_IN * WIDTH,
        moved=rows * C_IN * 2 + rows * WIDTH * 4,
        name="conv_one",
    )
    got_one = everyone(send)
    full_two, full_three = others(send)

    per, steps = split(PER_CONV_TWO)
    hat1, h2, stat1, send = call(
        functools.partial(conv_two_kernel, per),
        steps,
        [sides_in, near(got_one), blocks(h1), full(full_two), gain_in, shift_in],
        [blocks_out(WIDTH), blocks_out(2 * WIDTH, F32), small(8, WIDTH), payload(2, 2 * WIDTH)],
        [
            pltpu.VMEM((per * (PIX + SIDE) + 2 * SIDE, 6 * HALF), BF16),
            pltpu.VMEM((16, 2 * WIDTH), F32),
        ],
        flops=2 * rows * 9 * HALF * 2 * WIDTH,
        moved=rows * WIDTH * 14,
        name="conv_two",
    )
    got_two = everyone(send)

    per, steps = split(PER_ACT_TWO)
    hat2, pooled, zin, stat2, send = call(
        functools.partial(act_two_kernel, per),
        steps,
        [
            sides_in,
            full(stat1),
            near(got_two),
            blocks(h2),
            gain_in,
            shift_in,
            full(fc_first),
        ],
        [
            blocks_out(2 * WIDTH),
            small(images, WIDTH),
            small(images, INTER),
            small(8, 2 * WIDTH),
            payload(2, INTER),
        ],
        flops=rows * 2 * WIDTH * 20,
        moved=rows * 2 * WIDTH * 10,
        name="act_two",
    )
    got_att = everyone(send)

    per, steps = split(PER_SLOPE_TWO)
    a2, slope2, t2, t4 = call(
        functools.partial(slope_two_kernel, per),
        steps,
        [sides_in, blocks(hat2), gain_in, shift_in],
        [
            blocks_out(2 * WIDTH),
            blocks_out(2 * WIDTH),
            small(images, 2 * WIDTH),
            small(images, 2 * WIDTH),
        ],
        flops=rows * 2 * WIDTH * 20,
        moved=rows * 2 * WIDTH * 6,
        name="slope_two",
    )

    per, steps = split(PER_COMBINE)
    att, comb, gw, csum, hid, send = call(
        functools.partial(combine_kernel, per, n_images),
        steps,
        [
            near(got_att),
            full(zin),
            blocks(a2),
            full(full_three),
            full(fc_second),
            full(bias),
            gain_in,
            shift_in,
        ],
        [
            small(images, 2 * WIDTH),
            blocks_out(WIDTH),
            small(WIDTH, C_IN),
            small(1, WIDTH),
            small(4, images, INTER),
            payload(2, C_IN),
        ],
        [pltpu.VMEM((WIDTH, WIDTH), F32), pltpu.VMEM((8, WIDTH), F32)],
        flops=2 * rows * WIDTH * WIDTH,
        moved=rows * WIDTH * 6,
        name="combine",
    )
    got_three = everyone(send)

    per, steps = split(PER_OUTPUT)
    outputs, u3, stat3, send = call(
        functools.partial(output_kernel, per),
        steps,
        [
            sides_in,
            full(stat1),
            near(got_three),
            blocks(comb),
            blocks(x),
            blocks(cot),
            full(full_three),
            gain_in,
            shift_in,
        ],
        [blocks_out(C_IN), blocks_out(C_IN), small(8, C_IN), payload(2, C_IN)],
        [pltpu.VMEM((8, C_IN), F32), pltpu.VMEM((16, C_IN), F32)],
        flops=2 * rows * WIDTH * C_IN,
        moved=rows * C_IN * 8,
        name="output",
    )
    got_back_three = everyone(send)

    per, steps = split(PER_PROJECT)
    p, cu = call(
        project_kernel,
        steps,
        [blocks(comb), blocks(u3), full(full_three)],
        [blocks_out(WIDTH), small(WIDTH, C_IN)],
        flops=4 * rows * WIDTH * C_IN,
        moved=rows * C_IN * 4,
        name="project",
    )

    per, steps = split(PER_BACK_THREE)
    t1, t3, duz, w3_local, fc2_local, norm3, corr_weight, corr_row, send = call(
        functools.partial(back_three_kernel, per),
        steps,
        [
            full(stat3),
            near(got_back_three),
            full(hid),
            blocks(comb),
            blocks(p),
            blocks(a2),
            blocks(slope2),
            blocks(hat2),
            full(full_three),
            full(cu),
            full(gw),
            full(csum),
            full(att),
            full(fc_second),
        ],
        [
            small(images, 2 * WIDTH),
            small(images, 2 * WIDTH),
            small(images, INTER),
            small(WIDTH, C_IN),
            small(4 * INTER, 128),
            small(2, C_IN),
            ((WIDTH, WIDTH), BF16, whole((WIDTH, WIDTH))),
            small(8, WIDTH),
            payload(8, INTER),
        ],
        [pltpu.VMEM((images, 2 * WIDTH), F32)],
        flops=2 * rows * WIDTH * WIDTH,
        moved=rows * WIDTH * 16,
        name="back_three",
    )
    got_back_att = everyone(send)

    dpool, packed, fc_bias_grad, norm_att, send = call(
        functools.partial(back_att_kernel, n_images),
        1,
        [
            near(got_back_att),
            full(hid),
            full(duz),
            full(pooled),
            sides_in,
            full(fc_first),
            full(att),
            full(t1),
            full(t2),
            full(t3),
            full(t4),
            full(fc2_local),
            gain_in,
        ],
        [
            small(images, WIDTH),
            small(WIDTH + 4 * INTER, 128),
            small(1, 2 * WIDTH),
            small(2, INTER),
            payload(2, 2 * WIDTH),
        ],
        flops=10000000,
        moved=1000000,
        name="back_att",
    )
    got_back_two = everyone(send)

    shards = lax.axis_size("fsdp")
    w3_rows = WIDTH // shards
    fc_rows = packed.shape[0] // (2 * shards)
    slot = (shards, 4 * w3_rows + fc_rows, 128)
    keep, give = call(
        pack_three_kernel,
        1,
        [core_in, full(w3_local), full(packed)],
        [(slot, F32, whole(slot)), (slot, F32, whole(slot))],
        flops=1000000,
        moved=3000000,
        name="pack_three",
    )
    got_back_two, three = lax.optimization_barrier((got_back_two, keep + other_core(give)))
    three = slots(three)

    per, steps = split(PER_BACK_TWO)
    dh2, u1, norm2, send = call(
        functools.partial(back_two_kernel, per),
        steps,
        [
            sides_in,
            full(stat1),
            full(stat2),
            near(got_back_two),
            blocks(comb),
            blocks(p),
            full(corr_weight),
            full(corr_row),
            blocks(slope2),
            blocks(hat2),
            blocks(hat1),
            full(att),
            full(dpool),
            full(full_two),
            gain_in,
            shift_in,
        ],
        [
            blocks_out(2 * WIDTH),
            blocks_out(WIDTH),
            small(2, 2 * WIDTH),
            payload(2, WIDTH),
        ],
        [
            pltpu.VMEM((8, 2 * WIDTH), F32),
            pltpu.VMEM((per * (PIX + SIDE) + 2 * SIDE, 2 * WIDTH), BF16),
            pltpu.VMEM((16, WIDTH), F32),
        ],
        flops=2 * rows * 9 * HALF * 2 * WIDTH,
        moved=rows * WIDTH * 20,
        name="back_two",
    )
    send, three, dh2 = lax.optimization_barrier((send, three, dh2))
    got_back_one = everyone(send)

    per, steps = split(PER_WEIGHT_TWO)
    half = (9 * HALF, WIDTH)
    keep, give = call(
        functools.partial(weight_two_kernel, per),
        steps,
        [core_in, sides_in, blocks(hat1), blocks(dh2), gain_in, shift_in],
        [(half, F32, whole(half)), (half, F32, whole(half))],
        [
            pltpu.VMEM((per * (PIX + SIDE) + 2 * SIDE, 6 * HALF), BF16),
            pltpu.VMEM((2, WIDTH, 9 * HALF), F32),
        ],
        flops=2 * rows * 9 * HALF * 2 * WIDTH,
        moved=rows * WIDTH * 6,
        name="weight_two",
    )
    got_back_one, keep, give = lax.optimization_barrier((got_back_one, keep, give))
    three = jnp.sum(three, axis=0)
    w2_rows = 9 * HALF // shards
    w2_padded = round_up(w2_rows, 16)
    slot = (shards, w2_padded + round_up(fc_rows, 32) // 2, WIDTH)
    (parts,) = call(
        pack_two_kernel,
        1,
        [full(keep), near(other_core(give)), near(three[4 * w3_rows :])],
        [(slot, BF16, whole(slot))],
        flops=1000000,
        moved=3000000,
        name="pack_two",
    )
    got_back_one, parts = lax.optimization_barrier((got_back_one, parts))
    two = slots(parts)

    per, steps = split(PER_BACK_ONE)
    half = (C_IN, HALF)
    input_grad, keep, give, gain_grad, shift_grad = call(
        functools.partial(back_one_kernel, per),
        steps,
        [
            core_in,
            sides_in,
            full(stat1),
            full(stat3),
            near(got_back_one),
            blocks(u1),
            blocks(hat1),
            blocks(u3),
            blocks(x),
            full(full_one),
            gain_in,
            full(norm2),
            full(norm_att),
            full(norm3),
        ],
        [blocks_out(C_IN), small(*half), small(*half), small(1, n_ch), small(1, n_ch)],
        [
            pltpu.VMEM((8, WIDTH), F32),
            pltpu.VMEM((1, C_IN), F32),
            pltpu.VMEM((per * PIX, WIDTH), BF16),
            pltpu.VMEM((WIDTH, C_IN), F32),
        ],
        flops=4 * rows * WIDTH * C_IN,
        moved=rows * C_IN * 6,
        name="back_one",
    )

    one = (keep + other_core(give)).astype(BF16).reshape(shards, -1, HALF)
    one, two = lax.optimization_barrier((one, two))
    weight_one_grad = both_halves(jnp.sum(slots(one).astype(F32), axis=0))
    weight_two_grad = both_halves(jnp.sum(two[:, :w2_rows].astype(F32), axis=0))
    weight_three_grad = both_halves(
        jnp.concatenate([three[b * w3_rows : (b + 1) * w3_rows] for b in range(4)], axis=1)
    )
    fc = two[:, w2_padded:].astype(F32)
    fc = jnp.concatenate([fc[:, :, :128], fc[:, :, 128:]], axis=1)[:, :fc_rows].reshape(-1, 128)
    summed = both_halves(fc, 0)
    fc_first_grad = summed[:WIDTH]
    fc_second_grad = jnp.concatenate(
        [summed[WIDTH + b * INTER : WIDTH + (b + 1) * INTER] for b in range(4)], axis=1
    )
    return (
        outputs.reshape(inputs.shape),
        input_grad.reshape(inputs.shape),
        weight_one_grad,
        weight_two_grad,
        weight_three_grad,
        fc_first_grad,
        fc_second_grad,
        fc_bias_grad.reshape(-1),
        gain_grad.reshape(-1),
        shift_grad.reshape(-1),
    )


def solution(mesh):
    return jax.shard_map(
        body,
        mesh=mesh,
        in_specs=(
            P(("fsdp", "dp"), None, None),
            P(("fsdp", "dp")),
            P("fsdp", None),
            P("fsdp", None),
            P("fsdp", None),
            P(),
            P(),
            P(),
            P(),
            P(),
            P(("fsdp", "dp"), None, None),
        ),
        out_specs=(
            P(("fsdp", "dp"), None, None),
            P(("fsdp", "dp"), None, None),
            P("fsdp", None),
            P("fsdp", None),
            P("fsdp", None),
            P(),
            P(),
            P(),
            P(),
            P(),
        ),
        check_vma=False,
    )
```

```python
import functools

import jax
import jax.numpy as jnp
from jax import lax
from jax.experimental import pallas as pl
from jax.experimental.pallas import tpu as pltpu
from jax.sharding import PartitionSpec as P

C_IN = 1024
WIDTH = 256
INTER = 128
SIDE = 16
PIX = SIDE * SIDE
HALF = WIDTH // 2
EPS = 1e-05
AXES = ("fsdp", "dp")
HIGH = lax.Precision.HIGHEST
F32 = jnp.float32
BF16 = jnp.bfloat16
MIB = 1024 * 1024

AHEAD = 4
PER_CONV_ONE = 4
PER_CONV_TWO = 3
PER_ACT_TWO = 4
PER_SLOPE_TWO = 3
PER_COMBINE = 6
PER_OUTPUT = 2
PER_PROJECT = 4
PER_BACK_THREE = 4
PER_BACK_TWO = 2
PER_WEIGHT_TWO = 4
PER_BACK_ONE = 2


def dot_f(left, right):
    return jnp.dot(left, right, preferred_element_type=F32)


def dot_rows(left, right):
    return lax.dot_general(left, right, (((0,), (0,)), ((), ())), preferred_element_type=F32)


def dot_last(left, right):
    return lax.dot_general(left, right, (((1,), (1,)), ((), ())), preferred_element_type=F32)


def high_f(left, right):
    return jnp.dot(left, right, preferred_element_type=F32, precision=HIGH)


def high_rows(left, right):
    return lax.dot_general(
        left, right, (((0,), (0,)), ((), ())), preferred_element_type=F32, precision=HIGH
    )


def high_last(left, right):
    return lax.dot_general(
        left, right, (((1,), (1,)), ((), ())), preferred_element_type=F32, precision=HIGH
    )


def pixel_mask(image_side, width):
    row = lax.broadcasted_iota(jnp.int32, (PIX, 128), 0)
    inside = ((row >> 4) < image_side) & ((row & 15) < image_side)
    return wide(jnp.where(inside, 1.0, 0.0).astype(F32), width)


def wide(mask, width):
    if width == 128:
        return mask
    return jnp.concatenate([mask] * (width // 128), axis=1)


def fold(values):
    rows, n = values.shape
    return jnp.sum(values.reshape(rows // 8, 8, n), axis=0)


def row_sum(values):
    return jnp.sum(values, axis=0, keepdims=True)


def total(payload_ref):
    return jnp.sum(payload_ref[...], axis=0)


def norm_terms(sums, count):
    mean = sums[0:1] / count
    variance = sums[1:2] / count - mean * mean
    return mean, lax.rsqrt(variance + EPS)


def send_rows(payload_ref, rows):
    block = jnp.concatenate(rows, axis=0)
    payload_ref[...] = jnp.broadcast_to(block[None], payload_ref.shape)


def silu_parts(half_pre):
    t = jnp.tanh(half_pre)
    a = 1.0 + t
    value = half_pre * a
    slope = 0.5 * a * (1.0 + half_pre * (1.0 - t))
    return value, slope


def whole(shape):
    zeros = (0,) * len(shape)
    return pl.BlockSpec(shape, lambda *_: zeros)


SMEM_SPEC = pl.BlockSpec(memory_space=pltpu.SMEM)


def call(kernel, grid, ins, outs, scratch=(), vmem=56, flops=0, moved=0, name=None):
    arrays = [
        array
        if spec is SMEM_SPEC or near
        else pltpu.with_memory_space_constraint(array, pltpu.HBM)
        for array, spec, *near in ins
    ]
    shapes = [
        jax.ShapeDtypeStruct(shape, dtype) if near else pltpu.HBM(shape, dtype)
        for shape, dtype, _, *near in outs
    ]
    return pl.pallas_call(
        kernel,
        grid=(grid,),
        in_specs=[spec for _, spec, *_ in ins],
        out_specs=[spec for _, _, spec, *_ in outs],
        out_shape=shapes,
        scratch_shapes=list(scratch),
        compiler_params=pltpu.CompilerParams(
            dimension_semantics=("arbitrary",), vmem_limit_bytes=vmem * MIB
        ),
        cost_estimate=pl.CostEstimate(flops=flops, bytes_accessed=moved, transcendentals=0),
        name=name,
    )(*arrays)


class Stream:
    def __init__(self, over=None):
        self.over = over


BEGIN, END = "begin", "end"


def stream_call(kernel, per, steps, ins, outs, scratch=(), vmem=56, flops=0, moved=0, name=None):
    block = per * PIX
    in_specs, out_specs, arrays, shapes, rooms = [], [], [], [], []
    in_streams, out_streams, room_of = [], [], {}
    for at, (array, spec, *near) in enumerate(ins):
        if isinstance(spec, Stream):
            in_streams.append(at)
            room_of[at] = len(rooms)
            rooms.append(pltpu.VMEM(array.shape, array.dtype))
            spec = pl.BlockSpec(memory_space=pltpu.HBM)
        elif near:
            arrays.append(array)
            in_specs.append(spec)
            continue
        in_specs.append(spec)
        arrays.append(
            array if spec is SMEM_SPEC else pltpu.with_memory_space_constraint(array, pltpu.HBM)
        )
    for at, (shape, dtype, spec, *near) in enumerate(outs):
        shapes.append(jax.ShapeDtypeStruct(shape, dtype) if near else pltpu.HBM(shape, dtype))
        if isinstance(spec, Stream):
            out_streams.append(at)
            if spec.over is None:
                room_of[len(ins) + at] = len(rooms)
                rooms.append(pltpu.VMEM(shape, dtype))
            else:
                room_of[len(ins) + at] = room_of[spec.over]
            spec = pl.BlockSpec(memory_space=pltpu.HBM)
        out_specs.append(spec)
    n_in, n_out, n_rooms = len(ins), len(outs), len(rooms)

    def whole_kernel(*refs):
        in_refs, out_refs = refs[:n_in], refs[n_in : n_in + n_out]
        room_refs = refs[n_in + n_out : n_in + n_out + n_rooms]
        own_refs = refs[n_in + n_out + n_rooms : -2]
        in_sems, out_sems = refs[-2:]

        def rows(step):
            return pl.ds(pl.multiple_of(step * block, block), block)

        def copies_in(step):
            return [
                pltpu.make_async_copy(
                    in_refs[at].at[rows(step)],
                    room_refs[room_of[at]].at[rows(step)],
                    in_sems.at[k, step],
                )
                for k, at in enumerate(in_streams)
            ]

        def copies_out(step):
            return [
                pltpu.make_async_copy(
                    room_refs[room_of[n_in + at]].at[rows(step)],
                    out_refs[at].at[rows(step)],
                    out_sems.at[k, step],
                )
                for k, at in enumerate(out_streams)
            ]

        def views(step):
            both = []
            for at, ref in enumerate(in_refs + out_refs):
                if at in room_of:
                    ref = room_refs[room_of[at]].at[rows(step)]
                both.append(ref)
            return both + list(own_refs)

        ahead = min(AHEAD, steps)
        for step in range(ahead):
            for copy in copies_in(step):
                copy.start()
        kernel(BEGIN, *views(0))

        def one(step, carry):
            for copy in copies_in(step):
                copy.wait()

            @pl.when(step + ahead < steps)
            def _():
                for copy in copies_in(step + ahead):
                    copy.start()

            kernel(step, *views(step))
            for copy in copies_out(step):
                copy.start()
            return carry

        lax.fori_loop(0, steps, one, 0)
        kernel(END, *views(0))

        def last(step, carry):
            for copy in copies_out(step):
                copy.wait()
            return carry

        lax.fori_loop(0, steps, last, 0)

    return pl.pallas_call(
        whole_kernel,
        in_specs=in_specs,
        out_specs=out_specs,
        out_shape=shapes,
        scratch_shapes=rooms
        + list(scratch)
        + [
            pltpu.SemaphoreType.DMA((max(len(in_streams), 1), steps)),
            pltpu.SemaphoreType.DMA((max(len(out_streams), 1), steps)),
        ],
        compiler_params=pltpu.CompilerParams(vmem_limit_bytes=vmem * MIB),
        cost_estimate=pl.CostEstimate(flops=flops, bytes_accessed=moved, transcendentals=0),
        name=name,
    )(*arrays)


def pack_kernel(core_ref, one_ref, two_ref, three_ref, first_ref, second_ref):
    def put(half):
        first_ref[...] = jnp.broadcast_to(
            one_ref[:, half * HALF : (half + 1) * HALF][None], first_ref.shape
        )
        at = 0
        for ref, blocks in ((two_ref, 2), (three_ref, 4)):
            rows = ref.shape[0]
            for b in range(blocks):
                low = (half * blocks + b) * 128
                piece = ref[:, low : low + 128]
                for f in range(second_ref.shape[0]):
                    second_ref[f, pl.ds(at, rows)] = piece
                at += rows

    for core in range(2):
        pl.when(core_ref[0] == core)(functools.partial(put, core))


def unpack_kernel(core_ref, mine_ref, other_ref, two_ref, three_ref, wide_ref):
    shards = mine_ref.shape[0]
    two_rows = two_ref.shape[0] // shards
    three_rows = three_ref.shape[0] // shards

    def put(half, source_ref):
        for f in range(shards):
            at = 0
            for b in range(2):
                piece = source_ref[f, pl.ds(at, two_rows)].astype(F32)
                wide_ref[pl.ds(f * two_rows, two_rows), pl.ds(half * WIDTH + b * 128, 128)] = piece
                at += two_rows
            for b in range(4):
                piece = source_ref[f, pl.ds(at, three_rows)]
                three_ref[pl.ds(f * three_rows, three_rows), pl.ds(half * 512 + b * 128, 128)] = piece
                at += three_rows

    for core in range(2):

        @pl.when(core_ref[0] == core)
        def _():
            put(core, mine_ref)
            put(1 - core, other_ref)

    two_ref[...] = wide_ref[...].astype(BF16)


def conv_one_kernel(
    step, per, core_ref, sides_ref, x_ref, mine_ref, other_ref, h_ref, w_out_ref, send_ref,
    acc_ref, count_ref,
):
    if step is BEGIN:
        acc_ref[...] = jnp.zeros_like(acc_ref)
        count_ref[0] = 0.0

        def put(core):
            for half, ref in ((core, mine_ref), (1 - core, other_ref)):
                w_out_ref[:, half * HALF : (half + 1) * HALF] = ref[...].reshape(C_IN, HALF)

        for core in range(2):
            pl.when(core_ref[0] == core)(functools.partial(put, core))
        return

    if step is END:
        count = jnp.full((1, WIDTH), count_ref[0], F32)
        send_rows(
            send_ref,
            [row_sum(acc_ref[0:8]), row_sum(acc_ref[8:16]), count, jnp.zeros((1, WIDTH), F32)],
        )
        return

    h = dot_f(x_ref[...], w_out_ref[...])
    h_ref[...] = h
    for j in range(per):
        side = SIDE - 2 * sides_ref[step * per + j]
        mask = pixel_mask(side, WIDTH)
        one = h[j * PIX : (j + 1) * PIX]
        kept = one * mask
        acc_ref[0:8] += fold(kept)
        acc_ref[8:16] += fold(kept * one)
        count_ref[0] += (side * side).astype(F32)


def edge_masks(width):
    column = lax.broadcasted_iota(jnp.int32, (PIX, 128), 0) & 15
    first = jnp.where(column == 0, 0.0, 1.0).astype(F32)
    last = jnp.where(column == 15, 0.0, 1.0).astype(F32)
    return wide(first, width), wide(last, width)


def put_taps(taps_ref, j, act, first, last):
    shifted = (pltpu.roll(act, 1, 0) * first, act, pltpu.roll(act, PIX - 1, 0) * last)
    for d in range(3):
        piece = shifted[d].astype(BF16)
        for q in range(2):
            taps_ref[pl.ds(SIDE + j * (PIX + SIDE), PIX), pl.ds(q * 384 + d * 128, 128)] = piece[
                :, q * HALF : (q + 1) * HALF
            ]


def conv_two_kernel(
    step, per, sides_ref, got_ref, h_ref, w_ref, gain_ref, shift_ref, hat_ref, h2_ref, vec_ref, send_ref,
    taps_ref, acc_ref,
):
    if step is BEGIN:
        sums = total(got_ref)
        mean, inv = norm_terms(sums, sums[2:3])
        vec_ref[0:1] = mean
        vec_ref[1:2] = inv
        vec_ref[2:3] = sums[2:3]
        acc_ref[...] = jnp.zeros_like(acc_ref)
        taps_ref[...] = jnp.zeros_like(taps_ref)
        return

    if step is END:
        send_rows(send_ref, [row_sum(acc_ref[0:8]), row_sum(acc_ref[8:16])])
        return

    gain = gain_ref[:, :WIDTH] * 0.5
    shift = shift_ref[:, :WIDTH] * 0.5
    first, last = edge_masks(WIDTH)
    for j in range(per):
        side = SIDE - 2 * sides_ref[step * per + j]
        mask = pixel_mask(side, WIDTH)
        rows = pl.ds(j * PIX, PIX)
        hat = (h_ref[rows] - vec_ref[0:1]) * vec_ref[1:2]
        hat_ref[pl.ds(j * PIX, PIX)] = hat.astype(BF16)
        half_pre = hat * gain + shift
        act = half_pre * (1.0 + jnp.tanh(half_pre)) * mask
        put_taps(taps_ref, j, act, first, last)
    height = per * (PIX + SIDE)
    for q in range(2):
        cols = pl.ds(q * WIDTH, WIDTH)
        patches = jnp.concatenate(
            [taps_ref[pl.ds(SIDE * d, height), pl.ds(q * 384, 384)] for d in range(3)], axis=1
        )
        both = dot_f(patches, w_ref[:, cols])
        for j in range(per):
            h2 = both[j * (PIX + SIDE) : j * (PIX + SIDE) + PIX]
            h2_ref[pl.ds(j * PIX, PIX), cols] = h2
            side = SIDE - 2 * sides_ref[step * per + j]
            kept = h2 * pixel_mask(side, WIDTH)
            acc_ref[0:8, cols] += fold(kept)
            acc_ref[8:16, cols] += fold(kept * h2)


def act_two_kernel(
    step, per, sides_ref, one_ref, got_ref, h2_ref, gain_ref, shift_ref, fc_ref,
    hat_ref, pooled_ref, zin_ref, vec_ref, send_ref,
):
    if step is BEGIN:
        sums = total(got_ref)
        mean, inv = norm_terms(sums, jnp.concatenate([one_ref[2:3]] * 2, axis=1))
        vec_ref[0:1] = mean
        vec_ref[1:2] = inv
        return

    if step is END:
        z = high_f(pooled_ref[...], fc_ref[...])
        zin_ref[...] = z
        send_rows(send_ref, [row_sum(z), row_sum(z * z)])
        return

    gain = gain_ref[:, WIDTH : 3 * WIDTH] * 0.5
    shift = shift_ref[:, WIDTH : 3 * WIDTH] * 0.5
    for j in range(per):
        side = SIDE - 2 * sides_ref[step * per + j]
        mask = pixel_mask(side, 2 * WIDTH)
        rows = pl.ds(j * PIX, PIX)
        hat = (h2_ref[rows] - vec_ref[0:1]) * vec_ref[1:2]
        hat_ref[rows] = hat.astype(BF16)
        half_pre = hat * gain + shift
        value = half_pre * ((1.0 + jnp.tanh(half_pre)) * mask)
        sums = row_sum(fold(value))
        image = pl.ds(step * per + j, 1)
        pixels = (side * side).astype(F32)
        pooled_ref[image] = (sums[:, :WIDTH] + sums[:, WIDTH:]) / pixels


def slope_two_kernel(
    step, per, sides_ref, hat_ref, gain_ref, shift_ref, a2_ref, slope_ref, t2_ref, t4_ref
):
    if step is BEGIN:
        return

    if step is END:
        return

    gain = gain_ref[:, WIDTH : 3 * WIDTH] * 0.5
    shift = shift_ref[:, WIDTH : 3 * WIDTH] * 0.5
    for j in range(per):
        side = SIDE - 2 * sides_ref[step * per + j]
        mask = pixel_mask(side, 2 * WIDTH)
        rows = pl.ds(j * PIX, PIX)
        hat = hat_ref[rows].astype(F32)
        half_pre = hat * gain + shift
        a = (1.0 + jnp.tanh(half_pre)) * mask
        value = half_pre * a
        slope = (0.5 * a) * (1.0 + 2.0 * half_pre - value)
        a2_ref[rows] = value.astype(BF16)
        slope_ref[rows] = slope.astype(BF16)
        image = pl.ds(step * per + j, 1)
        t2_ref[image] = row_sum(fold(slope))
        t4_ref[image] = row_sum(fold(slope * hat))


def hidden_terms(zin, sums, n_images, gain_ref, shift_ref):
    mean, inv = norm_terms(sums, n_images)
    zhat = (zin - mean) * inv
    cols = slice(3 * WIDTH, 3 * WIDTH + INTER)
    half_z = (zhat * gain_ref[:, cols] + shift_ref[:, cols]) * 0.5
    value, slope = silu_parts(half_z)
    return zhat, inv, value, slope


def combine_kernel(
    step, per, n_images, got_ref, zin_ref, a2_ref, w3_ref, fc_ref, bias_ref, gain_ref, shift_ref,
    att_ref, comb_ref, gw_ref, csum_ref, hid_ref, send_ref, gram_ref, acc_ref,
):
    if step is BEGIN:
        zhat, inv, hidden, slope = hidden_terms(
            zin_ref[...], total(got_ref), n_images, gain_ref, shift_ref
        )
        hid_ref[0] = zhat
        hid_ref[1] = hidden
        hid_ref[2] = slope
        hid_ref[3] = jnp.broadcast_to(inv, slope.shape)
        logits = high_f(hidden, fc_ref[...]) + bias_ref[...]
        left, right = logits[:, :WIDTH], logits[:, WIDTH:]
        top = jnp.maximum(left, right)
        left, right = jnp.exp(left - top), jnp.exp(right - top)
        both = left + right
        att_ref[:, :WIDTH] = left / both
        att_ref[:, WIDTH:] = right / both
        gram_ref[...] = jnp.zeros_like(gram_ref)
        acc_ref[...] = jnp.zeros_like(acc_ref)
        return

    if step is END:
        w3 = w3_ref[...].astype(F32)
        csum = row_sum(acc_ref[...])
        csum_ref[...] = csum
        gw = high_f(gram_ref[...], w3)
        gw_ref[...] = gw
        send_rows(send_ref, [high_f(csum, w3), row_sum(w3 * gw)])
        return

    for j in range(per):
        rows = pl.ds(j * PIX, PIX)
        att = att_ref[pl.ds(step * per + j, 1)]
        a2 = a2_ref[rows].astype(F32)
        comb = (att[:, :WIDTH] * a2[:, :WIDTH] + att[:, WIDTH:] * a2[:, WIDTH:]).astype(BF16)
        comb_ref[rows] = comb
        acc_ref[...] += fold(comb.astype(F32))
    comb = comb_ref[...]
    gram_ref[...] += dot_rows(comb, comb)


def output_kernel(
    step, per, sides_ref, one_ref, got_ref, comb_ref, x_ref, cot_ref, w3_ref, gain_ref, shift_ref,
    out_ref, u3_ref, stat_ref, send_ref, vec_ref, acc_ref,
):
    if step is BEGIN:
        count = jnp.concatenate([one_ref[2:3]] * 4, axis=1)
        mean, inv = norm_terms(total(got_ref), count)
        scale = inv * gain_ref[:, 3 * WIDTH + INTER :]
        stat_ref[0:1] = mean
        stat_ref[1:2] = inv
        stat_ref[2:3] = scale
        stat_ref[3:4] = count
        vec_ref[0:1] = scale
        vec_ref[1:2] = shift_ref[:, 3 * WIDTH + INTER :] - mean * scale
        vec_ref[2:3] = 0.5 * scale
        acc_ref[...] = jnp.zeros_like(acc_ref)
        return

    if step is END:
        send_rows(
            send_ref,
            [0.5 * row_sum(acc_ref[0:8]), 0.5 * row_sum(acc_ref[8:16]) / vec_ref[0:1]],
        )
        return

    chunk = 16
    lanes = 512
    for j in range(per):
        side = SIDE - 2 * sides_ref[step * per + j]
        mask = pixel_mask(side, 128)
        h3 = dot_f(comb_ref[pl.ds(j * PIX, PIX)], w3_ref[...])
        for n in range(C_IN // lanes):
            cols = pl.ds(n * lanes, lanes)
            ups = jnp.zeros((8, lanes), F32)
            products = jnp.zeros((8, lanes), F32)
            for c in range(PIX // chunk):
                rows = pl.ds(j * PIX + c * chunk, chunk)
                scaled = (
                    h3[c * chunk : (c + 1) * chunk, n * lanes : (n + 1) * lanes] * vec_ref[0:1, cols]
                )
                pre = scaled + vec_ref[1:2, cols] + x_ref[rows, cols].astype(F32)
                half_pre = pre * 0.5
                a = (1.0 + jnp.tanh(half_pre)) * wide(mask[c * chunk : (c + 1) * chunk], lanes)
                value = half_pre * a
                out_ref[rows, cols] = value.astype(BF16)
                up = cot_ref[rows, cols].astype(F32) * (a * (1.0 + pre - value))
                u3_ref[rows, cols] = (up * vec_ref[2:3, cols]).astype(BF16)
                ups = ups + fold(up)
                products = products + fold(up * scaled)
            acc_ref[0:8, cols] += ups
            acc_ref[8:16, cols] += products


def project_kernel(step, comb_ref, u3_ref, w3_ref, p_ref, cu_ref):
    if step is BEGIN:
        cu_ref[...] = jnp.zeros_like(cu_ref)
        return

    if step is END:
        return

    u3 = u3_ref[...]
    p_ref[...] = dot_last(u3, w3_ref[...]).astype(BF16)
    cu_ref[...] += dot_rows(comb_ref[...], u3)


def back_three_kernel(
    step, per, three_ref, got_ref, hid_ref, comb_ref, p_ref, a2_ref, slope_ref,
    hat_ref, w3_ref, cu_ref, gw_ref, csum_ref, att_ref, fc_ref,
    t1_ref, t3_ref, duz_ref, w3g_ref, fcg_ref, norm_ref, s_ref, c_ref, send_ref, datt_ref,
):
    if step is BEGIN:
        mean, inv = three_ref[0:1], three_ref[1:2]
        scale, count = three_ref[2:3], three_ref[3:4]
        sums = total(got_ref)
        dshift = sums[0:1]
        dgain = (sums[1:2] - mean * dshift) * inv
        norm_ref[0:1] = dgain
        norm_ref[1:2] = dshift
        k2 = scale * inv * dgain / count
        k1 = scale * dshift / count - mean * k2
        w3 = w3_ref[...].astype(F32)
        s_ref[...] = dot_last((w3 * k2).astype(BF16), w3_ref[...]).astype(BF16)
        c_ref[...] = high_last(jnp.broadcast_to(k1, (8, C_IN)), w3)
        csum = jnp.broadcast_to(csum_ref[...], (8, WIDTH))
        outer = high_rows(csum, jnp.broadcast_to(k1, (8, C_IN))) * 0.125
        w3g_ref[...] = cu_ref[...] - outer - gw_ref[...] * k2
        return

    if step is END:
        att = att_ref[...]
        datt = datt_ref[...]
        both = att * datt
        inner = both[:, :WIDTH] + both[:, WIDTH:]
        dlog = both - att * jnp.concatenate([inner, inner], axis=1)
        zhat, hidden, slope = hid_ref[0], hid_ref[1], hid_ref[2]
        fcg = high_rows(hidden, dlog)
        duz = high_last(dlog, fc_ref[...]) * slope
        duz_ref[...] = duz
        bias = row_sum(dlog)
        rows = [row_sum(duz), row_sum(duz * zhat)]
        for b in range(4):
            cols = slice(b * 128, (b + 1) * 128)
            fcg_ref[pl.ds(b * INTER, INTER)] = fcg[:, cols]
            rows.append(bias[:, cols])
        send_rows(send_ref, rows + [jnp.zeros((2, 128), F32)])
        return

    corr = dot_f(comb_ref[...], s_ref[...])
    for j in range(per):
        rows = pl.ds(j * PIX, PIX)
        dcomb = p_ref[rows].astype(F32) - corr[j * PIX : (j + 1) * PIX] - c_ref[0:1]
        image = pl.ds(step * per + j, 1)
        for q in range(2):
            cols = pl.ds(q * WIDTH, WIDTH)
            datt_ref[image, cols] = row_sum(fold(dcomb * a2_ref[rows, cols].astype(F32)))
            u = dcomb * slope_ref[rows, cols].astype(F32)
            t1_ref[image, cols] = row_sum(fold(u))
            t3_ref[image, cols] = row_sum(fold(u * hat_ref[rows, cols].astype(F32)))


def back_att_kernel(
    n_images, got_ref, hid_ref, duz_ref, pooled_ref, sides_ref, fc_ref, att_ref,
    t1_ref, t2_ref, t3_ref, t4_ref, fcg_ref, gain_ref,
    dpool_ref, pack_ref, bias_ref, norm_ref, send_ref,
):
    zhat, inv = hid_ref[0], hid_ref[3, 0:1]
    sums = total(got_ref)
    norm_ref[0:1] = sums[1:2]
    norm_ref[1:2] = sums[0:1]
    for b in range(4):
        bias_ref[:, b * 128 : (b + 1) * 128] = sums[2 + b : 3 + b]
    scale = inv * gain_ref[:, 3 * WIDTH : 3 * WIDTH + INTER]
    dzin = scale * (duz_ref[...] - (sums[0:1] + zhat * sums[1:2]) / n_images)
    pack_ref[0:WIDTH] = high_rows(pooled_ref[...], dzin)
    pack_ref[WIDTH:] = fcg_ref[...]
    dpool_ref[...] = high_last(dzin, fc_ref[...])
    for i in range(dpool_ref.shape[0]):
        side = SIDE - 2 * sides_ref[i]
        dpool_ref[i : i + 1] = dpool_ref[i : i + 1] / (side * side).astype(F32)
    dpool = dpool_ref[...]
    both = jnp.concatenate([dpool, dpool], axis=1)
    att = att_ref[...]
    send_rows(
        send_ref,
        [
            row_sum(att * t1_ref[...] + both * t2_ref[...]),
            row_sum(att * t3_ref[...] + both * t4_ref[...]),
        ],
    )


def back_two_kernel(
    step, per, sides_ref, one_ref, two_ref, got_ref, comb_ref, p_ref, s_ref, c_ref, slope_ref, hat2_ref, hat1_ref, att_ref,
    dpool_ref, w_ref, gain_ref, shift_ref, dh2_ref, u1_ref, norm_ref, send_ref,
    vec_ref, pad_ref, acc_ref,
):
    if step is BEGIN:
        count = jnp.concatenate([one_ref[2:3]] * 2, axis=1)
        scale = two_ref[1:2] * gain_ref[:, WIDTH : 3 * WIDTH]
        sums = total(got_ref)
        norm_ref[0:1] = sums[1:2]
        norm_ref[1:2] = sums[0:1]
        vec_ref[0:1] = scale
        vec_ref[1:2] = scale * sums[0:1] / count
        vec_ref[2:3] = scale * sums[1:2] / count
        acc_ref[...] = jnp.zeros_like(acc_ref)
        pad_ref[...] = jnp.zeros_like(pad_ref)
        return

    if step is END:
        send_rows(send_ref, [row_sum(acc_ref[0:8]), row_sum(acc_ref[8:16])])
        return

    first, last = edge_masks(HALF)
    corr = dot_f(comb_ref[...], s_ref[...])
    for j in range(per):
        rows = pl.ds(j * PIX, PIX)
        side = SIDE - 2 * sides_ref[step * per + j]
        mask = pixel_mask(side, WIDTH)
        image = pl.ds(step * per + j, 1)
        dcomb = p_ref[rows].astype(F32) - corr[j * PIX : (j + 1) * PIX] - c_ref[0:1]
        dpool = dpool_ref[image]
        for q in range(2):
            cols = pl.ds(q * WIDTH, WIDTH)
            scale = vec_ref[0:1, cols]
            up = dcomb * (att_ref[image, cols] * scale) + dpool * scale
            dh2 = slope_ref[rows, cols].astype(F32) * up - mask * (
                vec_ref[1:2, cols] + hat2_ref[rows, cols].astype(F32) * vec_ref[2:3, cols]
            )
            dh2 = dh2.astype(BF16)
            dh2_ref[rows, cols] = dh2
            pad_ref[pl.ds(SIDE + j * (PIX + SIDE), PIX), cols] = dh2
    height = per * (PIX + SIDE)
    for q in range(2):
        lines = jnp.concatenate(
            [pad_ref[pl.ds(SIDE * (2 - d), height), pl.ds(q * WIDTH, WIDTH)] for d in range(3)],
            axis=1,
        )
        weight = jnp.concatenate(
            [
                jnp.concatenate(
                    [
                        w_ref[pl.ds((3 * r + d) * HALF, HALF), pl.ds(q * WIDTH, WIDTH)]
                        for r in range(3)
                    ],
                    axis=1,
                )
                for d in range(3)
            ],
            axis=0,
        )
        both = dot_last(lines, weight)
        for j in range(per):
            rows = pl.ds(j * PIX, PIX)
            side = SIDE - 2 * sides_ref[step * per + j]
            mask = pixel_mask(side, 128)
            y = both[j * (PIX + SIDE) : j * (PIX + SIDE) + PIX]
            da1 = (
                y[:, HALF : 2 * HALF]
                + pltpu.roll(y[:, :HALF], PIX - 1, 0) * last
                + pltpu.roll(y[:, 2 * HALF :], 1, 0) * first
            )
            cols = pl.ds(q * HALF, HALF)
            hat = hat1_ref[rows, cols].astype(F32)
            half_pre = 0.5 * (hat * gain_ref[:, cols] + shift_ref[:, cols])
            _, slope = silu_parts(half_pre)
            u1 = da1 * slope * mask
            u1_ref[rows, cols] = u1.astype(BF16)
            acc_ref[0:8, cols] += fold(u1)
            acc_ref[8:16, cols] += fold(u1 * hat)


def weight_two_kernel(
    step, per, core_ref, sides_ref, hat_ref, dh2_ref, gain_ref, shift_ref, keep_ref, give_ref,
    taps_ref, acc_ref,
):
    if step is BEGIN:
        acc_ref[...] = jnp.zeros_like(acc_ref)
        taps_ref[...] = jnp.zeros_like(taps_ref)
        return

    if step is END:
        def put(core):
            keep_ref[...] = acc_ref[core].T
            give_ref[...] = acc_ref[1 - core].T

        for core in range(2):
            pl.when(core_ref[0] == core)(functools.partial(put, core))
        return

    gain = gain_ref[:, :WIDTH] * 0.5
    shift = shift_ref[:, :WIDTH] * 0.5
    first, last = edge_masks(WIDTH)
    height = PIX + SIDE
    for j in range(per):
        side = SIDE - 2 * sides_ref[step * per + j]
        mask = pixel_mask(side, WIDTH)
        rows = pl.ds(j * PIX, PIX)
        half_pre = hat_ref[rows].astype(F32) * gain + shift
        act = half_pre * (1.0 + jnp.tanh(half_pre)) * mask
        put_taps(taps_ref, j, act, first, last)
    for q in range(2):
        patches = jnp.concatenate(
            [
                jnp.concatenate(
                    [
                        taps_ref[pl.ds(SIDE * d + j * height, PIX), pl.ds(q * 384, 384)]
                        for d in range(3)
                    ],
                    axis=1,
                )
                for j in range(per)
            ],
            axis=0,
        )
        acc_ref[q] += dot_rows(dh2_ref[:, q * WIDTH : (q + 1) * WIDTH], patches)


def back_one_kernel(
    step, per, core_ref, sides_ref, one_ref, three_ref, got_ref, u1_ref, hat_ref, u3_ref, x_ref, w_ref, gain_ref,
    norm2_ref, norm_att_ref, norm3_ref,
    ig_ref, keep_ref, give_ref, gain_out_ref, shift_out_ref, vec_ref, wide_ref, dh_ref, acc_ref,
):
    if step is BEGIN:
        count = one_ref[2:3]
        scale = one_ref[1:2] * gain_ref[:, :WIDTH]
        sums = total(got_ref)
        for row, out_ref in ((0, gain_out_ref), (1, shift_out_ref)):
            out_ref[:, :WIDTH] = sums[1 - row : 2 - row]
            out_ref[:, WIDTH : 3 * WIDTH] = norm2_ref[row : row + 1]
            out_ref[:, 3 * WIDTH : 3 * WIDTH + INTER] = norm_att_ref[row : row + 1]
            out_ref[:, 3 * WIDTH + INTER :] = norm3_ref[row : row + 1]
        vec_ref[0:1] = scale
        vec_ref[1:2] = scale * sums[0:1] / count
        vec_ref[2:3] = scale * sums[1:2] / count
        wide_ref[...] = 1.0 / three_ref[2:3]
        acc_ref[...] = jnp.zeros_like(acc_ref)
        return

    if step is END:
        def put(core):
            keep_ref[...] = acc_ref[core * HALF : (core + 1) * HALF].T
            give_ref[...] = acc_ref[(1 - core) * HALF : (2 - core) * HALF].T

        for core in range(2):
            pl.when(core_ref[0] == core)(functools.partial(put, core))
        return

    for j in range(per):
        rows = pl.ds(j * PIX, PIX)
        side = SIDE - 2 * sides_ref[step * per + j]
        mask = pixel_mask(side, WIDTH)
        dh_ref[rows] = (
            u1_ref[rows].astype(F32) * vec_ref[0:1]
            - mask * (vec_ref[1:2] + hat_ref[rows].astype(F32) * vec_ref[2:3])
        ).astype(BF16)
    dh = dh_ref[...]
    acc_ref[...] += dot_rows(dh, x_ref[...])
    dx = dot_last(dh, w_ref[...])
    ig_ref[...] = (u3_ref[...].astype(F32) * wide_ref[...] + dx).astype(BF16)


def round_up(value, multiple):
    return -(-value // multiple) * multiple


def pack_three_kernel(core_ref, w_ref, fc_ref, keep_ref, give_ref):
    shards = keep_ref.shape[0]
    w_rows = w_ref.shape[0] // shards
    fc_rows = fc_ref.shape[0] // (2 * shards)

    def put(half, out_ref):
        for f in range(shards):
            for b in range(4):
                low = (half * 4 + b) * 128
                out_ref[f, pl.ds(b * w_rows, w_rows)] = w_ref[
                    pl.ds(f * w_rows, w_rows), pl.ds(low, 128)
                ]
            out_ref[f, pl.ds(4 * w_rows, fc_rows)] = fc_ref[
                pl.ds((half * shards + f) * fc_rows, fc_rows)
            ]

    for core in range(2):

        @pl.when(core_ref[0] == core)
        def _():
            put(core, keep_ref)
            put(1 - core, give_ref)


def pack_two_kernel(keep_ref, other_ref, fc_ref, out_ref):
    shards, slot, _ = out_ref.shape
    rows = keep_ref.shape[0] // shards
    padded = round_up(rows, 16)
    fc = fc_ref[...]
    fc_half = (slot - padded) * 2 - fc.shape[0]
    if fc_half:
        fc = jnp.concatenate([fc, jnp.zeros((fc_half, 128), F32)], axis=0)
    fc = jnp.concatenate([fc[: slot - padded], fc[slot - padded :]], axis=1).astype(BF16)
    for f in range(shards):
        part = keep_ref[pl.ds(f * rows, rows)] + other_ref[pl.ds(f * rows, rows)]
        if padded > rows:
            part = jnp.concatenate([part, jnp.zeros((padded - rows, WIDTH), F32)], axis=0)
        out_ref[f, pl.ds(0, padded)] = part.astype(BF16)
        out_ref[f, pl.ds(padded, slot - padded)] = fc


def everyone(payload):
    return lax.all_to_all(payload, AXES, 0, 0, tiled=True)


def other_core(array):
    return lax.ppermute(array, "dp", [(0, 1), (1, 0)])


def both_halves(mine, axis=1):
    core = lax.axis_index("dp")
    other = other_core(mine)
    return jnp.where(
        core == 0,
        jnp.concatenate([mine, other], axis=axis),
        jnp.concatenate([other, mine], axis=axis),
    )


def gather_weights(core, weights):
    shards = lax.axis_size("fsdp")
    one, two, three = weights
    first = (shards, one.shape[0], HALF)
    second = (shards, 2 * two.shape[0] + 4 * three.shape[0], 128)
    spread_one, spread_two = call(
        pack_kernel,
        1,
        [(core, SMEM_SPEC)] + [(weight, whole(weight.shape)) for weight in weights],
        [(first, BF16, whole(first), True), (second, BF16, whole(second), True)],
        flops=1000000,
        moved=4000000,
        name="pack",
    )
    mine = lax.all_to_all(spread_one, "fsdp", 0, 0, tiled=True)
    other = other_core(mine)
    spread_two, mine, other = lax.optimization_barrier((spread_two, mine, other))
    mine_two = lax.all_to_all(spread_two, "fsdp", 0, 0, tiled=True)

    def others(mine_two, after):
        mine_two, _ = lax.optimization_barrier((mine_two, after))
        other_two = other_core(mine_two)
        shapes = [(shards * weight.shape[0], weight.shape[1]) for weight in (two, three)]
        return call(
            unpack_kernel,
            1,
            [(core, SMEM_SPEC), (mine_two, whole(second), True), (other_two, whole(second), True)],
            [(shape, BF16, whole(shape)) for shape in shapes],
            [pltpu.VMEM(shapes[0], F32)],
            flops=1000000,
            moved=4000000,
            name="unpack",
        )

    return mine, other, functools.partial(others, mine_two)


def slots(parts):
    return lax.all_to_all(parts, "fsdp", 0, 0, tiled=True)


def body(
    inputs,
    sides,
    weight_one,
    weight_two,
    weight_three,
    fc_first,
    fc_second,
    fc_bias,
    bn_gain,
    bn_shift,
    cotangent,
):
    images = inputs.shape[0]
    rows = images * PIX
    devices = lax.axis_size("fsdp") * lax.axis_size("dp")
    n_images = float(images * devices)
    x = inputs.reshape(rows, C_IN)
    cot = cotangent.reshape(rows, C_IN)
    gain = bn_gain.reshape(1, -1)
    shift = bn_shift.reshape(1, -1)
    bias = fc_bias.reshape(1, -1)
    n_ch = gain.shape[1]
    core = lax.axis_index("dp").astype(jnp.int32).reshape(1)

    def split(most):
        per = max(n for n in range(1, most + 1) if images % n == 0)
        return per, images // per

    core_in = (core, SMEM_SPEC)
    sides_in = (sides, SMEM_SPEC)
    gain_in = (gain, whole((1, n_ch)))
    shift_in = (shift, whole((1, n_ch)))

    def payload(k, n):
        return ((devices, k, n), F32, whole((devices, k, n)), True)

    def small(*shape):
        return (shape, F32, whole(shape))

    def full(array):
        return (array, whole(array.shape))

    def near(array):
        return (array, whole(array.shape), True)

    def blocks(array):
        return (array, Stream())

    def blocks_out(width, dtype=BF16, over=None):
        return ((rows, width), dtype, Stream(over))

    mine, other, others = gather_weights(core, (weight_one, weight_two, weight_three))

    per, steps = split(PER_CONV_ONE)
    h1, full_one, send = stream_call(
        lambda step, *refs, per=per: conv_one_kernel(step, per, *refs),
        per,
        steps,
        [core_in, sides_in, blocks(x), near(mine), near(other)],
        [blocks_out(WIDTH, F32), ((C_IN, WIDTH), BF16, whole((C_IN, WIDTH))), payload(4, WIDTH)],
        [pltpu.VMEM((16, WIDTH), F32), pltpu.SMEM((1,), F32)],
        flops=2 * rows * C_IN * WIDTH,
        moved=rows * C_IN * 2 + rows * WIDTH * 4,
        name="conv_one",
    )
    got_one = everyone(send)
    full_two, full_three = others(send)

    per, steps = split(PER_CONV_TWO)
    hat1, h2, stat1, send = stream_call(
        lambda step, *refs, per=per: conv_two_kernel(step, per, *refs),
        per,
        steps,
        [sides_in, near(got_one), blocks(h1), full(full_two), gain_in, shift_in],
        [blocks_out(WIDTH), blocks_out(2 * WIDTH, F32), small(8, WIDTH), payload(2, 2 * WIDTH)],
        [
            pltpu.VMEM((per * (PIX + SIDE) + 2 * SIDE, 6 * HALF), BF16),
            pltpu.VMEM((16, 2 * WIDTH), F32),
        ],
        flops=2 * rows * 9 * HALF * 2 * WIDTH,
        moved=rows * WIDTH * 14,
        name="conv_two",
    )
    got_two = everyone(send)

    per, steps = split(PER_ACT_TWO)
    hat2, pooled, zin, stat2, send = stream_call(
        lambda step, *refs, per=per: act_two_kernel(step, per, *refs),
        per,
        steps,
        [
            sides_in,
            full(stat1),
            near(got_two),
            blocks(h2),
            gain_in,
            shift_in,
            full(fc_first),
        ],
        [
            blocks_out(2 * WIDTH),
            small(images, WIDTH),
            small(images, INTER),
            small(8, 2 * WIDTH),
            payload(2, INTER),
        ],
        flops=rows * 2 * WIDTH * 20,
        moved=rows * 2 * WIDTH * 10,
        name="act_two",
    )
    got_att = everyone(send)

    per, steps = split(PER_SLOPE_TWO)
    a2, slope2, t2, t4 = stream_call(
        lambda step, *refs, per=per: slope_two_kernel(step, per, *refs),
        per,
        steps,
        [sides_in, blocks(hat2), gain_in, shift_in],
        [
            blocks_out(2 * WIDTH),
            blocks_out(2 * WIDTH),
            small(images, 2 * WIDTH),
            small(images, 2 * WIDTH),
        ],
        flops=rows * 2 * WIDTH * 20,
        moved=rows * 2 * WIDTH * 6,
        name="slope_two",
    )

    per, steps = split(PER_COMBINE)
    att, comb, gw, csum, hid, send = stream_call(
        lambda step, *refs, per=per: combine_kernel(step, per, n_images, *refs),
        per,
        steps,
        [
            near(got_att),
            full(zin),
            blocks(a2),
            full(full_three),
            full(fc_second),
            full(bias),
            gain_in,
            shift_in,
        ],
        [
            small(images, 2 * WIDTH),
            blocks_out(WIDTH),
            small(WIDTH, C_IN),
            small(1, WIDTH),
            small(4, images, INTER),
            payload(2, C_IN),
        ],
        [pltpu.VMEM((WIDTH, WIDTH), F32), pltpu.VMEM((8, WIDTH), F32)],
        flops=2 * rows * WIDTH * WIDTH,
        moved=rows * WIDTH * 6,
        name="combine",
    )
    got_three = everyone(send)

    per, steps = split(PER_OUTPUT)
    outputs, u3, stat3, send = stream_call(
        lambda step, *refs, per=per: output_kernel(step, per, *refs),
        per,
        steps,
        [
            sides_in,
            full(stat1),
            near(got_three),
            blocks(comb),
            blocks(x),
            blocks(cot),
            full(full_three),
            gain_in,
            shift_in,
        ],
        [
            blocks_out(C_IN, over=4),
            blocks_out(C_IN, over=5),
            small(8, C_IN),
            payload(2, C_IN),
        ],
        [pltpu.VMEM((8, C_IN), F32), pltpu.VMEM((16, C_IN), F32)],
        flops=2 * rows * WIDTH * C_IN,
        moved=rows * C_IN * 8,
        name="output",
    )
    got_back_three = everyone(send)

    per, steps = split(PER_PROJECT)
    p, cu = stream_call(
        project_kernel,
        per,
        steps,
        [blocks(comb), blocks(u3), full(full_three)],
        [blocks_out(WIDTH), small(WIDTH, C_IN)],
        flops=4 * rows * WIDTH * C_IN,
        moved=rows * C_IN * 4,
        name="project",
    )

    per, steps = split(PER_BACK_THREE)
    t1, t3, duz, w3_local, fc2_local, norm3, corr_weight, corr_row, send = stream_call(
        lambda step, *refs, per=per: back_three_kernel(step, per, *refs),
        per,
        steps,
        [
            full(stat3),
            near(got_back_three),
            full(hid),
            blocks(comb),
            blocks(p),
            blocks(a2),
            blocks(slope2),
            blocks(hat2),
            full(full_three),
            full(cu),
            full(gw),
            full(csum),
            full(att),
            full(fc_second),
        ],
        [
            small(images, 2 * WIDTH),
            small(images, 2 * WIDTH),
            small(images, INTER),
            small(WIDTH, C_IN),
            small(4 * INTER, 128),
            small(2, C_IN),
            ((WIDTH, WIDTH), BF16, whole((WIDTH, WIDTH))),
            small(8, WIDTH),
            payload(8, INTER),
        ],
        [pltpu.VMEM((images, 2 * WIDTH), F32)],
        flops=2 * rows * WIDTH * WIDTH,
        moved=rows * WIDTH * 16,
        name="back_three",
    )
    got_back_att = everyone(send)

    dpool, packed, fc_bias_grad, norm_att, send = call(
        functools.partial(back_att_kernel, n_images),
        1,
        [
            near(got_back_att),
            full(hid),
            full(duz),
            full(pooled),
            sides_in,
            full(fc_first),
            full(att),
            full(t1),
            full(t2),
            full(t3),
            full(t4),
            full(fc2_local),
            gain_in,
        ],
        [
            small(images, WIDTH),
            small(WIDTH + 4 * INTER, 128),
            small(1, 2 * WIDTH),
            small(2, INTER),
            payload(2, 2 * WIDTH),
        ],
        flops=10000000,
        moved=1000000,
        name="back_att",
    )
    got_back_two = everyone(send)

    shards = lax.axis_size("fsdp")
    w3_rows = WIDTH // shards
    fc_rows = packed.shape[0] // (2 * shards)
    slot = (shards, 4 * w3_rows + fc_rows, 128)
    keep, give = call(
        pack_three_kernel,
        1,
        [core_in, full(w3_local), full(packed)],
        [(slot, F32, whole(slot)), (slot, F32, whole(slot))],
        flops=1000000,
        moved=3000000,
        name="pack_three",
    )
    got_back_two, three = lax.optimization_barrier((got_back_two, keep + other_core(give)))
    three = slots(three)

    per, steps = split(PER_BACK_TWO)
    dh2, u1, norm2, send = stream_call(
        lambda step, *refs, per=per: back_two_kernel(step, per, *refs),
        per,
        steps,
        [
            sides_in,
            full(stat1),
            full(stat2),
            near(got_back_two),
            blocks(comb),
            blocks(p),
            full(corr_weight),
            full(corr_row),
            blocks(slope2),
            blocks(hat2),
            blocks(hat1),
            full(att),
            full(dpool),
            full(full_two),
            gain_in,
            shift_in,
        ],
        [
            blocks_out(2 * WIDTH),
            blocks_out(WIDTH),
            small(2, 2 * WIDTH),
            payload(2, WIDTH),
        ],
        [
            pltpu.VMEM((8, 2 * WIDTH), F32),
            pltpu.VMEM((per * (PIX + SIDE) + 2 * SIDE, 2 * WIDTH), BF16),
            pltpu.VMEM((16, WIDTH), F32),
        ],
        flops=2 * rows * 9 * HALF * 2 * WIDTH,
        moved=rows * WIDTH * 20,
        name="back_two",
    )
    send, three, dh2 = lax.optimization_barrier((send, three, dh2))
    got_back_one = everyone(send)

    per, steps = split(PER_WEIGHT_TWO)
    half = (9 * HALF, WIDTH)
    keep, give = stream_call(
        lambda step, *refs, per=per: weight_two_kernel(step, per, *refs),
        per,
        steps,
        [core_in, sides_in, blocks(hat1), blocks(dh2), gain_in, shift_in],
        [(half, F32, whole(half)), (half, F32, whole(half))],
        [
            pltpu.VMEM((per * (PIX + SIDE) + 2 * SIDE, 6 * HALF), BF16),
            pltpu.VMEM((2, WIDTH, 9 * HALF), F32),
        ],
        flops=2 * rows * 9 * HALF * 2 * WIDTH,
        moved=rows * WIDTH * 6,
        name="weight_two",
    )
    got_back_one, keep, give = lax.optimization_barrier((got_back_one, keep, give))
    three = jnp.sum(three, axis=0)
    w2_rows = 9 * HALF // shards
    w2_padded = round_up(w2_rows, 16)
    slot = (shards, w2_padded + round_up(fc_rows, 32) // 2, WIDTH)
    (parts,) = call(
        pack_two_kernel,
        1,
        [full(keep), near(other_core(give)), near(three[4 * w3_rows :])],
        [(slot, BF16, whole(slot))],
        flops=1000000,
        moved=3000000,
        name="pack_two",
    )
    got_back_one, parts = lax.optimization_barrier((got_back_one, parts))
    two = slots(parts)

    per, steps = split(PER_BACK_ONE)
    half = (C_IN, HALF)
    input_grad, keep, give, gain_grad, shift_grad = stream_call(
        lambda step, *refs, per=per: back_one_kernel(step, per, *refs),
        per,
        steps,
        [
            core_in,
            sides_in,
            full(stat1),
            full(stat3),
            near(got_back_one),
            blocks(u1),
            blocks(hat1),
            blocks(u3),
            blocks(x),
            full(full_one),
            gain_in,
            full(norm2),
            full(norm_att),
            full(norm3),
        ],
        [blocks_out(C_IN), small(*half), small(*half), small(1, n_ch), small(1, n_ch)],
        [
            pltpu.VMEM((8, WIDTH), F32),
            pltpu.VMEM((1, C_IN), F32),
            pltpu.VMEM((per * PIX, WIDTH), BF16),
            pltpu.VMEM((WIDTH, C_IN), F32),
        ],
        flops=4 * rows * WIDTH * C_IN,
        moved=rows * C_IN * 6,
        name="back_one",
    )

    one = (keep + other_core(give)).astype(BF16).reshape(shards, -1, HALF)
    one, two = lax.optimization_barrier((one, two))
    weight_one_grad = both_halves(jnp.sum(slots(one).astype(F32), axis=0))
    weight_two_grad = both_halves(jnp.sum(two[:, :w2_rows].astype(F32), axis=0))
    weight_three_grad = both_halves(
        jnp.concatenate([three[b * w3_rows : (b + 1) * w3_rows] for b in range(4)], axis=1)
    )
    fc = two[:, w2_padded:].astype(F32)
    fc = jnp.concatenate([fc[:, :, :128], fc[:, :, 128:]], axis=1)[:, :fc_rows].reshape(-1, 128)
    summed = both_halves(fc, 0)
    fc_first_grad = summed[:WIDTH]
    fc_second_grad = jnp.concatenate(
        [summed[WIDTH + b * INTER : WIDTH + (b + 1) * INTER] for b in range(4)], axis=1
    )
    return (
        outputs.reshape(inputs.shape),
        input_grad.reshape(inputs.shape),
        weight_one_grad,
        weight_two_grad,
        weight_three_grad,
        fc_first_grad,
        fc_second_grad,
        fc_bias_grad.reshape(-1),
        gain_grad.reshape(-1),
        shift_grad.reshape(-1),
    )


def solution(mesh):
    return jax.shard_map(
        body,
        mesh=mesh,
        in_specs=(
            P(("fsdp", "dp"), None, None),
            P(("fsdp", "dp")),
            P("fsdp", None),
            P("fsdp", None),
            P("fsdp", None),
            P(),
            P(),
            P(),
            P(),
            P(),
            P(("fsdp", "dp"), None, None),
        ),
        out_specs=(
            P(("fsdp", "dp"), None, None),
            P(("fsdp", "dp"), None, None),
            P("fsdp", None),
            P("fsdp", None),
            P("fsdp", None),
            P(),
            P(),
            P(),
            P(),
            P(),
        ),
        check_vma=False,
    )
```

```python
import functools

import jax
import jax.numpy as jnp
from jax import lax
from jax.experimental import pallas as pl
from jax.experimental.pallas import tpu as pltpu
from jax.sharding import PartitionSpec as P

C_IN = 1024
WIDTH = 256
INTER = 128
SIDE = 16
PIX = SIDE * SIDE
HALF = WIDTH // 2
EPS = 1e-05
AXES = ("fsdp", "dp")
HIGH = lax.Precision.HIGHEST
F32 = jnp.float32
BF16 = jnp.bfloat16
MIB = 1024 * 1024

AHEAD = 4
VMEM = 44
CHUNK = 32
PER_CONV_ONE = 4
PER_CONV_TWO = 3
PER_ACT_TWO = 4
PER_SLOPE_TWO = 3
PER_COMBINE = 6
PER_OUTPUT = 2
PER_PROJECT = 4
PER_BACK_THREE = 4
PER_BACK_TWO = 2
PER_WEIGHT_TWO = 4
PER_BACK_ONE = 2
PER_INPUT_GRAD = 2


def dot_f(left, right):
    return jnp.dot(left, right, preferred_element_type=F32)


def dot_rows(left, right):
    return lax.dot_general(left, right, (((0,), (0,)), ((), ())), preferred_element_type=F32)


def dot_last(left, right):
    return lax.dot_general(left, right, (((1,), (1,)), ((), ())), preferred_element_type=F32)


def high_f(left, right):
    return jnp.dot(left, right, preferred_element_type=F32, precision=HIGH)


def high_rows(left, right):
    return lax.dot_general(
        left, right, (((0,), (0,)), ((), ())), preferred_element_type=F32, precision=HIGH
    )


def high_last(left, right):
    return lax.dot_general(
        left, right, (((1,), (1,)), ((), ())), preferred_element_type=F32, precision=HIGH
    )


def exact_f(left, right):
    total_product = None
    for _ in range(3):
        piece = left.astype(BF16)
        product = dot_f(piece, right)
        total_product = product if total_product is None else total_product + product
        left = left - piece.astype(F32)
    return total_product


def pixel_mask(image_side, width):
    row = lax.broadcasted_iota(jnp.int32, (PIX, 128), 0)
    inside = ((row >> 4) < image_side) & ((row & 15) < image_side)
    return wide(jnp.where(inside, 1.0, 0.0).astype(F32), width)


def wide(mask, width):
    if width == 128:
        return mask
    return jnp.concatenate([mask] * (width // 128), axis=1)


def fold(values):
    rows, n = values.shape
    return jnp.sum(values.reshape(rows // 8, 8, n), axis=0)


def chunks(j=0):
    for low in range(0, PIX, CHUNK):
        yield pl.ds(j * PIX + low, CHUNK), slice(low, low + CHUNK)


def row_sum(values):
    return jnp.sum(values, axis=0, keepdims=True)


def total(payload_ref):
    return jnp.sum(payload_ref[...], axis=0)


def norm_terms(sums, count):
    mean = sums[0:1] / count
    variance = sums[1:2] / count - mean * mean
    return mean, lax.rsqrt(variance + EPS)


def send_rows(payload_ref, rows):
    block = jnp.concatenate(rows, axis=0)
    payload_ref[...] = jnp.broadcast_to(block[None], payload_ref.shape)


def silu_parts(half_pre):
    t = jnp.tanh(half_pre)
    a = 1.0 + t
    value = half_pre * a
    slope = 0.5 * a * (1.0 + half_pre * (1.0 - t))
    return value, slope


def whole(shape):
    zeros = (0,) * len(shape)
    return pl.BlockSpec(shape, lambda *_: zeros)


SMEM_SPEC = pl.BlockSpec(memory_space=pltpu.SMEM)


def call(kernel, grid, ins, outs, scratch=(), vmem=VMEM, flops=0, moved=0, name=None):
    arrays = [
        array
        if spec is SMEM_SPEC or near
        else pltpu.with_memory_space_constraint(array, pltpu.HBM)
        for array, spec, *near in ins
    ]
    shapes = [
        jax.ShapeDtypeStruct(shape, dtype) if near else pltpu.HBM(shape, dtype)
        for shape, dtype, _, *near in outs
    ]
    return pl.pallas_call(
        kernel,
        grid=(grid,),
        in_specs=[spec for _, spec, *_ in ins],
        out_specs=[spec for _, _, spec, *_ in outs],
        out_shape=shapes,
        scratch_shapes=list(scratch),
        compiler_params=pltpu.CompilerParams(
            dimension_semantics=("arbitrary",), vmem_limit_bytes=vmem * MIB
        ),
        cost_estimate=pl.CostEstimate(flops=flops, bytes_accessed=moved, transcendentals=0),
        name=name,
    )(*arrays)


class Stream:
    def __init__(self, over=None):
        self.over = over


BEGIN, END = "begin", "end"


def stream_call(kernel, per, steps, ins, outs, scratch=(), vmem=VMEM, flops=0, moved=0, name=None):
    block = per * PIX
    in_specs, out_specs, arrays, shapes, rooms = [], [], [], [], []
    in_streams, out_streams, room_of = [], [], {}
    for at, (array, spec, *near) in enumerate(ins):
        if isinstance(spec, Stream):
            in_streams.append(at)
            room_of[at] = len(rooms)
            rooms.append(pltpu.VMEM(array.shape, array.dtype))
            spec = pl.BlockSpec(memory_space=pltpu.HBM)
        elif near:
            arrays.append(array)
            in_specs.append(spec)
            continue
        in_specs.append(spec)
        arrays.append(
            array if spec is SMEM_SPEC else pltpu.with_memory_space_constraint(array, pltpu.HBM)
        )
    for at, (shape, dtype, spec, *near) in enumerate(outs):
        shapes.append(jax.ShapeDtypeStruct(shape, dtype) if near else pltpu.HBM(shape, dtype))
        if isinstance(spec, Stream):
            out_streams.append(at)
            if spec.over is None:
                room_of[len(ins) + at] = len(rooms)
                rooms.append(pltpu.VMEM(shape, dtype))
            else:
                room_of[len(ins) + at] = room_of[spec.over]
            spec = pl.BlockSpec(memory_space=pltpu.HBM)
        out_specs.append(spec)
    n_in, n_out, n_rooms = len(ins), len(outs), len(rooms)

    def whole_kernel(*refs):
        in_refs, out_refs = refs[:n_in], refs[n_in : n_in + n_out]
        room_refs = refs[n_in + n_out : n_in + n_out + n_rooms]
        own_refs = refs[n_in + n_out + n_rooms : -2]
        in_sems, out_sems = refs[-2:]

        def rows(step):
            return pl.ds(pl.multiple_of(step * block, block), block)

        def copies_in(step):
            return [
                pltpu.make_async_copy(
                    in_refs[at].at[rows(step)],
                    room_refs[room_of[at]].at[rows(step)],
                    in_sems.at[k, step],
                )
                for k, at in enumerate(in_streams)
            ]

        def copies_out(step):
            return [
                pltpu.make_async_copy(
                    room_refs[room_of[n_in + at]].at[rows(step)],
                    out_refs[at].at[rows(step)],
                    out_sems.at[k, step],
                )
                for k, at in enumerate(out_streams)
            ]

        def views(step):
            both = []
            for at, ref in enumerate(in_refs + out_refs):
                if at in room_of:
                    ref = room_refs[room_of[at]].at[rows(step)]
                both.append(ref)
            return both + list(own_refs)

        ahead = min(AHEAD, steps)
        for step in range(ahead):
            for copy in copies_in(step):
                copy.start()
        kernel(BEGIN, *views(0))

        def one(step, carry):
            for copy in copies_in(step):
                copy.wait()

            @pl.when(step + ahead < steps)
            def _():
                for copy in copies_in(step + ahead):
                    copy.start()

            kernel(step, *views(step))
            for copy in copies_out(step):
                copy.start()
            return carry

        lax.fori_loop(0, steps, one, 0)
        kernel(END, *views(0))

        def last(step, carry):
            for copy in copies_out(step):
                copy.wait()
            return carry

        lax.fori_loop(0, steps, last, 0)

    return pl.pallas_call(
        whole_kernel,
        in_specs=in_specs,
        out_specs=out_specs,
        out_shape=shapes,
        scratch_shapes=rooms
        + list(scratch)
        + [
            pltpu.SemaphoreType.DMA((max(len(in_streams), 1), steps)),
            pltpu.SemaphoreType.DMA((max(len(out_streams), 1), steps)),
        ],
        compiler_params=pltpu.CompilerParams(vmem_limit_bytes=vmem * MIB),
        cost_estimate=pl.CostEstimate(flops=flops, bytes_accessed=moved, transcendentals=0),
        name=name,
    )(*arrays)


def pack_kernel(core_ref, *refs):
    count = len(refs) // 2

    def put(half):
        for ref, out_ref in zip(refs[:count], refs[count:]):
            rows, cols = ref.shape
            for b in range(cols // 256):
                low = half * (cols // 2) + b * 128
                piece = ref[:, low : low + 128]
                for f in range(out_ref.shape[0]):
                    out_ref[f, pl.ds(b * rows, rows)] = piece

    for core in range(2):
        pl.when(core_ref[0] == core)(functools.partial(put, core))


def unpack_kernel(core_ref, mine_ref, other_ref, out_ref, *wide_refs):
    shards = mine_ref.shape[0]
    rows, cols = out_ref.shape[0] // shards, out_ref.shape[1]

    def put(half, source_ref):
        for f in range(shards):
            for b in range(cols // 256):
                piece = source_ref[f, pl.ds(b * rows, rows)]
                at = (pl.ds(f * rows, rows), pl.ds(half * (cols // 2) + b * 128, 128))
                if wide_refs:
                    wide_refs[0][at] = piece.astype(F32)
                else:
                    out_ref[at] = piece

    for core in range(2):

        @pl.when(core_ref[0] == core)
        def _():
            put(core, mine_ref)
            put(1 - core, other_ref)

    if wide_refs:
        out_ref[...] = wide_refs[0][...].astype(BF16)


def conv_one_kernel(
    step, per, core_ref, sides_ref, x_ref, mine_ref, other_ref, h_ref, w_out_ref, send_ref,
    acc_ref, count_ref,
):
    if step is BEGIN:
        acc_ref[...] = jnp.zeros_like(acc_ref)
        count_ref[0] = 0.0

        def put(core):
            for half, ref in ((core, mine_ref), (1 - core, other_ref)):
                w_out_ref[:, half * HALF : (half + 1) * HALF] = ref[...].reshape(C_IN, HALF)

        for core in range(2):
            pl.when(core_ref[0] == core)(functools.partial(put, core))
        return

    if step is END:
        count = jnp.full((1, WIDTH), count_ref[0], F32)
        send_rows(
            send_ref,
            [row_sum(acc_ref[0:8]), row_sum(acc_ref[8:16]), count, jnp.zeros((1, WIDTH), F32)],
        )
        return

    h = dot_f(x_ref[...], w_out_ref[...])
    h_ref[...] = h
    for j in range(per):
        side = SIDE - 2 * sides_ref[step * per + j]
        mask = pixel_mask(side, 128)
        sums = jnp.zeros((8, WIDTH), F32)
        squares = jnp.zeros((8, WIDTH), F32)
        for rows, part in chunks():
            one = h[j * PIX + part.start : j * PIX + part.stop]
            kept = one * wide(mask[part], WIDTH)
            sums = sums + fold(kept)
            squares = squares + fold(kept * one)
        acc_ref[0:8] += sums
        acc_ref[8:16] += squares
        count_ref[0] += (side * side).astype(F32)


def edge_masks(width):
    column = lax.broadcasted_iota(jnp.int32, (CHUNK, 128), 0) & 15
    first = jnp.where(column == 0, 0.0, 1.0).astype(F32)
    last = jnp.where(column == 15, 0.0, 1.0).astype(F32)
    return wide(first, width), wide(last, width)


def put_taps(taps_ref, j, part, act, first, last):
    shifted = (pltpu.roll(act, 1, 0) * first, act, pltpu.roll(act, CHUNK - 1, 0) * last)
    low = SIDE + j * (PIX + SIDE) + part.start
    for d in range(3):
        piece = shifted[d].astype(BF16)
        for q in range(2):
            taps_ref[pl.ds(low, CHUNK), pl.ds(q * 384 + d * 128, 128)] = piece[
                :, q * HALF : (q + 1) * HALF
            ]


def conv_two_kernel(
    step, per, sides_ref, got_ref, h_ref, w_ref, gain_ref, shift_ref, hat_ref, h2_ref, vec_ref, send_ref,
    taps_ref, acc_ref,
):
    if step is BEGIN:
        sums = total(got_ref)
        mean, inv = norm_terms(sums, sums[2:3])
        vec_ref[0:1] = mean
        vec_ref[1:2] = inv
        vec_ref[2:3] = sums[2:3]
        acc_ref[...] = jnp.zeros_like(acc_ref)
        taps_ref[...] = jnp.zeros_like(taps_ref)
        return

    if step is END:
        send_rows(send_ref, [row_sum(acc_ref[0:8]), row_sum(acc_ref[8:16])])
        return

    gain = gain_ref[:, :WIDTH] * 0.5
    shift = shift_ref[:, :WIDTH] * 0.5
    first, last = edge_masks(WIDTH)
    for j in range(per):
        side = SIDE - 2 * sides_ref[step * per + j]
        mask = pixel_mask(side, 128)
        for rows, part in chunks(j):
            hat = (h_ref[rows] - vec_ref[0:1]) * vec_ref[1:2]
            hat_ref[rows] = hat.astype(BF16)
            half_pre = hat * gain + shift
            act = half_pre * ((1.0 + jnp.tanh(half_pre)) * wide(mask[part], WIDTH))
            put_taps(taps_ref, j, part, act, first, last)
    height = per * (PIX + SIDE)
    for q in range(2):
        cols = pl.ds(q * WIDTH, WIDTH)
        patches = jnp.concatenate(
            [taps_ref[pl.ds(SIDE * d, height), pl.ds(q * 384, 384)] for d in range(3)], axis=1
        )
        both = dot_f(patches, w_ref[:, cols])
        for j in range(per):
            side = SIDE - 2 * sides_ref[step * per + j]
            mask = pixel_mask(side, 128)
            sums = jnp.zeros((8, WIDTH), F32)
            squares = jnp.zeros((8, WIDTH), F32)
            for rows, part in chunks(j):
                low = j * (PIX + SIDE) + part.start
                h2 = both[low : low + CHUNK]
                h2_ref[rows, cols] = h2
                kept = h2 * wide(mask[part], WIDTH)
                sums = sums + fold(kept)
                squares = squares + fold(kept * h2)
            acc_ref[0:8, cols] += sums
            acc_ref[8:16, cols] += squares


def act_two_kernel(
    step, per, sides_ref, one_ref, got_ref, h2_ref, gain_ref, shift_ref, fc_ref,
    hat_ref, pooled_ref, zin_ref, vec_ref, send_ref,
):
    if step is BEGIN:
        sums = total(got_ref)
        mean, inv = norm_terms(sums, jnp.concatenate([one_ref[2:3]] * 2, axis=1))
        vec_ref[0:1] = mean
        vec_ref[1:2] = inv
        return

    if step is END:
        z = high_f(pooled_ref[...], fc_ref[...])
        zin_ref[...] = z
        send_rows(send_ref, [row_sum(z), row_sum(z * z)])
        return

    gain = gain_ref[:, WIDTH : 3 * WIDTH] * 0.5
    shift = shift_ref[:, WIDTH : 3 * WIDTH] * 0.5
    for j in range(per):
        side = SIDE - 2 * sides_ref[step * per + j]
        mask = pixel_mask(side, 128)
        sums = jnp.zeros((8, WIDTH), F32)
        for q in range(2):
            cols = slice(q * WIDTH, (q + 1) * WIDTH)
            for rows, part in chunks(j):
                hat = (h2_ref[rows, cols] - vec_ref[0:1, cols]) * vec_ref[1:2, cols]
                hat_ref[rows, cols] = hat.astype(BF16)
                half_pre = hat * gain[:, cols] + shift[:, cols]
                value = half_pre * ((1.0 + jnp.tanh(half_pre)) * wide(mask[part], WIDTH))
                sums = sums + fold(value)
        image = pl.ds(step * per + j, 1)
        pixels = (side * side).astype(F32)
        pooled_ref[image] = row_sum(sums) / pixels


def slope_two_kernel(
    step, per, sides_ref, hat_ref, gain_ref, shift_ref, a2_ref, slope_ref, t2_ref, t4_ref
):
    if step is BEGIN:
        return

    if step is END:
        return

    gain = gain_ref[:, WIDTH : 3 * WIDTH] * 0.5
    shift = shift_ref[:, WIDTH : 3 * WIDTH] * 0.5
    for j in range(per):
        side = SIDE - 2 * sides_ref[step * per + j]
        mask = pixel_mask(side, 128)
        image = pl.ds(step * per + j, 1)
        for q in range(2):
            cols = slice(q * WIDTH, (q + 1) * WIDTH)
            sums = jnp.zeros((8, WIDTH), F32)
            products = jnp.zeros((8, WIDTH), F32)
            for rows, part in chunks(j):
                hat = hat_ref[rows, cols].astype(F32)
                half_pre = hat * gain[:, cols] + shift[:, cols]
                a = (1.0 + jnp.tanh(half_pre)) * wide(mask[part], WIDTH)
                value = half_pre * a
                slope = a * (0.5 + half_pre - 0.5 * value)
                a2_ref[rows, cols] = value.astype(BF16)
                slope_ref[rows, cols] = slope.astype(BF16)
                sums = sums + fold(slope)
                products = products + fold(slope * hat)
            t2_ref[image, cols] = row_sum(sums)
            t4_ref[image, cols] = row_sum(products)


def hidden_terms(zin, sums, n_images, gain_ref, shift_ref):
    mean, inv = norm_terms(sums, n_images)
    zhat = (zin - mean) * inv
    cols = slice(3 * WIDTH, 3 * WIDTH + INTER)
    half_z = (zhat * gain_ref[:, cols] + shift_ref[:, cols]) * 0.5
    value, slope = silu_parts(half_z)
    return zhat, inv, value, slope


def combine_kernel(
    step, per, n_images, got_ref, zin_ref, a2_ref, w3_ref, fc_ref, bias_ref, gain_ref, shift_ref,
    att_ref, comb_ref, gw_ref, csum_ref, hid_ref, send_ref, gram_ref, acc_ref,
):
    if step is BEGIN:
        zhat, inv, hidden, slope = hidden_terms(
            zin_ref[...], total(got_ref), n_images, gain_ref, shift_ref
        )
        hid_ref[0] = zhat
        hid_ref[1] = hidden
        hid_ref[2] = slope
        hid_ref[3] = jnp.broadcast_to(inv, slope.shape)
        logits = high_f(hidden, fc_ref[...]) + bias_ref[...]
        left, right = logits[:, :WIDTH], logits[:, WIDTH:]
        top = jnp.maximum(left, right)
        left, right = jnp.exp(left - top), jnp.exp(right - top)
        both = left + right
        att_ref[:, :WIDTH] = left / both
        att_ref[:, WIDTH:] = right / both
        gram_ref[...] = jnp.zeros_like(gram_ref)
        acc_ref[...] = jnp.zeros_like(acc_ref)
        return

    if step is END:
        csum = row_sum(acc_ref[...])
        csum_ref[...] = csum
        both = jnp.concatenate([gram_ref[...], jnp.broadcast_to(csum, (8, WIDTH))], axis=0)
        both = exact_f(both, w3_ref[...])
        gw = both[:WIDTH]
        gw_ref[...] = gw
        send_rows(send_ref, [both[WIDTH : WIDTH + 1], row_sum(w3_ref[...].astype(F32) * gw)])
        return

    for j in range(per):
        att = att_ref[pl.ds(step * per + j, 1)]
        sums = jnp.zeros((8, WIDTH), F32)
        for rows, _ in chunks(j):
            left = att[:, :WIDTH] * a2_ref[rows, :WIDTH].astype(F32)
            comb = (left + att[:, WIDTH:] * a2_ref[rows, WIDTH:].astype(F32)).astype(BF16)
            comb_ref[rows] = comb
            sums = sums + fold(comb.astype(F32))
        acc_ref[...] += sums
    comb = comb_ref[...]
    gram_ref[...] += dot_rows(comb, comb)


def output_kernel(
    step, per, sides_ref, one_ref, got_ref, comb_ref, x_ref, cot_ref, w3_ref, gain_ref, shift_ref,
    out_ref, u3_ref, stat_ref, send_ref, vec_ref, acc_ref,
):
    if step is BEGIN:
        count = jnp.concatenate([one_ref[2:3]] * 4, axis=1)
        mean, inv = norm_terms(total(got_ref), count)
        scale = inv * gain_ref[:, 3 * WIDTH + INTER :]
        stat_ref[0:1] = mean
        stat_ref[1:2] = inv
        stat_ref[2:3] = scale
        stat_ref[3:4] = count
        vec_ref[0:1] = scale
        vec_ref[1:2] = shift_ref[:, 3 * WIDTH + INTER :] - mean * scale
        vec_ref[2:3] = 0.5 * scale
        acc_ref[...] = jnp.zeros_like(acc_ref)
        return

    if step is END:
        send_rows(
            send_ref,
            [0.5 * row_sum(acc_ref[0:8]), 0.5 * row_sum(acc_ref[8:16]) / vec_ref[0:1]],
        )
        return

    chunk = 16
    lanes = 512
    for j in range(per):
        side = SIDE - 2 * sides_ref[step * per + j]
        mask = pixel_mask(side, 128)
        h3 = dot_f(comb_ref[pl.ds(j * PIX, PIX)], w3_ref[...])
        for n in range(C_IN // lanes):
            cols = pl.ds(n * lanes, lanes)
            ups = jnp.zeros((8, lanes), F32)
            products = jnp.zeros((8, lanes), F32)
            for c in range(PIX // chunk):
                rows = pl.ds(j * PIX + c * chunk, chunk)
                scaled = (
                    h3[c * chunk : (c + 1) * chunk, n * lanes : (n + 1) * lanes] * vec_ref[0:1, cols]
                )
                pre = scaled + vec_ref[1:2, cols] + x_ref[rows, cols].astype(F32)
                half_pre = pre * 0.5
                a = (1.0 + jnp.tanh(half_pre)) * wide(mask[c * chunk : (c + 1) * chunk], lanes)
                value = half_pre * a
                out_ref[rows, cols] = value.astype(BF16)
                up = cot_ref[rows, cols].astype(F32) * (a * (1.0 + pre - value))
                u3_ref[rows, cols] = (up * vec_ref[2:3, cols]).astype(BF16)
                ups = ups + fold(up)
                products = products + fold(up * scaled)
            acc_ref[0:8, cols] += ups
            acc_ref[8:16, cols] += products


def project_kernel(step, comb_ref, u3_ref, w3_ref, p_ref, cu_ref):
    if step is BEGIN:
        cu_ref[...] = jnp.zeros_like(cu_ref)
        return

    if step is END:
        return

    u3 = u3_ref[...]
    p_ref[...] = dot_last(u3, w3_ref[...]).astype(BF16)
    cu_ref[...] += dot_rows(comb_ref[...], u3)


def back_three_kernel(
    step, per, three_ref, got_ref, hid_ref, comb_ref, p_ref, a2_ref, slope_ref,
    hat_ref, w3_ref, cu_ref, gw_ref, csum_ref, att_ref, fc_ref,
    t1_ref, t3_ref, duz_ref, w3g_ref, fcg_ref, norm_ref, s_ref, c_ref, send_ref, datt_ref,
):
    if step is BEGIN:
        mean, inv = three_ref[0:1], three_ref[1:2]
        scale, count = three_ref[2:3], three_ref[3:4]
        sums = total(got_ref)
        dshift = sums[0:1]
        dgain = (sums[1:2] - mean * dshift) * inv
        norm_ref[0:1] = dgain
        norm_ref[1:2] = dshift
        k2 = scale * inv * dgain / count
        k1 = scale * dshift / count - mean * k2
        w3 = w3_ref[...].astype(F32)
        s_ref[...] = dot_last((w3 * k2).astype(BF16), w3_ref[...]).astype(BF16)
        c_ref[...] = high_last(jnp.broadcast_to(k1, (8, C_IN)), w3)
        csum = jnp.broadcast_to(csum_ref[...], (8, WIDTH))
        outer = high_rows(csum, jnp.broadcast_to(k1, (8, C_IN))) * 0.125
        w3g_ref[...] = cu_ref[...] - outer - gw_ref[...] * k2
        return

    if step is END:
        att = att_ref[...]
        datt = datt_ref[...]
        both = att * datt
        inner = both[:, :WIDTH] + both[:, WIDTH:]
        dlog = both - att * jnp.concatenate([inner, inner], axis=1)
        zhat, hidden, slope = hid_ref[0], hid_ref[1], hid_ref[2]
        fcg = high_rows(hidden, dlog)
        duz = high_last(dlog, fc_ref[...]) * slope
        duz_ref[...] = duz
        bias = row_sum(dlog)
        rows = [row_sum(duz), row_sum(duz * zhat)]
        for b in range(4):
            cols = slice(b * 128, (b + 1) * 128)
            fcg_ref[pl.ds(b * INTER, INTER)] = fcg[:, cols]
            rows.append(bias[:, cols])
        send_rows(send_ref, rows + [jnp.zeros((2, 128), F32)])
        return

    corr = dot_f(comb_ref[...], s_ref[...])
    for j in range(per):
        image = pl.ds(step * per + j, 1)
        sums = [jnp.zeros((8, WIDTH), F32)] * 6
        for rows, part in chunks(j):
            low = j * PIX + part.start
            dcomb = p_ref[rows].astype(F32) - corr[low : low + CHUNK] - c_ref[0:1]
            for q in range(2):
                cols = slice(q * WIDTH, (q + 1) * WIDTH)
                u = dcomb * slope_ref[rows, cols].astype(F32)
                sums[q] = sums[q] + fold(dcomb * a2_ref[rows, cols].astype(F32))
                sums[2 + q] = sums[2 + q] + fold(u)
                sums[4 + q] = sums[4 + q] + fold(u * hat_ref[rows, cols].astype(F32))
        for k, ref in enumerate((datt_ref, t1_ref, t3_ref)):
            for q in range(2):
                ref[image, q * WIDTH : (q + 1) * WIDTH] = row_sum(sums[2 * k + q])


def back_att_kernel(
    n_images, got_ref, hid_ref, duz_ref, pooled_ref, sides_ref, fc_ref, att_ref,
    t1_ref, t2_ref, t3_ref, t4_ref, fcg_ref, gain_ref,
    dpool_ref, pack_ref, bias_ref, norm_ref, send_ref,
):
    zhat, inv = hid_ref[0], hid_ref[3, 0:1]
    sums = total(got_ref)
    norm_ref[0:1] = sums[1:2]
    norm_ref[1:2] = sums[0:1]
    for b in range(4):
        bias_ref[:, b * 128 : (b + 1) * 128] = sums[2 + b : 3 + b]
    scale = inv * gain_ref[:, 3 * WIDTH : 3 * WIDTH + INTER]
    dzin = scale * (duz_ref[...] - (sums[0:1] + zhat * sums[1:2]) / n_images)
    pack_ref[0:WIDTH] = high_rows(pooled_ref[...], dzin)
    pack_ref[WIDTH:] = fcg_ref[...]
    dpool_ref[...] = high_last(dzin, fc_ref[...])
    for i in range(dpool_ref.shape[0]):
        side = SIDE - 2 * sides_ref[i]
        dpool_ref[i : i + 1] = dpool_ref[i : i + 1] / (side * side).astype(F32)
    dpool = dpool_ref[...]
    both = jnp.concatenate([dpool, dpool], axis=1)
    att = att_ref[...]
    send_rows(
        send_ref,
        [
            row_sum(att * t1_ref[...] + both * t2_ref[...]),
            row_sum(att * t3_ref[...] + both * t4_ref[...]),
        ],
    )


def back_two_kernel(
    step, per, sides_ref, one_ref, two_ref, got_ref, comb_ref, p_ref, s_ref, c_ref, slope_ref, hat2_ref, hat1_ref, att_ref,
    dpool_ref, w_ref, gain_ref, shift_ref, dh2_ref, u1_ref, norm_ref, send_ref,
    vec_ref, pad_ref, acc_ref,
):
    if step is BEGIN:
        count = jnp.concatenate([one_ref[2:3]] * 2, axis=1)
        scale = two_ref[1:2] * gain_ref[:, WIDTH : 3 * WIDTH]
        sums = total(got_ref)
        norm_ref[0:1] = sums[1:2]
        norm_ref[1:2] = sums[0:1]
        vec_ref[0:1] = scale
        vec_ref[1:2] = scale * sums[0:1] / count
        vec_ref[2:3] = scale * sums[1:2] / count
        acc_ref[...] = jnp.zeros_like(acc_ref)
        pad_ref[...] = jnp.zeros_like(pad_ref)
        return

    if step is END:
        send_rows(send_ref, [row_sum(acc_ref[0:8]), row_sum(acc_ref[8:16])])
        return

    first, last = edge_masks(HALF)
    corr = dot_f(comb_ref[...], s_ref[...])
    for j in range(per):
        side = SIDE - 2 * sides_ref[step * per + j]
        mask = pixel_mask(side, 128)
        image = pl.ds(step * per + j, 1)
        dpool = dpool_ref[image]
        for rows, part in chunks(j):
            low = j * PIX + part.start
            dcomb = p_ref[rows].astype(F32) - corr[low : low + CHUNK] - c_ref[0:1]
            for q in range(2):
                cols = slice(q * WIDTH, (q + 1) * WIDTH)
                scale = vec_ref[0:1, cols]
                up = dcomb * (att_ref[image, cols] * scale) + dpool * scale
                dh2 = slope_ref[rows, cols].astype(F32) * up - wide(mask[part], WIDTH) * (
                    vec_ref[1:2, cols] + hat2_ref[rows, cols].astype(F32) * vec_ref[2:3, cols]
                )
                dh2 = dh2.astype(BF16)
                dh2_ref[rows, cols] = dh2
                pad_ref[pl.ds(SIDE + j * (PIX + SIDE) + part.start, CHUNK), cols] = dh2
    height = per * (PIX + SIDE)
    for q in range(2):
        lines = jnp.concatenate(
            [pad_ref[pl.ds(SIDE * (2 - d), height), pl.ds(q * WIDTH, WIDTH)] for d in range(3)],
            axis=1,
        )
        weight = jnp.concatenate(
            [
                jnp.concatenate(
                    [
                        w_ref[pl.ds((3 * r + d) * HALF, HALF), pl.ds(q * WIDTH, WIDTH)]
                        for r in range(3)
                    ],
                    axis=1,
                )
                for d in range(3)
            ],
            axis=0,
        )
        both = dot_last(lines, weight)
        for j in range(per):
            side = SIDE - 2 * sides_ref[step * per + j]
            mask = pixel_mask(side, 128)
            cols = slice(q * HALF, (q + 1) * HALF)
            gain = gain_ref[:, cols] * 0.5
            shift = shift_ref[:, cols] * 0.5
            sums = jnp.zeros((8, HALF), F32)
            products = jnp.zeros((8, HALF), F32)
            for rows, part in chunks(j):
                low = j * (PIX + SIDE) + part.start
                y = both[low : low + CHUNK]
                da1 = (
                    y[:, HALF : 2 * HALF]
                    + pltpu.roll(y[:, :HALF], CHUNK - 1, 0) * last
                    + pltpu.roll(y[:, 2 * HALF :], 1, 0) * first
                )
                hat = hat1_ref[rows, cols].astype(F32)
                half_pre = hat * gain + shift
                a = (1.0 + jnp.tanh(half_pre)) * mask[part]
                u1 = da1 * (a * (0.5 + half_pre - 0.5 * half_pre * a))
                u1_ref[rows, cols] = u1.astype(BF16)
                sums = sums + fold(u1)
                products = products + fold(u1 * hat)
            acc_ref[0:8, cols] += sums
            acc_ref[8:16, cols] += products


def weight_two_kernel(
    step, per, core_ref, sides_ref, hat_ref, dh2_ref, gain_ref, shift_ref, keep_ref, give_ref,
    taps_ref, acc_ref,
):
    if step is BEGIN:
        acc_ref[...] = jnp.zeros_like(acc_ref)
        taps_ref[...] = jnp.zeros_like(taps_ref)
        return

    if step is END:
        def put(core):
            keep_ref[...] = acc_ref[core].T
            give_ref[...] = acc_ref[1 - core].T

        for core in range(2):
            pl.when(core_ref[0] == core)(functools.partial(put, core))
        return

    gain = gain_ref[:, :WIDTH] * 0.5
    shift = shift_ref[:, :WIDTH] * 0.5
    first, last = edge_masks(WIDTH)
    height = PIX + SIDE
    for j in range(per):
        side = SIDE - 2 * sides_ref[step * per + j]
        mask = pixel_mask(side, 128)
        for rows, part in chunks(j):
            half_pre = hat_ref[rows].astype(F32) * gain + shift
            act = half_pre * ((1.0 + jnp.tanh(half_pre)) * wide(mask[part], WIDTH))
            put_taps(taps_ref, j, part, act, first, last)
    for q in range(2):
        patches = jnp.concatenate(
            [
                jnp.concatenate(
                    [
                        taps_ref[pl.ds(SIDE * d + j * height, PIX), pl.ds(q * 384, 384)]
                        for d in range(3)
                    ],
                    axis=1,
                )
                for j in range(per)
            ],
            axis=0,
        )
        acc_ref[q] += dot_rows(dh2_ref[:, q * WIDTH : (q + 1) * WIDTH], patches)


def back_one_kernel(
    step, per, core_ref, sides_ref, one_ref, got_ref, u1_ref, hat_ref, x_ref, gain_ref, norm2_ref,
    norm_att_ref, norm3_ref, dh_ref, keep_ref, give_ref, gain_out_ref, shift_out_ref, vec_ref, acc_ref,
):
    if step is BEGIN:
        count = one_ref[2:3]
        scale = one_ref[1:2] * gain_ref[:, :WIDTH]
        sums = total(got_ref)
        for row, out_ref in ((0, gain_out_ref), (1, shift_out_ref)):
            out_ref[:, :WIDTH] = sums[1 - row : 2 - row]
            out_ref[:, WIDTH : 3 * WIDTH] = norm2_ref[row : row + 1]
            out_ref[:, 3 * WIDTH : 3 * WIDTH + INTER] = norm_att_ref[row : row + 1]
            out_ref[:, 3 * WIDTH + INTER :] = norm3_ref[row : row + 1]
        vec_ref[0:1] = scale
        vec_ref[1:2] = scale * sums[0:1] / count
        vec_ref[2:3] = scale * sums[1:2] / count
        acc_ref[...] = jnp.zeros_like(acc_ref)
        return

    if step is END:

        def put(core):
            keep_ref[...] = acc_ref[core * HALF : (core + 1) * HALF].T
            give_ref[...] = acc_ref[(1 - core) * HALF : (2 - core) * HALF].T

        for core in range(2):
            pl.when(core_ref[0] == core)(functools.partial(put, core))
        return

    for j in range(per):
        side = SIDE - 2 * sides_ref[step * per + j]
        mask = pixel_mask(side, 128)
        for rows, part in chunks(j):
            dh_ref[rows] = (
                u1_ref[rows].astype(F32) * vec_ref[0:1]
                - wide(mask[part], WIDTH) * (vec_ref[1:2] + hat_ref[rows].astype(F32) * vec_ref[2:3])
            ).astype(BF16)
    acc_ref[...] += dot_rows(dh_ref[...], x_ref[...])


def input_grad_kernel(step, dh_ref, u3_ref, three_ref, w_ref, ig_ref, wide_ref):
    if step is BEGIN:
        wide_ref[...] = 1.0 / three_ref[2:3]
        return

    if step is END:
        return

    dx = dot_last(dh_ref[...], w_ref[...])
    for low in range(0, dx.shape[0], 16):
        rows = pl.ds(low, 16)
        ig_ref[rows] = (u3_ref[rows].astype(F32) * wide_ref[...] + dx[low : low + 16]).astype(BF16)


def round_up(value, multiple):
    return -(-value // multiple) * multiple


def pack_three_kernel(core_ref, w_ref, fc_ref, keep_ref, give_ref):
    shards = keep_ref.shape[0]
    w_rows = w_ref.shape[0] // shards
    fc_rows = fc_ref.shape[0] // (2 * shards)

    def put(half, out_ref):
        for f in range(shards):
            for b in range(4):
                low = (half * 4 + b) * 128
                out_ref[f, pl.ds(b * w_rows, w_rows)] = w_ref[
                    pl.ds(f * w_rows, w_rows), pl.ds(low, 128)
                ]
            out_ref[f, pl.ds(4 * w_rows, fc_rows)] = fc_ref[
                pl.ds((half * shards + f) * fc_rows, fc_rows)
            ]

    for core in range(2):

        @pl.when(core_ref[0] == core)
        def _():
            put(core, keep_ref)
            put(1 - core, give_ref)


def two_wide(part, rows):
    missing = 2 * rows - part.shape[0]
    if missing:
        part = jnp.concatenate([part, jnp.zeros((missing, 128), F32)], axis=0)
    return jnp.concatenate([part[:rows], part[rows:]], axis=1)


def slot_rows(two_rows, fc_rows, one_rows):
    return round_up(two_rows, 16), round_up(fc_rows, 32) // 2, round_up(one_rows, 32) // 2


def add_slots(ref, at, rows):
    rows = pl.ds(at, rows)
    both = ref[0, rows].astype(F32)
    for f in range(1, ref.shape[0]):
        both = both + ref[f, rows].astype(F32)
    return both


def pack_last_kernel(
    fc_rows, keep2_ref, other2_ref, keep1_ref, other1_ref, three_ref, out_ref
):
    shards = out_ref.shape[0]
    two_rows = keep2_ref.shape[0] // shards
    one_rows = keep1_ref.shape[0] // shards
    two_slot, fc_slot, one_slot = slot_rows(two_rows, fc_rows, one_rows)
    fc = add_slots(three_ref, three_ref.shape[1] - fc_rows, fc_rows)
    fc = two_wide(fc, fc_slot).astype(BF16)
    for f in range(shards):
        rows = pl.ds(f * two_rows, two_rows)
        part = keep2_ref[rows] + other2_ref[rows]
        if two_slot > two_rows:
            part = jnp.concatenate([part, jnp.zeros((two_slot - two_rows, WIDTH), F32)], axis=0)
        out_ref[f, pl.ds(0, two_slot)] = part.astype(BF16)
        out_ref[f, pl.ds(two_slot, fc_slot)] = fc
        rows = pl.ds(f * one_rows, one_rows)
        part = two_wide(keep1_ref[rows] + other1_ref[rows], one_slot)
        out_ref[f, pl.ds(two_slot + fc_slot, one_slot)] = part.astype(BF16)


def sum_last_kernel(two_rows, fc_rows, one_rows, parts_ref, three_ref, out_ref):
    shards = parts_ref.shape[0]
    two_slot, fc_slot, one_slot = slot_rows(two_rows, fc_rows, one_rows)
    out_ref[pl.ds(0, two_slot)] = add_slots(parts_ref, 0, two_slot)
    out_ref[pl.ds(two_slot, one_slot)] = add_slots(parts_ref, two_slot + fc_slot, one_slot)
    at = two_slot + one_slot
    three_half = (three_ref.shape[1] - fc_rows) // 2
    three = add_slots(three_ref, 0, 2 * three_half)
    out_ref[pl.ds(at, three_half)] = two_wide(three, three_half)
    at += three_half
    for f in range(shards):
        out_ref[pl.ds(at + f * fc_slot, fc_slot)] = parts_ref[f, pl.ds(two_slot, fc_slot)].astype(F32)


def finish_kernel(
    two_rows, fc_rows, one_rows, three_rows, core_ref, mine_ref, other_ref,
    one_ref, two_ref, three_ref, fc1_ref, fc2_ref, pack_ref,
):
    two_slot, fc_slot, one_slot = slot_rows(two_rows, fc_rows, one_rows)
    three_half = 2 * three_rows
    at_three = two_slot + one_slot
    at_fc = at_three + three_half
    shards = (mine_ref.shape[0] - at_fc) // fc_slot

    def tall(ref, at, half_rows, rows):
        both = jnp.concatenate(
            [ref[pl.ds(at, half_rows), :128], ref[pl.ds(at, half_rows), 128:]], axis=0
        )
        return both[:rows]

    def put(half, ref):
        two_ref[:, half * WIDTH : (half + 1) * WIDTH] = ref[pl.ds(0, two_rows)]
        one_ref[:, half * HALF : (half + 1) * HALF] = tall(ref, two_slot, one_slot, one_rows)
        three = tall(ref, at_three, three_half, 4 * three_rows)
        for b in range(4):
            low = half * 512 + b * 128
            three_ref[:, low : low + 128] = three[b * three_rows : (b + 1) * three_rows]
        for f in range(shards):
            pack_ref[pl.ds((half * shards + f) * fc_rows, fc_rows)] = tall(
                ref, at_fc + f * fc_slot, fc_slot, fc_rows
            )

    for core in range(2):

        @pl.when(core_ref[0] == core)
        def _():
            put(core, mine_ref)
            put(1 - core, other_ref)

    fc1_ref[...] = pack_ref[0:WIDTH]
    for b in range(4):
        fc2_ref[:, b * 128 : (b + 1) * 128] = pack_ref[pl.ds(WIDTH + b * INTER, INTER)]


def everyone(payload):
    return lax.all_to_all(payload, AXES, 0, 0, tiled=True)


def other_core(array):
    return lax.ppermute(array, "dp", [(0, 1), (1, 0)])


def spread_weights(core, weights):
    shards = lax.axis_size("fsdp")
    shapes = [(shards, w.shape[0] * w.shape[1] // 256, 128) for w in weights]
    return call(
        pack_kernel,
        1,
        [(core, SMEM_SPEC)] + [(weight, whole(weight.shape)) for weight in weights],
        [(shape, BF16, whole(shape), True) for shape in shapes],
        flops=1000000,
        moved=4000000,
        name="pack",
    )


def join_weight(core, mine, shape):
    other = other_core(mine)
    rows = shape[0] // mine.shape[0]
    return call(
        unpack_kernel,
        1,
        [(core, SMEM_SPEC), (mine, whole(mine.shape), True), (other, whole(mine.shape), True)],
        [(shape, BF16, whole(shape))],
        [] if rows % 16 == 0 else [pltpu.VMEM(shape, F32)],
        flops=1000000,
        moved=4000000,
        name="unpack",
    )[0]


def slots(parts):
    return lax.all_to_all(parts, "fsdp", 0, 0, tiled=True)


def body(
    inputs,
    sides,
    weight_one,
    weight_two,
    weight_three,
    fc_first,
    fc_second,
    fc_bias,
    bn_gain,
    bn_shift,
    cotangent,
):
    images = inputs.shape[0]
    rows = images * PIX
    devices = lax.axis_size("fsdp") * lax.axis_size("dp")
    n_images = float(images * devices)
    x = inputs.reshape(rows, C_IN)
    cot = cotangent.reshape(rows, C_IN)
    gain = bn_gain.reshape(1, -1)
    shift = bn_shift.reshape(1, -1)
    bias = fc_bias.reshape(1, -1)
    n_ch = gain.shape[1]
    core = lax.axis_index("dp").astype(jnp.int32).reshape(1)

    def split(most):
        per = max(n for n in range(1, most + 1) if images % n == 0)
        return per, images // per

    core_in = (core, SMEM_SPEC)
    sides_in = (sides, SMEM_SPEC)
    gain_in = (gain, whole((1, n_ch)))
    shift_in = (shift, whole((1, n_ch)))

    def payload(k, n):
        return ((devices, k, n), F32, whole((devices, k, n)), True)

    def small(*shape):
        return (shape, F32, whole(shape))

    def full(array):
        return (array, whole(array.shape))

    def near(array):
        return (array, whole(array.shape), True)

    def blocks(array):
        return (array, Stream())

    def blocks_out(width, dtype=BF16, over=None):
        return ((rows, width), dtype, Stream(over))

    spread_one, spread_two, spread_three = spread_weights(
        core, (weight_one, weight_two, weight_three)
    )
    mine = slots(spread_one)
    other = other_core(mine)
    spread_two, mine, other = lax.optimization_barrier((spread_two, mine, other))
    mine_two = slots(spread_two)

    per, steps = split(PER_CONV_ONE)
    h1, full_one, send = stream_call(
        lambda step, *refs, per=per: conv_one_kernel(step, per, *refs),
        per,
        steps,
        [core_in, sides_in, blocks(x), near(mine), near(other)],
        [blocks_out(WIDTH, F32), ((C_IN, WIDTH), BF16, whole((C_IN, WIDTH))), payload(4, WIDTH)],
        [pltpu.VMEM((16, WIDTH), F32), pltpu.SMEM((1,), F32)],
        flops=2 * rows * C_IN * WIDTH,
        moved=rows * C_IN * 2 + rows * WIDTH * 4,
        name="conv_one",
    )
    send, mine_two = lax.optimization_barrier((send, mine_two))
    got_one = everyone(send)
    full_two = join_weight(core, mine_two, (9 * HALF, 2 * WIDTH))
    got_one, spread_three, full_two = lax.optimization_barrier((got_one, spread_three, full_two))
    mine_three = slots(spread_three)

    per, steps = split(PER_CONV_TWO)
    hat1, h2, stat1, send = stream_call(
        lambda step, *refs, per=per: conv_two_kernel(step, per, *refs),
        per,
        steps,
        [sides_in, near(got_one), blocks(h1), full(full_two), gain_in, shift_in],
        [blocks_out(WIDTH), blocks_out(2 * WIDTH, F32), small(8, WIDTH), payload(2, 2 * WIDTH)],
        [
            pltpu.VMEM((per * (PIX + SIDE) + 2 * SIDE, 6 * HALF), BF16),
            pltpu.VMEM((16, 2 * WIDTH), F32),
        ],
        flops=2 * rows * 9 * HALF * 2 * WIDTH,
        moved=rows * WIDTH * 14,
        name="conv_two",
    )
    send, mine_three = lax.optimization_barrier((send, mine_three))
    got_two = everyone(send)
    full_three = join_weight(core, mine_three, (WIDTH, C_IN))

    per, steps = split(PER_ACT_TWO)
    hat2, pooled, zin, stat2, send = stream_call(
        lambda step, *refs, per=per: act_two_kernel(step, per, *refs),
        per,
        steps,
        [
            sides_in,
            full(stat1),
            near(got_two),
            blocks(h2),
            gain_in,
            shift_in,
            full(fc_first),
        ],
        [
            blocks_out(2 * WIDTH),
            small(images, WIDTH),
            small(images, INTER),
            small(8, 2 * WIDTH),
            payload(2, INTER),
        ],
        flops=rows * 2 * WIDTH * 20,
        moved=rows * 2 * WIDTH * 10,
        name="act_two",
    )
    got_att = everyone(send)

    per, steps = split(PER_SLOPE_TWO)
    a2, slope2, t2, t4 = stream_call(
        lambda step, *refs, per=per: slope_two_kernel(step, per, *refs),
        per,
        steps,
        [sides_in, blocks(hat2), gain_in, shift_in],
        [
            blocks_out(2 * WIDTH),
            blocks_out(2 * WIDTH),
            small(images, 2 * WIDTH),
            small(images, 2 * WIDTH),
        ],
        flops=rows * 2 * WIDTH * 20,
        moved=rows * 2 * WIDTH * 6,
        name="slope_two",
    )

    per, steps = split(PER_COMBINE)
    att, comb, gw, csum, hid, send = stream_call(
        lambda step, *refs, per=per: combine_kernel(step, per, n_images, *refs),
        per,
        steps,
        [
            near(got_att),
            full(zin),
            blocks(a2),
            full(full_three),
            full(fc_second),
            full(bias),
            gain_in,
            shift_in,
        ],
        [
            small(images, 2 * WIDTH),
            blocks_out(WIDTH),
            small(WIDTH, C_IN),
            small(1, WIDTH),
            small(4, images, INTER),
            payload(2, C_IN),
        ],
        [pltpu.VMEM((WIDTH, WIDTH), F32), pltpu.VMEM((8, WIDTH), F32)],
        flops=2 * rows * WIDTH * WIDTH,
        moved=rows * WIDTH * 6,
        name="combine",
    )
    got_three = everyone(send)

    per, steps = split(PER_OUTPUT)
    outputs, u3, stat3, send = stream_call(
        lambda step, *refs, per=per: output_kernel(step, per, *refs),
        per,
        steps,
        [
            sides_in,
            full(stat1),
            near(got_three),
            blocks(comb),
            blocks(x),
            blocks(cot),
            full(full_three),
            gain_in,
            shift_in,
        ],
        [
            blocks_out(C_IN, over=4),
            blocks_out(C_IN, over=5),
            small(8, C_IN),
            payload(2, C_IN),
        ],
        [pltpu.VMEM((8, C_IN), F32), pltpu.VMEM((16, C_IN), F32)],
        flops=2 * rows * WIDTH * C_IN,
        moved=rows * C_IN * 8,
        name="output",
    )
    got_back_three = everyone(send)

    per, steps = split(PER_PROJECT)
    p, cu = stream_call(
        project_kernel,
        per,
        steps,
        [blocks(comb), blocks(u3), full(full_three)],
        [blocks_out(WIDTH), small(WIDTH, C_IN)],
        flops=4 * rows * WIDTH * C_IN,
        moved=rows * C_IN * 4,
        name="project",
    )

    per, steps = split(PER_BACK_THREE)
    t1, t3, duz, w3_local, fc2_local, norm3, corr_weight, corr_row, send = stream_call(
        lambda step, *refs, per=per: back_three_kernel(step, per, *refs),
        per,
        steps,
        [
            full(stat3),
            near(got_back_three),
            full(hid),
            blocks(comb),
            blocks(p),
            blocks(a2),
            blocks(slope2),
            blocks(hat2),
            full(full_three),
            full(cu),
            full(gw),
            full(csum),
            full(att),
            full(fc_second),
        ],
        [
            small(images, 2 * WIDTH),
            small(images, 2 * WIDTH),
            small(images, INTER),
            small(WIDTH, C_IN),
            small(4 * INTER, 128),
            small(2, C_IN),
            ((WIDTH, WIDTH), BF16, whole((WIDTH, WIDTH))),
            small(8, WIDTH),
            payload(8, INTER),
        ],
        [pltpu.VMEM((images, 2 * WIDTH), F32)],
        flops=2 * rows * WIDTH * WIDTH,
        moved=rows * WIDTH * 16,
        name="back_three",
    )
    got_back_att = everyone(send)

    dpool, packed, fc_bias_grad, norm_att, send = call(
        functools.partial(back_att_kernel, n_images),
        1,
        [
            near(got_back_att),
            full(hid),
            full(duz),
            full(pooled),
            sides_in,
            full(fc_first),
            full(att),
            full(t1),
            full(t2),
            full(t3),
            full(t4),
            full(fc2_local),
            gain_in,
        ],
        [
            small(images, WIDTH),
            small(WIDTH + 4 * INTER, 128),
            small(1, 2 * WIDTH),
            small(2, INTER),
            payload(2, 2 * WIDTH),
        ],
        flops=10000000,
        moved=1000000,
        name="back_att",
    )
    got_back_two = everyone(send)

    shards = lax.axis_size("fsdp")
    w3_rows = WIDTH // shards
    fc_rows = packed.shape[0] // (2 * shards)
    slot = (shards, 4 * w3_rows + fc_rows, 128)
    keep, give = call(
        pack_three_kernel,
        1,
        [core_in, full(w3_local), full(packed)],
        [(slot, F32, whole(slot)), (slot, F32, whole(slot))],
        flops=1000000,
        moved=3000000,
        name="pack_three",
    )
    three = slots(keep + other_core(give))

    per, steps = split(PER_BACK_TWO)
    dh2, u1, norm2, send = stream_call(
        lambda step, *refs, per=per: back_two_kernel(step, per, *refs),
        per,
        steps,
        [
            sides_in,
            full(stat1),
            full(stat2),
            near(got_back_two),
            blocks(comb),
            blocks(p),
            full(corr_weight),
            full(corr_row),
            blocks(slope2),
            blocks(hat2),
            blocks(hat1),
            full(att),
            full(dpool),
            full(full_two),
            gain_in,
            shift_in,
        ],
        [
            blocks_out(2 * WIDTH),
            blocks_out(WIDTH),
            small(2, 2 * WIDTH),
            payload(2, WIDTH),
        ],
        [
            pltpu.VMEM((8, 2 * WIDTH), F32),
            pltpu.VMEM((per * (PIX + SIDE) + 2 * SIDE, 2 * WIDTH), BF16),
            pltpu.VMEM((16, WIDTH), F32),
        ],
        flops=2 * rows * 9 * HALF * 2 * WIDTH,
        moved=rows * WIDTH * 20,
        name="back_two",
    )
    send, three, dh2 = lax.optimization_barrier((send, three, dh2))
    got_back_one = everyone(send)

    per, steps = split(PER_WEIGHT_TWO)
    half = (9 * HALF, WIDTH)
    keep, give = stream_call(
        lambda step, *refs, per=per: weight_two_kernel(step, per, *refs),
        per,
        steps,
        [core_in, sides_in, blocks(hat1), blocks(dh2), gain_in, shift_in],
        [(half, F32, whole(half)), (half, F32, whole(half))],
        [
            pltpu.VMEM((per * (PIX + SIDE) + 2 * SIDE, 6 * HALF), BF16),
            pltpu.VMEM((2, WIDTH, 9 * HALF), F32),
        ],
        flops=2 * rows * 9 * HALF * 2 * WIDTH,
        moved=rows * WIDTH * 6,
        name="weight_two",
    )
    got_back_one, keep, give = lax.optimization_barrier((got_back_one, keep, give))
    per, steps = split(PER_BACK_ONE)
    half_one = (C_IN, HALF)
    dh1, keep_one, give_one, gain_grad, shift_grad = stream_call(
        lambda step, *refs, per=per: back_one_kernel(step, per, *refs),
        per,
        steps,
        [
            core_in,
            sides_in,
            full(stat1),
            near(got_back_one),
            blocks(u1),
            blocks(hat1),
            blocks(x),
            gain_in,
            full(norm2),
            full(norm_att),
            full(norm3),
        ],
        [
            blocks_out(WIDTH),
            small(*half_one),
            small(*half_one),
            small(1, n_ch),
            small(1, n_ch),
        ],
        [pltpu.VMEM((8, WIDTH), F32), pltpu.VMEM((WIDTH, C_IN), F32)],
        flops=2 * rows * WIDTH * C_IN,
        moved=rows * C_IN * 4,
        name="back_one",
    )

    two_rows, one_rows = 9 * HALF // shards, C_IN // shards
    two_slot, fc_slot, one_slot = slot_rows(two_rows, fc_rows, one_rows)
    slot = (shards, two_slot + fc_slot + one_slot, WIDTH)
    (parts,) = call(
        functools.partial(pack_last_kernel, fc_rows),
        1,
        [
            full(keep),
            near(other_core(give)),
            full(keep_one),
            near(other_core(give_one)),
            near(three),
        ],
        [(slot, BF16, whole(slot))],
        flops=1000000,
        moved=5000000,
        name="pack_last",
    )
    dh1, parts = lax.optimization_barrier((dh1, parts))
    parts = slots(parts)

    per, steps = split(PER_INPUT_GRAD)
    (input_grad,) = stream_call(
        input_grad_kernel,
        per,
        steps,
        [blocks(dh1), blocks(u3), full(stat3), full(full_one)],
        [blocks_out(C_IN, over=1)],
        [pltpu.VMEM((1, C_IN), F32)],
        flops=2 * rows * WIDTH * C_IN,
        moved=rows * C_IN * 5,
        name="input_grad",
    )

    parts, input_grad = lax.optimization_barrier((parts, input_grad))
    sums = (two_slot + one_slot + 2 * w3_rows + shards * fc_slot, WIDTH)
    (mine,) = call(
        functools.partial(sum_last_kernel, two_rows, fc_rows, one_rows),
        1,
        [near(parts), near(three)],
        [(sums, F32, whole(sums), True)],
        flops=1000000,
        moved=2000000,
        name="sum_last",
    )
    (weight_one_grad, weight_two_grad, weight_three_grad, fc_first_grad, fc_second_grad) = call(
        functools.partial(finish_kernel, two_rows, fc_rows, one_rows, w3_rows),
        1,
        [core_in, near(mine), near(other_core(mine))],
        [
            small(one_rows, WIDTH),
            small(two_rows, 2 * WIDTH),
            small(w3_rows, C_IN),
            small(WIDTH, INTER),
            small(INTER, 2 * WIDTH),
        ],
        [pltpu.VMEM((2 * shards * fc_rows, 128), F32)],
        flops=1000000,
        moved=2000000,
        name="finish",
    )
    return (
        outputs.reshape(inputs.shape),
        input_grad.reshape(inputs.shape),
        weight_one_grad,
        weight_two_grad,
        weight_three_grad,
        fc_first_grad,
        fc_second_grad,
        fc_bias_grad.reshape(-1),
        gain_grad.reshape(-1),
        shift_grad.reshape(-1),
    )


def solution(mesh):
    return jax.shard_map(
        body,
        mesh=mesh,
        in_specs=(
            P(("fsdp", "dp"), None, None),
            P(("fsdp", "dp")),
            P("fsdp", None),
            P("fsdp", None),
            P("fsdp", None),
            P(),
            P(),
            P(),
            P(),
            P(),
            P(("fsdp", "dp"), None, None),
        ),
        out_specs=(
            P(("fsdp", "dp"), None, None),
            P(("fsdp", "dp"), None, None),
            P("fsdp", None),
            P("fsdp", None),
            P("fsdp", None),
            P(),
            P(),
            P(),
            P(),
            P(),
        ),
        check_vma=False,
    )
```

```python
import functools

import jax
import jax.numpy as jnp
from jax import lax
from jax.experimental import pallas as pl
from jax.experimental.pallas import tpu as pltpu
from jax.sharding import PartitionSpec as P

C_IN = 1024
WIDTH = 256
INTER = 128
SIDE = 16
PIX = SIDE * SIDE
HALF = WIDTH // 2
EPS = 1e-05
AXES = ("fsdp", "dp")
HIGH = lax.Precision.HIGHEST
F32 = jnp.float32
BF16 = jnp.bfloat16
MIB = 1024 * 1024

AHEAD = 4
VMEM = 44
CHUNK = 32
PER_CONV_ONE = 4
PER_CONV_TWO = 3
PER_ACT_TWO = 4
PER_COMBINE = 6
PER_OUTPUT = 2
PER_OUTER_THREE = 4
PER_BACK_THREE = 3
PER_BACK_TWO = 2
PER_WEIGHT_TWO = 4
PER_BACK_ONE = 3
PER_INPUT_GRAD = 3


def dot_f(left, right):
    return jnp.dot(left, right, preferred_element_type=F32)


def dot_rows(left, right):
    return lax.dot_general(left, right, (((0,), (0,)), ((), ())), preferred_element_type=F32)


def dot_last(left, right):
    return lax.dot_general(left, right, (((1,), (1,)), ((), ())), preferred_element_type=F32)


def high_f(left, right):
    return jnp.dot(left, right, preferred_element_type=F32, precision=HIGH)


def high_rows(left, right):
    return lax.dot_general(
        left, right, (((0,), (0,)), ((), ())), preferred_element_type=F32, precision=HIGH
    )


def high_last(left, right):
    return lax.dot_general(
        left, right, (((1,), (1,)), ((), ())), preferred_element_type=F32, precision=HIGH
    )


def exact_f(left, right):
    total_product = None
    for _ in range(3):
        piece = left.astype(BF16)
        product = dot_f(piece, right)
        total_product = product if total_product is None else total_product + product
        left = left - piece.astype(F32)
    return total_product


def pixel_mask(image_side, width):
    row = lax.broadcasted_iota(jnp.int32, (PIX, 128), 0)
    inside = ((row >> 4) < image_side) & ((row & 15) < image_side)
    return wide(jnp.where(inside, 1.0, 0.0).astype(F32), width)


def wide(mask, width):
    if width == 128:
        return mask
    return jnp.concatenate([mask] * (width // 128), axis=1)


def fold(values):
    rows, n = values.shape
    return jnp.sum(values.reshape(rows // 8, 8, n), axis=0)


def chunks(j=0):
    for low in range(0, PIX, CHUNK):
        yield pl.ds(j * PIX + low, CHUNK), slice(low, low + CHUNK)


def row_sum(values):
    return jnp.sum(values, axis=0, keepdims=True)


def total(payload_ref):
    return jnp.sum(payload_ref[...], axis=0)


def norm_terms(sums, count):
    mean = sums[0:1] / count
    variance = sums[1:2] / count - mean * mean
    return mean, lax.rsqrt(variance + EPS)


def send_rows(payload_ref, rows):
    block = jnp.concatenate(rows, axis=0)
    payload_ref[...] = jnp.broadcast_to(block[None], payload_ref.shape)


def silu_parts(half_pre):
    t = jnp.tanh(half_pre)
    a = 1.0 + t
    value = half_pre * a
    slope = 0.5 * a * (1.0 + half_pre * (1.0 - t))
    return value, slope


def whole(shape):
    zeros = (0,) * len(shape)
    return pl.BlockSpec(shape, lambda *_: zeros)


SMEM_SPEC = pl.BlockSpec(memory_space=pltpu.SMEM)


def call(kernel, grid, ins, outs, scratch=(), vmem=VMEM, flops=0, moved=0, name=None):
    arrays = [
        array
        if spec is SMEM_SPEC or near
        else pltpu.with_memory_space_constraint(array, pltpu.HBM)
        for array, spec, *near in ins
    ]
    shapes = [
        jax.ShapeDtypeStruct(shape, dtype) if near else pltpu.HBM(shape, dtype)
        for shape, dtype, _, *near in outs
    ]
    return pl.pallas_call(
        kernel,
        grid=(grid,),
        in_specs=[spec for _, spec, *_ in ins],
        out_specs=[spec for _, _, spec, *_ in outs],
        out_shape=shapes,
        scratch_shapes=list(scratch),
        compiler_params=pltpu.CompilerParams(
            dimension_semantics=("arbitrary",), vmem_limit_bytes=vmem * MIB
        ),
        cost_estimate=pl.CostEstimate(flops=flops, bytes_accessed=moved, transcendentals=0),
        name=name,
    )(*arrays)


class Stream:
    def __init__(self, over=None):
        self.over = over


BEGIN, END = "begin", "end"


def stream_call(kernel, per, steps, ins, outs, scratch=(), vmem=VMEM, flops=0, moved=0, name=None):
    block = per * PIX
    in_specs, out_specs, arrays, shapes, rooms = [], [], [], [], []
    in_streams, out_streams, room_of = [], [], {}
    for at, (array, spec, *near) in enumerate(ins):
        if isinstance(spec, Stream):
            in_streams.append(at)
            room_of[at] = len(rooms)
            rooms.append(pltpu.VMEM(array.shape, array.dtype))
            spec = pl.BlockSpec(memory_space=pltpu.HBM)
        elif near:
            arrays.append(array)
            in_specs.append(spec)
            continue
        in_specs.append(spec)
        arrays.append(
            array if spec is SMEM_SPEC else pltpu.with_memory_space_constraint(array, pltpu.HBM)
        )
    for at, (shape, dtype, spec, *near) in enumerate(outs):
        shapes.append(jax.ShapeDtypeStruct(shape, dtype) if near else pltpu.HBM(shape, dtype))
        if isinstance(spec, Stream):
            out_streams.append(at)
            if spec.over is None:
                room_of[len(ins) + at] = len(rooms)
                rooms.append(pltpu.VMEM(shape, dtype))
            else:
                room_of[len(ins) + at] = room_of[spec.over]
            spec = pl.BlockSpec(memory_space=pltpu.HBM)
        out_specs.append(spec)
    n_in, n_out, n_rooms = len(ins), len(outs), len(rooms)

    def whole_kernel(*refs):
        in_refs, out_refs = refs[:n_in], refs[n_in : n_in + n_out]
        room_refs = refs[n_in + n_out : n_in + n_out + n_rooms]
        own_refs = refs[n_in + n_out + n_rooms : -2]
        in_sems, out_sems = refs[-2:]

        def rows(step):
            return pl.ds(pl.multiple_of(step * block, block), block)

        def copies_in(step):
            return [
                pltpu.make_async_copy(
                    in_refs[at].at[rows(step)],
                    room_refs[room_of[at]].at[rows(step)],
                    in_sems.at[k, step],
                )
                for k, at in enumerate(in_streams)
            ]

        def copies_out(step):
            return [
                pltpu.make_async_copy(
                    room_refs[room_of[n_in + at]].at[rows(step)],
                    out_refs[at].at[rows(step)],
                    out_sems.at[k, step],
                )
                for k, at in enumerate(out_streams)
            ]

        def views(step):
            both = []
            for at, ref in enumerate(in_refs + out_refs):
                if at in room_of:
                    ref = room_refs[room_of[at]].at[rows(step)]
                both.append(ref)
            return both + list(own_refs)

        ahead = min(AHEAD, steps)
        for step in range(ahead):
            for copy in copies_in(step):
                copy.start()
        kernel(BEGIN, *views(0))

        def one(step, carry):
            for copy in copies_in(step):
                copy.wait()

            @pl.when(step + ahead < steps)
            def _():
                for copy in copies_in(step + ahead):
                    copy.start()

            kernel(step, *views(step))
            for copy in copies_out(step):
                copy.start()
            return carry

        lax.fori_loop(0, steps, one, 0)
        kernel(END, *views(0))

        def last(step, carry):
            for copy in copies_out(step):
                copy.wait()
            return carry

        lax.fori_loop(0, steps, last, 0)

    return pl.pallas_call(
        whole_kernel,
        in_specs=in_specs,
        out_specs=out_specs,
        out_shape=shapes,
        scratch_shapes=rooms
        + list(scratch)
        + [
            pltpu.SemaphoreType.DMA((max(len(in_streams), 1), steps)),
            pltpu.SemaphoreType.DMA((max(len(out_streams), 1), steps)),
        ],
        compiler_params=pltpu.CompilerParams(vmem_limit_bytes=vmem * MIB),
        cost_estimate=pl.CostEstimate(flops=flops, bytes_accessed=moved, transcendentals=0),
        name=name,
    )(*arrays)


def pack_kernel(core_ref, *refs):
    count = len(refs) // 2

    def put(half):
        for ref, out_ref in zip(refs[:count], refs[count:]):
            rows, cols = ref.shape
            for b in range(cols // 256):
                low = half * (cols // 2) + b * 128
                piece = ref[:, low : low + 128]
                for f in range(out_ref.shape[0]):
                    out_ref[f, pl.ds(b * rows, rows)] = piece

    for core in range(2):
        pl.when(core_ref[0] == core)(functools.partial(put, core))


def unpack_kernel(core_ref, mine_ref, other_ref, out_ref, *wide_refs):
    shards = mine_ref.shape[0]
    rows, cols = out_ref.shape[0] // shards, out_ref.shape[1]

    def put(half, source_ref):
        for f in range(shards):
            for b in range(cols // 256):
                piece = source_ref[f, pl.ds(b * rows, rows)]
                at = (pl.ds(f * rows, rows), pl.ds(half * (cols // 2) + b * 128, 128))
                if wide_refs:
                    wide_refs[0][at] = piece.astype(F32)
                else:
                    out_ref[at] = piece

    for core in range(2):

        @pl.when(core_ref[0] == core)
        def _():
            put(core, mine_ref)
            put(1 - core, other_ref)

    if wide_refs:
        out_ref[...] = wide_refs[0][...].astype(BF16)


def conv_one_kernel(
    step, per, core_ref, sides_ref, x_ref, mine_ref, other_ref, h_ref, w_out_ref, send_ref,
    acc_ref, count_ref,
):
    if step is BEGIN:
        acc_ref[...] = jnp.zeros_like(acc_ref)
        count_ref[0] = 0.0

        def put(core):
            for half, ref in ((core, mine_ref), (1 - core, other_ref)):
                w_out_ref[:, half * HALF : (half + 1) * HALF] = ref[...].reshape(C_IN, HALF)

        for core in range(2):
            pl.when(core_ref[0] == core)(functools.partial(put, core))
        return

    if step is END:
        count = jnp.full((1, WIDTH), count_ref[0], F32)
        send_rows(
            send_ref,
            [row_sum(acc_ref[0:8]), row_sum(acc_ref[8:16]), count, jnp.zeros((1, WIDTH), F32)],
        )
        return

    h = dot_f(x_ref[...], w_out_ref[...])
    h_ref[...] = h
    for j in range(per):
        side = SIDE - 2 * sides_ref[step * per + j]
        mask = pixel_mask(side, 128)
        sums = jnp.zeros((8, WIDTH), F32)
        squares = jnp.zeros((8, WIDTH), F32)
        for rows, part in chunks():
            one = h[j * PIX + part.start : j * PIX + part.stop]
            kept = one * wide(mask[part], WIDTH)
            sums = sums + fold(kept)
            squares = squares + fold(kept * one)
        acc_ref[0:8] += sums
        acc_ref[8:16] += squares
        count_ref[0] += (side * side).astype(F32)


def edge_masks(width):
    column = lax.broadcasted_iota(jnp.int32, (CHUNK, 128), 0) & 15
    first = jnp.where(column == 0, 0.0, 1.0).astype(F32)
    last = jnp.where(column == 15, 0.0, 1.0).astype(F32)
    return wide(first, width), wide(last, width)


def put_taps(taps_ref, j, part, act, first, last):
    shifted = (pltpu.roll(act, 1, 0) * first, act, pltpu.roll(act, CHUNK - 1, 0) * last)
    low = SIDE + j * (PIX + SIDE) + part.start
    for d in range(3):
        piece = shifted[d].astype(BF16)
        for q in range(2):
            taps_ref[pl.ds(low, CHUNK), pl.ds(q * 384 + d * 128, 128)] = piece[
                :, q * HALF : (q + 1) * HALF
            ]


def conv_two_kernel(
    step, per, sides_ref, got_ref, h_ref, w_ref, gain_ref, shift_ref, hat_ref, h2_ref, vec_ref, send_ref,
    taps_ref, acc_ref,
):
    if step is BEGIN:
        sums = total(got_ref)
        mean, inv = norm_terms(sums, sums[2:3])
        vec_ref[0:1] = mean
        vec_ref[1:2] = inv
        vec_ref[2:3] = sums[2:3]
        acc_ref[...] = jnp.zeros_like(acc_ref)
        taps_ref[...] = jnp.zeros_like(taps_ref)
        return

    if step is END:
        send_rows(send_ref, [row_sum(acc_ref[0:8]), row_sum(acc_ref[8:16])])
        return

    gain = gain_ref[:, :WIDTH] * 0.5
    shift = shift_ref[:, :WIDTH] * 0.5
    first, last = edge_masks(WIDTH)
    for j in range(per):
        side = SIDE - 2 * sides_ref[step * per + j]
        mask = pixel_mask(side, 128)
        for rows, part in chunks(j):
            hat = (h_ref[rows] - vec_ref[0:1]) * vec_ref[1:2]
            hat_ref[rows] = hat.astype(BF16)
            half_pre = hat * gain + shift
            act = half_pre * ((1.0 + jnp.tanh(half_pre)) * wide(mask[part], WIDTH))
            put_taps(taps_ref, j, part, act, first, last)
    height = per * (PIX + SIDE)
    for q in range(2):
        cols = pl.ds(q * WIDTH, WIDTH)
        patches = jnp.concatenate(
            [taps_ref[pl.ds(SIDE * d, height), pl.ds(q * 384, 384)] for d in range(3)], axis=1
        )
        both = dot_f(patches, w_ref[:, cols])
        for j in range(per):
            side = SIDE - 2 * sides_ref[step * per + j]
            mask = pixel_mask(side, 128)
            sums = jnp.zeros((8, WIDTH), F32)
            squares = jnp.zeros((8, WIDTH), F32)
            for rows, part in chunks(j):
                low = j * (PIX + SIDE) + part.start
                h2 = both[low : low + CHUNK]
                h2_ref[rows, cols] = h2
                kept = h2 * wide(mask[part], WIDTH)
                sums = sums + fold(kept)
                squares = squares + fold(kept * h2)
            acc_ref[0:8, cols] += sums
            acc_ref[8:16, cols] += squares


def act_two_kernel(
    step, per, sides_ref, one_ref, got_ref, h2_ref, gain_ref, shift_ref, fc_ref,
    hat_ref, a2_ref, slope_ref, pooled_ref, zin_ref, t2_ref, t4_ref, vec_ref, send_ref,
):
    if step is BEGIN:
        sums = total(got_ref)
        mean, inv = norm_terms(sums, jnp.concatenate([one_ref[2:3]] * 2, axis=1))
        vec_ref[0:1] = mean
        vec_ref[1:2] = inv
        return

    if step is END:
        z = high_f(pooled_ref[...], fc_ref[...])
        zin_ref[...] = z
        send_rows(send_ref, [row_sum(z), row_sum(z * z)])
        return

    gain = gain_ref[:, WIDTH : 3 * WIDTH] * 0.5
    shift = shift_ref[:, WIDTH : 3 * WIDTH] * 0.5
    for j in range(per):
        side = SIDE - 2 * sides_ref[step * per + j]
        mask = pixel_mask(side, 128)
        image = pl.ds(step * per + j, 1)
        values = jnp.zeros((8, WIDTH), F32)
        for q in range(2):
            cols = slice(q * WIDTH, (q + 1) * WIDTH)
            sums = jnp.zeros((8, WIDTH), F32)
            products = jnp.zeros((8, WIDTH), F32)
            for rows, part in chunks(j):
                hat = (h2_ref[rows, cols] - vec_ref[0:1, cols]) * vec_ref[1:2, cols]
                hat_ref[rows, cols] = hat.astype(BF16)
                half_pre = hat * gain[:, cols] + shift[:, cols]
                a = (1.0 + jnp.tanh(half_pre)) * wide(mask[part], WIDTH)
                value = half_pre * a
                slope = a * (0.5 + half_pre - 0.5 * value)
                a2_ref[rows, cols] = value.astype(BF16)
                slope_ref[rows, cols] = slope.astype(BF16)
                values = values + fold(value)
                sums = sums + fold(slope)
                products = products + fold(slope * hat)
            t2_ref[image, cols] = row_sum(sums)
            t4_ref[image, cols] = row_sum(products)
        pooled_ref[image] = row_sum(values) / (side * side).astype(F32)


def hidden_terms(zin, sums, n_images, gain_ref, shift_ref):
    mean, inv = norm_terms(sums, n_images)
    zhat = (zin - mean) * inv
    cols = slice(3 * WIDTH, 3 * WIDTH + INTER)
    half_z = (zhat * gain_ref[:, cols] + shift_ref[:, cols]) * 0.5
    value, slope = silu_parts(half_z)
    return zhat, inv, value, slope


def combine_kernel(
    step, per, n_images, got_ref, zin_ref, a2_ref, w3_ref, fc_ref, bias_ref, gain_ref, shift_ref,
    att_ref, comb_ref, gw_ref, csum_ref, hid_ref, send_ref, gram_ref, acc_ref,
):
    if step is BEGIN:
        zhat, inv, hidden, slope = hidden_terms(
            zin_ref[...], total(got_ref), n_images, gain_ref, shift_ref
        )
        hid_ref[0] = zhat
        hid_ref[1] = hidden
        hid_ref[2] = slope
        hid_ref[3] = jnp.broadcast_to(inv, slope.shape)
        logits = high_f(hidden, fc_ref[...]) + bias_ref[...]
        left, right = logits[:, :WIDTH], logits[:, WIDTH:]
        top = jnp.maximum(left, right)
        left, right = jnp.exp(left - top), jnp.exp(right - top)
        both = left + right
        att_ref[:, :WIDTH] = left / both
        att_ref[:, WIDTH:] = right / both
        gram_ref[...] = jnp.zeros_like(gram_ref)
        acc_ref[...] = jnp.zeros_like(acc_ref)
        return

    if step is END:
        csum = row_sum(acc_ref[...])
        csum_ref[...] = csum
        both = jnp.concatenate([gram_ref[...], jnp.broadcast_to(csum, (8, WIDTH))], axis=0)
        both = exact_f(both, w3_ref[...])
        gw = both[:WIDTH]
        gw_ref[...] = gw
        send_rows(send_ref, [both[WIDTH : WIDTH + 1], row_sum(w3_ref[...].astype(F32) * gw)])
        return

    for j in range(per):
        att = att_ref[pl.ds(step * per + j, 1)]
        sums = jnp.zeros((8, WIDTH), F32)
        for rows, _ in chunks(j):
            left = att[:, :WIDTH] * a2_ref[rows, :WIDTH].astype(F32)
            comb = (left + att[:, WIDTH:] * a2_ref[rows, WIDTH:].astype(F32)).astype(BF16)
            comb_ref[rows] = comb
            sums = sums + fold(comb.astype(F32))
        acc_ref[...] += sums
    comb = comb_ref[...]
    gram_ref[...] += dot_rows(comb, comb)


def output_kernel(
    step, per, sides_ref, one_ref, got_ref, comb_ref, x_ref, cot_ref, w3_ref, gain_ref, shift_ref,
    out_ref, u3_ref, stat_ref, send_ref, vec_ref, acc_ref,
):
    if step is BEGIN:
        count = jnp.concatenate([one_ref[2:3]] * 4, axis=1)
        mean, inv = norm_terms(total(got_ref), count)
        scale = inv * gain_ref[:, 3 * WIDTH + INTER :]
        stat_ref[0:1] = mean
        stat_ref[1:2] = inv
        stat_ref[2:3] = scale
        stat_ref[3:4] = count
        vec_ref[0:1] = scale
        vec_ref[1:2] = shift_ref[:, 3 * WIDTH + INTER :] - mean * scale
        vec_ref[2:3] = 0.5 * scale
        acc_ref[...] = jnp.zeros_like(acc_ref)
        return

    if step is END:
        send_rows(
            send_ref,
            [0.5 * row_sum(acc_ref[0:8]), 0.5 * row_sum(acc_ref[8:16]) / vec_ref[0:1]],
        )
        return

    chunk = 16
    lanes = 512
    for j in range(per):
        side = SIDE - 2 * sides_ref[step * per + j]
        mask = pixel_mask(side, 128)
        h3 = dot_f(comb_ref[pl.ds(j * PIX, PIX)], w3_ref[...])
        for n in range(C_IN // lanes):
            cols = pl.ds(n * lanes, lanes)
            ups = jnp.zeros((8, lanes), F32)
            products = jnp.zeros((8, lanes), F32)
            for c in range(PIX // chunk):
                rows = pl.ds(j * PIX + c * chunk, chunk)
                scaled = (
                    h3[c * chunk : (c + 1) * chunk, n * lanes : (n + 1) * lanes] * vec_ref[0:1, cols]
                )
                pre = scaled + vec_ref[1:2, cols] + x_ref[rows, cols].astype(F32)
                half_pre = pre * 0.5
                a = (1.0 + jnp.tanh(half_pre)) * wide(mask[c * chunk : (c + 1) * chunk], lanes)
                value = half_pre * a
                out_ref[rows, cols] = value.astype(BF16)
                up = cot_ref[rows, cols].astype(F32) * (a * (1.0 + pre - value))
                u3_ref[rows, cols] = (up * vec_ref[2:3, cols]).astype(BF16)
                ups = ups + fold(up)
                products = products + fold(up * scaled)
            acc_ref[0:8, cols] += ups
            acc_ref[8:16, cols] += products


def outer_three_kernel(step, comb_ref, u3_ref, cu_ref):
    if step is BEGIN:
        cu_ref[...] = jnp.zeros_like(cu_ref)
        return

    if step is END:
        return

    cu_ref[...] += dot_rows(comb_ref[...], u3_ref[...])


def back_three_kernel(
    step, per, three_ref, got_ref, hid_ref, comb_ref, u3_ref, a2_ref, slope_ref,
    hat_ref, w3_ref, cu_ref, gw_ref, csum_ref, att_ref, fc_ref,
    p_ref, t1_ref, t3_ref, duz_ref, w3g_ref, fcg_ref, norm_ref, s_ref, c_ref, send_ref, datt_ref, k_ref,
):
    if step is BEGIN:
        mean, inv = three_ref[0:1], three_ref[1:2]
        scale, count = three_ref[2:3], three_ref[3:4]
        sums = total(got_ref)
        dshift = sums[0:1]
        dgain = (sums[1:2] - mean * dshift) * inv
        norm_ref[0:1] = dgain
        norm_ref[1:2] = dshift
        k2 = scale * inv * dgain / count
        k1 = scale * dshift / count - mean * k2
        w3 = w3_ref[...].astype(F32)
        s_ref[...] = dot_last((w3 * k2).astype(BF16), w3_ref[...]).astype(BF16)
        c_ref[...] = high_last(jnp.broadcast_to(k1, (8, C_IN)), w3)
        k_ref[0:1] = k1
        k_ref[1:2] = k2
        return

    if step is END:
        csum = jnp.broadcast_to(csum_ref[...], (8, WIDTH))
        outer = high_rows(csum, jnp.broadcast_to(k_ref[0:1], (8, C_IN))) * 0.125
        w3g_ref[...] = cu_ref[...] - outer - gw_ref[...] * k_ref[1:2]
        att = att_ref[...]
        datt = datt_ref[...]
        both = att * datt
        inner = both[:, :WIDTH] + both[:, WIDTH:]
        dlog = both - att * jnp.concatenate([inner, inner], axis=1)
        zhat, hidden, slope = hid_ref[0], hid_ref[1], hid_ref[2]
        fcg = high_rows(hidden, dlog)
        duz = high_last(dlog, fc_ref[...]) * slope
        duz_ref[...] = duz
        bias = row_sum(dlog)
        rows = [row_sum(duz), row_sum(duz * zhat)]
        for b in range(4):
            cols = slice(b * 128, (b + 1) * 128)
            fcg_ref[pl.ds(b * INTER, INTER)] = fcg[:, cols]
            rows.append(bias[:, cols])
        send_rows(send_ref, rows + [jnp.zeros((2, 128), F32)])
        return

    corr = dot_f(comb_ref[...], s_ref[...])
    p_ref[...] = dot_last(u3_ref[...], w3_ref[...]).astype(BF16)
    for j in range(per):
        image = pl.ds(step * per + j, 1)
        sums = [jnp.zeros((8, WIDTH), F32)] * 6
        for rows, part in chunks(j):
            low = j * PIX + part.start
            dcomb = p_ref[rows].astype(F32) - corr[low : low + CHUNK] - c_ref[0:1]
            for q in range(2):
                cols = slice(q * WIDTH, (q + 1) * WIDTH)
                u = dcomb * slope_ref[rows, cols].astype(F32)
                sums[q] = sums[q] + fold(dcomb * a2_ref[rows, cols].astype(F32))
                sums[2 + q] = sums[2 + q] + fold(u)
                sums[4 + q] = sums[4 + q] + fold(u * hat_ref[rows, cols].astype(F32))
        for k, ref in enumerate((datt_ref, t1_ref, t3_ref)):
            for q in range(2):
                ref[image, q * WIDTH : (q + 1) * WIDTH] = row_sum(sums[2 * k + q])


def back_att_kernel(
    n_images, got_ref, hid_ref, duz_ref, pooled_ref, sides_ref, fc_ref, att_ref,
    t1_ref, t2_ref, t3_ref, t4_ref, fcg_ref, gain_ref,
    dpool_ref, pack_ref, bias_ref, norm_ref, send_ref,
):
    zhat, inv = hid_ref[0], hid_ref[3, 0:1]
    sums = total(got_ref)
    norm_ref[0:1] = sums[1:2]
    norm_ref[1:2] = sums[0:1]
    for b in range(4):
        bias_ref[:, b * 128 : (b + 1) * 128] = sums[2 + b : 3 + b]
    scale = inv * gain_ref[:, 3 * WIDTH : 3 * WIDTH + INTER]
    dzin = scale * (duz_ref[...] - (sums[0:1] + zhat * sums[1:2]) / n_images)
    pack_ref[0:WIDTH] = high_rows(pooled_ref[...], dzin)
    pack_ref[WIDTH:] = fcg_ref[...]
    dpool_ref[...] = high_last(dzin, fc_ref[...])
    for i in range(dpool_ref.shape[0]):
        side = SIDE - 2 * sides_ref[i]
        dpool_ref[i : i + 1] = dpool_ref[i : i + 1] / (side * side).astype(F32)
    dpool = dpool_ref[...]
    both = jnp.concatenate([dpool, dpool], axis=1)
    att = att_ref[...]
    send_rows(
        send_ref,
        [
            row_sum(att * t1_ref[...] + both * t2_ref[...]),
            row_sum(att * t3_ref[...] + both * t4_ref[...]),
        ],
    )


def back_two_kernel(
    step, per, sides_ref, one_ref, two_ref, got_ref, comb_ref, p_ref, s_ref, c_ref, slope_ref, hat2_ref, hat1_ref, att_ref,
    dpool_ref, w_ref, gain_ref, shift_ref, dh2_ref, u1_ref, norm_ref, send_ref,
    vec_ref, pad_ref, acc_ref,
):
    if step is BEGIN:
        count = jnp.concatenate([one_ref[2:3]] * 2, axis=1)
        scale = two_ref[1:2] * gain_ref[:, WIDTH : 3 * WIDTH]
        sums = total(got_ref)
        norm_ref[0:1] = sums[1:2]
        norm_ref[1:2] = sums[0:1]
        vec_ref[0:1] = scale
        vec_ref[1:2] = scale * sums[0:1] / count
        vec_ref[2:3] = scale * sums[1:2] / count
        acc_ref[...] = jnp.zeros_like(acc_ref)
        pad_ref[...] = jnp.zeros_like(pad_ref)
        return

    if step is END:
        send_rows(send_ref, [row_sum(acc_ref[0:8]), row_sum(acc_ref[8:16])])
        return

    first, last = edge_masks(HALF)
    corr = dot_f(comb_ref[...], s_ref[...])
    for j in range(per):
        side = SIDE - 2 * sides_ref[step * per + j]
        mask = pixel_mask(side, 128)
        image = pl.ds(step * per + j, 1)
        dpool = dpool_ref[image]
        for rows, part in chunks(j):
            low = j * PIX + part.start
            dcomb = p_ref[rows].astype(F32) - corr[low : low + CHUNK] - c_ref[0:1]
            for q in range(2):
                cols = slice(q * WIDTH, (q + 1) * WIDTH)
                scale = vec_ref[0:1, cols]
                up = dcomb * (att_ref[image, cols] * scale) + dpool * scale
                dh2 = slope_ref[rows, cols].astype(F32) * up - wide(mask[part], WIDTH) * (
                    vec_ref[1:2, cols] + hat2_ref[rows, cols].astype(F32) * vec_ref[2:3, cols]
                )
                dh2 = dh2.astype(BF16)
                dh2_ref[rows, cols] = dh2
                pad_ref[pl.ds(SIDE + j * (PIX + SIDE) + part.start, CHUNK), cols] = dh2
    height = per * (PIX + SIDE)
    for q in range(2):
        lines = jnp.concatenate(
            [pad_ref[pl.ds(SIDE * (2 - d), height), pl.ds(q * WIDTH, WIDTH)] for d in range(3)],
            axis=1,
        )
        weight = jnp.concatenate(
            [
                jnp.concatenate(
                    [
                        w_ref[pl.ds((3 * r + d) * HALF, HALF), pl.ds(q * WIDTH, WIDTH)]
                        for r in range(3)
                    ],
                    axis=1,
                )
                for d in range(3)
            ],
            axis=0,
        )
        both = dot_last(lines, weight)
        for j in range(per):
            side = SIDE - 2 * sides_ref[step * per + j]
            mask = pixel_mask(side, 128)
            cols = slice(q * HALF, (q + 1) * HALF)
            gain = gain_ref[:, cols] * 0.5
            shift = shift_ref[:, cols] * 0.5
            sums = jnp.zeros((8, HALF), F32)
            products = jnp.zeros((8, HALF), F32)
            for rows, part in chunks(j):
                low = j * (PIX + SIDE) + part.start
                y = both[low : low + CHUNK]
                da1 = (
                    y[:, HALF : 2 * HALF]
                    + pltpu.roll(y[:, :HALF], CHUNK - 1, 0) * last
                    + pltpu.roll(y[:, 2 * HALF :], 1, 0) * first
                )
                hat = hat1_ref[rows, cols].astype(F32)
                half_pre = hat * gain + shift
                a = (1.0 + jnp.tanh(half_pre)) * mask[part]
                u1 = da1 * (a * (0.5 + half_pre - 0.5 * half_pre * a))
                u1_ref[rows, cols] = u1.astype(BF16)
                sums = sums + fold(u1)
                products = products + fold(u1 * hat)
            acc_ref[0:8, cols] += sums
            acc_ref[8:16, cols] += products


def weight_two_kernel(
    step, per, core_ref, sides_ref, hat_ref, dh2_ref, gain_ref, shift_ref, keep_ref, give_ref,
    taps_ref, acc_ref,
):
    if step is BEGIN:
        acc_ref[...] = jnp.zeros_like(acc_ref)
        taps_ref[...] = jnp.zeros_like(taps_ref)
        return

    if step is END:
        def put(core):
            keep_ref[...] = acc_ref[core].T
            give_ref[...] = acc_ref[1 - core].T

        for core in range(2):
            pl.when(core_ref[0] == core)(functools.partial(put, core))
        return

    gain = gain_ref[:, :WIDTH] * 0.5
    shift = shift_ref[:, :WIDTH] * 0.5
    first, last = edge_masks(WIDTH)
    height = PIX + SIDE
    for j in range(per):
        side = SIDE - 2 * sides_ref[step * per + j]
        mask = pixel_mask(side, 128)
        for rows, part in chunks(j):
            half_pre = hat_ref[rows].astype(F32) * gain + shift
            act = half_pre * ((1.0 + jnp.tanh(half_pre)) * wide(mask[part], WIDTH))
            put_taps(taps_ref, j, part, act, first, last)
    for q in range(2):
        patches = jnp.concatenate(
            [
                jnp.concatenate(
                    [
                        taps_ref[pl.ds(SIDE * d + j * height, PIX), pl.ds(q * 384, 384)]
                        for d in range(3)
                    ],
                    axis=1,
                )
                for j in range(per)
            ],
            axis=0,
        )
        acc_ref[q] += dot_rows(dh2_ref[:, q * WIDTH : (q + 1) * WIDTH], patches)


def back_one_kernel(
    step, per, core_ref, sides_ref, one_ref, got_ref, u1_ref, hat_ref, x_ref, gain_ref, norm2_ref,
    norm_att_ref, norm3_ref, dh_ref, keep_ref, give_ref, gain_out_ref, shift_out_ref, vec_ref, acc_ref,
):
    if step is BEGIN:
        count = one_ref[2:3]
        scale = one_ref[1:2] * gain_ref[:, :WIDTH]
        sums = total(got_ref)
        for row, out_ref in ((0, gain_out_ref), (1, shift_out_ref)):
            out_ref[:, :WIDTH] = sums[1 - row : 2 - row]
            out_ref[:, WIDTH : 3 * WIDTH] = norm2_ref[row : row + 1]
            out_ref[:, 3 * WIDTH : 3 * WIDTH + INTER] = norm_att_ref[row : row + 1]
            out_ref[:, 3 * WIDTH + INTER :] = norm3_ref[row : row + 1]
        vec_ref[0:1] = scale
        vec_ref[1:2] = scale * sums[0:1] / count
        vec_ref[2:3] = scale * sums[1:2] / count
        acc_ref[...] = jnp.zeros_like(acc_ref)
        return

    if step is END:

        def put(core):
            keep_ref[...] = acc_ref[core * HALF : (core + 1) * HALF].T
            give_ref[...] = acc_ref[(1 - core) * HALF : (2 - core) * HALF].T

        for core in range(2):
            pl.when(core_ref[0] == core)(functools.partial(put, core))
        return

    for j in range(per):
        side = SIDE - 2 * sides_ref[step * per + j]
        mask = pixel_mask(side, 128)
        for rows, part in chunks(j):
            dh_ref[rows] = (
                u1_ref[rows].astype(F32) * vec_ref[0:1]
                - wide(mask[part], WIDTH) * (vec_ref[1:2] + hat_ref[rows].astype(F32) * vec_ref[2:3])
            ).astype(BF16)
    acc_ref[...] += dot_rows(dh_ref[...], x_ref[...])


def input_grad_kernel(step, dh_ref, u3_ref, three_ref, w_ref, ig_ref, wide_ref):
    if step is BEGIN:
        wide_ref[...] = 1.0 / three_ref[2:3]
        return

    if step is END:
        return

    dx = dot_last(dh_ref[...], w_ref[...])
    for low in range(0, dx.shape[0], 16):
        rows = pl.ds(low, 16)
        ig_ref[rows] = (u3_ref[rows].astype(F32) * wide_ref[...] + dx[low : low + 16]).astype(BF16)


def round_up(value, multiple):
    return -(-value // multiple) * multiple


def pack_three_kernel(core_ref, w_ref, fc_ref, keep_ref, give_ref):
    shards = keep_ref.shape[0]
    w_rows = w_ref.shape[0] // shards
    fc_rows = fc_ref.shape[0] // (2 * shards)

    def put(half, out_ref):
        for f in range(shards):
            for b in range(4):
                low = (half * 4 + b) * 128
                out_ref[f, pl.ds(b * w_rows, w_rows)] = w_ref[
                    pl.ds(f * w_rows, w_rows), pl.ds(low, 128)
                ]
            out_ref[f, pl.ds(4 * w_rows, fc_rows)] = fc_ref[
                pl.ds((half * shards + f) * fc_rows, fc_rows)
            ]

    for core in range(2):

        @pl.when(core_ref[0] == core)
        def _():
            put(core, keep_ref)
            put(1 - core, give_ref)


def two_wide(part, rows):
    missing = 2 * rows - part.shape[0]
    if missing:
        part = jnp.concatenate([part, jnp.zeros((missing, 128), F32)], axis=0)
    return jnp.concatenate([part[:rows], part[rows:]], axis=1)


def slot_rows(two_rows, fc_rows, one_rows):
    return round_up(two_rows, 16), round_up(fc_rows, 32) // 2, round_up(one_rows, 32) // 2


def add_slots(ref, at, rows):
    rows = pl.ds(at, rows)
    both = ref[0, rows].astype(F32)
    for f in range(1, ref.shape[0]):
        both = both + ref[f, rows].astype(F32)
    return both


def pack_last_kernel(
    fc_rows, keep2_ref, other2_ref, keep1_ref, other1_ref, three_ref, out_ref
):
    shards = out_ref.shape[0]
    two_rows = keep2_ref.shape[0] // shards
    one_rows = keep1_ref.shape[0] // shards
    two_slot, fc_slot, one_slot = slot_rows(two_rows, fc_rows, one_rows)
    fc = add_slots(three_ref, three_ref.shape[1] - fc_rows, fc_rows)
    fc = two_wide(fc, fc_slot).astype(BF16)
    for f in range(shards):
        rows = pl.ds(f * two_rows, two_rows)
        part = keep2_ref[rows] + other2_ref[rows]
        if two_slot > two_rows:
            part = jnp.concatenate([part, jnp.zeros((two_slot - two_rows, WIDTH), F32)], axis=0)
        out_ref[f, pl.ds(0, two_slot)] = part.astype(BF16)
        out_ref[f, pl.ds(two_slot, fc_slot)] = fc
        rows = pl.ds(f * one_rows, one_rows)
        part = two_wide(keep1_ref[rows] + other1_ref[rows], one_slot)
        out_ref[f, pl.ds(two_slot + fc_slot, one_slot)] = part.astype(BF16)


def sum_last_kernel(two_rows, fc_rows, one_rows, parts_ref, three_ref, out_ref):
    shards = parts_ref.shape[0]
    two_slot, fc_slot, one_slot = slot_rows(two_rows, fc_rows, one_rows)
    out_ref[pl.ds(0, two_slot)] = add_slots(parts_ref, 0, two_slot)
    out_ref[pl.ds(two_slot, one_slot)] = add_slots(parts_ref, two_slot + fc_slot, one_slot)
    at = two_slot + one_slot
    three_half = (three_ref.shape[1] - fc_rows) // 2
    three = add_slots(three_ref, 0, 2 * three_half)
    out_ref[pl.ds(at, three_half)] = two_wide(three, three_half)
    at += three_half
    for f in range(shards):
        out_ref[pl.ds(at + f * fc_slot, fc_slot)] = parts_ref[f, pl.ds(two_slot, fc_slot)].astype(F32)


def finish_kernel(
    two_rows, fc_rows, one_rows, three_rows, core_ref, mine_ref, other_ref,
    one_ref, two_ref, three_ref, fc1_ref, fc2_ref, pack_ref,
):
    two_slot, fc_slot, one_slot = slot_rows(two_rows, fc_rows, one_rows)
    three_half = 2 * three_rows
    at_three = two_slot + one_slot
    at_fc = at_three + three_half
    shards = (mine_ref.shape[0] - at_fc) // fc_slot

    def tall(ref, at, half_rows, rows):
        both = jnp.concatenate(
            [ref[pl.ds(at, half_rows), :128], ref[pl.ds(at, half_rows), 128:]], axis=0
        )
        return both[:rows]

    def put(half, ref):
        two_ref[:, half * WIDTH : (half + 1) * WIDTH] = ref[pl.ds(0, two_rows)]
        one_ref[:, half * HALF : (half + 1) * HALF] = tall(ref, two_slot, one_slot, one_rows)
        three = tall(ref, at_three, three_half, 4 * three_rows)
        for b in range(4):
            low = half * 512 + b * 128
            three_ref[:, low : low + 128] = three[b * three_rows : (b + 1) * three_rows]
        for f in range(shards):
            pack_ref[pl.ds((half * shards + f) * fc_rows, fc_rows)] = tall(
                ref, at_fc + f * fc_slot, fc_slot, fc_rows
            )

    for core in range(2):

        @pl.when(core_ref[0] == core)
        def _():
            put(core, mine_ref)
            put(1 - core, other_ref)

    fc1_ref[...] = pack_ref[0:WIDTH]
    for b in range(4):
        fc2_ref[:, b * 128 : (b + 1) * 128] = pack_ref[pl.ds(WIDTH + b * INTER, INTER)]


def everyone(payload):
    return lax.all_to_all(payload, AXES, 0, 0, tiled=True)


def other_core(array):
    return lax.ppermute(array, "dp", [(0, 1), (1, 0)])


def spread_weights(core, weights):
    shards = lax.axis_size("fsdp")
    shapes = [(shards, w.shape[0] * w.shape[1] // 256, 128) for w in weights]
    return call(
        pack_kernel,
        1,
        [(core, SMEM_SPEC)] + [(weight, whole(weight.shape)) for weight in weights],
        [(shape, BF16, whole(shape), True) for shape in shapes],
        flops=1000000,
        moved=4000000,
        name="pack",
    )


def join_weight(core, mine, shape):
    other = other_core(mine)
    rows = shape[0] // mine.shape[0]
    return call(
        unpack_kernel,
        1,
        [(core, SMEM_SPEC), (mine, whole(mine.shape), True), (other, whole(mine.shape), True)],
        [(shape, BF16, whole(shape))],
        [] if rows % 16 == 0 else [pltpu.VMEM(shape, F32)],
        flops=1000000,
        moved=4000000,
        name="unpack",
    )[0]


def slots(parts):
    return lax.all_to_all(parts, "fsdp", 0, 0, tiled=True)


def body(
    inputs,
    sides,
    weight_one,
    weight_two,
    weight_three,
    fc_first,
    fc_second,
    fc_bias,
    bn_gain,
    bn_shift,
    cotangent,
):
    images = inputs.shape[0]
    rows = images * PIX
    devices = lax.axis_size("fsdp") * lax.axis_size("dp")
    n_images = float(images * devices)
    x = inputs.reshape(rows, C_IN)
    cot = cotangent.reshape(rows, C_IN)
    gain = bn_gain.reshape(1, -1)
    shift = bn_shift.reshape(1, -1)
    bias = fc_bias.reshape(1, -1)
    n_ch = gain.shape[1]
    core = lax.axis_index("dp").astype(jnp.int32).reshape(1)

    def split(most):
        per = max(n for n in range(1, most + 1) if images % n == 0)
        return per, images // per

    core_in = (core, SMEM_SPEC)
    sides_in = (sides, SMEM_SPEC)
    gain_in = (gain, whole((1, n_ch)))
    shift_in = (shift, whole((1, n_ch)))

    def payload(k, n):
        return ((devices, k, n), F32, whole((devices, k, n)), True)

    def small(*shape):
        return (shape, F32, whole(shape))

    def full(array):
        return (array, whole(array.shape))

    def near(array):
        return (array, whole(array.shape), True)

    def blocks(array):
        return (array, Stream())

    def blocks_out(width, dtype=BF16, over=None):
        return ((rows, width), dtype, Stream(over))

    spread_one, spread_two, spread_three = spread_weights(
        core, (weight_one, weight_two, weight_three)
    )
    mine = slots(spread_one)
    other = other_core(mine)
    spread_two, mine, other = lax.optimization_barrier((spread_two, mine, other))
    mine_two = slots(spread_two)

    per, steps = split(PER_CONV_ONE)
    h1, full_one, send = stream_call(
        lambda step, *refs, per=per: conv_one_kernel(step, per, *refs),
        per,
        steps,
        [core_in, sides_in, blocks(x), near(mine), near(other)],
        [blocks_out(WIDTH, F32), ((C_IN, WIDTH), BF16, whole((C_IN, WIDTH))), payload(4, WIDTH)],
        [pltpu.VMEM((16, WIDTH), F32), pltpu.SMEM((1,), F32)],
        flops=2 * rows * C_IN * WIDTH,
        moved=rows * C_IN * 2 + rows * WIDTH * 4,
        name="conv_one",
    )
    send, mine_two = lax.optimization_barrier((send, mine_two))
    got_one = everyone(send)
    full_two = join_weight(core, mine_two, (9 * HALF, 2 * WIDTH))
    got_one, spread_three, full_two = lax.optimization_barrier((got_one, spread_three, full_two))
    mine_three = slots(spread_three)

    per, steps = split(PER_CONV_TWO)
    hat1, h2, stat1, send = stream_call(
        lambda step, *refs, per=per: conv_two_kernel(step, per, *refs),
        per,
        steps,
        [sides_in, near(got_one), blocks(h1), full(full_two), gain_in, shift_in],
        [blocks_out(WIDTH), blocks_out(2 * WIDTH, F32), small(8, WIDTH), payload(2, 2 * WIDTH)],
        [
            pltpu.VMEM((per * (PIX + SIDE) + 2 * SIDE, 6 * HALF), BF16),
            pltpu.VMEM((16, 2 * WIDTH), F32),
        ],
        flops=2 * rows * 9 * HALF * 2 * WIDTH,
        moved=rows * WIDTH * 14,
        name="conv_two",
    )
    send, mine_three = lax.optimization_barrier((send, mine_three))
    got_two = everyone(send)
    full_three = join_weight(core, mine_three, (WIDTH, C_IN))

    per, steps = split(PER_ACT_TWO)
    hat2, a2, slope2, pooled, zin, t2, t4, stat2, send = stream_call(
        lambda step, *refs, per=per: act_two_kernel(step, per, *refs),
        per,
        steps,
        [
            sides_in,
            full(stat1),
            near(got_two),
            blocks(h2),
            gain_in,
            shift_in,
            full(fc_first),
        ],
        [
            blocks_out(2 * WIDTH),
            blocks_out(2 * WIDTH),
            blocks_out(2 * WIDTH),
            small(images, WIDTH),
            small(images, INTER),
            small(images, 2 * WIDTH),
            small(images, 2 * WIDTH),
            small(8, 2 * WIDTH),
            payload(2, INTER),
        ],
        flops=rows * 2 * WIDTH * 20,
        moved=rows * 2 * WIDTH * 10,
        name="act_two",
    )
    got_att = everyone(send)

    per, steps = split(PER_COMBINE)
    att, comb, gw, csum, hid, send = stream_call(
        lambda step, *refs, per=per: combine_kernel(step, per, n_images, *refs),
        per,
        steps,
        [
            near(got_att),
            full(zin),
            blocks(a2),
            full(full_three),
            full(fc_second),
            full(bias),
            gain_in,
            shift_in,
        ],
        [
            small(images, 2 * WIDTH),
            blocks_out(WIDTH),
            small(WIDTH, C_IN),
            small(1, WIDTH),
            small(4, images, INTER),
            payload(2, C_IN),
        ],
        [pltpu.VMEM((WIDTH, WIDTH), F32), pltpu.VMEM((8, WIDTH), F32)],
        flops=2 * rows * WIDTH * WIDTH,
        moved=rows * WIDTH * 6,
        name="combine",
    )
    got_three = everyone(send)

    per, steps = split(PER_OUTPUT)
    outputs, u3, stat3, send = stream_call(
        lambda step, *refs, per=per: output_kernel(step, per, *refs),
        per,
        steps,
        [
            sides_in,
            full(stat1),
            near(got_three),
            blocks(comb),
            blocks(x),
            blocks(cot),
            full(full_three),
            gain_in,
            shift_in,
        ],
        [
            blocks_out(C_IN, over=4),
            blocks_out(C_IN, over=5),
            small(8, C_IN),
            payload(2, C_IN),
        ],
        [pltpu.VMEM((8, C_IN), F32), pltpu.VMEM((16, C_IN), F32)],
        flops=2 * rows * WIDTH * C_IN,
        moved=rows * C_IN * 8,
        name="output",
    )
    got_back_three = everyone(send)

    per, steps = split(PER_OUTER_THREE)
    (cu,) = stream_call(
        outer_three_kernel,
        per,
        steps,
        [blocks(comb), blocks(u3)],
        [small(WIDTH, C_IN)],
        flops=2 * rows * WIDTH * C_IN,
        moved=rows * C_IN * 3,
        name="outer_three",
    )

    per, steps = split(PER_BACK_THREE)
    p, t1, t3, duz, w3_local, fc2_local, norm3, corr_weight, corr_row, send = stream_call(
        lambda step, *refs, per=per: back_three_kernel(step, per, *refs),
        per,
        steps,
        [
            full(stat3),
            near(got_back_three),
            full(hid),
            blocks(comb),
            blocks(u3),
            blocks(a2),
            blocks(slope2),
            blocks(hat2),
            full(full_three),
            full(cu),
            full(gw),
            full(csum),
            full(att),
            full(fc_second),
        ],
        [
            blocks_out(WIDTH, over=3),
            small(images, 2 * WIDTH),
            small(images, 2 * WIDTH),
            small(images, INTER),
            small(WIDTH, C_IN),
            small(4 * INTER, 128),
            small(2, C_IN),
            ((WIDTH, WIDTH), BF16, whole((WIDTH, WIDTH))),
            small(8, WIDTH),
            payload(8, INTER),
        ],
        [pltpu.VMEM((images, 2 * WIDTH), F32), pltpu.VMEM((2, C_IN), F32)],
        flops=4 * rows * WIDTH * C_IN,
        moved=rows * WIDTH * 16,
        name="back_three",
    )
    got_back_att = everyone(send)

    dpool, packed, fc_bias_grad, norm_att, send = call(
        functools.partial(back_att_kernel, n_images),
        1,
        [
            near(got_back_att),
            full(hid),
            full(duz),
            full(pooled),
            sides_in,
            full(fc_first),
            full(att),
            full(t1),
            full(t2),
            full(t3),
            full(t4),
            full(fc2_local),
            gain_in,
        ],
        [
            small(images, WIDTH),
            small(WIDTH + 4 * INTER, 128),
            small(1, 2 * WIDTH),
            small(2, INTER),
            payload(2, 2 * WIDTH),
        ],
        flops=10000000,
        moved=1000000,
        name="back_att",
    )
    got_back_two = everyone(send)

    shards = lax.axis_size("fsdp")
    w3_rows = WIDTH // shards
    fc_rows = packed.shape[0] // (2 * shards)
    slot = (shards, 4 * w3_rows + fc_rows, 128)
    keep, give = call(
        pack_three_kernel,
        1,
        [core_in, full(w3_local), full(packed)],
        [(slot, F32, whole(slot)), (slot, F32, whole(slot))],
        flops=1000000,
        moved=3000000,
        name="pack_three",
    )
    three = slots(keep + other_core(give))

    per, steps = split(PER_BACK_TWO)
    dh2, u1, norm2, send = stream_call(
        lambda step, *refs, per=per: back_two_kernel(step, per, *refs),
        per,
        steps,
        [
            sides_in,
            full(stat1),
            full(stat2),
            near(got_back_two),
            blocks(comb),
            blocks(p),
            full(corr_weight),
            full(corr_row),
            blocks(slope2),
            blocks(hat2),
            blocks(hat1),
            full(att),
            full(dpool),
            full(full_two),
            gain_in,
            shift_in,
        ],
        [
            blocks_out(2 * WIDTH),
            blocks_out(WIDTH),
            small(2, 2 * WIDTH),
            payload(2, WIDTH),
        ],
        [
            pltpu.VMEM((8, 2 * WIDTH), F32),
            pltpu.VMEM((per * (PIX + SIDE) + 2 * SIDE, 2 * WIDTH), BF16),
            pltpu.VMEM((16, WIDTH), F32),
        ],
        flops=2 * rows * 9 * HALF * 2 * WIDTH,
        moved=rows * WIDTH * 20,
        name="back_two",
    )
    send, three, dh2 = lax.optimization_barrier((send, three, dh2))
    got_back_one = everyone(send)

    per, steps = split(PER_WEIGHT_TWO)
    half = (9 * HALF, WIDTH)
    keep, give = stream_call(
        lambda step, *refs, per=per: weight_two_kernel(step, per, *refs),
        per,
        steps,
        [core_in, sides_in, blocks(hat1), blocks(dh2), gain_in, shift_in],
        [(half, F32, whole(half)), (half, F32, whole(half))],
        [
            pltpu.VMEM((per * (PIX + SIDE) + 2 * SIDE, 6 * HALF), BF16),
            pltpu.VMEM((2, WIDTH, 9 * HALF), F32),
        ],
        flops=2 * rows * 9 * HALF * 2 * WIDTH,
        moved=rows * WIDTH * 6,
        name="weight_two",
    )
    got_back_one, keep, give = lax.optimization_barrier((got_back_one, keep, give))
    per, steps = split(PER_BACK_ONE)
    half_one = (C_IN, HALF)
    dh1, keep_one, give_one, gain_grad, shift_grad = stream_call(
        lambda step, *refs, per=per: back_one_kernel(step, per, *refs),
        per,
        steps,
        [
            core_in,
            sides_in,
            full(stat1),
            near(got_back_one),
            blocks(u1),
            blocks(hat1),
            blocks(x),
            gain_in,
            full(norm2),
            full(norm_att),
            full(norm3),
        ],
        [
            blocks_out(WIDTH),
            small(*half_one),
            small(*half_one),
            small(1, n_ch),
            small(1, n_ch),
        ],
        [pltpu.VMEM((8, WIDTH), F32), pltpu.VMEM((WIDTH, C_IN), F32)],
        flops=2 * rows * WIDTH * C_IN,
        moved=rows * C_IN * 4,
        name="back_one",
    )

    two_rows, one_rows = 9 * HALF // shards, C_IN // shards
    two_slot, fc_slot, one_slot = slot_rows(two_rows, fc_rows, one_rows)
    slot = (shards, two_slot + fc_slot + one_slot, WIDTH)
    (parts,) = call(
        functools.partial(pack_last_kernel, fc_rows),
        1,
        [
            full(keep),
            near(other_core(give)),
            full(keep_one),
            near(other_core(give_one)),
            near(three),
        ],
        [(slot, BF16, whole(slot))],
        flops=1000000,
        moved=5000000,
        name="pack_last",
    )
    dh1, parts = lax.optimization_barrier((dh1, parts))
    parts = slots(parts)

    per, steps = split(PER_INPUT_GRAD)
    (input_grad,) = stream_call(
        input_grad_kernel,
        per,
        steps,
        [blocks(dh1), blocks(u3), full(stat3), full(full_one)],
        [blocks_out(C_IN, over=1)],
        [pltpu.VMEM((1, C_IN), F32)],
        flops=2 * rows * WIDTH * C_IN,
        moved=rows * C_IN * 5,
        name="input_grad",
    )

    parts, input_grad = lax.optimization_barrier((parts, input_grad))
    sums = (two_slot + one_slot + 2 * w3_rows + shards * fc_slot, WIDTH)
    (mine,) = call(
        functools.partial(sum_last_kernel, two_rows, fc_rows, one_rows),
        1,
        [near(parts), near(three)],
        [(sums, F32, whole(sums), True)],
        flops=1000000,
        moved=2000000,
        name="sum_last",
    )
    (weight_one_grad, weight_two_grad, weight_three_grad, fc_first_grad, fc_second_grad) = call(
        functools.partial(finish_kernel, two_rows, fc_rows, one_rows, w3_rows),
        1,
        [core_in, near(mine), near(other_core(mine))],
        [
            small(one_rows, WIDTH),
            small(two_rows, 2 * WIDTH),
            small(w3_rows, C_IN),
            small(WIDTH, INTER),
            small(INTER, 2 * WIDTH),
        ],
        [pltpu.VMEM((2 * shards * fc_rows, 128), F32)],
        flops=1000000,
        moved=2000000,
        name="finish",
    )
    return (
        outputs.reshape(inputs.shape),
        input_grad.reshape(inputs.shape),
        weight_one_grad,
        weight_two_grad,
        weight_three_grad,
        fc_first_grad,
        fc_second_grad,
        fc_bias_grad.reshape(-1),
        gain_grad.reshape(-1),
        shift_grad.reshape(-1),
    )


def solution(mesh):
    return jax.shard_map(
        body,
        mesh=mesh,
        in_specs=(
            P(("fsdp", "dp"), None, None),
            P(("fsdp", "dp")),
            P("fsdp", None),
            P("fsdp", None),
            P("fsdp", None),
            P(),
            P(),
            P(),
            P(),
            P(),
            P(("fsdp", "dp"), None, None),
        ),
        out_specs=(
            P(("fsdp", "dp"), None, None),
            P(("fsdp", "dp"), None, None),
            P("fsdp", None),
            P("fsdp", None),
            P("fsdp", None),
            P(),
            P(),
            P(),
            P(),
            P(),
        ),
        check_vma=False,
    )
```

```python
import functools

import jax
import jax.numpy as jnp
from jax import lax
from jax.experimental import pallas as pl
from jax.experimental.pallas import tpu as pltpu
from jax.sharding import PartitionSpec as P

C_IN = 1024
WIDTH = 256
INTER = 128
SIDE = 16
PIX = SIDE * SIDE
HALF = WIDTH // 2
EPS = 1e-05
AXES = ("fsdp", "dp")
HIGH = lax.Precision.HIGHEST
F32 = jnp.float32
BF16 = jnp.bfloat16
MIB = 1024 * 1024

AHEAD = 4
VMEM = 44
CHUNK = 32
PER_CONV_ONE = 4
PER_CONV_TWO = 3
PER_ACT_TWO = 4
PER_COMBINE = 6
PER_OUTPUT = 2
PER_OUTER_THREE = 4
PER_BACK_THREE = 3
PER_BACK_TWO = 2
PER_WEIGHT_TWO = 4
PER_BACK_ONE = 3
PER_INPUT_GRAD = 3


def dot_f(left, right):
    return jnp.dot(left, right, preferred_element_type=F32)


def dot_rows(left, right):
    return lax.dot_general(left, right, (((0,), (0,)), ((), ())), preferred_element_type=F32)


def dot_last(left, right):
    return lax.dot_general(left, right, (((1,), (1,)), ((), ())), preferred_element_type=F32)


def high_f(left, right):
    return jnp.dot(left, right, preferred_element_type=F32, precision=HIGH)


def high_rows(left, right):
    return lax.dot_general(
        left, right, (((0,), (0,)), ((), ())), preferred_element_type=F32, precision=HIGH
    )


def high_last(left, right):
    return lax.dot_general(
        left, right, (((1,), (1,)), ((), ())), preferred_element_type=F32, precision=HIGH
    )


def exact_f(left, right):
    total_product = None
    for _ in range(3):
        piece = left.astype(BF16)
        product = dot_f(piece, right)
        total_product = product if total_product is None else total_product + product
        left = left - piece.astype(F32)
    return total_product


def pixel_mask(image_side, width):
    row = lax.broadcasted_iota(jnp.int32, (PIX, 128), 0)
    inside = ((row >> 4) < image_side) & ((row & 15) < image_side)
    return wide(jnp.where(inside, 1.0, 0.0).astype(F32), width)


def wide(mask, width):
    if width == 128:
        return mask
    return jnp.concatenate([mask] * (width // 128), axis=1)


def fold(values):
    rows, n = values.shape
    return jnp.sum(values.reshape(rows // 8, 8, n), axis=0)


def chunks(j=0):
    for low in range(0, PIX, CHUNK):
        yield pl.ds(j * PIX + low, CHUNK), slice(low, low + CHUNK)


def row_sum(values):
    return jnp.sum(values, axis=0, keepdims=True)


def total(payload_ref):
    return jnp.sum(payload_ref[...], axis=0)


def norm_terms(sums, count):
    mean = sums[0:1] / count
    variance = sums[1:2] / count - mean * mean
    return mean, lax.rsqrt(variance + EPS)


def send_rows(payload_ref, rows):
    block = jnp.concatenate(rows, axis=0)
    payload_ref[...] = jnp.broadcast_to(block[None], payload_ref.shape)


def silu_parts(half_pre):
    t = jnp.tanh(half_pre)
    a = 1.0 + t
    value = half_pre * a
    slope = 0.5 * a * (1.0 + half_pre * (1.0 - t))
    return value, slope


def whole(shape):
    zeros = (0,) * len(shape)
    return pl.BlockSpec(shape, lambda *_: zeros)


SMEM_SPEC = pl.BlockSpec(memory_space=pltpu.SMEM)


def call(kernel, grid, ins, outs, scratch=(), vmem=VMEM, flops=0, moved=0, name=None):
    arrays = [
        array
        if spec is SMEM_SPEC or near
        else pltpu.with_memory_space_constraint(array, pltpu.HBM)
        for array, spec, *near in ins
    ]
    shapes = [
        jax.ShapeDtypeStruct(shape, dtype) if near else pltpu.HBM(shape, dtype)
        for shape, dtype, _, *near in outs
    ]
    return pl.pallas_call(
        kernel,
        grid=(grid,),
        in_specs=[spec for _, spec, *_ in ins],
        out_specs=[spec for _, _, spec, *_ in outs],
        out_shape=shapes,
        scratch_shapes=list(scratch),
        compiler_params=pltpu.CompilerParams(
            dimension_semantics=("arbitrary",), vmem_limit_bytes=vmem * MIB
        ),
        cost_estimate=pl.CostEstimate(flops=flops, bytes_accessed=moved, transcendentals=0),
        name=name,
    )(*arrays)


class Stream:
    def __init__(self, over=None):
        self.over = over


BEGIN, END = "begin", "end"


def stream_call(kernel, per, steps, ins, outs, scratch=(), vmem=VMEM, flops=0, moved=0, name=None):
    block = per * PIX
    in_specs, out_specs, arrays, shapes, rooms = [], [], [], [], []
    in_streams, out_streams, room_of = [], [], {}
    for at, (array, spec, *near) in enumerate(ins):
        if isinstance(spec, Stream):
            in_streams.append(at)
            room_of[at] = len(rooms)
            rooms.append(pltpu.VMEM(array.shape, array.dtype))
            spec = pl.BlockSpec(memory_space=pltpu.HBM)
        elif near:
            arrays.append(array)
            in_specs.append(spec)
            continue
        in_specs.append(spec)
        arrays.append(
            array if spec is SMEM_SPEC else pltpu.with_memory_space_constraint(array, pltpu.HBM)
        )
    for at, (shape, dtype, spec, *near) in enumerate(outs):
        shapes.append(jax.ShapeDtypeStruct(shape, dtype) if near else pltpu.HBM(shape, dtype))
        if isinstance(spec, Stream):
            out_streams.append(at)
            if spec.over is None:
                room_of[len(ins) + at] = len(rooms)
                rooms.append(pltpu.VMEM(shape, dtype))
            else:
                room_of[len(ins) + at] = room_of[spec.over]
            spec = pl.BlockSpec(memory_space=pltpu.HBM)
        out_specs.append(spec)
    n_in, n_out, n_rooms = len(ins), len(outs), len(rooms)

    def whole_kernel(*refs):
        in_refs, out_refs = refs[:n_in], refs[n_in : n_in + n_out]
        room_refs = refs[n_in + n_out : n_in + n_out + n_rooms]
        own_refs = refs[n_in + n_out + n_rooms : -2]
        in_sems, out_sems = refs[-2:]

        def rows(step):
            return pl.ds(pl.multiple_of(step * block, block), block)

        def copies_in(step):
            return [
                pltpu.make_async_copy(
                    in_refs[at].at[rows(step)],
                    room_refs[room_of[at]].at[rows(step)],
                    in_sems.at[k, step],
                )
                for k, at in enumerate(in_streams)
            ]

        def copies_out(step):
            return [
                pltpu.make_async_copy(
                    room_refs[room_of[n_in + at]].at[rows(step)],
                    out_refs[at].at[rows(step)],
                    out_sems.at[k, step],
                )
                for k, at in enumerate(out_streams)
            ]

        def views(step):
            both = []
            for at, ref in enumerate(in_refs + out_refs):
                if at in room_of:
                    ref = room_refs[room_of[at]].at[rows(step)]
                both.append(ref)
            return both + list(own_refs)

        ahead = min(AHEAD, steps)
        for step in range(ahead):
            for copy in copies_in(step):
                copy.start()
        kernel(BEGIN, *views(0))

        def one(step, carry):
            for copy in copies_in(step):
                copy.wait()

            @pl.when(step + ahead < steps)
            def _():
                for copy in copies_in(step + ahead):
                    copy.start()

            kernel(step, *views(step))
            for copy in copies_out(step):
                copy.start()
            return carry

        lax.fori_loop(0, steps, one, 0)
        kernel(END, *views(0))

        def last(step, carry):
            for copy in copies_out(step):
                copy.wait()
            return carry

        lax.fori_loop(0, steps, last, 0)

    return pl.pallas_call(
        whole_kernel,
        in_specs=in_specs,
        out_specs=out_specs,
        out_shape=shapes,
        scratch_shapes=rooms
        + list(scratch)
        + [
            pltpu.SemaphoreType.DMA((max(len(in_streams), 1), steps)),
            pltpu.SemaphoreType.DMA((max(len(out_streams), 1), steps)),
        ],
        compiler_params=pltpu.CompilerParams(vmem_limit_bytes=vmem * MIB),
        cost_estimate=pl.CostEstimate(flops=flops, bytes_accessed=moved, transcendentals=0),
        name=name,
    )(*arrays)


def pack_kernel(core_ref, *refs):
    count = len(refs) // 2

    def put(half):
        for ref, out_ref in zip(refs[:count], refs[count:]):
            rows, cols = ref.shape
            for b in range(cols // 256):
                low = half * (cols // 2) + b * 128
                piece = ref[:, low : low + 128]
                for f in range(out_ref.shape[0]):
                    out_ref[f, pl.ds(b * rows, rows)] = piece

    for core in range(2):
        pl.when(core_ref[0] == core)(functools.partial(put, core))


def unpack_kernel(core_ref, mine_ref, other_ref, out_ref, *wide_refs):
    shards = mine_ref.shape[0]
    rows, cols = out_ref.shape[0] // shards, out_ref.shape[1]

    def put(half, source_ref):
        for f in range(shards):
            for b in range(cols // 256):
                piece = source_ref[f, pl.ds(b * rows, rows)]
                at = (pl.ds(f * rows, rows), pl.ds(half * (cols // 2) + b * 128, 128))
                if wide_refs:
                    wide_refs[0][at] = piece.astype(F32)
                else:
                    out_ref[at] = piece

    for core in range(2):

        @pl.when(core_ref[0] == core)
        def _():
            put(core, mine_ref)
            put(1 - core, other_ref)

    if wide_refs:
        out_ref[...] = wide_refs[0][...].astype(BF16)


def conv_one_kernel(
    step, per, core_ref, sides_ref, x_ref, mine_ref, other_ref, h_ref, w_out_ref, send_ref,
    acc_ref, count_ref,
):
    if step is BEGIN:
        acc_ref[...] = jnp.zeros_like(acc_ref)
        count_ref[0] = 0.0

        def put(core):
            for half, ref in ((core, mine_ref), (1 - core, other_ref)):
                w_out_ref[:, half * HALF : (half + 1) * HALF] = ref[...].reshape(C_IN, HALF)

        for core in range(2):
            pl.when(core_ref[0] == core)(functools.partial(put, core))
        return

    if step is END:
        count = jnp.full((1, WIDTH), count_ref[0], F32)
        send_rows(
            send_ref,
            [row_sum(acc_ref[0:8]), row_sum(acc_ref[8:16]), count, jnp.zeros((1, WIDTH), F32)],
        )
        return

    h = dot_f(x_ref[...], w_out_ref[...])
    h_ref[...] = h
    for j in range(per):
        side = SIDE - 2 * sides_ref[step * per + j]
        mask = pixel_mask(side, 128)
        sums = jnp.zeros((8, WIDTH), F32)
        squares = jnp.zeros((8, WIDTH), F32)
        for rows, part in chunks():
            one = h[j * PIX + part.start : j * PIX + part.stop]
            kept = one * wide(mask[part], WIDTH)
            sums = sums + fold(kept)
            squares = squares + fold(kept * one)
        acc_ref[0:8] += sums
        acc_ref[8:16] += squares
        count_ref[0] += (side * side).astype(F32)


def edge_masks(width):
    column = lax.broadcasted_iota(jnp.int32, (CHUNK, 128), 0) & 15
    first = jnp.where(column == 0, 0.0, 1.0).astype(F32)
    last = jnp.where(column == 15, 0.0, 1.0).astype(F32)
    return wide(first, width), wide(last, width)


def put_taps(taps_ref, j, part, act, first, last):
    shifted = (pltpu.roll(act, 1, 0) * first, act, pltpu.roll(act, CHUNK - 1, 0) * last)
    low = SIDE + j * (PIX + SIDE) + part.start
    for d in range(3):
        piece = shifted[d].astype(BF16)
        for q in range(2):
            taps_ref[pl.ds(low, CHUNK), pl.ds(q * 384 + d * 128, 128)] = piece[
                :, q * HALF : (q + 1) * HALF
            ]


def conv_two_kernel(
    step, per, sides_ref, got_ref, h_ref, w_ref, gain_ref, shift_ref, hat_ref, h2_ref, vec_ref, send_ref,
    taps_ref, acc_ref,
):
    if step is BEGIN:
        sums = total(got_ref)
        mean, inv = norm_terms(sums, sums[2:3])
        vec_ref[0:1] = mean
        vec_ref[1:2] = inv
        vec_ref[2:3] = sums[2:3]
        acc_ref[...] = jnp.zeros_like(acc_ref)
        taps_ref[...] = jnp.zeros_like(taps_ref)
        return

    if step is END:
        send_rows(send_ref, [row_sum(acc_ref[0:8]), row_sum(acc_ref[8:16])])
        return

    gain = gain_ref[:, :WIDTH] * 0.5
    shift = shift_ref[:, :WIDTH] * 0.5
    first, last = edge_masks(WIDTH)
    for j in range(per):
        side = SIDE - 2 * sides_ref[step * per + j]
        mask = pixel_mask(side, 128)
        for rows, part in chunks(j):
            hat = (h_ref[rows] - vec_ref[0:1]) * vec_ref[1:2]
            hat_ref[rows] = hat.astype(BF16)
            half_pre = hat * gain + shift
            act = half_pre * ((1.0 + jnp.tanh(half_pre)) * wide(mask[part], WIDTH))
            put_taps(taps_ref, j, part, act, first, last)
    height = per * (PIX + SIDE)
    for q in range(2):
        cols = pl.ds(q * WIDTH, WIDTH)
        patches = jnp.concatenate(
            [taps_ref[pl.ds(SIDE * d, height), pl.ds(q * 384, 384)] for d in range(3)], axis=1
        )
        both = dot_f(patches, w_ref[:, cols])
        for j in range(per):
            side = SIDE - 2 * sides_ref[step * per + j]
            mask = pixel_mask(side, 128)
            sums = jnp.zeros((8, WIDTH), F32)
            squares = jnp.zeros((8, WIDTH), F32)
            for rows, part in chunks(j):
                low = j * (PIX + SIDE) + part.start
                h2 = both[low : low + CHUNK]
                h2_ref[rows, cols] = h2
                kept = h2 * wide(mask[part], WIDTH)
                sums = sums + fold(kept)
                squares = squares + fold(kept * h2)
            acc_ref[0:8, cols] += sums
            acc_ref[8:16, cols] += squares


def act_two_kernel(
    step, per, sides_ref, one_ref, got_ref, h2_ref, gain_ref, shift_ref, fc_ref,
    hat_ref, a2_ref, slope_ref, pooled_ref, zin_ref, t2_ref, t4_ref, vec_ref, send_ref,
):
    if step is BEGIN:
        sums = total(got_ref)
        mean, inv = norm_terms(sums, jnp.concatenate([one_ref[2:3]] * 2, axis=1))
        vec_ref[0:1] = mean
        vec_ref[1:2] = inv
        return

    if step is END:
        z = high_f(pooled_ref[...], fc_ref[...])
        zin_ref[...] = z
        send_rows(send_ref, [row_sum(z), row_sum(z * z)])
        return

    gain = gain_ref[:, WIDTH : 3 * WIDTH] * 0.5
    shift = shift_ref[:, WIDTH : 3 * WIDTH] * 0.5
    for j in range(per):
        side = SIDE - 2 * sides_ref[step * per + j]
        mask = pixel_mask(side, 128)
        image = pl.ds(step * per + j, 1)
        values = jnp.zeros((8, WIDTH), F32)
        for q in range(2):
            cols = slice(q * WIDTH, (q + 1) * WIDTH)
            sums = jnp.zeros((8, WIDTH), F32)
            products = jnp.zeros((8, WIDTH), F32)
            for rows, part in chunks(j):
                hat = (h2_ref[rows, cols] - vec_ref[0:1, cols]) * vec_ref[1:2, cols]
                hat_ref[rows, cols] = hat.astype(BF16)
                half_pre = hat * gain[:, cols] + shift[:, cols]
                a = (1.0 + jnp.tanh(half_pre)) * wide(mask[part], WIDTH)
                value = half_pre * a
                slope = a * (0.5 + half_pre - 0.5 * value)
                a2_ref[rows, cols] = value.astype(BF16)
                slope_ref[rows, cols] = slope.astype(BF16)
                values = values + fold(value)
                sums = sums + fold(slope)
                products = products + fold(slope * hat)
            t2_ref[image, cols] = row_sum(sums)
            t4_ref[image, cols] = row_sum(products)
        pooled_ref[image] = row_sum(values) / (side * side).astype(F32)


def hidden_terms(zin, sums, n_images, gain_ref, shift_ref):
    mean, inv = norm_terms(sums, n_images)
    zhat = (zin - mean) * inv
    cols = slice(3 * WIDTH, 3 * WIDTH + INTER)
    half_z = (zhat * gain_ref[:, cols] + shift_ref[:, cols]) * 0.5
    value, slope = silu_parts(half_z)
    return zhat, inv, value, slope


def combine_kernel(
    step, per, n_images, got_ref, zin_ref, a2_ref, w3_ref, fc_ref, bias_ref, gain_ref, shift_ref,
    att_ref, comb_ref, gw_ref, csum_ref, hid_ref, send_ref, gram_ref, acc_ref,
):
    if step is BEGIN:
        zhat, inv, hidden, slope = hidden_terms(
            zin_ref[...], total(got_ref), n_images, gain_ref, shift_ref
        )
        hid_ref[0] = zhat
        hid_ref[1] = hidden
        hid_ref[2] = slope
        hid_ref[3] = jnp.broadcast_to(inv, slope.shape)
        logits = high_f(hidden, fc_ref[...]) + bias_ref[...]
        left, right = logits[:, :WIDTH], logits[:, WIDTH:]
        top = jnp.maximum(left, right)
        left, right = jnp.exp(left - top), jnp.exp(right - top)
        both = left + right
        att_ref[:, :WIDTH] = left / both
        att_ref[:, WIDTH:] = right / both
        gram_ref[...] = jnp.zeros_like(gram_ref)
        acc_ref[...] = jnp.zeros_like(acc_ref)
        return

    if step is END:
        csum = row_sum(acc_ref[...])
        csum_ref[...] = csum
        both = jnp.concatenate([gram_ref[...], jnp.broadcast_to(csum, (8, WIDTH))], axis=0)
        both = exact_f(both, w3_ref[...])
        gw = both[:WIDTH]
        gw_ref[...] = gw
        send_rows(send_ref, [both[WIDTH : WIDTH + 1], row_sum(w3_ref[...].astype(F32) * gw)])
        return

    for j in range(per):
        att = att_ref[pl.ds(step * per + j, 1)]
        sums = jnp.zeros((8, WIDTH), F32)
        for rows, _ in chunks(j):
            left = att[:, :WIDTH] * a2_ref[rows, :WIDTH].astype(F32)
            comb = (left + att[:, WIDTH:] * a2_ref[rows, WIDTH:].astype(F32)).astype(BF16)
            comb_ref[rows] = comb
            sums = sums + fold(comb.astype(F32))
        acc_ref[...] += sums
    comb = comb_ref[...]
    gram_ref[...] += dot_rows(comb, comb)


def output_kernel(
    step, per, sides_ref, one_ref, got_ref, comb_ref, x_ref, cot_ref, w3_ref, gain_ref, shift_ref,
    out_ref, u3_ref, stat_ref, send_ref, vec_ref, acc_ref,
):
    if step is BEGIN:
        count = jnp.concatenate([one_ref[2:3]] * 4, axis=1)
        mean, inv = norm_terms(total(got_ref), count)
        scale = inv * gain_ref[:, 3 * WIDTH + INTER :]
        stat_ref[0:1] = mean
        stat_ref[1:2] = inv
        stat_ref[2:3] = scale
        stat_ref[3:4] = count
        vec_ref[0:1] = scale
        vec_ref[1:2] = shift_ref[:, 3 * WIDTH + INTER :] - mean * scale
        vec_ref[2:3] = 0.5 * scale
        acc_ref[...] = jnp.zeros_like(acc_ref)
        return

    if step is END:
        send_rows(
            send_ref,
            [0.5 * row_sum(acc_ref[0:8]), 0.5 * row_sum(acc_ref[8:16]) / vec_ref[0:1]],
        )
        return

    chunk = 16
    lanes = 512
    for j in range(per):
        side = SIDE - 2 * sides_ref[step * per + j]
        mask = pixel_mask(side, 128)
        h3 = dot_f(comb_ref[pl.ds(j * PIX, PIX)], w3_ref[...])
        for n in range(C_IN // lanes):
            cols = pl.ds(n * lanes, lanes)
            ups = jnp.zeros((8, lanes), F32)
            products = jnp.zeros((8, lanes), F32)
            for c in range(PIX // chunk):
                rows = pl.ds(j * PIX + c * chunk, chunk)
                scaled = (
                    h3[c * chunk : (c + 1) * chunk, n * lanes : (n + 1) * lanes] * vec_ref[0:1, cols]
                )
                pre = scaled + vec_ref[1:2, cols] + x_ref[rows, cols].astype(F32)
                half_pre = pre * 0.5
                a = (1.0 + jnp.tanh(half_pre)) * wide(mask[c * chunk : (c + 1) * chunk], lanes)
                value = half_pre * a
                out_ref[rows, cols] = value.astype(BF16)
                up = cot_ref[rows, cols].astype(F32) * (a * (1.0 + pre - value))
                u3_ref[rows, cols] = (up * vec_ref[2:3, cols]).astype(BF16)
                ups = ups + fold(up)
                products = products + fold(up * scaled)
            acc_ref[0:8, cols] += ups
            acc_ref[8:16, cols] += products


def outer_three_kernel(step, comb_ref, u3_ref, cu_ref):
    if step is BEGIN:
        cu_ref[...] = jnp.zeros_like(cu_ref)
        return

    if step is END:
        return

    cu_ref[...] += dot_rows(comb_ref[...], u3_ref[...])


def back_three_kernel(
    step, per, three_ref, got_ref, hid_ref, comb_ref, u3_ref, a2_ref, slope_ref,
    hat_ref, w3_ref, cu_ref, gw_ref, csum_ref, att_ref, fc_ref, core_ref,
    p_ref, t1_ref, t3_ref, duz_ref, keep_ref, give_ref, fcg_ref, norm_ref, s_ref, c_ref, send_ref, datt_ref, k_ref,
):
    if step is BEGIN:
        mean, inv = three_ref[0:1], three_ref[1:2]
        scale, count = three_ref[2:3], three_ref[3:4]
        sums = total(got_ref)
        dshift = sums[0:1]
        dgain = (sums[1:2] - mean * dshift) * inv
        norm_ref[0:1] = dgain
        norm_ref[1:2] = dshift
        k2 = scale * inv * dgain / count
        k1 = scale * dshift / count - mean * k2
        w3 = w3_ref[...].astype(F32)
        s_ref[...] = dot_last((w3 * k2).astype(BF16), w3_ref[...]).astype(BF16)
        c_ref[...] = high_last(jnp.broadcast_to(k1, (8, C_IN)), w3)
        k_ref[0:1] = k1
        k_ref[1:2] = k2
        return

    if step is END:
        csum = jnp.broadcast_to(csum_ref[...], (8, WIDTH))
        outer = high_rows(csum, jnp.broadcast_to(k_ref[0:1], (8, C_IN))) * 0.125
        w3g = cu_ref[...] - outer - gw_ref[...] * k_ref[1:2]

        def put(core):
            keep_ref[...] = w3g[:, core * 512 : (core + 1) * 512]
            give_ref[...] = w3g[:, (1 - core) * 512 : (2 - core) * 512]

        for core in range(2):
            pl.when(core_ref[0] == core)(functools.partial(put, core))
        att = att_ref[...]
        datt = datt_ref[...]
        both = att * datt
        inner = both[:, :WIDTH] + both[:, WIDTH:]
        dlog = both - att * jnp.concatenate([inner, inner], axis=1)
        zhat, hidden, slope = hid_ref[0], hid_ref[1], hid_ref[2]
        fcg = high_rows(hidden, dlog)
        duz = high_last(dlog, fc_ref[...]) * slope
        duz_ref[...] = duz
        bias = row_sum(dlog)
        rows = [row_sum(duz), row_sum(duz * zhat)]
        for b in range(4):
            cols = slice(b * 128, (b + 1) * 128)
            fcg_ref[pl.ds(b * INTER, INTER)] = fcg[:, cols]
            rows.append(bias[:, cols])
        send_rows(send_ref, rows + [jnp.zeros((2, 128), F32)])
        return

    corr = dot_f(comb_ref[...], s_ref[...])
    p_ref[...] = dot_last(u3_ref[...], w3_ref[...]).astype(BF16)
    for j in range(per):
        image = pl.ds(step * per + j, 1)
        sums = [jnp.zeros((8, WIDTH), F32)] * 6
        for rows, part in chunks(j):
            low = j * PIX + part.start
            dcomb = p_ref[rows].astype(F32) - corr[low : low + CHUNK] - c_ref[0:1]
            for q in range(2):
                cols = slice(q * WIDTH, (q + 1) * WIDTH)
                u = dcomb * slope_ref[rows, cols].astype(F32)
                sums[q] = sums[q] + fold(dcomb * a2_ref[rows, cols].astype(F32))
                sums[2 + q] = sums[2 + q] + fold(u)
                sums[4 + q] = sums[4 + q] + fold(u * hat_ref[rows, cols].astype(F32))
        for k, ref in enumerate((datt_ref, t1_ref, t3_ref)):
            for q in range(2):
                ref[image, q * WIDTH : (q + 1) * WIDTH] = row_sum(sums[2 * k + q])


def back_att_kernel(
    n_images, got_ref, hid_ref, duz_ref, pooled_ref, sides_ref, fc_ref, att_ref,
    t1_ref, t2_ref, t3_ref, t4_ref, fcg_ref, gain_ref,
    dpool_ref, pack_ref, bias_ref, norm_ref, send_ref,
):
    zhat, inv = hid_ref[0], hid_ref[3, 0:1]
    sums = total(got_ref)
    norm_ref[0:1] = sums[1:2]
    norm_ref[1:2] = sums[0:1]
    for b in range(4):
        bias_ref[:, b * 128 : (b + 1) * 128] = sums[2 + b : 3 + b]
    scale = inv * gain_ref[:, 3 * WIDTH : 3 * WIDTH + INTER]
    dzin = scale * (duz_ref[...] - (sums[0:1] + zhat * sums[1:2]) / n_images)
    pack_ref[0:WIDTH] = high_rows(pooled_ref[...], dzin)
    pack_ref[WIDTH:] = fcg_ref[...]
    dpool_ref[...] = high_last(dzin, fc_ref[...])
    for i in range(dpool_ref.shape[0]):
        side = SIDE - 2 * sides_ref[i]
        dpool_ref[i : i + 1] = dpool_ref[i : i + 1] / (side * side).astype(F32)
    dpool = dpool_ref[...]
    both = jnp.concatenate([dpool, dpool], axis=1)
    att = att_ref[...]
    send_rows(
        send_ref,
        [
            row_sum(att * t1_ref[...] + both * t2_ref[...]),
            row_sum(att * t3_ref[...] + both * t4_ref[...]),
        ],
    )


def back_two_kernel(
    step, per, sides_ref, one_ref, two_ref, got_ref, comb_ref, p_ref, s_ref, c_ref, slope_ref, hat2_ref, hat1_ref, att_ref,
    dpool_ref, w_ref, gain_ref, shift_ref, fc_ref, dh2_ref, u1_ref, norm_ref, send_ref,
    vec_ref, pad_ref, acc_ref,
):
    if step is BEGIN:
        count = jnp.concatenate([one_ref[2:3]] * 2, axis=1)
        scale = two_ref[1:2] * gain_ref[:, WIDTH : 3 * WIDTH]
        sums = total(got_ref)
        norm_ref[0:1] = sums[1:2]
        norm_ref[1:2] = sums[0:1]
        vec_ref[0:1] = scale
        vec_ref[1:2] = scale * sums[0:1] / count
        vec_ref[2:3] = scale * sums[1:2] / count
        acc_ref[...] = jnp.zeros_like(acc_ref)
        pad_ref[...] = jnp.zeros_like(pad_ref)
        return

    if step is END:
        rows = []
        for k in range(2):
            both = row_sum(acc_ref[8 * k : 8 * k + 8])
            rows += [both[:, :HALF], both[:, HALF:]]
        sums = jnp.concatenate(rows, axis=0)
        devices, height, _ = send_ref.shape
        for d in range(devices):
            send_ref[d, pl.ds(0, 4)] = sums
            send_ref[d, pl.ds(4, height - 4)] = fc_ref[pl.ds(d * (height - 4), height - 4)]
        return

    first, last = edge_masks(HALF)
    corr = dot_f(comb_ref[...], s_ref[...])
    for j in range(per):
        side = SIDE - 2 * sides_ref[step * per + j]
        mask = pixel_mask(side, 128)
        image = pl.ds(step * per + j, 1)
        dpool = dpool_ref[image]
        for rows, part in chunks(j):
            low = j * PIX + part.start
            dcomb = p_ref[rows].astype(F32) - corr[low : low + CHUNK] - c_ref[0:1]
            for q in range(2):
                cols = slice(q * WIDTH, (q + 1) * WIDTH)
                scale = vec_ref[0:1, cols]
                up = dcomb * (att_ref[image, cols] * scale) + dpool * scale
                dh2 = slope_ref[rows, cols].astype(F32) * up - wide(mask[part], WIDTH) * (
                    vec_ref[1:2, cols] + hat2_ref[rows, cols].astype(F32) * vec_ref[2:3, cols]
                )
                dh2 = dh2.astype(BF16)
                dh2_ref[rows, cols] = dh2
                pad_ref[pl.ds(SIDE + j * (PIX + SIDE) + part.start, CHUNK), cols] = dh2
    height = per * (PIX + SIDE)
    for q in range(2):
        lines = jnp.concatenate(
            [pad_ref[pl.ds(SIDE * (2 - d), height), pl.ds(q * WIDTH, WIDTH)] for d in range(3)],
            axis=1,
        )
        weight = jnp.concatenate(
            [
                jnp.concatenate(
                    [
                        w_ref[pl.ds((3 * r + d) * HALF, HALF), pl.ds(q * WIDTH, WIDTH)]
                        for r in range(3)
                    ],
                    axis=1,
                )
                for d in range(3)
            ],
            axis=0,
        )
        both = dot_last(lines, weight)
        for j in range(per):
            side = SIDE - 2 * sides_ref[step * per + j]
            mask = pixel_mask(side, 128)
            cols = slice(q * HALF, (q + 1) * HALF)
            gain = gain_ref[:, cols] * 0.5
            shift = shift_ref[:, cols] * 0.5
            sums = jnp.zeros((8, HALF), F32)
            products = jnp.zeros((8, HALF), F32)
            for rows, part in chunks(j):
                low = j * (PIX + SIDE) + part.start
                y = both[low : low + CHUNK]
                da1 = (
                    y[:, HALF : 2 * HALF]
                    + pltpu.roll(y[:, :HALF], CHUNK - 1, 0) * last
                    + pltpu.roll(y[:, 2 * HALF :], 1, 0) * first
                )
                hat = hat1_ref[rows, cols].astype(F32)
                half_pre = hat * gain + shift
                a = (1.0 + jnp.tanh(half_pre)) * mask[part]
                u1 = da1 * (a * (0.5 + half_pre - 0.5 * half_pre * a))
                u1_ref[rows, cols] = u1.astype(BF16)
                sums = sums + fold(u1)
                products = products + fold(u1 * hat)
            acc_ref[0:8, cols] += sums
            acc_ref[8:16, cols] += products


def weight_two_kernel(
    step, per, core_ref, sides_ref, hat_ref, dh2_ref, gain_ref, shift_ref, keep_ref, give_ref,
    taps_ref, acc_ref,
):
    if step is BEGIN:
        acc_ref[...] = jnp.zeros_like(acc_ref)
        taps_ref[...] = jnp.zeros_like(taps_ref)
        return

    if step is END:
        def put(core):
            keep_ref[...] = acc_ref[core].T
            give_ref[...] = acc_ref[1 - core].T

        for core in range(2):
            pl.when(core_ref[0] == core)(functools.partial(put, core))
        return

    gain = gain_ref[:, :WIDTH] * 0.5
    shift = shift_ref[:, :WIDTH] * 0.5
    first, last = edge_masks(WIDTH)
    height = PIX + SIDE
    for j in range(per):
        side = SIDE - 2 * sides_ref[step * per + j]
        mask = pixel_mask(side, 128)
        for rows, part in chunks(j):
            half_pre = hat_ref[rows].astype(F32) * gain + shift
            act = half_pre * ((1.0 + jnp.tanh(half_pre)) * wide(mask[part], WIDTH))
            put_taps(taps_ref, j, part, act, first, last)
    for q in range(2):
        patches = jnp.concatenate(
            [
                jnp.concatenate(
                    [
                        taps_ref[pl.ds(SIDE * d + j * height, PIX), pl.ds(q * 384, 384)]
                        for d in range(3)
                    ],
                    axis=1,
                )
                for j in range(per)
            ],
            axis=0,
        )
        acc_ref[q] += dot_rows(dh2_ref[:, q * WIDTH : (q + 1) * WIDTH], patches)


def back_one_kernel(
    step, per, core_ref, sides_ref, one_ref, got_ref, u1_ref, hat_ref, x_ref, gain_ref, norm2_ref,
    norm_att_ref, norm3_ref, dh_ref, keep_ref, give_ref, gain_out_ref, shift_out_ref, vec_ref, acc_ref,
):
    if step is BEGIN:
        count = one_ref[2:3]
        scale = one_ref[1:2] * gain_ref[:, :WIDTH]
        sums = total(got_ref)
        sums = [jnp.concatenate([sums[k : k + 1], sums[k + 1 : k + 2]], axis=1) for k in (0, 2)]
        for row, out_ref in ((0, gain_out_ref), (1, shift_out_ref)):
            out_ref[:, :WIDTH] = sums[1 - row]
            out_ref[:, WIDTH : 3 * WIDTH] = norm2_ref[row : row + 1]
            out_ref[:, 3 * WIDTH : 3 * WIDTH + INTER] = norm_att_ref[row : row + 1]
            out_ref[:, 3 * WIDTH + INTER :] = norm3_ref[row : row + 1]
        vec_ref[0:1] = scale
        vec_ref[1:2] = scale * sums[0] / count
        vec_ref[2:3] = scale * sums[1] / count
        acc_ref[...] = jnp.zeros_like(acc_ref)
        return

    if step is END:

        def put(core):
            keep_ref[...] = acc_ref[core * HALF : (core + 1) * HALF].T
            give_ref[...] = acc_ref[(1 - core) * HALF : (2 - core) * HALF].T

        for core in range(2):
            pl.when(core_ref[0] == core)(functools.partial(put, core))
        return

    for j in range(per):
        side = SIDE - 2 * sides_ref[step * per + j]
        mask = pixel_mask(side, 128)
        for rows, part in chunks(j):
            dh_ref[rows] = (
                u1_ref[rows].astype(F32) * vec_ref[0:1]
                - wide(mask[part], WIDTH) * (vec_ref[1:2] + hat_ref[rows].astype(F32) * vec_ref[2:3])
            ).astype(BF16)
    acc_ref[...] += dot_rows(dh_ref[...], x_ref[...])


def input_grad_kernel(step, dh_ref, u3_ref, three_ref, w_ref, ig_ref, wide_ref):
    if step is BEGIN:
        wide_ref[...] = 1.0 / three_ref[2:3]
        return

    if step is END:
        return

    dx = dot_last(dh_ref[...], w_ref[...])
    for low in range(0, dx.shape[0], 16):
        rows = pl.ds(low, 16)
        ig_ref[rows] = (u3_ref[rows].astype(F32) * wide_ref[...] + dx[low : low + 16]).astype(BF16)


def round_up(value, multiple):
    return -(-value // multiple) * multiple


def two_wide(part, rows):
    missing = 2 * rows - part.shape[0]
    if missing:
        part = jnp.concatenate([part, jnp.zeros((missing, 128), F32)], axis=0)
    return jnp.concatenate([part[:rows], part[rows:]], axis=1)


def slot_rows(two_rows, fc_rows, one_rows, three_rows):
    return (
        round_up(two_rows, 16),
        round_up(fc_rows, 32) // 2,
        round_up(one_rows, 32) // 2,
        round_up(2 * three_rows, 16),
    )


def add_slots(ref, at, rows):
    rows = pl.ds(at, rows)
    both = ref[0, rows].astype(F32)
    for f in range(1, ref.shape[0]):
        both = both + ref[f, rows].astype(F32)
    return both


def lengthen(part, rows):
    if rows == part.shape[0]:
        return part
    return jnp.concatenate([part, jnp.zeros((rows - part.shape[0], part.shape[1]), F32)], axis=0)


def pack_last_kernel(
    fc_rows, keep2_ref, other2_ref, keep1_ref, other1_ref, keep3_ref, other3_ref, got_ref, out_ref
):
    shards = out_ref.shape[0]
    two_rows = keep2_ref.shape[0] // shards
    one_rows = keep1_ref.shape[0] // shards
    three_rows = keep3_ref.shape[0] // shards
    two_slot, fc_slot, one_slot, three_slot = slot_rows(two_rows, fc_rows, one_rows, three_rows)
    fc = two_wide(add_slots(got_ref, 4, fc_rows), fc_slot).astype(BF16)
    for f in range(shards):
        rows = pl.ds(f * two_rows, two_rows)
        part = lengthen(keep2_ref[rows] + other2_ref[rows], two_slot)
        out_ref[f, pl.ds(0, two_slot)] = part.astype(BF16)
        at = two_slot
        out_ref[f, pl.ds(at, fc_slot)] = fc
        at += fc_slot
        rows = pl.ds(f * one_rows, one_rows)
        part = two_wide(keep1_ref[rows] + other1_ref[rows], one_slot)
        out_ref[f, pl.ds(at, one_slot)] = part.astype(BF16)
        at += one_slot
        rows = pl.ds(f * three_rows, three_rows)
        part = keep3_ref[rows] + other3_ref[rows]
        part = jnp.concatenate([part[:, :WIDTH], part[:, WIDTH:]], axis=0)
        out_ref[f, pl.ds(at, three_slot)] = lengthen(part, three_slot).astype(BF16)


def sum_last_kernel(two_rows, fc_rows, one_rows, three_rows, parts_ref, out_ref):
    shards = parts_ref.shape[0]
    two_slot, fc_slot, one_slot, three_slot = slot_rows(two_rows, fc_rows, one_rows, three_rows)
    out_ref[pl.ds(0, two_slot)] = add_slots(parts_ref, 0, two_slot)
    after = two_slot + fc_slot
    out_ref[pl.ds(two_slot, one_slot + three_slot)] = add_slots(
        parts_ref, after, one_slot + three_slot
    )
    at = two_slot + one_slot + three_slot
    for f in range(shards):
        out_ref[pl.ds(at + f * fc_slot, fc_slot)] = parts_ref[f, pl.ds(two_slot, fc_slot)].astype(F32)


def finish_kernel(
    two_rows, fc_rows, one_rows, three_rows, core_ref, mine_ref, other_ref,
    one_ref, two_ref, three_ref, fc1_ref, fc2_ref, pack_ref,
):
    two_slot, fc_slot, one_slot, three_slot = slot_rows(two_rows, fc_rows, one_rows, three_rows)
    at_three = two_slot + one_slot
    at_fc = at_three + three_slot
    shards = (mine_ref.shape[0] - at_fc) // fc_slot

    def tall(ref, at, half_rows, rows):
        both = jnp.concatenate(
            [ref[pl.ds(at, half_rows), :128], ref[pl.ds(at, half_rows), 128:]], axis=0
        )
        return both[:rows]

    def put(half, ref):
        two_ref[:, half * WIDTH : (half + 1) * WIDTH] = ref[pl.ds(0, two_rows)]
        one_ref[:, half * HALF : (half + 1) * HALF] = tall(ref, two_slot, one_slot, one_rows)
        for b in range(2):
            low = (half * 2 + b) * WIDTH
            three_ref[:, low : low + WIDTH] = ref[pl.ds(at_three + b * three_rows, three_rows)]
        for f in range(shards):
            pack_ref[pl.ds((2 * f + half) * fc_rows, fc_rows)] = tall(
                ref, at_fc + f * fc_slot, fc_slot, fc_rows
            )

    for core in range(2):

        @pl.when(core_ref[0] == core)
        def _():
            put(core, mine_ref)
            put(1 - core, other_ref)

    fc1_ref[...] = pack_ref[0:WIDTH]
    for b in range(4):
        fc2_ref[:, b * 128 : (b + 1) * 128] = pack_ref[pl.ds(WIDTH + b * INTER, INTER)]


def everyone(payload):
    return lax.all_to_all(payload, AXES, 0, 0, tiled=True)


def other_core(array):
    return lax.ppermute(array, "dp", [(0, 1), (1, 0)])


def spread_weights(core, weights):
    shards = lax.axis_size("fsdp")
    shapes = [(shards, w.shape[0] * w.shape[1] // 256, 128) for w in weights]
    return call(
        pack_kernel,
        1,
        [(core, SMEM_SPEC)] + [(weight, whole(weight.shape)) for weight in weights],
        [(shape, BF16, whole(shape), True) for shape in shapes],
        flops=1000000,
        moved=4000000,
        name="pack",
    )


def join_weight(core, mine, shape):
    other = other_core(mine)
    rows = shape[0] // mine.shape[0]
    return call(
        unpack_kernel,
        1,
        [(core, SMEM_SPEC), (mine, whole(mine.shape), True), (other, whole(mine.shape), True)],
        [(shape, BF16, whole(shape))],
        [] if rows % 16 == 0 else [pltpu.VMEM(shape, F32)],
        flops=1000000,
        moved=4000000,
        name="unpack",
    )[0]


def slots(parts):
    return lax.all_to_all(parts, "fsdp", 0, 0, tiled=True)


def body(
    inputs,
    sides,
    weight_one,
    weight_two,
    weight_three,
    fc_first,
    fc_second,
    fc_bias,
    bn_gain,
    bn_shift,
    cotangent,
):
    images = inputs.shape[0]
    rows = images * PIX
    devices = lax.axis_size("fsdp") * lax.axis_size("dp")
    n_images = float(images * devices)
    x = inputs.reshape(rows, C_IN)
    cot = cotangent.reshape(rows, C_IN)
    gain = bn_gain.reshape(1, -1)
    shift = bn_shift.reshape(1, -1)
    bias = fc_bias.reshape(1, -1)
    n_ch = gain.shape[1]
    core = lax.axis_index("dp").astype(jnp.int32).reshape(1)

    def split(most):
        per = max(n for n in range(1, most + 1) if images % n == 0)
        return per, images // per

    core_in = (core, SMEM_SPEC)
    sides_in = (sides, SMEM_SPEC)
    gain_in = (gain, whole((1, n_ch)))
    shift_in = (shift, whole((1, n_ch)))

    def payload(k, n):
        return ((devices, k, n), F32, whole((devices, k, n)), True)

    def small(*shape):
        return (shape, F32, whole(shape))

    def full(array):
        return (array, whole(array.shape))

    def near(array):
        return (array, whole(array.shape), True)

    def blocks(array):
        return (array, Stream())

    def blocks_out(width, dtype=BF16, over=None):
        return ((rows, width), dtype, Stream(over))

    spread_one, spread_two, spread_three = spread_weights(
        core, (weight_one, weight_two, weight_three)
    )
    mine = slots(spread_one)
    other = other_core(mine)
    spread_two, mine, other = lax.optimization_barrier((spread_two, mine, other))
    mine_two = slots(spread_two)

    per, steps = split(PER_CONV_ONE)
    h1, full_one, send = stream_call(
        lambda step, *refs, per=per: conv_one_kernel(step, per, *refs),
        per,
        steps,
        [core_in, sides_in, blocks(x), near(mine), near(other)],
        [blocks_out(WIDTH, F32), ((C_IN, WIDTH), BF16, whole((C_IN, WIDTH))), payload(4, WIDTH)],
        [pltpu.VMEM((16, WIDTH), F32), pltpu.SMEM((1,), F32)],
        flops=2 * rows * C_IN * WIDTH,
        moved=rows * C_IN * 2 + rows * WIDTH * 4,
        name="conv_one",
    )
    send, mine_two = lax.optimization_barrier((send, mine_two))
    got_one = everyone(send)
    full_two = join_weight(core, mine_two, (9 * HALF, 2 * WIDTH))
    got_one, spread_three, full_two = lax.optimization_barrier((got_one, spread_three, full_two))
    mine_three = slots(spread_three)

    per, steps = split(PER_CONV_TWO)
    hat1, h2, stat1, send = stream_call(
        lambda step, *refs, per=per: conv_two_kernel(step, per, *refs),
        per,
        steps,
        [sides_in, near(got_one), blocks(h1), full(full_two), gain_in, shift_in],
        [blocks_out(WIDTH), blocks_out(2 * WIDTH, F32), small(8, WIDTH), payload(2, 2 * WIDTH)],
        [
            pltpu.VMEM((per * (PIX + SIDE) + 2 * SIDE, 6 * HALF), BF16),
            pltpu.VMEM((16, 2 * WIDTH), F32),
        ],
        flops=2 * rows * 9 * HALF * 2 * WIDTH,
        moved=rows * WIDTH * 14,
        name="conv_two",
    )
    send, mine_three = lax.optimization_barrier((send, mine_three))
    got_two = everyone(send)
    full_three = join_weight(core, mine_three, (WIDTH, C_IN))

    per, steps = split(PER_ACT_TWO)
    hat2, a2, slope2, pooled, zin, t2, t4, stat2, send = stream_call(
        lambda step, *refs, per=per: act_two_kernel(step, per, *refs),
        per,
        steps,
        [
            sides_in,
            full(stat1),
            near(got_two),
            blocks(h2),
            gain_in,
            shift_in,
            full(fc_first),
        ],
        [
            blocks_out(2 * WIDTH),
            blocks_out(2 * WIDTH),
            blocks_out(2 * WIDTH),
            small(images, WIDTH),
            small(images, INTER),
            small(images, 2 * WIDTH),
            small(images, 2 * WIDTH),
            small(8, 2 * WIDTH),
            payload(2, INTER),
        ],
        flops=rows * 2 * WIDTH * 20,
        moved=rows * 2 * WIDTH * 10,
        name="act_two",
    )
    got_att = everyone(send)

    per, steps = split(PER_COMBINE)
    att, comb, gw, csum, hid, send = stream_call(
        lambda step, *refs, per=per: combine_kernel(step, per, n_images, *refs),
        per,
        steps,
        [
            near(got_att),
            full(zin),
            blocks(a2),
            full(full_three),
            full(fc_second),
            full(bias),
            gain_in,
            shift_in,
        ],
        [
            small(images, 2 * WIDTH),
            blocks_out(WIDTH),
            small(WIDTH, C_IN),
            small(1, WIDTH),
            small(4, images, INTER),
            payload(2, C_IN),
        ],
        [pltpu.VMEM((WIDTH, WIDTH), F32), pltpu.VMEM((8, WIDTH), F32)],
        flops=2 * rows * WIDTH * WIDTH,
        moved=rows * WIDTH * 6,
        name="combine",
    )
    got_three = everyone(send)

    per, steps = split(PER_OUTPUT)
    outputs, u3, stat3, send = stream_call(
        lambda step, *refs, per=per: output_kernel(step, per, *refs),
        per,
        steps,
        [
            sides_in,
            full(stat1),
            near(got_three),
            blocks(comb),
            blocks(x),
            blocks(cot),
            full(full_three),
            gain_in,
            shift_in,
        ],
        [
            blocks_out(C_IN, over=4),
            blocks_out(C_IN, over=5),
            small(8, C_IN),
            payload(2, C_IN),
        ],
        [pltpu.VMEM((8, C_IN), F32), pltpu.VMEM((16, C_IN), F32)],
        flops=2 * rows * WIDTH * C_IN,
        moved=rows * C_IN * 8,
        name="output",
    )
    got_back_three = everyone(send)

    per, steps = split(PER_OUTER_THREE)
    (cu,) = stream_call(
        outer_three_kernel,
        per,
        steps,
        [blocks(comb), blocks(u3)],
        [small(WIDTH, C_IN)],
        flops=2 * rows * WIDTH * C_IN,
        moved=rows * C_IN * 3,
        name="outer_three",
    )

    per, steps = split(PER_BACK_THREE)
    p, t1, t3, duz, keep_three, give_three, fc2_local, norm3, corr_weight, corr_row, send = stream_call(
        lambda step, *refs, per=per: back_three_kernel(step, per, *refs),
        per,
        steps,
        [
            full(stat3),
            near(got_back_three),
            full(hid),
            blocks(comb),
            blocks(u3),
            blocks(a2),
            blocks(slope2),
            blocks(hat2),
            full(full_three),
            full(cu),
            full(gw),
            full(csum),
            full(att),
            full(fc_second),
            core_in,
        ],
        [
            blocks_out(WIDTH, over=3),
            small(images, 2 * WIDTH),
            small(images, 2 * WIDTH),
            small(images, INTER),
            small(WIDTH, C_IN // 2),
            small(WIDTH, C_IN // 2),
            small(4 * INTER, 128),
            small(2, C_IN),
            ((WIDTH, WIDTH), BF16, whole((WIDTH, WIDTH))),
            small(8, WIDTH),
            payload(8, INTER),
        ],
        [pltpu.VMEM((images, 2 * WIDTH), F32), pltpu.VMEM((2, C_IN), F32)],
        flops=4 * rows * WIDTH * C_IN,
        moved=rows * WIDTH * 16,
        name="back_three",
    )
    got_back_att = everyone(send)

    dpool, packed, fc_bias_grad, norm_att, send = call(
        functools.partial(back_att_kernel, n_images),
        1,
        [
            near(got_back_att),
            full(hid),
            full(duz),
            full(pooled),
            sides_in,
            full(fc_first),
            full(att),
            full(t1),
            full(t2),
            full(t3),
            full(t4),
            full(fc2_local),
            gain_in,
        ],
        [
            small(images, WIDTH),
            small(WIDTH + 4 * INTER, 128),
            small(1, 2 * WIDTH),
            small(2, INTER),
            payload(2, 2 * WIDTH),
        ],
        flops=10000000,
        moved=1000000,
        name="back_att",
    )
    got_back_two = everyone(send)
    shards = lax.axis_size("fsdp")
    w3_rows = WIDTH // shards
    fc_rows = packed.shape[0] // devices

    per, steps = split(PER_BACK_TWO)
    dh2, u1, norm2, send = stream_call(
        lambda step, *refs, per=per: back_two_kernel(step, per, *refs),
        per,
        steps,
        [
            sides_in,
            full(stat1),
            full(stat2),
            near(got_back_two),
            blocks(comb),
            blocks(p),
            full(corr_weight),
            full(corr_row),
            blocks(slope2),
            blocks(hat2),
            blocks(hat1),
            full(att),
            full(dpool),
            full(full_two),
            gain_in,
            shift_in,
            full(packed),
        ],
        [
            blocks_out(2 * WIDTH),
            blocks_out(WIDTH),
            small(2, 2 * WIDTH),
            payload(4 + fc_rows, 128),
        ],
        [
            pltpu.VMEM((8, 2 * WIDTH), F32),
            pltpu.VMEM((per * (PIX + SIDE) + 2 * SIDE, 2 * WIDTH), BF16),
            pltpu.VMEM((16, WIDTH), F32),
        ],
        flops=2 * rows * 9 * HALF * 2 * WIDTH,
        moved=rows * WIDTH * 20,
        name="back_two",
    )
    got_back_one = everyone(send)

    per, steps = split(PER_WEIGHT_TWO)
    half = (9 * HALF, WIDTH)
    keep, give = stream_call(
        lambda step, *refs, per=per: weight_two_kernel(step, per, *refs),
        per,
        steps,
        [core_in, sides_in, blocks(hat1), blocks(dh2), gain_in, shift_in],
        [(half, F32, whole(half)), (half, F32, whole(half))],
        [
            pltpu.VMEM((per * (PIX + SIDE) + 2 * SIDE, 6 * HALF), BF16),
            pltpu.VMEM((2, WIDTH, 9 * HALF), F32),
        ],
        flops=2 * rows * 9 * HALF * 2 * WIDTH,
        moved=rows * WIDTH * 6,
        name="weight_two",
    )
    got_back_one, keep, give = lax.optimization_barrier((got_back_one, keep, give))
    per, steps = split(PER_BACK_ONE)
    half_one = (C_IN, HALF)
    dh1, keep_one, give_one, gain_grad, shift_grad = stream_call(
        lambda step, *refs, per=per: back_one_kernel(step, per, *refs),
        per,
        steps,
        [
            core_in,
            sides_in,
            full(stat1),
            near(got_back_one),
            blocks(u1),
            blocks(hat1),
            blocks(x),
            gain_in,
            full(norm2),
            full(norm_att),
            full(norm3),
        ],
        [
            blocks_out(WIDTH),
            small(*half_one),
            small(*half_one),
            small(1, n_ch),
            small(1, n_ch),
        ],
        [pltpu.VMEM((8, WIDTH), F32), pltpu.VMEM((WIDTH, C_IN), F32)],
        flops=2 * rows * WIDTH * C_IN,
        moved=rows * C_IN * 4,
        name="back_one",
    )

    two_rows, one_rows = 9 * HALF // shards, C_IN // shards
    two_slot, fc_slot, one_slot, three_slot = slot_rows(two_rows, fc_rows, one_rows, w3_rows)
    slot = (shards, two_slot + fc_slot + one_slot + three_slot, WIDTH)
    (parts,) = call(
        functools.partial(pack_last_kernel, fc_rows),
        1,
        [
            full(keep),
            near(other_core(give)),
            full(keep_one),
            near(other_core(give_one)),
            full(keep_three),
            near(other_core(give_three)),
            near(got_back_one),
        ],
        [(slot, BF16, whole(slot))],
        flops=1000000,
        moved=5000000,
        name="pack_last",
    )
    dh1, parts = lax.optimization_barrier((dh1, parts))
    parts = slots(parts)

    per, steps = split(PER_INPUT_GRAD)
    (input_grad,) = stream_call(
        input_grad_kernel,
        per,
        steps,
        [blocks(dh1), blocks(u3), full(stat3), full(full_one)],
        [blocks_out(C_IN, over=1)],
        [pltpu.VMEM((1, C_IN), F32)],
        flops=2 * rows * WIDTH * C_IN,
        moved=rows * C_IN * 5,
        name="input_grad",
    )

    parts, input_grad = lax.optimization_barrier((parts, input_grad))
    sums = (two_slot + one_slot + three_slot + shards * fc_slot, WIDTH)
    (mine,) = call(
        functools.partial(sum_last_kernel, two_rows, fc_rows, one_rows, w3_rows),
        1,
        [near(parts)],
        [(sums, F32, whole(sums), True)],
        flops=1000000,
        moved=2000000,
        name="sum_last",
    )
    (weight_one_grad, weight_two_grad, weight_three_grad, fc_first_grad, fc_second_grad) = call(
        functools.partial(finish_kernel, two_rows, fc_rows, one_rows, w3_rows),
        1,
        [core_in, near(mine), near(other_core(mine))],
        [
            small(one_rows, WIDTH),
            small(two_rows, 2 * WIDTH),
            small(w3_rows, C_IN),
            small(WIDTH, INTER),
            small(INTER, 2 * WIDTH),
        ],
        [pltpu.VMEM((2 * shards * fc_rows, 128), F32)],
        flops=1000000,
        moved=2000000,
        name="finish",
    )
    return (
        outputs.reshape(inputs.shape),
        input_grad.reshape(inputs.shape),
        weight_one_grad,
        weight_two_grad,
        weight_three_grad,
        fc_first_grad,
        fc_second_grad,
        fc_bias_grad.reshape(-1),
        gain_grad.reshape(-1),
        shift_grad.reshape(-1),
    )


def solution(mesh):
    return jax.shard_map(
        body,
        mesh=mesh,
        in_specs=(
            P(("fsdp", "dp"), None, None),
            P(("fsdp", "dp")),
            P("fsdp", None),
            P("fsdp", None),
            P("fsdp", None),
            P(),
            P(),
            P(),
            P(),
            P(),
            P(("fsdp", "dp"), None, None),
        ),
        out_specs=(
            P(("fsdp", "dp"), None, None),
            P(("fsdp", "dp"), None, None),
            P("fsdp", None),
            P("fsdp", None),
            P("fsdp", None),
            P(),
            P(),
            P(),
            P(),
            P(),
        ),
        check_vma=False,
    )
```

```python
import functools

import jax
import jax.numpy as jnp
from jax import lax
from jax.experimental import pallas as pl
from jax.experimental.pallas import tpu as pltpu
from jax.sharding import PartitionSpec as P

C_IN = 1024
WIDTH = 256
INTER = 128
SIDE = 16
PIX = SIDE * SIDE
HALF = WIDTH // 2
EPS = 1e-05
AXES = ("fsdp", "dp")
HIGH = lax.Precision.HIGHEST
F32 = jnp.float32
BF16 = jnp.bfloat16
MIB = 1024 * 1024

AHEAD = 4
VMEM = 44
CHUNK = 32
PER_CONV_ONE = 3
PER_CONV_TWO = 3
PER_ACT_TWO = 4
PER_COMBINE = 6
PER_OUTPUT = 2
PER_OUTER_THREE = 4
PER_BACK_THREE = 3
PER_BACK_TWO = 2
PER_WEIGHT_TWO = 4
PER_BACK_ONE = 3
PER_INPUT_GRAD = 3


def dot_f(left, right):
    return jnp.dot(left, right, preferred_element_type=F32)


def dot_rows(left, right):
    return lax.dot_general(left, right, (((0,), (0,)), ((), ())), preferred_element_type=F32)


def dot_last(left, right):
    return lax.dot_general(left, right, (((1,), (1,)), ((), ())), preferred_element_type=F32)


def high_f(left, right):
    return jnp.dot(left, right, preferred_element_type=F32, precision=HIGH)


def high_rows(left, right):
    return lax.dot_general(
        left, right, (((0,), (0,)), ((), ())), preferred_element_type=F32, precision=HIGH
    )


def high_last(left, right):
    return lax.dot_general(
        left, right, (((1,), (1,)), ((), ())), preferred_element_type=F32, precision=HIGH
    )


def exact_f(left, right):
    total_product = None
    for _ in range(3):
        piece = left.astype(BF16)
        product = dot_f(piece, right)
        total_product = product if total_product is None else total_product + product
        left = left - piece.astype(F32)
    return total_product


def pixel_mask(image_side, width):
    row = lax.broadcasted_iota(jnp.int32, (PIX, 128), 0)
    inside = ((row >> 4) < image_side) & ((row & 15) < image_side)
    return wide(jnp.where(inside, 1.0, 0.0).astype(F32), width)


def wide(mask, width):
    if width == 128:
        return mask
    return jnp.concatenate([mask] * (width // 128), axis=1)


def fold(values):
    rows, n = values.shape
    return jnp.sum(values.reshape(rows // 8, 8, n), axis=0)


def chunks(j=0):
    for low in range(0, PIX, CHUNK):
        yield pl.ds(j * PIX + low, CHUNK), slice(low, low + CHUNK)


def row_sum(values):
    return jnp.sum(values, axis=0, keepdims=True)


def total(payload_ref):
    return jnp.sum(payload_ref[...], axis=0)


def norm_terms(sums, count):
    mean = sums[0:1] / count
    variance = sums[1:2] / count - mean * mean
    return mean, lax.rsqrt(variance + EPS)


def send_rows(payload_ref, rows):
    block = jnp.concatenate(rows, axis=0)
    payload_ref[...] = jnp.broadcast_to(block[None], payload_ref.shape)


def silu_parts(half_pre):
    t = jnp.tanh(half_pre)
    a = 1.0 + t
    value = half_pre * a
    slope = 0.5 * a * (1.0 + half_pre * (1.0 - t))
    return value, slope


def whole(shape):
    zeros = (0,) * len(shape)
    return pl.BlockSpec(shape, lambda *_: zeros)


SMEM_SPEC = pl.BlockSpec(memory_space=pltpu.SMEM)


def call(kernel, grid, ins, outs, scratch=(), vmem=VMEM, flops=0, moved=0, name=None):
    arrays = [
        array
        if spec is SMEM_SPEC or near
        else pltpu.with_memory_space_constraint(array, pltpu.HBM)
        for array, spec, *near in ins
    ]
    shapes = [
        jax.ShapeDtypeStruct(shape, dtype) if near else pltpu.HBM(shape, dtype)
        for shape, dtype, _, *near in outs
    ]
    return pl.pallas_call(
        kernel,
        grid=(grid,),
        in_specs=[spec for _, spec, *_ in ins],
        out_specs=[spec for _, _, spec, *_ in outs],
        out_shape=shapes,
        scratch_shapes=list(scratch),
        compiler_params=pltpu.CompilerParams(
            dimension_semantics=("arbitrary",), vmem_limit_bytes=vmem * MIB
        ),
        cost_estimate=pl.CostEstimate(flops=flops, bytes_accessed=moved, transcendentals=0),
        name=name,
    )(*arrays)


class Stream:
    def __init__(self, over=None):
        self.over = over


BEGIN, END = "begin", "end"


def stream_call(kernel, per, steps, ins, outs, scratch=(), vmem=VMEM, flops=0, moved=0, name=None):
    block = per * PIX
    in_specs, out_specs, arrays, shapes, rooms = [], [], [], [], []
    in_streams, out_streams, room_of = [], [], {}
    for at, (array, spec, *near) in enumerate(ins):
        if isinstance(spec, Stream):
            in_streams.append(at)
            room_of[at] = len(rooms)
            rooms.append(pltpu.VMEM(array.shape, array.dtype))
            spec = pl.BlockSpec(memory_space=pltpu.HBM)
        elif near:
            arrays.append(array)
            in_specs.append(spec)
            continue
        in_specs.append(spec)
        arrays.append(
            array if spec is SMEM_SPEC else pltpu.with_memory_space_constraint(array, pltpu.HBM)
        )
    for at, (shape, dtype, spec, *near) in enumerate(outs):
        shapes.append(jax.ShapeDtypeStruct(shape, dtype) if near else pltpu.HBM(shape, dtype))
        if isinstance(spec, Stream):
            out_streams.append(at)
            if spec.over is None:
                room_of[len(ins) + at] = len(rooms)
                rooms.append(pltpu.VMEM(shape, dtype))
            else:
                room_of[len(ins) + at] = room_of[spec.over]
            spec = pl.BlockSpec(memory_space=pltpu.HBM)
        out_specs.append(spec)
    n_in, n_out, n_rooms = len(ins), len(outs), len(rooms)

    def whole_kernel(*refs):
        in_refs, out_refs = refs[:n_in], refs[n_in : n_in + n_out]
        room_refs = refs[n_in + n_out : n_in + n_out + n_rooms]
        own_refs = refs[n_in + n_out + n_rooms : -2]
        in_sems, out_sems = refs[-2:]

        def rows(step):
            return pl.ds(pl.multiple_of(step * block, block), block)

        def copies_in(step):
            return [
                pltpu.make_async_copy(
                    in_refs[at].at[rows(step)],
                    room_refs[room_of[at]].at[rows(step)],
                    in_sems.at[k, step],
                )
                for k, at in enumerate(in_streams)
            ]

        def copies_out(step):
            return [
                pltpu.make_async_copy(
                    room_refs[room_of[n_in + at]].at[rows(step)],
                    out_refs[at].at[rows(step)],
                    out_sems.at[k, step],
                )
                for k, at in enumerate(out_streams)
            ]

        def views(step):
            both = []
            for at, ref in enumerate(in_refs + out_refs):
                if at in room_of:
                    ref = room_refs[room_of[at]].at[rows(step)]
                both.append(ref)
            return both + list(own_refs)

        ahead = min(AHEAD, steps)
        for step in range(ahead):
            for copy in copies_in(step):
                copy.start()
        kernel(BEGIN, *views(0))

        def one(step, carry):
            for copy in copies_in(step):
                copy.wait()

            @pl.when(step + ahead < steps)
            def _():
                for copy in copies_in(step + ahead):
                    copy.start()

            kernel(step, *views(step))
            for copy in copies_out(step):
                copy.start()
            return carry

        lax.fori_loop(0, steps, one, 0)
        kernel(END, *views(0))

        def last(step, carry):
            for copy in copies_out(step):
                copy.wait()
            return carry

        lax.fori_loop(0, steps, last, 0)

    return pl.pallas_call(
        whole_kernel,
        in_specs=in_specs,
        out_specs=out_specs,
        out_shape=shapes,
        scratch_shapes=rooms
        + list(scratch)
        + [
            pltpu.SemaphoreType.DMA((max(len(in_streams), 1), steps)),
            pltpu.SemaphoreType.DMA((max(len(out_streams), 1), steps)),
        ],
        compiler_params=pltpu.CompilerParams(vmem_limit_bytes=vmem * MIB),
        cost_estimate=pl.CostEstimate(flops=flops, bytes_accessed=moved, transcendentals=0),
        name=name,
    )(*arrays)


def pack_kernel(core_ref, *refs):
    count = len(refs) // 2

    def put(half):
        for ref, out_ref in zip(refs[:count], refs[count:]):
            rows, cols = ref.shape
            for b in range(cols // 256):
                low = half * (cols // 2) + b * 128
                piece = ref[:, low : low + 128]
                for f in range(out_ref.shape[0]):
                    out_ref[f, pl.ds(b * rows, rows)] = piece

    for core in range(2):
        pl.when(core_ref[0] == core)(functools.partial(put, core))


def unpack_kernel(core_ref, mine_ref, other_ref, out_ref, *wide_refs):
    shards = mine_ref.shape[0]
    rows, cols = out_ref.shape[0] // shards, out_ref.shape[1]

    def put(half, source_ref):
        for f in range(shards):
            for b in range(cols // 256):
                piece = source_ref[f, pl.ds(b * rows, rows)]
                at = (pl.ds(f * rows, rows), pl.ds(half * (cols // 2) + b * 128, 128))
                if wide_refs:
                    wide_refs[0][at] = piece.astype(F32)
                else:
                    out_ref[at] = piece

    for core in range(2):

        @pl.when(core_ref[0] == core)
        def _():
            put(core, mine_ref)
            put(1 - core, other_ref)

    if wide_refs:
        out_ref[...] = wide_refs[0][...].astype(BF16)


def conv_one_kernel(
    step, per, core_ref, sides_ref, x_ref, mine_ref, other_ref, h_ref, w_out_ref, send_ref,
    acc_ref, count_ref,
):
    if step is BEGIN:
        acc_ref[...] = jnp.zeros_like(acc_ref)
        count_ref[0] = 0.0

        def put(core):
            for half, ref in ((core, mine_ref), (1 - core, other_ref)):
                w_out_ref[:, half * HALF : (half + 1) * HALF] = ref[...].reshape(C_IN, HALF)

        for core in range(2):
            pl.when(core_ref[0] == core)(functools.partial(put, core))
        return

    if step is END:
        count = jnp.full((1, WIDTH), count_ref[0], F32)
        send_rows(
            send_ref,
            [row_sum(acc_ref[0:8]), row_sum(acc_ref[8:16]), count, jnp.zeros((1, WIDTH), F32)],
        )
        return

    h = dot_f(x_ref[...], w_out_ref[...])
    h_ref[...] = h
    for j in range(per):
        side = SIDE - 2 * sides_ref[step * per + j]
        mask = pixel_mask(side, 128)
        sums = jnp.zeros((8, WIDTH), F32)
        squares = jnp.zeros((8, WIDTH), F32)
        for rows, part in chunks():
            one = h[j * PIX + part.start : j * PIX + part.stop]
            kept = one * wide(mask[part], WIDTH)
            sums = sums + fold(kept)
            squares = squares + fold(kept * one)
        acc_ref[0:8] += sums
        acc_ref[8:16] += squares
        count_ref[0] += (side * side).astype(F32)


def edge_masks(width):
    column = lax.broadcasted_iota(jnp.int32, (CHUNK, 128), 0) & 15
    first = jnp.where(column == 0, 0.0, 1.0).astype(F32)
    last = jnp.where(column == 15, 0.0, 1.0).astype(F32)
    return wide(first, width), wide(last, width)


def put_taps(taps_ref, j, part, act, first, last):
    shifted = (pltpu.roll(act, 1, 0) * first, act, pltpu.roll(act, CHUNK - 1, 0) * last)
    low = SIDE + j * (PIX + SIDE) + part.start
    for d in range(3):
        piece = shifted[d].astype(BF16)
        for q in range(2):
            taps_ref[pl.ds(low, CHUNK), pl.ds(q * 384 + d * 128, 128)] = piece[
                :, q * HALF : (q + 1) * HALF
            ]


def conv_two_kernel(
    step, per, sides_ref, got_ref, h_ref, w_ref, gain_ref, shift_ref, hat_ref, h2_ref, vec_ref, send_ref,
    taps_ref, acc_ref,
):
    if step is BEGIN:
        sums = total(got_ref)
        mean, inv = norm_terms(sums, sums[2:3])
        vec_ref[0:1] = mean
        vec_ref[1:2] = inv
        vec_ref[2:3] = sums[2:3]
        acc_ref[...] = jnp.zeros_like(acc_ref)
        taps_ref[...] = jnp.zeros_like(taps_ref)
        return

    if step is END:
        send_rows(send_ref, [row_sum(acc_ref[0:8]), row_sum(acc_ref[8:16])])
        return

    gain = gain_ref[:, :WIDTH] * 0.5
    shift = shift_ref[:, :WIDTH] * 0.5
    first, last = edge_masks(WIDTH)
    for j in range(per):
        side = SIDE - 2 * sides_ref[step * per + j]
        mask = pixel_mask(side, 128)
        for rows, part in chunks(j):
            hat = (h_ref[rows] - vec_ref[0:1]) * vec_ref[1:2]
            hat_ref[rows] = hat.astype(BF16)
            half_pre = hat * gain + shift
            act = half_pre * ((1.0 + jnp.tanh(half_pre)) * wide(mask[part], WIDTH))
            put_taps(taps_ref, j, part, act, first, last)
    height = per * (PIX + SIDE)
    for q in range(2):
        cols = pl.ds(q * WIDTH, WIDTH)
        patches = jnp.concatenate(
            [taps_ref[pl.ds(SIDE * d, height), pl.ds(q * 384, 384)] for d in range(3)], axis=1
        )
        both = dot_f(patches, w_ref[:, cols])
        for j in range(per):
            side = SIDE - 2 * sides_ref[step * per + j]
            mask = pixel_mask(side, 128)
            sums = jnp.zeros((8, WIDTH), F32)
            squares = jnp.zeros((8, WIDTH), F32)
            for rows, part in chunks(j):
                low = j * (PIX + SIDE) + part.start
                h2 = both[low : low + CHUNK]
                h2_ref[rows, cols] = h2
                kept = h2 * wide(mask[part], WIDTH)
                sums = sums + fold(kept)
                squares = squares + fold(kept * h2)
            acc_ref[0:8, cols] += sums
            acc_ref[8:16, cols] += squares


def act_two_kernel(
    step, per, sides_ref, one_ref, got_ref, h2_ref, gain_ref, shift_ref, fc_ref,
    hat_ref, a2_ref, slope_ref, pooled_ref, zin_ref, t2_ref, t4_ref, vec_ref, send_ref,
):
    if step is BEGIN:
        sums = total(got_ref)
        mean, inv = norm_terms(sums, jnp.concatenate([one_ref[2:3]] * 2, axis=1))
        vec_ref[0:1] = mean
        vec_ref[1:2] = inv
        return

    if step is END:
        z = high_f(pooled_ref[...], fc_ref[...])
        zin_ref[...] = z
        send_rows(send_ref, [row_sum(z), row_sum(z * z)])
        return

    gain = gain_ref[:, WIDTH : 3 * WIDTH] * 0.5
    shift = shift_ref[:, WIDTH : 3 * WIDTH] * 0.5
    for j in range(per):
        side = SIDE - 2 * sides_ref[step * per + j]
        mask = pixel_mask(side, 128)
        image = pl.ds(step * per + j, 1)
        values = jnp.zeros((8, WIDTH), F32)
        for q in range(2):
            cols = slice(q * WIDTH, (q + 1) * WIDTH)
            sums = jnp.zeros((8, WIDTH), F32)
            products = jnp.zeros((8, WIDTH), F32)
            for rows, part in chunks(j):
                hat = (h2_ref[rows, cols] - vec_ref[0:1, cols]) * vec_ref[1:2, cols]
                hat_ref[rows, cols] = hat.astype(BF16)
                half_pre = hat * gain[:, cols] + shift[:, cols]
                a = (1.0 + jnp.tanh(half_pre)) * wide(mask[part], WIDTH)
                value = half_pre * a
                slope = a * (0.5 + half_pre - 0.5 * value)
                a2_ref[rows, cols] = value.astype(BF16)
                slope_ref[rows, cols] = slope.astype(BF16)
                values = values + fold(value)
                sums = sums + fold(slope)
                products = products + fold(slope * hat)
            t2_ref[image, cols] = row_sum(sums)
            t4_ref[image, cols] = row_sum(products)
        pooled_ref[image] = row_sum(values) / (side * side).astype(F32)


def hidden_terms(zin, sums, n_images, gain_ref, shift_ref):
    mean, inv = norm_terms(sums, n_images)
    zhat = (zin - mean) * inv
    cols = slice(3 * WIDTH, 3 * WIDTH + INTER)
    half_z = (zhat * gain_ref[:, cols] + shift_ref[:, cols]) * 0.5
    value, slope = silu_parts(half_z)
    return zhat, inv, value, slope


def combine_kernel(
    step, per, n_images, got_ref, zin_ref, a2_ref, w3_ref, fc_ref, bias_ref, gain_ref, shift_ref,
    att_ref, comb_ref, gw_ref, csum_ref, hid_ref, send_ref, gram_ref, acc_ref,
):
    if step is BEGIN:
        zhat, inv, hidden, slope = hidden_terms(
            zin_ref[...], total(got_ref), n_images, gain_ref, shift_ref
        )
        hid_ref[0] = zhat
        hid_ref[1] = hidden
        hid_ref[2] = slope
        hid_ref[3] = jnp.broadcast_to(inv, slope.shape)
        logits = high_f(hidden, fc_ref[...]) + bias_ref[...]
        left, right = logits[:, :WIDTH], logits[:, WIDTH:]
        top = jnp.maximum(left, right)
        left, right = jnp.exp(left - top), jnp.exp(right - top)
        both = left + right
        att_ref[:, :WIDTH] = left / both
        att_ref[:, WIDTH:] = right / both
        gram_ref[...] = jnp.zeros_like(gram_ref)
        acc_ref[...] = jnp.zeros_like(acc_ref)
        return

    if step is END:
        csum = row_sum(acc_ref[...])
        csum_ref[...] = csum
        both = jnp.concatenate([gram_ref[...], jnp.broadcast_to(csum, (8, WIDTH))], axis=0)
        both = exact_f(both, w3_ref[...])
        gw = both[:WIDTH]
        gw_ref[...] = gw
        send_rows(send_ref, [both[WIDTH : WIDTH + 1], row_sum(w3_ref[...].astype(F32) * gw)])
        return

    for j in range(per):
        att = att_ref[pl.ds(step * per + j, 1)]
        sums = jnp.zeros((8, WIDTH), F32)
        for rows, _ in chunks(j):
            left = att[:, :WIDTH] * a2_ref[rows, :WIDTH].astype(F32)
            comb = (left + att[:, WIDTH:] * a2_ref[rows, WIDTH:].astype(F32)).astype(BF16)
            comb_ref[rows] = comb
            sums = sums + fold(comb.astype(F32))
        acc_ref[...] += sums
    comb = comb_ref[...]
    gram_ref[...] += dot_rows(comb, comb)


def output_kernel(
    step, per, sides_ref, one_ref, got_ref, comb_ref, x_ref, cot_ref, w3_ref, gain_ref, shift_ref,
    out_ref, u3_ref, stat_ref, send_ref, vec_ref, acc_ref,
):
    if step is BEGIN:
        count = jnp.concatenate([one_ref[2:3]] * 4, axis=1)
        mean, inv = norm_terms(total(got_ref), count)
        scale = inv * gain_ref[:, 3 * WIDTH + INTER :]
        stat_ref[0:1] = mean
        stat_ref[1:2] = inv
        stat_ref[2:3] = scale
        stat_ref[3:4] = count
        vec_ref[0:1] = scale
        vec_ref[1:2] = shift_ref[:, 3 * WIDTH + INTER :] - mean * scale
        vec_ref[2:3] = 0.5 * scale
        acc_ref[...] = jnp.zeros_like(acc_ref)
        return

    if step is END:
        send_rows(
            send_ref,
            [0.5 * row_sum(acc_ref[0:8]), 0.5 * row_sum(acc_ref[8:16]) / vec_ref[0:1]],
        )
        return

    chunk = 16
    lanes = 512
    for j in range(per):
        side = SIDE - 2 * sides_ref[step * per + j]
        mask = pixel_mask(side, 128)
        h3 = dot_f(comb_ref[pl.ds(j * PIX, PIX)], w3_ref[...])
        for n in range(C_IN // lanes):
            cols = pl.ds(n * lanes, lanes)
            ups = jnp.zeros((8, lanes), F32)
            products = jnp.zeros((8, lanes), F32)
            for c in range(PIX // chunk):
                rows = pl.ds(j * PIX + c * chunk, chunk)
                scaled = (
                    h3[c * chunk : (c + 1) * chunk, n * lanes : (n + 1) * lanes] * vec_ref[0:1, cols]
                )
                pre = scaled + vec_ref[1:2, cols] + x_ref[rows, cols].astype(F32)
                half_pre = pre * 0.5
                a = (1.0 + jnp.tanh(half_pre)) * wide(mask[c * chunk : (c + 1) * chunk], lanes)
                value = half_pre * a
                out_ref[rows, cols] = value.astype(BF16)
                up = cot_ref[rows, cols].astype(F32) * (a * (1.0 + pre - value))
                u3_ref[rows, cols] = (up * vec_ref[2:3, cols]).astype(BF16)
                ups = ups + fold(up)
                products = products + fold(up * scaled)
            acc_ref[0:8, cols] += ups
            acc_ref[8:16, cols] += products


def outer_three_kernel(step, comb_ref, u3_ref, cu_ref):
    if step is BEGIN:
        cu_ref[...] = jnp.zeros_like(cu_ref)
        return

    if step is END:
        return

    cu_ref[...] += dot_rows(comb_ref[...], u3_ref[...])


def back_three_kernel(
    step, per, three_ref, got_ref, hid_ref, comb_ref, u3_ref, a2_ref, slope_ref,
    hat_ref, w3_ref, cu_ref, gw_ref, csum_ref, att_ref, fc_ref, core_ref,
    p_ref, t1_ref, t3_ref, duz_ref, keep_ref, give_ref, fcg_ref, norm_ref, s_ref, c_ref, send_ref, datt_ref, k_ref,
):
    if step is BEGIN:
        mean, inv = three_ref[0:1], three_ref[1:2]
        scale, count = three_ref[2:3], three_ref[3:4]
        sums = total(got_ref)
        dshift = sums[0:1]
        dgain = (sums[1:2] - mean * dshift) * inv
        norm_ref[0:1] = dgain
        norm_ref[1:2] = dshift
        k2 = scale * inv * dgain / count
        k1 = scale * dshift / count - mean * k2
        w3 = w3_ref[...].astype(F32)
        s_ref[...] = dot_last((w3 * k2).astype(BF16), w3_ref[...]).astype(BF16)
        c_ref[...] = high_last(jnp.broadcast_to(k1, (8, C_IN)), w3)
        k_ref[0:1] = k1
        k_ref[1:2] = k2
        return

    if step is END:
        csum = jnp.broadcast_to(csum_ref[...], (8, WIDTH))
        outer = high_rows(csum, jnp.broadcast_to(k_ref[0:1], (8, C_IN))) * 0.125
        w3g = cu_ref[...] - outer - gw_ref[...] * k_ref[1:2]

        def put(core):
            keep_ref[...] = w3g[:, core * 512 : (core + 1) * 512]
            give_ref[...] = w3g[:, (1 - core) * 512 : (2 - core) * 512]

        for core in range(2):
            pl.when(core_ref[0] == core)(functools.partial(put, core))
        att = att_ref[...]
        datt = datt_ref[...]
        both = att * datt
        inner = both[:, :WIDTH] + both[:, WIDTH:]
        dlog = both - att * jnp.concatenate([inner, inner], axis=1)
        zhat, hidden, slope = hid_ref[0], hid_ref[1], hid_ref[2]
        fcg = high_rows(hidden, dlog)
        duz = high_last(dlog, fc_ref[...]) * slope
        duz_ref[...] = duz
        bias = row_sum(dlog)
        rows = [row_sum(duz), row_sum(duz * zhat)]
        for b in range(4):
            cols = slice(b * 128, (b + 1) * 128)
            fcg_ref[pl.ds(b * INTER, INTER)] = fcg[:, cols]
            rows.append(bias[:, cols])
        send_rows(send_ref, rows + [jnp.zeros((2, 128), F32)])
        return

    corr = dot_f(comb_ref[...], s_ref[...])
    p_ref[...] = dot_last(u3_ref[...], w3_ref[...]).astype(BF16)
    for j in range(per):
        image = pl.ds(step * per + j, 1)
        sums = [jnp.zeros((8, WIDTH), F32)] * 6
        for rows, part in chunks(j):
            low = j * PIX + part.start
            dcomb = p_ref[rows].astype(F32) - corr[low : low + CHUNK] - c_ref[0:1]
            for q in range(2):
                cols = slice(q * WIDTH, (q + 1) * WIDTH)
                u = dcomb * slope_ref[rows, cols].astype(F32)
                sums[q] = sums[q] + fold(dcomb * a2_ref[rows, cols].astype(F32))
                sums[2 + q] = sums[2 + q] + fold(u)
                sums[4 + q] = sums[4 + q] + fold(u * hat_ref[rows, cols].astype(F32))
        for k, ref in enumerate((datt_ref, t1_ref, t3_ref)):
            for q in range(2):
                ref[image, q * WIDTH : (q + 1) * WIDTH] = row_sum(sums[2 * k + q])


def back_att_kernel(
    n_images, got_ref, hid_ref, duz_ref, pooled_ref, sides_ref, fc_ref, att_ref,
    t1_ref, t2_ref, t3_ref, t4_ref, fcg_ref, gain_ref,
    dpool_ref, pack_ref, bias_ref, norm_ref, send_ref,
):
    zhat, inv = hid_ref[0], hid_ref[3, 0:1]
    sums = total(got_ref)
    norm_ref[0:1] = sums[1:2]
    norm_ref[1:2] = sums[0:1]
    for b in range(4):
        bias_ref[:, b * 128 : (b + 1) * 128] = sums[2 + b : 3 + b]
    scale = inv * gain_ref[:, 3 * WIDTH : 3 * WIDTH + INTER]
    dzin = scale * (duz_ref[...] - (sums[0:1] + zhat * sums[1:2]) / n_images)
    pack_ref[0:WIDTH] = high_rows(pooled_ref[...], dzin)
    pack_ref[WIDTH:] = fcg_ref[...]
    dpool_ref[...] = high_last(dzin, fc_ref[...])
    for i in range(dpool_ref.shape[0]):
        side = SIDE - 2 * sides_ref[i]
        dpool_ref[i : i + 1] = dpool_ref[i : i + 1] / (side * side).astype(F32)
    dpool = dpool_ref[...]
    both = jnp.concatenate([dpool, dpool], axis=1)
    att = att_ref[...]
    send_rows(
        send_ref,
        [
            row_sum(att * t1_ref[...] + both * t2_ref[...]),
            row_sum(att * t3_ref[...] + both * t4_ref[...]),
        ],
    )


def back_two_kernel(
    step, per, sides_ref, one_ref, two_ref, got_ref, comb_ref, p_ref, s_ref, c_ref, slope_ref, hat2_ref, hat1_ref, att_ref,
    dpool_ref, w_ref, gain_ref, shift_ref, fc_ref, dh2_ref, u1_ref, norm_ref, send_ref,
    vec_ref, pad_ref, acc_ref,
):
    if step is BEGIN:
        count = jnp.concatenate([one_ref[2:3]] * 2, axis=1)
        scale = two_ref[1:2] * gain_ref[:, WIDTH : 3 * WIDTH]
        sums = total(got_ref)
        norm_ref[0:1] = sums[1:2]
        norm_ref[1:2] = sums[0:1]
        vec_ref[0:1] = scale
        vec_ref[1:2] = scale * sums[0:1] / count
        vec_ref[2:3] = scale * sums[1:2] / count
        acc_ref[...] = jnp.zeros_like(acc_ref)
        pad_ref[...] = jnp.zeros_like(pad_ref)
        return

    if step is END:
        rows = []
        for k in range(2):
            both = row_sum(acc_ref[8 * k : 8 * k + 8])
            rows += [both[:, :HALF], both[:, HALF:]]
        sums = jnp.concatenate(rows, axis=0)
        devices, height, _ = send_ref.shape
        for d in range(devices):
            send_ref[d, pl.ds(0, 4)] = sums
            send_ref[d, pl.ds(4, height - 4)] = fc_ref[pl.ds(d * (height - 4), height - 4)]
        return

    first, last = edge_masks(HALF)
    corr = dot_f(comb_ref[...], s_ref[...])
    for j in range(per):
        side = SIDE - 2 * sides_ref[step * per + j]
        mask = pixel_mask(side, 128)
        image = pl.ds(step * per + j, 1)
        dpool = dpool_ref[image]
        for rows, part in chunks(j):
            low = j * PIX + part.start
            dcomb = p_ref[rows].astype(F32) - corr[low : low + CHUNK] - c_ref[0:1]
            for q in range(2):
                cols = slice(q * WIDTH, (q + 1) * WIDTH)
                scale = vec_ref[0:1, cols]
                up = dcomb * (att_ref[image, cols] * scale) + dpool * scale
                dh2 = slope_ref[rows, cols].astype(F32) * up - wide(mask[part], WIDTH) * (
                    vec_ref[1:2, cols] + hat2_ref[rows, cols].astype(F32) * vec_ref[2:3, cols]
                )
                dh2 = dh2.astype(BF16)
                dh2_ref[rows, cols] = dh2
                pad_ref[pl.ds(SIDE + j * (PIX + SIDE) + part.start, CHUNK), cols] = dh2
    height = per * (PIX + SIDE)
    for q in range(2):
        lines = jnp.concatenate(
            [pad_ref[pl.ds(SIDE * (2 - d), height), pl.ds(q * WIDTH, WIDTH)] for d in range(3)],
            axis=1,
        )
        weight = jnp.concatenate(
            [
                jnp.concatenate(
                    [
                        w_ref[pl.ds((3 * r + d) * HALF, HALF), pl.ds(q * WIDTH, WIDTH)]
                        for r in range(3)
                    ],
                    axis=1,
                )
                for d in range(3)
            ],
            axis=0,
        )
        both = dot_last(lines, weight)
        for j in range(per):
            side = SIDE - 2 * sides_ref[step * per + j]
            mask = pixel_mask(side, 128)
            cols = slice(q * HALF, (q + 1) * HALF)
            gain = gain_ref[:, cols] * 0.5
            shift = shift_ref[:, cols] * 0.5
            sums = jnp.zeros((8, HALF), F32)
            products = jnp.zeros((8, HALF), F32)
            for rows, part in chunks(j):
                low = j * (PIX + SIDE) + part.start
                y = both[low : low + CHUNK]
                da1 = (
                    y[:, HALF : 2 * HALF]
                    + pltpu.roll(y[:, :HALF], CHUNK - 1, 0) * last
                    + pltpu.roll(y[:, 2 * HALF :], 1, 0) * first
                )
                hat = hat1_ref[rows, cols].astype(F32)
                half_pre = hat * gain + shift
                a = (1.0 + jnp.tanh(half_pre)) * mask[part]
                u1 = da1 * (a * (0.5 + half_pre - 0.5 * half_pre * a))
                u1_ref[rows, cols] = u1.astype(BF16)
                sums = sums + fold(u1)
                products = products + fold(u1 * hat)
            acc_ref[0:8, cols] += sums
            acc_ref[8:16, cols] += products


def weight_two_kernel(
    step, per, core_ref, sides_ref, hat_ref, dh2_ref, gain_ref, shift_ref, keep_ref, give_ref,
    taps_ref, acc_ref,
):
    if step is BEGIN:
        acc_ref[...] = jnp.zeros_like(acc_ref)
        taps_ref[...] = jnp.zeros_like(taps_ref)
        return

    if step is END:
        def put(core):
            keep_ref[...] = acc_ref[core].T
            give_ref[...] = acc_ref[1 - core].T

        for core in range(2):
            pl.when(core_ref[0] == core)(functools.partial(put, core))
        return

    gain = gain_ref[:, :WIDTH] * 0.5
    shift = shift_ref[:, :WIDTH] * 0.5
    first, last = edge_masks(WIDTH)
    height = PIX + SIDE
    for j in range(per):
        side = SIDE - 2 * sides_ref[step * per + j]
        mask = pixel_mask(side, 128)
        for rows, part in chunks(j):
            half_pre = hat_ref[rows].astype(F32) * gain + shift
            act = half_pre * ((1.0 + jnp.tanh(half_pre)) * wide(mask[part], WIDTH))
            put_taps(taps_ref, j, part, act, first, last)
    for q in range(2):
        patches = jnp.concatenate(
            [
                jnp.concatenate(
                    [
                        taps_ref[pl.ds(SIDE * d + j * height, PIX), pl.ds(q * 384, 384)]
                        for d in range(3)
                    ],
                    axis=1,
                )
                for j in range(per)
            ],
            axis=0,
        )
        acc_ref[q] += dot_rows(dh2_ref[:, q * WIDTH : (q + 1) * WIDTH], patches)


def back_one_kernel(
    step, per, core_ref, sides_ref, one_ref, got_ref, u1_ref, hat_ref, x_ref, gain_ref, norm2_ref,
    norm_att_ref, norm3_ref, dh_ref, keep_ref, give_ref, gain_out_ref, shift_out_ref, vec_ref, acc_ref,
):
    if step is BEGIN:
        count = one_ref[2:3]
        scale = one_ref[1:2] * gain_ref[:, :WIDTH]
        sums = total(got_ref)
        sums = [jnp.concatenate([sums[k : k + 1], sums[k + 1 : k + 2]], axis=1) for k in (0, 2)]
        for row, out_ref in ((0, gain_out_ref), (1, shift_out_ref)):
            out_ref[:, :WIDTH] = sums[1 - row]
            out_ref[:, WIDTH : 3 * WIDTH] = norm2_ref[row : row + 1]
            out_ref[:, 3 * WIDTH : 3 * WIDTH + INTER] = norm_att_ref[row : row + 1]
            out_ref[:, 3 * WIDTH + INTER :] = norm3_ref[row : row + 1]
        vec_ref[0:1] = scale
        vec_ref[1:2] = scale * sums[0] / count
        vec_ref[2:3] = scale * sums[1] / count
        acc_ref[...] = jnp.zeros_like(acc_ref)
        return

    if step is END:

        def put(core):
            keep_ref[...] = acc_ref[core * HALF : (core + 1) * HALF].T
            give_ref[...] = acc_ref[(1 - core) * HALF : (2 - core) * HALF].T

        for core in range(2):
            pl.when(core_ref[0] == core)(functools.partial(put, core))
        return

    for j in range(per):
        side = SIDE - 2 * sides_ref[step * per + j]
        mask = pixel_mask(side, 128)
        for rows, part in chunks(j):
            dh_ref[rows] = (
                u1_ref[rows].astype(F32) * vec_ref[0:1]
                - wide(mask[part], WIDTH) * (vec_ref[1:2] + hat_ref[rows].astype(F32) * vec_ref[2:3])
            ).astype(BF16)
    acc_ref[...] += dot_rows(dh_ref[...], x_ref[...])


def input_grad_kernel(step, dh_ref, u3_ref, three_ref, w_ref, ig_ref, wide_ref):
    if step is BEGIN:
        wide_ref[...] = 1.0 / three_ref[2:3]
        return

    if step is END:
        return

    dx = dot_last(dh_ref[...], w_ref[...])
    for low in range(0, dx.shape[0], 16):
        rows = pl.ds(low, 16)
        ig_ref[rows] = (u3_ref[rows].astype(F32) * wide_ref[...] + dx[low : low + 16]).astype(BF16)


def round_up(value, multiple):
    return -(-value // multiple) * multiple


def two_wide(part, rows):
    missing = 2 * rows - part.shape[0]
    if missing:
        part = jnp.concatenate([part, jnp.zeros((missing, 128), F32)], axis=0)
    return jnp.concatenate([part[:rows], part[rows:]], axis=1)


def slot_rows(two_rows, fc_rows, one_rows, three_rows):
    return (
        round_up(two_rows, 16),
        round_up(fc_rows, 32) // 2,
        round_up(one_rows, 32) // 2,
        round_up(2 * three_rows, 16),
    )


def add_slots(ref, at, rows):
    rows = pl.ds(at, rows)
    both = ref[0, rows].astype(F32)
    for f in range(1, ref.shape[0]):
        both = both + ref[f, rows].astype(F32)
    return both


def lengthen(part, rows):
    if rows == part.shape[0]:
        return part
    return jnp.concatenate([part, jnp.zeros((rows - part.shape[0], part.shape[1]), F32)], axis=0)


def pack_last_kernel(
    fc_rows, keep2_ref, other2_ref, keep1_ref, other1_ref, keep3_ref, other3_ref, got_ref, out_ref
):
    shards = out_ref.shape[0]
    two_rows = keep2_ref.shape[0] // shards
    one_rows = keep1_ref.shape[0] // shards
    three_rows = keep3_ref.shape[0] // shards
    two_slot, fc_slot, one_slot, three_slot = slot_rows(two_rows, fc_rows, one_rows, three_rows)
    fc = two_wide(add_slots(got_ref, 4, fc_rows), fc_slot).astype(BF16)
    for f in range(shards):
        rows = pl.ds(f * two_rows, two_rows)
        part = lengthen(keep2_ref[rows] + other2_ref[rows], two_slot)
        out_ref[f, pl.ds(0, two_slot)] = part.astype(BF16)
        at = two_slot
        out_ref[f, pl.ds(at, fc_slot)] = fc
        at += fc_slot
        rows = pl.ds(f * one_rows, one_rows)
        part = two_wide(keep1_ref[rows] + other1_ref[rows], one_slot)
        out_ref[f, pl.ds(at, one_slot)] = part.astype(BF16)
        at += one_slot
        rows = pl.ds(f * three_rows, three_rows)
        part = keep3_ref[rows] + other3_ref[rows]
        part = jnp.concatenate([part[:, :WIDTH], part[:, WIDTH:]], axis=0)
        out_ref[f, pl.ds(at, three_slot)] = lengthen(part, three_slot).astype(BF16)


def sum_last_kernel(two_rows, fc_rows, one_rows, three_rows, parts_ref, out_ref):
    shards = parts_ref.shape[0]
    two_slot, fc_slot, one_slot, three_slot = slot_rows(two_rows, fc_rows, one_rows, three_rows)
    out_ref[pl.ds(0, two_slot)] = add_slots(parts_ref, 0, two_slot)
    after = two_slot + fc_slot
    out_ref[pl.ds(two_slot, one_slot + three_slot)] = add_slots(
        parts_ref, after, one_slot + three_slot
    )
    at = two_slot + one_slot + three_slot
    for f in range(shards):
        out_ref[pl.ds(at + f * fc_slot, fc_slot)] = parts_ref[f, pl.ds(two_slot, fc_slot)].astype(F32)


def finish_kernel(
    two_rows, fc_rows, one_rows, three_rows, core_ref, mine_ref, other_ref,
    one_ref, two_ref, three_ref, fc1_ref, fc2_ref, pack_ref,
):
    two_slot, fc_slot, one_slot, three_slot = slot_rows(two_rows, fc_rows, one_rows, three_rows)
    at_three = two_slot + one_slot
    at_fc = at_three + three_slot
    shards = (mine_ref.shape[0] - at_fc) // fc_slot

    def tall(ref, at, half_rows, rows):
        both = jnp.concatenate(
            [ref[pl.ds(at, half_rows), :128], ref[pl.ds(at, half_rows), 128:]], axis=0
        )
        return both[:rows]

    def put(half, ref):
        two_ref[:, half * WIDTH : (half + 1) * WIDTH] = ref[pl.ds(0, two_rows)]
        one_ref[:, half * HALF : (half + 1) * HALF] = tall(ref, two_slot, one_slot, one_rows)
        for b in range(2):
            low = (half * 2 + b) * WIDTH
            three_ref[:, low : low + WIDTH] = ref[pl.ds(at_three + b * three_rows, three_rows)]
        for f in range(shards):
            pack_ref[pl.ds((2 * f + half) * fc_rows, fc_rows)] = tall(
                ref, at_fc + f * fc_slot, fc_slot, fc_rows
            )

    for core in range(2):

        @pl.when(core_ref[0] == core)
        def _():
            put(core, mine_ref)
            put(1 - core, other_ref)

    fc1_ref[...] = pack_ref[0:WIDTH]
    for b in range(4):
        fc2_ref[:, b * 128 : (b + 1) * 128] = pack_ref[pl.ds(WIDTH + b * INTER, INTER)]


def everyone(payload):
    return lax.all_to_all(payload, AXES, 0, 0, tiled=True)


def other_core(array):
    return lax.ppermute(array, "dp", [(0, 1), (1, 0)])


def spread_weights(core, weights):
    shards = lax.axis_size("fsdp")
    shapes = [(shards, w.shape[0] * w.shape[1] // 256, 128) for w in weights]
    return call(
        pack_kernel,
        1,
        [(core, SMEM_SPEC)] + [(weight, whole(weight.shape)) for weight in weights],
        [(shape, BF16, whole(shape), True) for shape in shapes],
        flops=1000000,
        moved=4000000,
        name="pack",
    )


def join_weight(core, mine, shape):
    other = other_core(mine)
    rows = shape[0] // mine.shape[0]
    return call(
        unpack_kernel,
        1,
        [(core, SMEM_SPEC), (mine, whole(mine.shape), True), (other, whole(mine.shape), True)],
        [(shape, BF16, whole(shape))],
        [] if rows % 16 == 0 else [pltpu.VMEM(shape, F32)],
        flops=1000000,
        moved=4000000,
        name="unpack",
    )[0]


def slots(parts):
    return lax.all_to_all(parts, "fsdp", 0, 0, tiled=True)


def body(
    inputs,
    sides,
    weight_one,
    weight_two,
    weight_three,
    fc_first,
    fc_second,
    fc_bias,
    bn_gain,
    bn_shift,
    cotangent,
):
    images = inputs.shape[0]
    rows = images * PIX
    devices = lax.axis_size("fsdp") * lax.axis_size("dp")
    n_images = float(images * devices)
    x = inputs.reshape(rows, C_IN)
    cot = cotangent.reshape(rows, C_IN)
    gain = bn_gain.reshape(1, -1)
    shift = bn_shift.reshape(1, -1)
    bias = fc_bias.reshape(1, -1)
    n_ch = gain.shape[1]
    core = lax.axis_index("dp").astype(jnp.int32).reshape(1)

    def split(most):
        per = max(n for n in range(1, most + 1) if images % n == 0)
        return per, images // per

    core_in = (core, SMEM_SPEC)
    sides_in = (sides, SMEM_SPEC)
    gain_in = (gain, whole((1, n_ch)))
    shift_in = (shift, whole((1, n_ch)))

    def payload(k, n):
        return ((devices, k, n), F32, whole((devices, k, n)), True)

    def small(*shape):
        return (shape, F32, whole(shape))

    def full(array):
        return (array, whole(array.shape))

    def near(array):
        return (array, whole(array.shape), True)

    def blocks(array):
        return (array, Stream())

    def blocks_out(width, dtype=BF16, over=None):
        return ((rows, width), dtype, Stream(over))

    spread_one, spread_two, spread_three = spread_weights(
        core, (weight_one, weight_two, weight_three)
    )
    mine = slots(spread_one)
    other = other_core(mine)
    spread_two, mine, other = lax.optimization_barrier((spread_two, mine, other))
    mine_two = slots(spread_two)

    per, steps = split(PER_CONV_ONE)
    h1, full_one, send = stream_call(
        lambda step, *refs, per=per: conv_one_kernel(step, per, *refs),
        per,
        steps,
        [core_in, sides_in, blocks(x), near(mine), near(other)],
        [blocks_out(WIDTH, F32), ((C_IN, WIDTH), BF16, whole((C_IN, WIDTH))), payload(4, WIDTH)],
        [pltpu.VMEM((16, WIDTH), F32), pltpu.SMEM((1,), F32)],
        flops=2 * rows * C_IN * WIDTH,
        moved=rows * C_IN * 2 + rows * WIDTH * 4,
        name="conv_one",
    )
    send, mine_two = lax.optimization_barrier((send, mine_two))
    got_one = everyone(send)
    full_two = join_weight(core, mine_two, (9 * HALF, 2 * WIDTH))
    got_one, spread_three, full_two = lax.optimization_barrier((got_one, spread_three, full_two))
    mine_three = slots(spread_three)

    per, steps = split(PER_CONV_TWO)
    hat1, h2, stat1, send = stream_call(
        lambda step, *refs, per=per: conv_two_kernel(step, per, *refs),
        per,
        steps,
        [sides_in, near(got_one), blocks(h1), full(full_two), gain_in, shift_in],
        [blocks_out(WIDTH), blocks_out(2 * WIDTH, F32), small(8, WIDTH), payload(2, 2 * WIDTH)],
        [
            pltpu.VMEM((per * (PIX + SIDE) + 2 * SIDE, 6 * HALF), BF16),
            pltpu.VMEM((16, 2 * WIDTH), F32),
        ],
        flops=2 * rows * 9 * HALF * 2 * WIDTH,
        moved=rows * WIDTH * 14,
        name="conv_two",
    )
    send, mine_three = lax.optimization_barrier((send, mine_three))
    got_two = everyone(send)

    per, steps = split(PER_ACT_TWO)
    hat2, a2, slope2, pooled, zin, t2, t4, stat2, send = stream_call(
        lambda step, *refs, per=per: act_two_kernel(step, per, *refs),
        per,
        steps,
        [
            sides_in,
            full(stat1),
            near(got_two),
            blocks(h2),
            gain_in,
            shift_in,
            full(fc_first),
        ],
        [
            blocks_out(2 * WIDTH),
            blocks_out(2 * WIDTH),
            blocks_out(2 * WIDTH),
            small(images, WIDTH),
            small(images, INTER),
            small(images, 2 * WIDTH),
            small(images, 2 * WIDTH),
            small(8, 2 * WIDTH),
            payload(2, INTER),
        ],
        flops=rows * 2 * WIDTH * 20,
        moved=rows * 2 * WIDTH * 10,
        name="act_two",
    )
    send, mine_three = lax.optimization_barrier((send, mine_three))
    got_att = everyone(send)
    full_three = join_weight(core, mine_three, (WIDTH, C_IN))

    per, steps = split(PER_COMBINE)
    att, comb, gw, csum, hid, send = stream_call(
        lambda step, *refs, per=per: combine_kernel(step, per, n_images, *refs),
        per,
        steps,
        [
            near(got_att),
            full(zin),
            blocks(a2),
            full(full_three),
            full(fc_second),
            full(bias),
            gain_in,
            shift_in,
        ],
        [
            small(images, 2 * WIDTH),
            blocks_out(WIDTH),
            small(WIDTH, C_IN),
            small(1, WIDTH),
            small(4, images, INTER),
            payload(2, C_IN),
        ],
        [pltpu.VMEM((WIDTH, WIDTH), F32), pltpu.VMEM((8, WIDTH), F32)],
        flops=2 * rows * WIDTH * WIDTH,
        moved=rows * WIDTH * 6,
        name="combine",
    )
    got_three = everyone(send)

    per, steps = split(PER_OUTPUT)
    outputs, u3, stat3, send = stream_call(
        lambda step, *refs, per=per: output_kernel(step, per, *refs),
        per,
        steps,
        [
            sides_in,
            full(stat1),
            near(got_three),
            blocks(comb),
            blocks(x),
            blocks(cot),
            full(full_three),
            gain_in,
            shift_in,
        ],
        [
            blocks_out(C_IN, over=4),
            blocks_out(C_IN, over=5),
            small(8, C_IN),
            payload(2, C_IN),
        ],
        [pltpu.VMEM((8, C_IN), F32), pltpu.VMEM((16, C_IN), F32)],
        flops=2 * rows * WIDTH * C_IN,
        moved=rows * C_IN * 8,
        name="output",
    )
    got_back_three = everyone(send)

    per, steps = split(PER_OUTER_THREE)
    (cu,) = stream_call(
        outer_three_kernel,
        per,
        steps,
        [blocks(comb), blocks(u3)],
        [small(WIDTH, C_IN)],
        flops=2 * rows * WIDTH * C_IN,
        moved=rows * C_IN * 3,
        name="outer_three",
    )

    per, steps = split(PER_BACK_THREE)
    p, t1, t3, duz, keep_three, give_three, fc2_local, norm3, corr_weight, corr_row, send = stream_call(
        lambda step, *refs, per=per: back_three_kernel(step, per, *refs),
        per,
        steps,
        [
            full(stat3),
            near(got_back_three),
            full(hid),
            blocks(comb),
            blocks(u3),
            blocks(a2),
            blocks(slope2),
            blocks(hat2),
            full(full_three),
            full(cu),
            full(gw),
            full(csum),
            full(att),
            full(fc_second),
            core_in,
        ],
        [
            blocks_out(WIDTH, over=3),
            small(images, 2 * WIDTH),
            small(images, 2 * WIDTH),
            small(images, INTER),
            small(WIDTH, C_IN // 2),
            small(WIDTH, C_IN // 2),
            small(4 * INTER, 128),
            small(2, C_IN),
            ((WIDTH, WIDTH), BF16, whole((WIDTH, WIDTH))),
            small(8, WIDTH),
            payload(8, INTER),
        ],
        [pltpu.VMEM((images, 2 * WIDTH), F32), pltpu.VMEM((2, C_IN), F32)],
        flops=4 * rows * WIDTH * C_IN,
        moved=rows * WIDTH * 16,
        name="back_three",
    )
    got_back_att = everyone(send)

    dpool, packed, fc_bias_grad, norm_att, send = call(
        functools.partial(back_att_kernel, n_images),
        1,
        [
            near(got_back_att),
            full(hid),
            full(duz),
            full(pooled),
            sides_in,
            full(fc_first),
            full(att),
            full(t1),
            full(t2),
            full(t3),
            full(t4),
            full(fc2_local),
            gain_in,
        ],
        [
            small(images, WIDTH),
            small(WIDTH + 4 * INTER, 128),
            small(1, 2 * WIDTH),
            small(2, INTER),
            payload(2, 2 * WIDTH),
        ],
        flops=10000000,
        moved=1000000,
        name="back_att",
    )
    got_back_two = everyone(send)
    shards = lax.axis_size("fsdp")
    w3_rows = WIDTH // shards
    fc_rows = packed.shape[0] // devices

    per, steps = split(PER_BACK_TWO)
    dh2, u1, norm2, send = stream_call(
        lambda step, *refs, per=per: back_two_kernel(step, per, *refs),
        per,
        steps,
        [
            sides_in,
            full(stat1),
            full(stat2),
            near(got_back_two),
            blocks(comb),
            blocks(p),
            full(corr_weight),
            full(corr_row),
            blocks(slope2),
            blocks(hat2),
            blocks(hat1),
            full(att),
            full(dpool),
            full(full_two),
            gain_in,
            shift_in,
            full(packed),
        ],
        [
            blocks_out(2 * WIDTH),
            blocks_out(WIDTH),
            small(2, 2 * WIDTH),
            payload(4 + fc_rows, 128),
        ],
        [
            pltpu.VMEM((8, 2 * WIDTH), F32),
            pltpu.VMEM((per * (PIX + SIDE) + 2 * SIDE, 2 * WIDTH), BF16),
            pltpu.VMEM((16, WIDTH), F32),
        ],
        flops=2 * rows * 9 * HALF * 2 * WIDTH,
        moved=rows * WIDTH * 20,
        name="back_two",
    )
    got_back_one = everyone(send)

    per, steps = split(PER_WEIGHT_TWO)
    half = (9 * HALF, WIDTH)
    keep, give = stream_call(
        lambda step, *refs, per=per: weight_two_kernel(step, per, *refs),
        per,
        steps,
        [core_in, sides_in, blocks(hat1), blocks(dh2), gain_in, shift_in],
        [(half, F32, whole(half)), (half, F32, whole(half))],
        [
            pltpu.VMEM((per * (PIX + SIDE) + 2 * SIDE, 6 * HALF), BF16),
            pltpu.VMEM((2, WIDTH, 9 * HALF), F32),
        ],
        flops=2 * rows * 9 * HALF * 2 * WIDTH,
        moved=rows * WIDTH * 6,
        name="weight_two",
    )
    got_back_one, keep, give = lax.optimization_barrier((got_back_one, keep, give))
    per, steps = split(PER_BACK_ONE)
    half_one = (C_IN, HALF)
    dh1, keep_one, give_one, gain_grad, shift_grad = stream_call(
        lambda step, *refs, per=per: back_one_kernel(step, per, *refs),
        per,
        steps,
        [
            core_in,
            sides_in,
            full(stat1),
            near(got_back_one),
            blocks(u1),
            blocks(hat1),
            blocks(x),
            gain_in,
            full(norm2),
            full(norm_att),
            full(norm3),
        ],
        [
            blocks_out(WIDTH),
            small(*half_one),
            small(*half_one),
            small(1, n_ch),
            small(1, n_ch),
        ],
        [pltpu.VMEM((8, WIDTH), F32), pltpu.VMEM((WIDTH, C_IN), F32)],
        flops=2 * rows * WIDTH * C_IN,
        moved=rows * C_IN * 4,
        name="back_one",
    )

    two_rows, one_rows = 9 * HALF // shards, C_IN // shards
    two_slot, fc_slot, one_slot, three_slot = slot_rows(two_rows, fc_rows, one_rows, w3_rows)
    slot = (shards, two_slot + fc_slot + one_slot + three_slot, WIDTH)
    (parts,) = call(
        functools.partial(pack_last_kernel, fc_rows),
        1,
        [
            full(keep),
            near(other_core(give)),
            full(keep_one),
            near(other_core(give_one)),
            full(keep_three),
            near(other_core(give_three)),
            near(got_back_one),
        ],
        [(slot, BF16, whole(slot))],
        flops=1000000,
        moved=5000000,
        name="pack_last",
    )
    dh1, parts = lax.optimization_barrier((dh1, parts))
    parts = slots(parts)

    per, steps = split(PER_INPUT_GRAD)
    (input_grad,) = stream_call(
        input_grad_kernel,
        per,
        steps,
        [blocks(dh1), blocks(u3), full(stat3), full(full_one)],
        [blocks_out(C_IN, over=1)],
        [pltpu.VMEM((1, C_IN), F32)],
        flops=2 * rows * WIDTH * C_IN,
        moved=rows * C_IN * 5,
        name="input_grad",
    )

    parts, input_grad = lax.optimization_barrier((parts, input_grad))
    sums = (two_slot + one_slot + three_slot + shards * fc_slot, WIDTH)
    (mine,) = call(
        functools.partial(sum_last_kernel, two_rows, fc_rows, one_rows, w3_rows),
        1,
        [near(parts)],
        [(sums, F32, whole(sums), True)],
        flops=1000000,
        moved=2000000,
        name="sum_last",
    )
    (weight_one_grad, weight_two_grad, weight_three_grad, fc_first_grad, fc_second_grad) = call(
        functools.partial(finish_kernel, two_rows, fc_rows, one_rows, w3_rows),
        1,
        [core_in, near(mine), near(other_core(mine))],
        [
            small(one_rows, WIDTH),
            small(two_rows, 2 * WIDTH),
            small(w3_rows, C_IN),
            small(WIDTH, INTER),
            small(INTER, 2 * WIDTH),
        ],
        [pltpu.VMEM((2 * shards * fc_rows, 128), F32)],
        flops=1000000,
        moved=2000000,
        name="finish",
    )
    return (
        outputs.reshape(inputs.shape),
        input_grad.reshape(inputs.shape),
        weight_one_grad,
        weight_two_grad,
        weight_three_grad,
        fc_first_grad,
        fc_second_grad,
        fc_bias_grad.reshape(-1),
        gain_grad.reshape(-1),
        shift_grad.reshape(-1),
    )


def solution(mesh):
    return jax.shard_map(
        body,
        mesh=mesh,
        in_specs=(
            P(("fsdp", "dp"), None, None),
            P(("fsdp", "dp")),
            P("fsdp", None),
            P("fsdp", None),
            P("fsdp", None),
            P(),
            P(),
            P(),
            P(),
            P(),
            P(("fsdp", "dp"), None, None),
        ),
        out_specs=(
            P(("fsdp", "dp"), None, None),
            P(("fsdp", "dp"), None, None),
            P("fsdp", None),
            P("fsdp", None),
            P("fsdp", None),
            P(),
            P(),
            P(),
            P(),
            P(),
        ),
        check_vma=False,
    )
```

```python
import functools

import jax
import jax.numpy as jnp
from jax import lax
from jax.experimental import pallas as pl
from jax.experimental.pallas import tpu as pltpu
from jax.sharding import PartitionSpec as P

C_IN = 1024
WIDTH = 256
INTER = 128
SIDE = 16
PIX = SIDE * SIDE
HALF = WIDTH // 2
EPS = 1e-05
AXES = ("fsdp", "dp")
HIGH = lax.Precision.HIGHEST
F32 = jnp.float32
BF16 = jnp.bfloat16
MIB = 1024 * 1024

AHEAD = 4
VMEM = 44
CHUNK = 32
PER_CONV_ONE = 3
PER_CONV_TWO = 3
PER_ACT_TWO = 4
PER_COMBINE = 6
PER_OUTPUT = 2
PER_OUTER_THREE = 4
PER_BACK_THREE = 3
PER_BACK_TWO = 2
PER_WEIGHT_TWO = 4
PER_BACK_ONE = 3
PER_INPUT_GRAD = 3


def dot_f(left, right):
    return jnp.dot(left, right, preferred_element_type=F32)


def dot_rows(left, right):
    return lax.dot_general(left, right, (((0,), (0,)), ((), ())), preferred_element_type=F32)


def dot_last(left, right):
    return lax.dot_general(left, right, (((1,), (1,)), ((), ())), preferred_element_type=F32)


def high_f(left, right):
    return jnp.dot(left, right, preferred_element_type=F32, precision=HIGH)


def high_rows(left, right):
    return lax.dot_general(
        left, right, (((0,), (0,)), ((), ())), preferred_element_type=F32, precision=HIGH
    )


def high_last(left, right):
    return lax.dot_general(
        left, right, (((1,), (1,)), ((), ())), preferred_element_type=F32, precision=HIGH
    )


def exact_f(left, right):
    total_product = None
    for _ in range(3):
        piece = left.astype(BF16)
        product = dot_f(piece, right)
        total_product = product if total_product is None else total_product + product
        left = left - piece.astype(F32)
    return total_product


def pixel_mask(image_side, width):
    row = lax.broadcasted_iota(jnp.int32, (PIX, 128), 0)
    inside = ((row >> 4) < image_side) & ((row & 15) < image_side)
    return wide(jnp.where(inside, 1.0, 0.0).astype(F32), width)


def wide(mask, width):
    if width == 128:
        return mask
    return jnp.concatenate([mask] * (width // 128), axis=1)


def fold(values):
    rows, n = values.shape
    return jnp.sum(values.reshape(rows // 8, 8, n), axis=0)


def chunks(j=0):
    for low in range(0, PIX, CHUNK):
        yield pl.ds(j * PIX + low, CHUNK), slice(low, low + CHUNK)


def row_sum(values):
    return jnp.sum(values, axis=0, keepdims=True)


def total(payload_ref):
    return jnp.sum(payload_ref[...], axis=0)


def norm_terms(sums, count):
    mean = sums[0:1] / count
    variance = sums[1:2] / count - mean * mean
    return mean, lax.rsqrt(variance + EPS)


def send_rows(payload_ref, rows):
    block = jnp.concatenate(rows, axis=0)
    payload_ref[...] = jnp.broadcast_to(block[None], payload_ref.shape)


def silu_parts(half_pre):
    t = jnp.tanh(half_pre)
    a = 1.0 + t
    value = half_pre * a
    slope = 0.5 * a * (1.0 + half_pre * (1.0 - t))
    return value, slope


def whole(shape):
    zeros = (0,) * len(shape)
    return pl.BlockSpec(shape, lambda *_: zeros)


SMEM_SPEC = pl.BlockSpec(memory_space=pltpu.SMEM)


def call(kernel, grid, ins, outs, scratch=(), vmem=VMEM, flops=0, moved=0, name=None):
    arrays = [
        array
        if near
        else pltpu.with_memory_space_constraint(array, pltpu.HBM)
        for array, spec, *near in ins
    ]
    shapes = [
        jax.ShapeDtypeStruct(shape, dtype) if near else pltpu.HBM(shape, dtype)
        for shape, dtype, _, *near in outs
    ]
    return pl.pallas_call(
        kernel,
        grid=(grid,),
        in_specs=[spec for _, spec, *_ in ins],
        out_specs=[spec for _, _, spec, *_ in outs],
        out_shape=shapes,
        scratch_shapes=list(scratch),
        compiler_params=pltpu.CompilerParams(
            dimension_semantics=("arbitrary",), vmem_limit_bytes=vmem * MIB
        ),
        cost_estimate=pl.CostEstimate(flops=flops, bytes_accessed=moved, transcendentals=0),
        name=name,
    )(*arrays)


class Stream:
    def __init__(self, over=None):
        self.over = over


BEGIN, END = "begin", "end"


def stream_call(kernel, per, steps, ins, outs, scratch=(), vmem=VMEM, flops=0, moved=0, name=None):
    block = per * PIX
    in_specs, out_specs, arrays, shapes, rooms = [], [], [], [], []
    in_streams, out_streams, room_of = [], [], {}
    for at, (array, spec, *near) in enumerate(ins):
        if isinstance(spec, Stream):
            in_streams.append(at)
            room_of[at] = len(rooms)
            rooms.append(pltpu.VMEM(array.shape, array.dtype))
            spec = pl.BlockSpec(memory_space=pltpu.HBM)
        elif near:
            arrays.append(array)
            in_specs.append(spec)
            continue
        in_specs.append(spec)
        arrays.append(
            pltpu.with_memory_space_constraint(array, pltpu.HBM)
        )
    for at, (shape, dtype, spec, *near) in enumerate(outs):
        shapes.append(jax.ShapeDtypeStruct(shape, dtype) if near else pltpu.HBM(shape, dtype))
        if isinstance(spec, Stream):
            out_streams.append(at)
            if spec.over is None:
                room_of[len(ins) + at] = len(rooms)
                rooms.append(pltpu.VMEM(shape, dtype))
            else:
                room_of[len(ins) + at] = room_of[spec.over]
            spec = pl.BlockSpec(memory_space=pltpu.HBM)
        out_specs.append(spec)
    n_in, n_out, n_rooms = len(ins), len(outs), len(rooms)

    def whole_kernel(*refs):
        in_refs, out_refs = refs[:n_in], refs[n_in : n_in + n_out]
        room_refs = refs[n_in + n_out : n_in + n_out + n_rooms]
        own_refs = refs[n_in + n_out + n_rooms : -2]
        in_sems, out_sems = refs[-2:]

        def rows(step):
            return pl.ds(pl.multiple_of(step * block, block), block)

        def copies_in(step):
            return [
                pltpu.make_async_copy(
                    in_refs[at].at[rows(step)],
                    room_refs[room_of[at]].at[rows(step)],
                    in_sems.at[k, step],
                )
                for k, at in enumerate(in_streams)
            ]

        def copies_out(step):
            return [
                pltpu.make_async_copy(
                    room_refs[room_of[n_in + at]].at[rows(step)],
                    out_refs[at].at[rows(step)],
                    out_sems.at[k, step],
                )
                for k, at in enumerate(out_streams)
            ]

        def views(step):
            both = []
            for at, ref in enumerate(in_refs + out_refs):
                if at in room_of:
                    ref = room_refs[room_of[at]].at[rows(step)]
                both.append(ref)
            return both + list(own_refs)

        ahead = min(AHEAD, steps)
        for step in range(ahead):
            for copy in copies_in(step):
                copy.start()
        kernel(BEGIN, *views(0))

        def one(step, carry):
            for copy in copies_in(step):
                copy.wait()

            @pl.when(step + ahead < steps)
            def _():
                for copy in copies_in(step + ahead):
                    copy.start()

            kernel(step, *views(step))
            for copy in copies_out(step):
                copy.start()
            return carry

        lax.fori_loop(0, steps, one, 0)
        kernel(END, *views(0))

        def last(step, carry):
            for copy in copies_out(step):
                copy.wait()
            return carry

        lax.fori_loop(0, steps, last, 0)

    return pl.pallas_call(
        whole_kernel,
        in_specs=in_specs,
        out_specs=out_specs,
        out_shape=shapes,
        scratch_shapes=rooms
        + list(scratch)
        + [
            pltpu.SemaphoreType.DMA((max(len(in_streams), 1), steps)),
            pltpu.SemaphoreType.DMA((max(len(out_streams), 1), steps)),
        ],
        compiler_params=pltpu.CompilerParams(vmem_limit_bytes=vmem * MIB),
        cost_estimate=pl.CostEstimate(flops=flops, bytes_accessed=moved, transcendentals=0),
        name=name,
    )(*arrays)


def pack_kernel(core_ref, *refs):
    count = len(refs) // 2

    def put(half):
        for ref, out_ref in zip(refs[:count], refs[count:]):
            rows, cols = ref.shape
            for b in range(cols // 256):
                low = half * (cols // 2) + b * 128
                piece = ref[:, low : low + 128]
                for f in range(out_ref.shape[0]):
                    out_ref[f, pl.ds(b * rows, rows)] = piece

    for core in range(2):
        pl.when(core_ref[0] == core)(functools.partial(put, core))


def unpack_kernel(core_ref, mine_ref, other_ref, out_ref, *wide_refs):
    shards = mine_ref.shape[0]
    rows, cols = out_ref.shape[0] // shards, out_ref.shape[1]

    def put(half, source_ref):
        for f in range(shards):
            for b in range(cols // 256):
                piece = source_ref[f, pl.ds(b * rows, rows)]
                at = (pl.ds(f * rows, rows), pl.ds(half * (cols // 2) + b * 128, 128))
                if wide_refs:
                    wide_refs[0][at] = piece.astype(F32)
                else:
                    out_ref[at] = piece

    for core in range(2):

        @pl.when(core_ref[0] == core)
        def _():
            put(core, mine_ref)
            put(1 - core, other_ref)

    if wide_refs:
        out_ref[...] = wide_refs[0][...].astype(BF16)


def conv_one_kernel(
    step, per, core_ref, sides_ref, x_ref, mine_ref, other_ref, h_ref, w_out_ref, send_ref,
    acc_ref, count_ref,
):
    if step is BEGIN:
        acc_ref[...] = jnp.zeros_like(acc_ref)
        count_ref[0] = 0.0

        def put(core):
            for half, ref in ((core, mine_ref), (1 - core, other_ref)):
                w_out_ref[:, half * HALF : (half + 1) * HALF] = ref[...].reshape(C_IN, HALF)

        for core in range(2):
            pl.when(core_ref[0] == core)(functools.partial(put, core))
        return

    if step is END:
        count = jnp.full((1, WIDTH), count_ref[0], F32)
        send_rows(
            send_ref,
            [row_sum(acc_ref[0:8]), row_sum(acc_ref[8:16]), count, jnp.zeros((1, WIDTH), F32)],
        )
        return

    h = dot_f(x_ref[...], w_out_ref[...])
    h_ref[...] = h
    for j in range(per):
        side = SIDE - 2 * sides_ref[step * per + j]
        mask = pixel_mask(side, 128)
        sums = jnp.zeros((8, WIDTH), F32)
        squares = jnp.zeros((8, WIDTH), F32)
        for rows, part in chunks():
            one = h[j * PIX + part.start : j * PIX + part.stop]
            kept = one * wide(mask[part], WIDTH)
            sums = sums + fold(kept)
            squares = squares + fold(kept * one)
        acc_ref[0:8] += sums
        acc_ref[8:16] += squares
        count_ref[0] += (side * side).astype(F32)


def edge_masks(width):
    column = lax.broadcasted_iota(jnp.int32, (CHUNK, 128), 0) & 15
    first = jnp.where(column == 0, 0.0, 1.0).astype(F32)
    last = jnp.where(column == 15, 0.0, 1.0).astype(F32)
    return wide(first, width), wide(last, width)


def put_taps(taps_ref, j, part, act, first, last):
    shifted = (pltpu.roll(act, 1, 0) * first, act, pltpu.roll(act, CHUNK - 1, 0) * last)
    low = SIDE + j * (PIX + SIDE) + part.start
    for d in range(3):
        piece = shifted[d].astype(BF16)
        for q in range(2):
            taps_ref[pl.ds(low, CHUNK), pl.ds(q * 384 + d * 128, 128)] = piece[
                :, q * HALF : (q + 1) * HALF
            ]


def conv_two_kernel(
    step, per, sides_ref, got_ref, h_ref, w_ref, gain_ref, shift_ref, hat_ref, h2_ref, vec_ref, send_ref,
    taps_ref, acc_ref,
):
    if step is BEGIN:
        sums = total(got_ref)
        mean, inv = norm_terms(sums, sums[2:3])
        vec_ref[0:1] = mean
        vec_ref[1:2] = inv
        vec_ref[2:3] = sums[2:3]
        acc_ref[...] = jnp.zeros_like(acc_ref)
        taps_ref[...] = jnp.zeros_like(taps_ref)
        return

    if step is END:
        send_rows(send_ref, [row_sum(acc_ref[0:8]), row_sum(acc_ref[8:16])])
        return

    gain = gain_ref[:, :WIDTH] * 0.5
    shift = shift_ref[:, :WIDTH] * 0.5
    first, last = edge_masks(WIDTH)
    for j in range(per):
        side = SIDE - 2 * sides_ref[step * per + j]
        mask = pixel_mask(side, 128)
        for rows, part in chunks(j):
            hat = (h_ref[rows] - vec_ref[0:1]) * vec_ref[1:2]
            hat_ref[rows] = hat.astype(BF16)
            half_pre = hat * gain + shift
            act = half_pre * ((1.0 + jnp.tanh(half_pre)) * wide(mask[part], WIDTH))
            put_taps(taps_ref, j, part, act, first, last)
    height = per * (PIX + SIDE)
    for q in range(2):
        cols = pl.ds(q * WIDTH, WIDTH)
        patches = jnp.concatenate(
            [taps_ref[pl.ds(SIDE * d, height), pl.ds(q * 384, 384)] for d in range(3)], axis=1
        )
        both = dot_f(patches, w_ref[:, cols])
        for j in range(per):
            side = SIDE - 2 * sides_ref[step * per + j]
            mask = pixel_mask(side, 128)
            sums = jnp.zeros((8, WIDTH), F32)
            squares = jnp.zeros((8, WIDTH), F32)
            for rows, part in chunks(j):
                low = j * (PIX + SIDE) + part.start
                h2 = both[low : low + CHUNK]
                h2_ref[rows, cols] = h2
                kept = h2 * wide(mask[part], WIDTH)
                sums = sums + fold(kept)
                squares = squares + fold(kept * h2)
            acc_ref[0:8, cols] += sums
            acc_ref[8:16, cols] += squares


def act_two_kernel(
    step, per, sides_ref, one_ref, got_ref, h2_ref, gain_ref, shift_ref, fc_ref,
    hat_ref, a2_ref, slope_ref, pooled_ref, zin_ref, t2_ref, t4_ref, vec_ref, send_ref,
):
    if step is BEGIN:
        sums = total(got_ref)
        mean, inv = norm_terms(sums, jnp.concatenate([one_ref[2:3]] * 2, axis=1))
        vec_ref[0:1] = mean
        vec_ref[1:2] = inv
        return

    if step is END:
        z = high_f(pooled_ref[...], fc_ref[...])
        zin_ref[...] = z
        send_rows(send_ref, [row_sum(z), row_sum(z * z)])
        return

    gain = gain_ref[:, WIDTH : 3 * WIDTH] * 0.5
    shift = shift_ref[:, WIDTH : 3 * WIDTH] * 0.5
    for j in range(per):
        side = SIDE - 2 * sides_ref[step * per + j]
        mask = pixel_mask(side, 128)
        image = pl.ds(step * per + j, 1)
        values = jnp.zeros((8, WIDTH), F32)
        for q in range(2):
            cols = slice(q * WIDTH, (q + 1) * WIDTH)
            sums = jnp.zeros((8, WIDTH), F32)
            products = jnp.zeros((8, WIDTH), F32)
            for rows, part in chunks(j):
                hat = (h2_ref[rows, cols] - vec_ref[0:1, cols]) * vec_ref[1:2, cols]
                hat_ref[rows, cols] = hat.astype(BF16)
                half_pre = hat * gain[:, cols] + shift[:, cols]
                a = (1.0 + jnp.tanh(half_pre)) * wide(mask[part], WIDTH)
                value = half_pre * a
                slope = a * (0.5 + half_pre - 0.5 * value)
                a2_ref[rows, cols] = value.astype(BF16)
                slope_ref[rows, cols] = slope.astype(BF16)
                values = values + fold(value)
                sums = sums + fold(slope)
                products = products + fold(slope * hat)
            t2_ref[image, cols] = row_sum(sums)
            t4_ref[image, cols] = row_sum(products)
        pooled_ref[image] = row_sum(values) / (side * side).astype(F32)


def hidden_terms(zin, sums, n_images, gain_ref, shift_ref):
    mean, inv = norm_terms(sums, n_images)
    zhat = (zin - mean) * inv
    cols = slice(3 * WIDTH, 3 * WIDTH + INTER)
    half_z = (zhat * gain_ref[:, cols] + shift_ref[:, cols]) * 0.5
    value, slope = silu_parts(half_z)
    return zhat, inv, value, slope


def combine_kernel(
    step, per, n_images, got_ref, zin_ref, a2_ref, w3_ref, fc_ref, bias_ref, gain_ref, shift_ref,
    att_ref, comb_ref, gw_ref, csum_ref, hid_ref, send_ref, gram_ref, acc_ref,
):
    if step is BEGIN:
        zhat, inv, hidden, slope = hidden_terms(
            zin_ref[...], total(got_ref), n_images, gain_ref, shift_ref
        )
        hid_ref[0] = zhat
        hid_ref[1] = hidden
        hid_ref[2] = slope
        hid_ref[3] = jnp.broadcast_to(inv, slope.shape)
        logits = high_f(hidden, fc_ref[...]) + bias_ref[...]
        left, right = logits[:, :WIDTH], logits[:, WIDTH:]
        top = jnp.maximum(left, right)
        left, right = jnp.exp(left - top), jnp.exp(right - top)
        both = left + right
        att_ref[:, :WIDTH] = left / both
        att_ref[:, WIDTH:] = right / both
        gram_ref[...] = jnp.zeros_like(gram_ref)
        acc_ref[...] = jnp.zeros_like(acc_ref)
        return

    if step is END:
        csum = row_sum(acc_ref[...])
        csum_ref[...] = csum
        both = jnp.concatenate([gram_ref[...], jnp.broadcast_to(csum, (8, WIDTH))], axis=0)
        both = exact_f(both, w3_ref[...])
        gw = both[:WIDTH]
        gw_ref[...] = gw
        send_rows(send_ref, [both[WIDTH : WIDTH + 1], row_sum(w3_ref[...].astype(F32) * gw)])
        return

    for j in range(per):
        att = att_ref[pl.ds(step * per + j, 1)]
        sums = jnp.zeros((8, WIDTH), F32)
        for rows, _ in chunks(j):
            left = att[:, :WIDTH] * a2_ref[rows, :WIDTH].astype(F32)
            comb = (left + att[:, WIDTH:] * a2_ref[rows, WIDTH:].astype(F32)).astype(BF16)
            comb_ref[rows] = comb
            sums = sums + fold(comb.astype(F32))
        acc_ref[...] += sums
    comb = comb_ref[...]
    gram_ref[...] += dot_rows(comb, comb)


def output_kernel(
    step, per, sides_ref, one_ref, got_ref, comb_ref, x_ref, cot_ref, w3_ref, gain_ref, shift_ref,
    out_ref, u3_ref, stat_ref, send_ref, vec_ref, acc_ref,
):
    if step is BEGIN:
        count = jnp.concatenate([one_ref[2:3]] * 4, axis=1)
        mean, inv = norm_terms(total(got_ref), count)
        scale = inv * gain_ref[:, 3 * WIDTH + INTER :]
        stat_ref[0:1] = mean
        stat_ref[1:2] = inv
        stat_ref[2:3] = scale
        stat_ref[3:4] = count
        vec_ref[0:1] = scale
        vec_ref[1:2] = shift_ref[:, 3 * WIDTH + INTER :] - mean * scale
        vec_ref[2:3] = 0.5 * scale
        acc_ref[...] = jnp.zeros_like(acc_ref)
        return

    if step is END:
        send_rows(
            send_ref,
            [0.5 * row_sum(acc_ref[0:8]), 0.5 * row_sum(acc_ref[8:16]) / vec_ref[0:1]],
        )
        return

    chunk = 16
    lanes = 512
    for j in range(per):
        side = SIDE - 2 * sides_ref[step * per + j]
        mask = pixel_mask(side, 128)
        h3 = dot_f(comb_ref[pl.ds(j * PIX, PIX)], w3_ref[...])
        for n in range(C_IN // lanes):
            cols = pl.ds(n * lanes, lanes)
            ups = jnp.zeros((8, lanes), F32)
            products = jnp.zeros((8, lanes), F32)
            for c in range(PIX // chunk):
                rows = pl.ds(j * PIX + c * chunk, chunk)
                scaled = (
                    h3[c * chunk : (c + 1) * chunk, n * lanes : (n + 1) * lanes] * vec_ref[0:1, cols]
                )
                pre = scaled + vec_ref[1:2, cols] + x_ref[rows, cols].astype(F32)
                half_pre = pre * 0.5
                a = (1.0 + jnp.tanh(half_pre)) * wide(mask[c * chunk : (c + 1) * chunk], lanes)
                value = half_pre * a
                out_ref[rows, cols] = value.astype(BF16)
                up = cot_ref[rows, cols].astype(F32) * (a * (1.0 + pre - value))
                u3_ref[rows, cols] = (up * vec_ref[2:3, cols]).astype(BF16)
                ups = ups + fold(up)
                products = products + fold(up * scaled)
            acc_ref[0:8, cols] += ups
            acc_ref[8:16, cols] += products


def outer_three_kernel(step, comb_ref, u3_ref, cu_ref):
    if step is BEGIN:
        cu_ref[...] = jnp.zeros_like(cu_ref)
        return

    if step is END:
        return

    cu_ref[...] += dot_rows(comb_ref[...], u3_ref[...])


def back_three_kernel(
    step, per, three_ref, got_ref, hid_ref, comb_ref, u3_ref, a2_ref, slope_ref,
    hat_ref, w3_ref, cu_ref, gw_ref, csum_ref, att_ref, fc_ref, core_ref,
    p_ref, t1_ref, t3_ref, duz_ref, keep_ref, give_ref, fcg_ref, norm_ref, s_ref, c_ref, send_ref, datt_ref, k_ref,
):
    if step is BEGIN:
        mean, inv = three_ref[0:1], three_ref[1:2]
        scale, count = three_ref[2:3], three_ref[3:4]
        sums = total(got_ref)
        dshift = sums[0:1]
        dgain = (sums[1:2] - mean * dshift) * inv
        norm_ref[0:1] = dgain
        norm_ref[1:2] = dshift
        k2 = scale * inv * dgain / count
        k1 = scale * dshift / count - mean * k2
        w3 = w3_ref[...].astype(F32)
        s_ref[...] = dot_last((w3 * k2).astype(BF16), w3_ref[...]).astype(BF16)
        c_ref[...] = high_last(jnp.broadcast_to(k1, (8, C_IN)), w3)
        k_ref[0:1] = k1
        k_ref[1:2] = k2
        return

    if step is END:
        csum = jnp.broadcast_to(csum_ref[...], (8, WIDTH))
        outer = high_rows(csum, jnp.broadcast_to(k_ref[0:1], (8, C_IN))) * 0.125
        w3g = cu_ref[...] - outer - gw_ref[...] * k_ref[1:2]

        def put(core):
            keep_ref[...] = w3g[:, core * 512 : (core + 1) * 512]
            give_ref[...] = w3g[:, (1 - core) * 512 : (2 - core) * 512]

        for core in range(2):
            pl.when(core_ref[0] == core)(functools.partial(put, core))
        att = att_ref[...]
        datt = datt_ref[...]
        both = att * datt
        inner = both[:, :WIDTH] + both[:, WIDTH:]
        dlog = both - att * jnp.concatenate([inner, inner], axis=1)
        zhat, hidden, slope = hid_ref[0], hid_ref[1], hid_ref[2]
        fcg = high_rows(hidden, dlog)
        duz = high_last(dlog, fc_ref[...]) * slope
        duz_ref[...] = duz
        bias = row_sum(dlog)
        rows = [row_sum(duz), row_sum(duz * zhat)]
        for b in range(4):
            cols = slice(b * 128, (b + 1) * 128)
            fcg_ref[pl.ds(b * INTER, INTER)] = fcg[:, cols]
            rows.append(bias[:, cols])
        send_rows(send_ref, rows + [jnp.zeros((2, 128), F32)])
        return

    corr = dot_f(comb_ref[...], s_ref[...])
    p_ref[...] = dot_last(u3_ref[...], w3_ref[...]).astype(BF16)
    for j in range(per):
        image = pl.ds(step * per + j, 1)
        sums = [jnp.zeros((8, WIDTH), F32)] * 6
        for rows, part in chunks(j):
            low = j * PIX + part.start
            dcomb = p_ref[rows].astype(F32) - corr[low : low + CHUNK] - c_ref[0:1]
            for q in range(2):
                cols = slice(q * WIDTH, (q + 1) * WIDTH)
                u = dcomb * slope_ref[rows, cols].astype(F32)
                sums[q] = sums[q] + fold(dcomb * a2_ref[rows, cols].astype(F32))
                sums[2 + q] = sums[2 + q] + fold(u)
                sums[4 + q] = sums[4 + q] + fold(u * hat_ref[rows, cols].astype(F32))
        for k, ref in enumerate((datt_ref, t1_ref, t3_ref)):
            for q in range(2):
                ref[image, q * WIDTH : (q + 1) * WIDTH] = row_sum(sums[2 * k + q])


def back_att_kernel(
    n_images, got_ref, hid_ref, duz_ref, pooled_ref, sides_ref, fc_ref, att_ref,
    t1_ref, t2_ref, t3_ref, t4_ref, fcg_ref, gain_ref,
    dpool_ref, pack_ref, bias_ref, norm_ref, send_ref,
):
    zhat, inv = hid_ref[0], hid_ref[3, 0:1]
    sums = total(got_ref)
    norm_ref[0:1] = sums[1:2]
    norm_ref[1:2] = sums[0:1]
    for b in range(4):
        bias_ref[:, b * 128 : (b + 1) * 128] = sums[2 + b : 3 + b]
    scale = inv * gain_ref[:, 3 * WIDTH : 3 * WIDTH + INTER]
    dzin = scale * (duz_ref[...] - (sums[0:1] + zhat * sums[1:2]) / n_images)
    pack_ref[0:WIDTH] = high_rows(pooled_ref[...], dzin)
    pack_ref[WIDTH:] = fcg_ref[...]
    dpool_ref[...] = high_last(dzin, fc_ref[...])
    for i in range(dpool_ref.shape[0]):
        side = SIDE - 2 * sides_ref[i]
        dpool_ref[i : i + 1] = dpool_ref[i : i + 1] / (side * side).astype(F32)
    dpool = dpool_ref[...]
    both = jnp.concatenate([dpool, dpool], axis=1)
    att = att_ref[...]
    send_rows(
        send_ref,
        [
            row_sum(att * t1_ref[...] + both * t2_ref[...]),
            row_sum(att * t3_ref[...] + both * t4_ref[...]),
        ],
    )


def back_two_kernel(
    step, per, sides_ref, one_ref, two_ref, got_ref, comb_ref, p_ref, s_ref, c_ref, slope_ref, hat2_ref, hat1_ref, att_ref,
    dpool_ref, w_ref, gain_ref, shift_ref, fc_ref, dh2_ref, u1_ref, norm_ref, send_ref,
    vec_ref, pad_ref, acc_ref,
):
    if step is BEGIN:
        count = jnp.concatenate([one_ref[2:3]] * 2, axis=1)
        scale = two_ref[1:2] * gain_ref[:, WIDTH : 3 * WIDTH]
        sums = total(got_ref)
        norm_ref[0:1] = sums[1:2]
        norm_ref[1:2] = sums[0:1]
        vec_ref[0:1] = scale
        vec_ref[1:2] = scale * sums[0:1] / count
        vec_ref[2:3] = scale * sums[1:2] / count
        acc_ref[...] = jnp.zeros_like(acc_ref)
        pad_ref[...] = jnp.zeros_like(pad_ref)
        return

    if step is END:
        rows = []
        for k in range(2):
            both = row_sum(acc_ref[8 * k : 8 * k + 8])
            rows += [both[:, :HALF], both[:, HALF:]]
        sums = jnp.concatenate(rows, axis=0)
        devices, height, _ = send_ref.shape
        for d in range(devices):
            send_ref[d, pl.ds(0, 4)] = sums
            send_ref[d, pl.ds(4, height - 4)] = fc_ref[pl.ds(d * (height - 4), height - 4)]
        return

    first, last = edge_masks(HALF)
    corr = dot_f(comb_ref[...], s_ref[...])
    for j in range(per):
        side = SIDE - 2 * sides_ref[step * per + j]
        mask = pixel_mask(side, 128)
        image = pl.ds(step * per + j, 1)
        dpool = dpool_ref[image]
        for rows, part in chunks(j):
            low = j * PIX + part.start
            dcomb = p_ref[rows].astype(F32) - corr[low : low + CHUNK] - c_ref[0:1]
            for q in range(2):
                cols = slice(q * WIDTH, (q + 1) * WIDTH)
                scale = vec_ref[0:1, cols]
                up = dcomb * (att_ref[image, cols] * scale) + dpool * scale
                dh2 = slope_ref[rows, cols].astype(F32) * up - wide(mask[part], WIDTH) * (
                    vec_ref[1:2, cols] + hat2_ref[rows, cols].astype(F32) * vec_ref[2:3, cols]
                )
                dh2 = dh2.astype(BF16)
                dh2_ref[rows, cols] = dh2
                pad_ref[pl.ds(SIDE + j * (PIX + SIDE) + part.start, CHUNK), cols] = dh2
    height = per * (PIX + SIDE)
    for q in range(2):
        lines = jnp.concatenate(
            [pad_ref[pl.ds(SIDE * (2 - d), height), pl.ds(q * WIDTH, WIDTH)] for d in range(3)],
            axis=1,
        )
        weight = jnp.concatenate(
            [
                jnp.concatenate(
                    [
                        w_ref[pl.ds((3 * r + d) * HALF, HALF), pl.ds(q * WIDTH, WIDTH)]
                        for r in range(3)
                    ],
                    axis=1,
                )
                for d in range(3)
            ],
            axis=0,
        )
        both = dot_last(lines, weight)
        for j in range(per):
            side = SIDE - 2 * sides_ref[step * per + j]
            mask = pixel_mask(side, 128)
            cols = slice(q * HALF, (q + 1) * HALF)
            gain = gain_ref[:, cols] * 0.5
            shift = shift_ref[:, cols] * 0.5
            sums = jnp.zeros((8, HALF), F32)
            products = jnp.zeros((8, HALF), F32)
            for rows, part in chunks(j):
                low = j * (PIX + SIDE) + part.start
                y = both[low : low + CHUNK]
                da1 = (
                    y[:, HALF : 2 * HALF]
                    + pltpu.roll(y[:, :HALF], CHUNK - 1, 0) * last
                    + pltpu.roll(y[:, 2 * HALF :], 1, 0) * first
                )
                hat = hat1_ref[rows, cols].astype(F32)
                half_pre = hat * gain + shift
                a = (1.0 + jnp.tanh(half_pre)) * mask[part]
                u1 = da1 * (a * (0.5 + half_pre - 0.5 * half_pre * a))
                u1_ref[rows, cols] = u1.astype(BF16)
                sums = sums + fold(u1)
                products = products + fold(u1 * hat)
            acc_ref[0:8, cols] += sums
            acc_ref[8:16, cols] += products


def weight_two_kernel(
    step, per, core_ref, sides_ref, hat_ref, dh2_ref, gain_ref, shift_ref, keep_ref, give_ref,
    taps_ref, acc_ref,
):
    if step is BEGIN:
        acc_ref[...] = jnp.zeros_like(acc_ref)
        taps_ref[...] = jnp.zeros_like(taps_ref)
        return

    if step is END:
        def put(core):
            keep_ref[...] = acc_ref[core].T
            give_ref[...] = acc_ref[1 - core].T

        for core in range(2):
            pl.when(core_ref[0] == core)(functools.partial(put, core))
        return

    gain = gain_ref[:, :WIDTH] * 0.5
    shift = shift_ref[:, :WIDTH] * 0.5
    first, last = edge_masks(WIDTH)
    height = PIX + SIDE
    for j in range(per):
        side = SIDE - 2 * sides_ref[step * per + j]
        mask = pixel_mask(side, 128)
        for rows, part in chunks(j):
            half_pre = hat_ref[rows].astype(F32) * gain + shift
            act = half_pre * ((1.0 + jnp.tanh(half_pre)) * wide(mask[part], WIDTH))
            put_taps(taps_ref, j, part, act, first, last)
    for q in range(2):
        patches = jnp.concatenate(
            [
                jnp.concatenate(
                    [
                        taps_ref[pl.ds(SIDE * d + j * height, PIX), pl.ds(q * 384, 384)]
                        for d in range(3)
                    ],
                    axis=1,
                )
                for j in range(per)
            ],
            axis=0,
        )
        acc_ref[q] += dot_rows(dh2_ref[:, q * WIDTH : (q + 1) * WIDTH], patches)


def back_one_kernel(
    step, per, core_ref, sides_ref, one_ref, got_ref, u1_ref, hat_ref, x_ref, gain_ref, norm2_ref,
    norm_att_ref, norm3_ref, dh_ref, keep_ref, give_ref, gain_out_ref, shift_out_ref, vec_ref, acc_ref,
):
    if step is BEGIN:
        count = one_ref[2:3]
        scale = one_ref[1:2] * gain_ref[:, :WIDTH]
        sums = total(got_ref)
        sums = [jnp.concatenate([sums[k : k + 1], sums[k + 1 : k + 2]], axis=1) for k in (0, 2)]
        for row, out_ref in ((0, gain_out_ref), (1, shift_out_ref)):
            out_ref[:, :WIDTH] = sums[1 - row]
            out_ref[:, WIDTH : 3 * WIDTH] = norm2_ref[row : row + 1]
            out_ref[:, 3 * WIDTH : 3 * WIDTH + INTER] = norm_att_ref[row : row + 1]
            out_ref[:, 3 * WIDTH + INTER :] = norm3_ref[row : row + 1]
        vec_ref[0:1] = scale
        vec_ref[1:2] = scale * sums[0] / count
        vec_ref[2:3] = scale * sums[1] / count
        acc_ref[...] = jnp.zeros_like(acc_ref)
        return

    if step is END:

        def put(core):
            keep_ref[...] = acc_ref[core * HALF : (core + 1) * HALF].T
            give_ref[...] = acc_ref[(1 - core) * HALF : (2 - core) * HALF].T

        for core in range(2):
            pl.when(core_ref[0] == core)(functools.partial(put, core))
        return

    for j in range(per):
        side = SIDE - 2 * sides_ref[step * per + j]
        mask = pixel_mask(side, 128)
        for rows, part in chunks(j):
            dh_ref[rows] = (
                u1_ref[rows].astype(F32) * vec_ref[0:1]
                - wide(mask[part], WIDTH) * (vec_ref[1:2] + hat_ref[rows].astype(F32) * vec_ref[2:3])
            ).astype(BF16)
    acc_ref[...] += dot_rows(dh_ref[...], x_ref[...])


def input_grad_kernel(step, dh_ref, u3_ref, three_ref, w_ref, ig_ref, wide_ref):
    if step is BEGIN:
        wide_ref[...] = 1.0 / three_ref[2:3]
        return

    if step is END:
        return

    dx = dot_last(dh_ref[...], w_ref[...])
    for low in range(0, dx.shape[0], 16):
        rows = pl.ds(low, 16)
        ig_ref[rows] = (u3_ref[rows].astype(F32) * wide_ref[...] + dx[low : low + 16]).astype(BF16)


def round_up(value, multiple):
    return -(-value // multiple) * multiple


def two_wide(part, rows):
    missing = 2 * rows - part.shape[0]
    if missing:
        part = jnp.concatenate([part, jnp.zeros((missing, 128), F32)], axis=0)
    return jnp.concatenate([part[:rows], part[rows:]], axis=1)


def slot_rows(two_rows, fc_rows, one_rows, three_rows):
    return (
        round_up(two_rows, 16),
        round_up(fc_rows, 32) // 2,
        round_up(one_rows, 32) // 2,
        round_up(2 * three_rows, 16),
    )


def add_slots(ref, at, rows):
    rows = pl.ds(at, rows)
    both = ref[0, rows].astype(F32)
    for f in range(1, ref.shape[0]):
        both = both + ref[f, rows].astype(F32)
    return both


def lengthen(part, rows):
    if rows == part.shape[0]:
        return part
    return jnp.concatenate([part, jnp.zeros((rows - part.shape[0], part.shape[1]), F32)], axis=0)


def pack_last_kernel(
    fc_rows, keep2_ref, other2_ref, keep1_ref, other1_ref, keep3_ref, other3_ref, got_ref, out_ref
):
    shards = out_ref.shape[0]
    two_rows = keep2_ref.shape[0] // shards
    one_rows = keep1_ref.shape[0] // shards
    three_rows = keep3_ref.shape[0] // shards
    two_slot, fc_slot, one_slot, three_slot = slot_rows(two_rows, fc_rows, one_rows, three_rows)
    fc = two_wide(add_slots(got_ref, 4, fc_rows), fc_slot).astype(BF16)
    for f in range(shards):
        rows = pl.ds(f * two_rows, two_rows)
        part = lengthen(keep2_ref[rows] + other2_ref[rows], two_slot)
        out_ref[f, pl.ds(0, two_slot)] = part.astype(BF16)
        at = two_slot
        out_ref[f, pl.ds(at, fc_slot)] = fc
        at += fc_slot
        rows = pl.ds(f * one_rows, one_rows)
        part = two_wide(keep1_ref[rows] + other1_ref[rows], one_slot)
        out_ref[f, pl.ds(at, one_slot)] = part.astype(BF16)
        at += one_slot
        rows = pl.ds(f * three_rows, three_rows)
        part = keep3_ref[rows] + other3_ref[rows]
        part = jnp.concatenate([part[:, :WIDTH], part[:, WIDTH:]], axis=0)
        out_ref[f, pl.ds(at, three_slot)] = lengthen(part, three_slot).astype(BF16)


def sum_last_kernel(two_rows, fc_rows, one_rows, three_rows, parts_ref, out_ref):
    shards = parts_ref.shape[0]
    two_slot, fc_slot, one_slot, three_slot = slot_rows(two_rows, fc_rows, one_rows, three_rows)
    out_ref[pl.ds(0, two_slot)] = add_slots(parts_ref, 0, two_slot)
    after = two_slot + fc_slot
    out_ref[pl.ds(two_slot, one_slot + three_slot)] = add_slots(
        parts_ref, after, one_slot + three_slot
    )
    at = two_slot + one_slot + three_slot
    for f in range(shards):
        out_ref[pl.ds(at + f * fc_slot, fc_slot)] = parts_ref[f, pl.ds(two_slot, fc_slot)].astype(F32)


def finish_kernel(
    two_rows, fc_rows, one_rows, three_rows, core_ref, mine_ref, other_ref,
    one_ref, two_ref, three_ref, fc1_ref, fc2_ref, pack_ref,
):
    two_slot, fc_slot, one_slot, three_slot = slot_rows(two_rows, fc_rows, one_rows, three_rows)
    at_three = two_slot + one_slot
    at_fc = at_three + three_slot
    shards = (mine_ref.shape[0] - at_fc) // fc_slot

    def tall(ref, at, half_rows, rows):
        both = jnp.concatenate(
            [ref[pl.ds(at, half_rows), :128], ref[pl.ds(at, half_rows), 128:]], axis=0
        )
        return both[:rows]

    def put(half, ref):
        two_ref[:, half * WIDTH : (half + 1) * WIDTH] = ref[pl.ds(0, two_rows)]
        one_ref[:, half * HALF : (half + 1) * HALF] = tall(ref, two_slot, one_slot, one_rows)
        for b in range(2):
            low = (half * 2 + b) * WIDTH
            three_ref[:, low : low + WIDTH] = ref[pl.ds(at_three + b * three_rows, three_rows)]
        for f in range(shards):
            pack_ref[pl.ds((2 * f + half) * fc_rows, fc_rows)] = tall(
                ref, at_fc + f * fc_slot, fc_slot, fc_rows
            )

    for core in range(2):

        @pl.when(core_ref[0] == core)
        def _():
            put(core, mine_ref)
            put(1 - core, other_ref)

    fc1_ref[...] = pack_ref[0:WIDTH]
    for b in range(4):
        fc2_ref[:, b * 128 : (b + 1) * 128] = pack_ref[pl.ds(WIDTH + b * INTER, INTER)]


def everyone(payload):
    return lax.all_to_all(payload, AXES, 0, 0, tiled=True)


def other_core(array):
    return lax.ppermute(array, "dp", [(0, 1), (1, 0)])


def spread_weights(core, weights):
    shards = lax.axis_size("fsdp")
    shapes = [(shards, w.shape[0] * w.shape[1] // 256, 128) for w in weights]
    return call(
        pack_kernel,
        1,
        [(core, SMEM_SPEC)] + [(weight, whole(weight.shape)) for weight in weights],
        [(shape, BF16, whole(shape), True) for shape in shapes],
        flops=1000000,
        moved=4000000,
        name="pack",
    )


def join_weight(core, mine, shape):
    other = other_core(mine)
    rows = shape[0] // mine.shape[0]
    return call(
        unpack_kernel,
        1,
        [(core, SMEM_SPEC), (mine, whole(mine.shape), True), (other, whole(mine.shape), True)],
        [(shape, BF16, whole(shape))],
        [] if rows % 16 == 0 else [pltpu.VMEM(shape, F32)],
        flops=1000000,
        moved=4000000,
        name="unpack",
    )[0]


def slots(parts):
    return lax.all_to_all(parts, "fsdp", 0, 0, tiled=True)


def body(
    inputs,
    sides,
    weight_one,
    weight_two,
    weight_three,
    fc_first,
    fc_second,
    fc_bias,
    bn_gain,
    bn_shift,
    cotangent,
):
    images = inputs.shape[0]
    rows = images * PIX
    devices = lax.axis_size("fsdp") * lax.axis_size("dp")
    n_images = float(images * devices)
    x = inputs.reshape(rows, C_IN)
    cot = cotangent.reshape(rows, C_IN)
    gain = bn_gain.reshape(1, -1)
    shift = bn_shift.reshape(1, -1)
    bias = fc_bias.reshape(1, -1)
    n_ch = gain.shape[1]
    core = lax.axis_index("dp").astype(jnp.int32).reshape(1)

    def split(most):
        per = max(n for n in range(1, most + 1) if images % n == 0)
        return per, images // per

    core_in = (core, SMEM_SPEC)
    sides_in = (sides, SMEM_SPEC)
    gain_in = (gain, whole((1, n_ch)))
    shift_in = (shift, whole((1, n_ch)))

    def payload(k, n):
        return ((devices, k, n), F32, whole((devices, k, n)), True)

    def small(*shape):
        return (shape, F32, whole(shape))

    def full(array):
        return (array, whole(array.shape))

    def near(array):
        return (array, whole(array.shape), True)

    def blocks(array):
        return (array, Stream())

    def blocks_out(width, dtype=BF16, over=None):
        return ((rows, width), dtype, Stream(over))

    spread_one, spread_two, spread_three = spread_weights(
        core, (weight_one, weight_two, weight_three)
    )
    mine = slots(spread_one)
    other = other_core(mine)
    spread_two, mine, other = lax.optimization_barrier((spread_two, mine, other))
    mine_two = slots(spread_two)

    per, steps = split(PER_CONV_ONE)
    h1, full_one, send = stream_call(
        lambda step, *refs, per=per: conv_one_kernel(step, per, *refs),
        per,
        steps,
        [core_in, sides_in, blocks(x), near(mine), near(other)],
        [blocks_out(WIDTH, F32), ((C_IN, WIDTH), BF16, whole((C_IN, WIDTH))), payload(4, WIDTH)],
        [pltpu.VMEM((16, WIDTH), F32), pltpu.SMEM((1,), F32)],
        flops=2 * rows * C_IN * WIDTH,
        moved=rows * C_IN * 2 + rows * WIDTH * 4,
        name="conv_one",
    )
    send, mine_two = lax.optimization_barrier((send, mine_two))
    got_one = everyone(send)
    full_two = join_weight(core, mine_two, (9 * HALF, 2 * WIDTH))
    got_one, spread_three, full_two = lax.optimization_barrier((got_one, spread_three, full_two))
    mine_three = slots(spread_three)

    per, steps = split(PER_CONV_TWO)
    hat1, h2, stat1, send = stream_call(
        lambda step, *refs, per=per: conv_two_kernel(step, per, *refs),
        per,
        steps,
        [sides_in, near(got_one), blocks(h1), full(full_two), gain_in, shift_in],
        [blocks_out(WIDTH), blocks_out(2 * WIDTH, F32), small(8, WIDTH), payload(2, 2 * WIDTH)],
        [
            pltpu.VMEM((per * (PIX + SIDE) + 2 * SIDE, 6 * HALF), BF16),
            pltpu.VMEM((16, 2 * WIDTH), F32),
        ],
        flops=2 * rows * 9 * HALF * 2 * WIDTH,
        moved=rows * WIDTH * 14,
        name="conv_two",
    )
    send, mine_three = lax.optimization_barrier((send, mine_three))
    got_two = everyone(send)

    per, steps = split(PER_ACT_TWO)
    hat2, a2, slope2, pooled, zin, t2, t4, stat2, send = stream_call(
        lambda step, *refs, per=per: act_two_kernel(step, per, *refs),
        per,
        steps,
        [
            sides_in,
            full(stat1),
            near(got_two),
            blocks(h2),
            gain_in,
            shift_in,
            full(fc_first),
        ],
        [
            blocks_out(2 * WIDTH),
            blocks_out(2 * WIDTH),
            blocks_out(2 * WIDTH),
            small(images, WIDTH),
            small(images, INTER),
            small(images, 2 * WIDTH),
            small(images, 2 * WIDTH),
            small(8, 2 * WIDTH),
            payload(2, INTER),
        ],
        flops=rows * 2 * WIDTH * 20,
        moved=rows * 2 * WIDTH * 10,
        name="act_two",
    )
    send, mine_three = lax.optimization_barrier((send, mine_three))
    got_att = everyone(send)
    full_three = join_weight(core, mine_three, (WIDTH, C_IN))

    per, steps = split(PER_COMBINE)
    att, comb, gw, csum, hid, send = stream_call(
        lambda step, *refs, per=per: combine_kernel(step, per, n_images, *refs),
        per,
        steps,
        [
            near(got_att),
            full(zin),
            blocks(a2),
            full(full_three),
            full(fc_second),
            full(bias),
            gain_in,
            shift_in,
        ],
        [
            small(images, 2 * WIDTH),
            blocks_out(WIDTH),
            small(WIDTH, C_IN),
            small(1, WIDTH),
            small(4, images, INTER),
            payload(2, C_IN),
        ],
        [pltpu.VMEM((WIDTH, WIDTH), F32), pltpu.VMEM((8, WIDTH), F32)],
        flops=2 * rows * WIDTH * WIDTH,
        moved=rows * WIDTH * 6,
        name="combine",
    )
    got_three = everyone(send)

    per, steps = split(PER_OUTPUT)
    outputs, u3, stat3, send = stream_call(
        lambda step, *refs, per=per: output_kernel(step, per, *refs),
        per,
        steps,
        [
            sides_in,
            full(stat1),
            near(got_three),
            blocks(comb),
            blocks(x),
            blocks(cot),
            full(full_three),
            gain_in,
            shift_in,
        ],
        [
            blocks_out(C_IN, over=4),
            blocks_out(C_IN, over=5),
            small(8, C_IN),
            payload(2, C_IN),
        ],
        [pltpu.VMEM((8, C_IN), F32), pltpu.VMEM((16, C_IN), F32)],
        flops=2 * rows * WIDTH * C_IN,
        moved=rows * C_IN * 8,
        name="output",
    )
    got_back_three = everyone(send)

    per, steps = split(PER_OUTER_THREE)
    (cu,) = stream_call(
        outer_three_kernel,
        per,
        steps,
        [blocks(comb), blocks(u3)],
        [small(WIDTH, C_IN)],
        flops=2 * rows * WIDTH * C_IN,
        moved=rows * C_IN * 3,
        name="outer_three",
    )

    per, steps = split(PER_BACK_THREE)
    p, t1, t3, duz, keep_three, give_three, fc2_local, norm3, corr_weight, corr_row, send = stream_call(
        lambda step, *refs, per=per: back_three_kernel(step, per, *refs),
        per,
        steps,
        [
            full(stat3),
            near(got_back_three),
            full(hid),
            blocks(comb),
            blocks(u3),
            blocks(a2),
            blocks(slope2),
            blocks(hat2),
            full(full_three),
            full(cu),
            full(gw),
            full(csum),
            full(att),
            full(fc_second),
            core_in,
        ],
        [
            blocks_out(WIDTH, over=3),
            small(images, 2 * WIDTH),
            small(images, 2 * WIDTH),
            small(images, INTER),
            small(WIDTH, C_IN // 2),
            small(WIDTH, C_IN // 2),
            small(4 * INTER, 128),
            small(2, C_IN),
            ((WIDTH, WIDTH), BF16, whole((WIDTH, WIDTH))),
            small(8, WIDTH),
            payload(8, INTER),
        ],
        [pltpu.VMEM((images, 2 * WIDTH), F32), pltpu.VMEM((2, C_IN), F32)],
        flops=4 * rows * WIDTH * C_IN,
        moved=rows * WIDTH * 16,
        name="back_three",
    )
    got_back_att = everyone(send)

    dpool, packed, fc_bias_grad, norm_att, send = call(
        functools.partial(back_att_kernel, n_images),
        1,
        [
            near(got_back_att),
            full(hid),
            full(duz),
            full(pooled),
            sides_in,
            full(fc_first),
            full(att),
            full(t1),
            full(t2),
            full(t3),
            full(t4),
            full(fc2_local),
            gain_in,
        ],
        [
            small(images, WIDTH),
            small(WIDTH + 4 * INTER, 128),
            small(1, 2 * WIDTH),
            small(2, INTER),
            payload(2, 2 * WIDTH),
        ],
        flops=10000000,
        moved=1000000,
        name="back_att",
    )
    got_back_two = everyone(send)
    shards = lax.axis_size("fsdp")
    w3_rows = WIDTH // shards
    fc_rows = packed.shape[0] // devices

    per, steps = split(PER_BACK_TWO)
    dh2, u1, norm2, send = stream_call(
        lambda step, *refs, per=per: back_two_kernel(step, per, *refs),
        per,
        steps,
        [
            sides_in,
            full(stat1),
            full(stat2),
            near(got_back_two),
            blocks(comb),
            blocks(p),
            full(corr_weight),
            full(corr_row),
            blocks(slope2),
            blocks(hat2),
            blocks(hat1),
            full(att),
            full(dpool),
            full(full_two),
            gain_in,
            shift_in,
            full(packed),
        ],
        [
            blocks_out(2 * WIDTH),
            blocks_out(WIDTH),
            small(2, 2 * WIDTH),
            payload(4 + fc_rows, 128),
        ],
        [
            pltpu.VMEM((8, 2 * WIDTH), F32),
            pltpu.VMEM((per * (PIX + SIDE) + 2 * SIDE, 2 * WIDTH), BF16),
            pltpu.VMEM((16, WIDTH), F32),
        ],
        flops=2 * rows * 9 * HALF * 2 * WIDTH,
        moved=rows * WIDTH * 20,
        name="back_two",
    )
    got_back_one = everyone(send)

    per, steps = split(PER_WEIGHT_TWO)
    half = (9 * HALF, WIDTH)
    keep, give = stream_call(
        lambda step, *refs, per=per: weight_two_kernel(step, per, *refs),
        per,
        steps,
        [core_in, sides_in, blocks(hat1), blocks(dh2), gain_in, shift_in],
        [(half, F32, whole(half)), (half, F32, whole(half))],
        [
            pltpu.VMEM((per * (PIX + SIDE) + 2 * SIDE, 6 * HALF), BF16),
            pltpu.VMEM((2, WIDTH, 9 * HALF), F32),
        ],
        flops=2 * rows * 9 * HALF * 2 * WIDTH,
        moved=rows * WIDTH * 6,
        name="weight_two",
    )
    got_back_one, keep, give = lax.optimization_barrier((got_back_one, keep, give))
    per, steps = split(PER_BACK_ONE)
    half_one = (C_IN, HALF)
    dh1, keep_one, give_one, gain_grad, shift_grad = stream_call(
        lambda step, *refs, per=per: back_one_kernel(step, per, *refs),
        per,
        steps,
        [
            core_in,
            sides_in,
            full(stat1),
            near(got_back_one),
            blocks(u1),
            blocks(hat1),
            blocks(x),
            gain_in,
            full(norm2),
            full(norm_att),
            full(norm3),
        ],
        [
            blocks_out(WIDTH),
            small(*half_one),
            small(*half_one),
            small(1, n_ch),
            small(1, n_ch),
        ],
        [pltpu.VMEM((8, WIDTH), F32), pltpu.VMEM((WIDTH, C_IN), F32)],
        flops=2 * rows * WIDTH * C_IN,
        moved=rows * C_IN * 4,
        name="back_one",
    )

    two_rows, one_rows = 9 * HALF // shards, C_IN // shards
    two_slot, fc_slot, one_slot, three_slot = slot_rows(two_rows, fc_rows, one_rows, w3_rows)
    slot = (shards, two_slot + fc_slot + one_slot + three_slot, WIDTH)
    (parts,) = call(
        functools.partial(pack_last_kernel, fc_rows),
        1,
        [
            full(keep),
            near(other_core(give)),
            full(keep_one),
            near(other_core(give_one)),
            full(keep_three),
            near(other_core(give_three)),
            near(got_back_one),
        ],
        [(slot, BF16, whole(slot))],
        flops=1000000,
        moved=5000000,
        name="pack_last",
    )
    dh1, parts = lax.optimization_barrier((dh1, parts))
    parts = slots(parts)

    per, steps = split(PER_INPUT_GRAD)
    (input_grad,) = stream_call(
        input_grad_kernel,
        per,
        steps,
        [blocks(dh1), blocks(u3), full(stat3), full(full_one)],
        [blocks_out(C_IN, over=1)],
        [pltpu.VMEM((1, C_IN), F32)],
        flops=2 * rows * WIDTH * C_IN,
        moved=rows * C_IN * 5,
        name="input_grad",
    )

    parts, input_grad = lax.optimization_barrier((parts, input_grad))
    sums = (two_slot + one_slot + three_slot + shards * fc_slot, WIDTH)
    (mine,) = call(
        functools.partial(sum_last_kernel, two_rows, fc_rows, one_rows, w3_rows),
        1,
        [near(parts)],
        [(sums, F32, whole(sums), True)],
        flops=1000000,
        moved=2000000,
        name="sum_last",
    )
    (weight_one_grad, weight_two_grad, weight_three_grad, fc_first_grad, fc_second_grad) = call(
        functools.partial(finish_kernel, two_rows, fc_rows, one_rows, w3_rows),
        1,
        [core_in, near(mine), near(other_core(mine))],
        [
            small(one_rows, WIDTH),
            small(two_rows, 2 * WIDTH),
            small(w3_rows, C_IN),
            small(WIDTH, INTER),
            small(INTER, 2 * WIDTH),
        ],
        [pltpu.VMEM((2 * shards * fc_rows, 128), F32)],
        flops=1000000,
        moved=2000000,
        name="finish",
    )
    return (
        outputs.reshape(inputs.shape),
        input_grad.reshape(inputs.shape),
        weight_one_grad,
        weight_two_grad,
        weight_three_grad,
        fc_first_grad,
        fc_second_grad,
        fc_bias_grad.reshape(-1),
        gain_grad.reshape(-1),
        shift_grad.reshape(-1),
    )


def solution(mesh):
    return jax.shard_map(
        body,
        mesh=mesh,
        in_specs=(
            P(("fsdp", "dp"), None, None),
            P(("fsdp", "dp")),
            P("fsdp", None),
            P("fsdp", None),
            P("fsdp", None),
            P(),
            P(),
            P(),
            P(),
            P(),
            P(("fsdp", "dp"), None, None),
        ),
        out_specs=(
            P(("fsdp", "dp"), None, None),
            P(("fsdp", "dp"), None, None),
            P("fsdp", None),
            P("fsdp", None),
            P("fsdp", None),
            P(),
            P(),
            P(),
            P(),
            P(),
        ),
        check_vma=False,
    )
```
